128 devices in a mesh: fsdp: 8 (over x, z_hi), seq: 16 (over z_lo, y, core).
Axes of the slice: x: 4, y: 4, z: 4 (z_hi: 2, z_lo: 2; z = z_hi * 2 + z_lo), core: 2. Of those that a mesh axis runs over, the one named last changes fastest.
Arguments:
- inputs: bfloat16 [8, 6144, 768], P('fsdp', 'seq'), may hold values from -6 to 6
- first_gain: bfloat16 [768], P('fsdp'), may hold values from 0.5 to 1.5
- joint_weight: bfloat16 [768, 2304], P('fsdp'), may hold values from -0.21875 to 0.21875
- merge_weight: bfloat16 [768, 768], P('fsdp'), may hold values from -1.25 to 1.25
- second_gain: bfloat16 [768], P('fsdp'), may hold values from 0.5 to 1.5
- expand_weight: bfloat16 [768, 2304], P('fsdp'), may hold values from -0.21875 to 0.21875
- shrink_weight: bfloat16 [1152, 768], P('fsdp'), may hold values from -0.375 to 0.375
- cotangent: bfloat16 [8, 6144, 768], P('fsdp', 'seq'), may hold values from -6 to 6
Outputs:
- block_out: bfloat16 [8, 6144, 768], P('fsdp', 'seq')
- input_grad: bfloat16 [8, 6144, 768], P('fsdp', 'seq')
- first_grad: float32 [768], P('fsdp')
- joint_grad: float32 [768, 2304], P('fsdp')
- merge_grad: float32 [768, 768], P('fsdp')
- second_grad: float32 [768], P('fsdp')
- expand_grad: float32 [768, 2304], P('fsdp')
- shrink_grad: float32 [1152, 768], P('fsdp')
The draws below stay inside these ranges and needn't reach their ends.
All inputs are finite; a program needn't handle non-finite values.
Results may differ from the reference program's by a relative error of at most 0.025.
Values may be sent and summed in bfloat16 or wider, within the bound.
No kernel may reach another device: no remote copies, remote signals or barrier semaphores. Data moves between devices by JAX's collectives and lax.ppermute only.
A program may use at most 128 MiB of HBM per device.

```python
import math
import jax
import jax.numpy as jnp
from jax import lax

D = 768
HEADS = 12
HEAD_DIM = 64
FF = 1152
WINDOW = 128
LENGTH = 6144
SEQS = 8


def steps_of(key, dims, pieces, low, largest):
    factor_of = 1.0
    for position, shards_of in pieces:
        draws = jax.random.uniform(jax.random.fold_in(jax.random.fold_in(key, 6), position), (shards_of,), jnp.float32, low / len(pieces), largest / len(pieces))
        factor_of = factor_of * jnp.repeat(jnp.exp(draws), dims[position] // shards_of).reshape((-1,) + (1,) * (len(dims) - 1 - position))
    return factor_of


def gaussian(stream_key, dims, scale, reach, cuts=(), kind=jnp.bfloat16):
    array = jax.random.normal(stream_key, dims, jnp.float32) * scale
    if len(cuts) > 0:
        array = steps_of(stream_key, dims, cuts, -0.22, 0.18) * array
    return jnp.clip(array, min=-reach, max=reach).astype(kind)


def setup_inputs(seed: int = 0) -> dict:
    streams_of = jax.random.split(jax.random.key(seed), 9)
    return {
        "inputs": gaussian(streams_of[0], (SEQS, LENGTH, D), 1.0, 6.0, ((0, 8), (1, 16))),
        "first_gain": jnp.clip(1.0 + 0.1 * jax.random.normal(streams_of[1], (D,), jnp.float32), 0.5, 1.5).astype(jnp.bfloat16),
        "joint_weight": gaussian(streams_of[2], (D, 3 * D), D ** -0.5, 0.21875, ((0, 8),)),
        "merge_weight": gaussian(streams_of[3], (D, D), (D // 32) ** -0.5, 1.25, ((0, 8),)),
        "second_gain": jnp.clip(1.0 + 0.1 * jax.random.normal(streams_of[4], (D,), jnp.float32), 0.5, 1.5).astype(jnp.bfloat16),
        "expand_weight": gaussian(streams_of[5], (D, 2 * FF), D ** -0.5, 0.21875, ((0, 8),)),
        "shrink_weight": gaussian(streams_of[6], (FF, D), (FF // 4) ** -0.5, 0.375, ((0, 8),)),
        "cotangent": gaussian(streams_of[7], (SEQS, LENGTH, D), 1.0, 6.0, ((0, 8), (1, 16))),
    }


@jax.custom_vjp
def low(v):
    return lax.optimization_barrier(v.astype(jnp.bfloat16)).astype(jnp.float32)

@jax.custom_vjp
def low_back(v):
    return v

def low_keep(v):
    return (low(v), None)

def low_pass(kept, grad):
    return (grad,)

def back_keep(v):
    return (v, None)

def back_low(kept, grad):
    return (low(grad),)
low.defvjp(low_keep, low_pass)
low_back.defvjp(back_keep, back_low)
epsilon = 1e-05
precise = lax.Precision.HIGHEST
query_block = 512

def matmul(left, right):
    return jnp.dot(left, right, precision=precise, preferred_element_type=jnp.float32)

def layer_norm(values, gain):
    centred = values - lax.optimization_barrier(jnp.mean(values, axis=-1, keepdims=True))
    spread = lax.optimization_barrier(jnp.mean(centred * centred, axis=-1, keepdims=True))
    return centred * lax.rsqrt(spread + epsilon) * gain

def rotate(values, cosine, sine):
    middle = values.shape[-1] // 2
    former = values[..., :middle]
    latter = values[..., middle:]
    return jnp.concatenate([former * cosine - latter * sine, latter * cosine + former * sine], axis=-1)

def sequence_forward(row, first_gain, joint_weight, merge_weight, second_gain, expand_weight, shrink_weight):
    length = row.shape[0]
    rim_width = WINDOW // 2
    normed = low(layer_norm(row, first_gain))
    joint = low_back(matmul(normed, joint_weight))
    frequencies = jnp.exp(jnp.arange(HEAD_DIM // 2, dtype=jnp.float32) * (-2.0 * math.log(10000.0) / HEAD_DIM))
    angles = jnp.arange(length, dtype=jnp.float32)[:, None] * frequencies[None, :]
    cosine = jnp.cos(angles)[:, None, :]
    sine = jnp.sin(angles)[:, None, :]
    queries = low(rotate(joint[:, :D].reshape(length, HEADS, HEAD_DIM), cosine, sine))
    keys_rot = low(rotate(joint[:, D:2 * D].reshape(length, HEADS, HEAD_DIM), cosine, sine))
    values = low(joint[:, 2 * D:].reshape(length, HEADS, HEAD_DIM))
    padded_keys = jnp.pad(keys_rot, ((rim_width, rim_width), (0, 0), (0, 0)))
    padded_values = jnp.pad(values, ((rim_width, rim_width), (0, 0), (0, 0)))
    span = query_block + 2 * rim_width

    def block(start):
        q_part = lax.dynamic_slice_in_dim(queries, start, query_block, 0)
        k_part = lax.dynamic_slice_in_dim(padded_keys, start, span, 0)
        v_part = lax.dynamic_slice_in_dim(padded_values, start, span, 0)
        scores = low_back(jnp.einsum('qhd,khd->hqk', q_part, k_part, precision=precise) * (1.0 / math.sqrt(HEAD_DIM)))
        query_pos = lax.broadcasted_iota(jnp.int32, (query_block, span), 0) + start
        key_pos = lax.broadcasted_iota(jnp.int32, (query_block, span), 1) + start - rim_width
        allowed = (jnp.abs(query_pos - key_pos) <= rim_width) & (key_pos >= 0) & (key_pos < length)
        scores = jnp.where(allowed[None], scores, -1e+30)
        highest = lax.optimization_barrier(jnp.max(scores, axis=-1, keepdims=True))
        expo = jnp.exp(scores - highest)
        probs = low(expo / lax.optimization_barrier(jnp.sum(expo, axis=-1, keepdims=True)))
        return jnp.einsum('hqk,khd->qhd', probs, v_part, precision=precise)
    starts = jnp.arange(length // query_block, dtype=jnp.int32) * query_block
    mixed = lax.map(jax.checkpoint(block), starts).reshape(length, D)
    attended = low_back(low(mixed))
    first_res = row + low_back(matmul(attended, merge_weight))
    normed_two = low(layer_norm(first_res, second_gain))
    expanded = low_back(matmul(normed_two, expand_weight))
    hidden_val = low(jax.nn.gelu(expanded[:, :FF], approximate=False) * expanded[:, FF:])
    return first_res + low_back(matmul(hidden_val, shrink_weight))

def reference(inputs, first_gain, joint_weight, merge_weight, second_gain, expand_weight, shrink_weight, cotangent):
    floats = tuple((item.astype(jnp.float32) for item in (inputs, first_gain, joint_weight, merge_weight, second_gain, expand_weight, shrink_weight)))

    def whole(series, gain_one, joint_w, merge_w, gain_two, expand_w, shrink_w):

        def single(row):
            return sequence_forward(row, gain_one, joint_w, merge_w, gain_two, expand_w, shrink_w)
        return lax.map(jax.checkpoint(single), series)
    result, pullback = jax.vjp(whole, *floats)
    grads = pullback(cotangent.astype(jnp.float32))
    return (result.astype(jnp.bfloat16), grads[0].astype(jnp.bfloat16), grads[1], grads[2], grads[3], grads[4], grads[5], grads[6])
```

```python
import math

import jax
import jax.numpy as jnp
from jax import lax
from jax.sharding import PartitionSpec as P

D = 768
HEADS = 12
HEAD_DIM = 64
FF = 1152
WINDOW = 128
RIM = WINDOW // 2
EPSILON = 1e-05
F32 = jnp.float32
BF16 = jnp.bfloat16


def over_fsdp(value, dx, dz):
    pairs = [
        (x * 2 + z, ((x + dx) % 4) * 2 + (z + dz) % 2) for x in range(4) for z in range(2)
    ]
    return lax.ppermute(value, "fsdp", pairs)


def over_seq(value, dz, dy, dc):
    pairs = [
        (z * 8 + y * 2 + c, ((z + dz) % 2) * 8 + ((y + dy) % 4) * 2 + (c + dc) % 2)
        for z in range(2)
        for y in range(4)
        for c in range(2)
    ]
    return lax.ppermute(value, "seq", pairs)


def core_swap(value):
    return over_seq(value, 0, 0, 1)


def passed_along(value, steps):
    first, last = (max(0, -steps), min(16, 16 - steps))
    return lax.ppermute(value, "seq", [(i, i + steps) for i in range(first, last)])


def gather_pieces(own):
    from_low = over_fsdp(own, 1, 0)
    from_high = over_fsdp(own, -1, 0)
    across = over_fsdp(own, 0, 1)
    from_far = over_fsdp(own, 2, 0)
    across_low = over_fsdp(across, 1, 0)
    across_high = over_fsdp(across, -1, 0)
    across_far = over_fsdp(from_far, 0, 1)
    return [own, across, from_high, across_high, from_far, across_far, from_low, across_low]


def assembled(pieces, core, x, zh):
    mine = jnp.stack(pieces)
    other = core_swap(mine)
    halves = jnp.where(core == 0, jnp.stack([mine, other], 1), jnp.stack([other, mine], 1))
    rel = halves.reshape((4, 2) + halves.shape[1:])
    rel = jnp.where(zh == 0, rel, rel[:, ::-1])
    twice = jnp.concatenate([rel, rel], 0)
    out = lax.dynamic_slice_in_dim(twice, (4 - x) % 4, 4, 0)
    return out.reshape((8,) + halves.shape[1:])


def spread_sum(parts, x, zh):
    by_x = parts.reshape((4, 2) + parts.shape[1:])

    def block(dx):
        return lax.dynamic_index_in_dim(by_x, (x + dx) % 4, 0, keepdims=False)

    got = [over_fsdp(block(d), d, 0) for d in (1, -1, 2)]
    total = block(0).astype(F32) + sum(g.astype(F32) for g in got)
    total = total.astype(BF16)
    keep = jnp.where(zh == 0, total[0], total[1])
    give = jnp.where(zh == 0, total[1], total[0])
    total = (keep.astype(F32) + over_fsdp(give, 0, 1).astype(F32)).astype(BF16)
    low, high, far = (over_seq(total, 0, d, 0) for d in (1, -1, 2))
    total = (
        (total.astype(F32) + far.astype(F32)) + (low.astype(F32) + high.astype(F32))
    ).astype(BF16)
    return (total.astype(F32) + over_seq(total, 1, 0, 0).astype(F32)).astype(BF16)


def outer_sum(left, right):
    return lax.dot_general(
        left, right, (((0,), (0,)), ((), ())), preferred_element_type=jnp.float32
    )


def back_product(left, weight):
    return lax.dot_general(
        left, weight, (((1,), (1,)), ((), ())), preferred_element_type=jnp.float32
    )


def normalize(values):
    centred = values - jnp.mean(values, axis=-1, keepdims=True)
    spread = jnp.mean(centred * centred, axis=-1, keepdims=True)
    inverse = lax.rsqrt(spread + EPSILON)
    return (centred * inverse, inverse)


def norm_back(upstream, normed, inverse, gain):
    gain_part = jnp.sum(upstream * normed, axis=0)
    scaled = upstream * gain
    centred = scaled - jnp.mean(scaled, axis=-1, keepdims=True)
    return (
        inverse * (centred - normed * jnp.mean(scaled * normed, axis=-1, keepdims=True)),
        gain_part,
    )


def rotate(values, cosine, sine):
    middle = values.shape[-1] // 2
    former = values[..., :middle]
    latter = values[..., middle:]
    return jnp.concatenate(
        [former * cosine - latter * sine, latter * cosine + former * sine], axis=-1
    )


def unrotate(upstream, cosine, sine):
    return rotate(upstream, cosine, -sine)


def band_windows(extended, tokens, tile_rows):
    tiles = tokens // tile_rows
    lower = extended[:tokens].reshape(tiles, tile_rows, extended.shape[1])
    upper = extended[tile_rows : tokens + tile_rows].reshape(tiles, tile_rows, extended.shape[1])
    return jnp.concatenate([lower, upper], axis=1)


def band_scores(queries, keys_all, offset, seq_length):
    scores = jnp.einsum(
        "tqhd,tkhd->thqk", queries, keys_all, preferred_element_type=jnp.float32
    ) * (1.0 / math.sqrt(HEAD_DIM))
    shape = (queries.shape[0], queries.shape[1], keys_all.shape[1])
    query_pos = lax.broadcasted_iota(jnp.int32, shape, 1)
    key_pos = lax.broadcasted_iota(jnp.int32, shape, 2) - RIM
    tile_base = lax.broadcasted_iota(jnp.int32, shape, 0) * queries.shape[1]
    global_key = offset + tile_base + key_pos
    allowed = (
        (jnp.abs(query_pos - key_pos) <= RIM) & (global_key >= 0) & (global_key < seq_length)
    )
    return jnp.where(allowed[:, None], scores, -1e30)


def column_half(value, core):
    width = value.shape[1] // 2
    mine = lax.dynamic_slice_in_dim(value, core * width, width, 1)
    other = lax.dynamic_slice_in_dim(value, (1 - core) * width, width, 1)
    return mine, other


def pair_outer(left, right, core):
    mine, give = column_half(right, core)
    got = core_swap(give)
    left_other = core_swap(left)
    return outer_sum(left, mine) + outer_sum(left_other, got)


def joined(total, core):
    other = core_swap(total)
    return jnp.where(
        core == 0,
        jnp.concatenate([total, other], 1),
        jnp.concatenate([other, total], 1),
    ).astype(F32)


def shards(
    inputs,
    first_gain,
    joint_weight,
    merge_weight,
    second_gain,
    expand_weight,
    shrink_weight,
    cotangent,
):
    tokens = inputs.shape[1]
    tile_rows = 2 * RIM
    tiles = tokens // tile_rows
    fsdp, seq = lax.axis_index("fsdp"), lax.axis_index("seq")
    x, zh, core = fsdp // 2, fsdp % 2, seq % 2
    offset = seq * tokens
    seq_length = tokens * 16
    rows = joint_weight.shape[0]

    def half(w):
        n = w.shape[0] // 2
        return lax.dynamic_slice_in_dim(w, core * n, n, 0)

    gains = jnp.zeros((rows // 2, 128), BF16)
    gains = gains.at[0, :rows].set(first_gain).at[1, :rows].set(second_gain)
    first_group = gather_pieces(jnp.concatenate([half(joint_weight), gains], 1))
    low_halo = passed_along(inputs[0, tokens - RIM :], 1)
    high_halo = passed_along(inputs[0, :RIM], -1)
    first_all = assembled(first_group, core, x, zh)
    joint_w = first_all[:, :, :, : 3 * D].reshape(D, 3 * D)
    gain_one = first_all[:, 0, 0, 3 * D : 3 * D + rows].reshape(D).astype(F32)
    gain_two = first_all[:, 0, 1, 3 * D : 3 * D + rows].reshape(D).astype(F32)
    expand_h = half(expand_weight)
    second_own = jnp.concatenate(
        [half(merge_weight)]
        + [expand_h[:, i * D : (i + 1) * D] for i in range(3)]
        + [half(shrink_weight)],
        0,
    )
    second_all = assembled(gather_pieces(second_own), core, x, zh)
    hr = rows // 2
    merge_w = second_all[:, :, :hr].reshape(D, D)
    expand_w = jnp.concatenate(
        [second_all[:, :, hr * (i + 1) : hr * (i + 2)].reshape(D, D) for i in range(3)], 1
    )
    shrink_w = second_all[:, :, hr * 4 :].reshape(FF, D)

    frequencies = jnp.exp(
        jnp.arange(HEAD_DIM // 2, dtype=jnp.float32) * (-2.0 * math.log(10000.0) / HEAD_DIM)
    )
    wide = tokens + 2 * RIM
    positions = (offset - RIM + lax.iota(jnp.int32, wide)).astype(jnp.float32)
    angles = positions[:, None] * frequencies[None, :]
    cosine = jnp.cos(angles)[:, None, :]
    sine = jnp.sin(angles)[:, None, :]
    own = slice(RIM, RIM + tokens)
    extended = jnp.concatenate([low_halo, inputs[0], high_halo], 0).astype(F32)
    source = inputs[0].astype(jnp.float32)
    normed_one, inverse_one = normalize(extended)
    h_first = (normed_one * gain_one).astype(jnp.bfloat16)
    joint = jnp.dot(h_first, joint_w, preferred_element_type=jnp.float32)
    queries = rotate(
        joint[own, :D].reshape(tokens, HEADS, HEAD_DIM), cosine[own], sine[own]
    ).astype(jnp.bfloat16)
    keys_rot = rotate(joint[:, D : 2 * D].reshape(wide, HEADS, HEAD_DIM), cosine, sine).astype(
        jnp.bfloat16
    )
    values_b = joint[:, 2 * D :].astype(jnp.bfloat16)
    paired = jnp.concatenate([keys_rot.reshape(wide, D), values_b], axis=1)
    windows = band_windows(paired, tokens, tile_rows)
    col_count = windows.shape[1]
    keys_all = windows[:, :, :D].reshape(tiles, col_count, HEADS, HEAD_DIM)
    values_all = windows[:, :, D:].reshape(tiles, col_count, HEADS, HEAD_DIM)
    queries_t = queries.reshape(tiles, tile_rows, HEADS, HEAD_DIM)
    scores = band_scores(queries_t, keys_all, offset, seq_length)
    highest = jnp.max(scores, axis=-1, keepdims=True)
    expo = jnp.exp(scores - highest)
    totals = jnp.sum(expo, axis=-1, keepdims=True)
    log_total = highest + jnp.log(totals)
    probs_b = (expo / totals).astype(jnp.bfloat16)
    mixed = jnp.einsum("thqk,tkhd->tqhd", probs_b, values_all, preferred_element_type=jnp.float32)
    attended = mixed.reshape(tokens, D).astype(jnp.bfloat16)
    first_res = source + jnp.dot(attended, merge_w, preferred_element_type=jnp.float32)
    normed_two, inverse_two = normalize(first_res)
    h_second = (normed_two * gain_two).astype(jnp.bfloat16)
    expanded = jnp.dot(h_second, expand_w, preferred_element_type=jnp.float32)
    gate_val = expanded[:, :FF]
    up_val = expanded[:, FF:]

    def geglu(gate_in, up_in):
        return jax.nn.gelu(gate_in, approximate=False) * up_in

    activated, geglu_pull = jax.vjp(geglu, gate_val, up_val)
    hidden_b = activated.astype(jnp.bfloat16)
    result = (first_res + jnp.dot(hidden_b, shrink_w, preferred_element_type=jnp.float32)).astype(
        jnp.bfloat16
    )
    upstream = cotangent[0].astype(jnp.float32)
    upstream_b = cotangent[0]
    shrink_part = pair_outer(hidden_b, upstream_b, core)
    hidden_grad = back_product(upstream_b, shrink_w)
    gate_grad, up_grad = geglu_pull(hidden_grad)
    expand_in = jnp.concatenate([gate_grad, up_grad], axis=1).astype(jnp.bfloat16)
    expand_part = pair_outer(h_second, expand_in, core)
    second_up = back_product(expand_in, expand_w)
    res_back, second_part = norm_back(second_up, normed_two, inverse_two, gain_two)
    first_res_grad = upstream + res_back
    res_grad_b = first_res_grad.astype(jnp.bfloat16)
    merge_part = pair_outer(attended, res_grad_b, core)
    early = jnp.concatenate(
        [
            merge_part.reshape(8, rows, D // 2),
            expand_part[:, :384].reshape(8, rows, D // 2),
            expand_part[:, 384:768].reshape(8, rows, D // 2),
            expand_part[:, 768:].reshape(8, rows, D // 2),
            shrink_part.reshape(8, -1, D // 2),
        ],
        1,
    ).astype(BF16)
    early_sum = joined(spread_sum(early, x, zh), core)
    att_grad = (
        back_product(res_grad_b, merge_w)
        .astype(jnp.bfloat16)
        .reshape(tiles, tile_rows, HEADS, HEAD_DIM)
    )
    probs = jnp.exp(band_scores(queries_t, keys_all, offset, seq_length) - log_total)
    prob_grad = jnp.einsum(
        "tqhd,tkhd->thqk", att_grad, values_all, preferred_element_type=jnp.float32
    )
    row_delta = jnp.sum(probs * prob_grad, axis=-1, keepdims=True)
    score_grad = (probs * (prob_grad - row_delta)).astype(jnp.bfloat16)
    query_grad = jnp.einsum(
        "thqk,tkhd->tqhd", score_grad, keys_all, preferred_element_type=jnp.float32
    ) * (1.0 / math.sqrt(HEAD_DIM))
    key_grad = jnp.einsum(
        "thqk,tqhd->tkhd", score_grad, queries_t, preferred_element_type=jnp.float32
    ) * (1.0 / math.sqrt(HEAD_DIM))
    value_grad = jnp.einsum(
        "thqk,tqhd->tkhd", probs_b, att_grad, preferred_element_type=jnp.float32
    )
    window_grad = jnp.concatenate(
        [key_grad.reshape(tiles, col_count, D), value_grad.reshape(tiles, col_count, D)], axis=2
    )
    lower_grad = window_grad[:, :tile_rows].reshape(tokens, 2 * D)
    upper_grad = window_grad[:, tile_rows:].reshape(tokens, 2 * D)
    pair_grad = jnp.pad(lower_grad, ((0, tile_rows), (0, 0))) + jnp.pad(
        upper_grad, ((tile_rows, 0), (0, 0))
    )
    query_back = unrotate(
        query_grad.reshape(tokens, HEADS, HEAD_DIM), cosine[own], sine[own]
    ).reshape(tokens, D)
    query_back = jnp.pad(query_back, ((RIM, RIM), (0, 0)))
    key_back = unrotate(pair_grad[:, :D].reshape(wide, HEADS, HEAD_DIM), cosine, sine).reshape(
        wide, D
    )
    joint_in = jnp.concatenate([query_back, key_back, pair_grad[:, D:]], axis=1).astype(
        jnp.bfloat16
    )
    joint_part = pair_outer(h_first, joint_in, core)
    first_up = back_product(joint_in, joint_w)
    input_back, first_part = norm_back(first_up, normed_one, inverse_one, gain_one)
    gain_rows = jnp.zeros((8, rows, 128), F32)
    gain_rows = gain_rows.at[:, 0, :rows].set(first_part.reshape(8, rows))
    gain_rows = gain_rows.at[:, 1, :rows].set(second_part.reshape(8, rows))
    late = jnp.concatenate([joint_part.reshape(8, rows, -1), gain_rows], 2).astype(BF16)
    late_sum = spread_sum(late, x, zh)
    gain_mine = late_sum[:2, 3 * D // 2 :].astype(F32)
    late_other = core_swap(late_sum)
    gain_other = late_other[:2, 3 * D // 2 :].astype(F32)
    gain_sum = gain_mine + gain_other
    a, b = late_sum[:, : 3 * D // 2], late_other[:, : 3 * D // 2]
    joint_grad = jnp.where(
        core == 0, jnp.concatenate([a, b], 1), jnp.concatenate([b, a], 1)
    ).astype(F32)
    to_low = passed_along(input_back[:RIM].astype(BF16), -1).astype(F32)
    to_high = passed_along(input_back[RIM + tokens :].astype(BF16), 1).astype(F32)
    input_back = (
        input_back[own]
        + jnp.pad(to_low, ((tokens - RIM, 0), (0, 0)))
        + jnp.pad(to_high, ((0, tokens - RIM), (0, 0)))
    )
    input_grad = (first_res_grad + input_back).astype(jnp.bfloat16)
    merge_grad = early_sum[:rows]
    expand_grad = jnp.concatenate(
        [early_sum[rows * (i + 1) : rows * (i + 2), :384] for i in range(3)]
        + [early_sum[rows * (i + 1) : rows * (i + 2), 384:] for i in range(3)],
        1,
    )
    shrink_grad = early_sum[rows * 4 :]
    return (
        result[None],
        input_grad[None],
        gain_sum[0, :rows],
        joint_grad,
        merge_grad,
        gain_sum[1, :rows],
        expand_grad,
        shrink_grad,
    )


def solution(mesh):
    placed = (
        P("fsdp", "seq", None),
        P("fsdp"),
        P("fsdp", None),
        P("fsdp", None),
        P("fsdp"),
        P("fsdp", None),
        P("fsdp", None),
        P("fsdp", "seq", None),
    )
    return jax.shard_map(
        shards,
        mesh=mesh,
        in_specs=placed,
        out_specs=(
            P("fsdp", "seq", None),
            P("fsdp", "seq", None),
            P("fsdp"),
            P("fsdp", None),
            P("fsdp", None),
            P("fsdp"),
            P("fsdp", None),
            P("fsdp", None),
        ),
        check_vma=False,
    )
```

```python
import math

import jax
import jax.numpy as jnp
from jax import lax
from jax.experimental import pallas as pl
from jax.experimental.pallas import tpu as pltpu
from jax.sharding import PartitionSpec as P

D = 768
HEADS = 12
HEAD_DIM = 64
FF = 1152
RIM = 64
TOKENS = 384
WIDE = TOKENS + 2 * RIM
TILE = 128
TILES = TOKENS // TILE
PAIRS = HEADS // 2
OWNERS = 8
ROWS = D // OWNERS
FF_ROWS = FF // OWNERS
HALF = 3 * D // 2
PACKED = 4 * ROWS + FF_ROWS
EPSILON = 1e-05
F32 = jnp.float32
BF16 = jnp.bfloat16
VMEM_BYTES = 48 * 1024 * 1024


def over_fsdp(value, dx, dz):
    pairs = [
        (x * 2 + z, ((x + dx) % 4) * 2 + (z + dz) % 2) for x in range(4) for z in range(2)
    ]
    return lax.ppermute(value, "fsdp", pairs)


def over_seq(value, dz, dy, dc):
    pairs = [
        (z * 8 + y * 2 + c, ((z + dz) % 2) * 8 + ((y + dy) % 4) * 2 + (c + dc) % 2)
        for z in range(2)
        for y in range(4)
        for c in range(2)
    ]
    return lax.ppermute(value, "seq", pairs)


def core_swap(value):
    return over_seq(value, 0, 0, 1)


def passed_along(value, steps):
    first, last = (max(0, -steps), min(16, 16 - steps))
    return lax.ppermute(value, "seq", [(i, i + steps) for i in range(first, last)])


def place():
    fsdp, seq = lax.axis_index("fsdp"), lax.axis_index("seq")
    return fsdp // 2, fsdp % 2, seq % 2, seq


def owner(x, zh, dx, dz):
    return ((x + dx) % 4) * 2 + (zh + dz) % 2


def dot(left, right):
    return jnp.dot(left, right, preferred_element_type=F32)


def dot_back(left, right):
    return lax.dot_general(left, right, (((1,), (1,)), ((), ())), preferred_element_type=F32)


def dot_outer(left, right):
    return lax.dot_general(left, right, (((0,), (0,)), ((), ())), preferred_element_type=F32)


def row_mean(values):
    return jnp.sum(values, axis=-1, keepdims=True) * (1.0 / D)


def normalize(values):
    centred = values - row_mean(values)
    inverse = lax.rsqrt(row_mean(centred * centred) + EPSILON)
    return (centred * inverse, inverse)


def norm_back(upstream, normed, inverse, gain):
    scaled = upstream * gain
    centred = scaled - row_mean(scaled)
    return inverse * (centred - normed * row_mean(scaled * normed))


def rope(values, cosine, sine):
    lane = lax.broadcasted_iota(jnp.int32, values.shape, 1) % HEAD_DIM
    partner = jnp.where(
        lane < HEAD_DIM // 2,
        pltpu.roll(values, 128 - HEAD_DIM // 2, 1),
        pltpu.roll(values, HEAD_DIM // 2, 1),
    )
    return values * cosine + partner * sine


def call(kernel, outs, scratch, flops, moved, n_args, vmem_args):
    vmem = pl.BlockSpec(memory_space=pltpu.VMEM)
    anywhere = pl.BlockSpec(memory_space=pl.ANY)
    return pl.pallas_call(
        kernel,
        out_shape=[jax.ShapeDtypeStruct(shape, kind) for shape, kind, _ in outs],
        in_specs=[vmem if i < vmem_args else anywhere for i in range(n_args)],
        out_specs=[vmem if inside else anywhere for _, _, inside in outs],
        scratch_shapes=scratch,
        cost_estimate=pl.CostEstimate(flops=flops, bytes_accessed=moved, transcendentals=0),
        compiler_params=pltpu.CompilerParams(vmem_limit_bytes=VMEM_BYTES),
    )


def start_all(copies):
    for copy in copies:
        copy.start()


def wait_all(copies):
    for copy in copies:
        copy.wait()


def piece_places():
    x, zh, core, _ = place()
    return [
        (side * 8 + dx * 2 + dz, owner(x, zh, dx, dz), (core + side) % 2)
        for side in range(2)
        for dx in range(4)
        for dz in range(2)
    ]


def joint_copies(pieces, joint_w, sems):
    return [
        pltpu.make_async_copy(
            pieces[i].at[:, pl.ds(0, HALF)],
            joint_w.at[
                pl.ds(pl.multiple_of(who * ROWS, 16), ROWS),
                pl.ds(pl.multiple_of(half * HALF, 128), HALF),
            ],
            sems.at[i],
        )
        for i, who, half in piece_places()
    ]


def gain_chunk(gain_ref, row, j):
    return gain_ref[row + j : row + j + 1, :]


def joint_kernel(normed_ref, cos_ref, sin_ref, *refs):
    pieces, refs = refs[:16], refs[16:]
    q_ref, k_ref, v_ref, h_ref, att_ref, probs_ref, gain_ref, joint_w, gains, sems = refs
    copies = joint_copies(pieces, joint_w, sems)
    gain_copies = [
        pltpu.make_async_copy(
            pieces[i].at[pl.ds(0, 16), pl.ds(HALF, 128)], gains.at[i], sems.at[16 + i]
        )
        for i in range(8)
    ]
    start_all(gain_copies)
    start_all(copies)
    wait_all(gain_copies)
    gain_ref[...] = jnp.sum(gains[...].astype(F32), axis=0)
    for j in range(D // 128):
        cols = slice(128 * j, 128 * (j + 1))
        h_ref[:, cols] = (normed_ref[:, cols] * gain_chunk(gain_ref, 0, j)).astype(BF16)
    wait_all(copies)
    own = slice(RIM, RIM + TOKENS)
    for j in range(9):
        cols = slice(256 * j, 256 * (j + 1))
        rows = own if j < 3 else slice(0, WIDE)
        got = dot(h_ref[rows, :], joint_w[:, cols])
        out = (q_ref, k_ref, v_ref)[j // 3]
        for a in range(2):
            part = got[:, 128 * a : 128 * (a + 1)]
            if j < 6:
                part = rope(part, cos_ref[rows, :], sin_ref[rows, :])
            at = 256 * (j % 3) + 128 * a
            out[:, at : at + 128] = part.astype(BF16)

    offset = lax.axis_index("seq") * TOKENS
    row = lax.broadcasted_iota(jnp.int32, (TILE, 2 * TILE), 0)
    col = lax.broadcasted_iota(jnp.int32, (TILE, 2 * TILE), 1)
    lane = lax.broadcasted_iota(jnp.int32, (TILE, 128), 1)
    band = (col >= row) & (col - row <= 2 * RIM)

    @pl.loop(0, PAIRS)
    def _(pair):
        lanes = pl.ds(pl.multiple_of(pair * 128, 128), 128)
        for t in range(TILES):
            key = col + (offset + t * TILE - RIM)
            allowed = band & (key >= 0) & (key < 16 * TOKENS)
            query = q_ref[t * TILE : (t + 1) * TILE, lanes].astype(F32) * (HEAD_DIM**-0.5)
            stacked = jnp.concatenate(
                [jnp.where(lane < HEAD_DIM, query, 0.0), jnp.where(lane < HEAD_DIM, 0.0, query)], 0
            ).astype(BF16)
            window = slice(t * TILE, (t + 2) * TILE)
            scores = dot_back(stacked, k_ref[window, lanes])
            scores = jnp.where(jnp.concatenate([allowed, allowed], 0), scores, -1e30)
            expo = jnp.exp(scores - jnp.max(scores, axis=-1, keepdims=True))
            probs = (expo / jnp.sum(expo, axis=-1, keepdims=True)).astype(BF16)
            probs_ref[pair * TILES + t] = probs
            mixed = dot(probs, v_ref[window, lanes])
            att_ref[t * TILE : (t + 1) * TILE, lanes] = jnp.where(
                lane < HEAD_DIM, mixed[:TILE], mixed[TILE:]
            ).astype(BF16)


def joint_forward(normed, cosine, sine, pieces):
    return call(
        joint_kernel,
        [
            ((TOKENS, D), BF16, True),
            ((WIDE, D), BF16, True),
            ((WIDE, D), BF16, True),
            ((WIDE, D), BF16, True),
            ((TOKENS, D), BF16, True),
            ((PAIRS * TILES, 2 * TILE, 2 * TILE), BF16, True),
            ((16, 128), F32, True),
        ],
        [
            pltpu.VMEM((D, 3 * D), BF16),
            pltpu.VMEM((8, 16, 128), BF16),
            pltpu.SemaphoreType.DMA((24,)),
        ],
        2 * WIDE * D * 3 * D,
        12 * 2**20,
        19,
        3,
    )(normed, cosine, sine, *pieces)


def packed_copies(pieces, merge_w, expand_w, shrink_w, sems):
    merge, shrink, expand = [], [], []
    for i, who, half in piece_places():
        rows = pl.ds(pl.multiple_of(who * ROWS, 16), ROWS)
        cols = pl.ds(pl.multiple_of(half * 384, 128), 384)
        merge.append(
            pltpu.make_async_copy(
                pieces[i].at[pl.ds(0, ROWS), :], merge_w.at[rows, cols], sems.at[i * 5]
            )
        )
        for part in range(3):
            expand.append(
                pltpu.make_async_copy(
                    pieces[i].at[pl.ds(ROWS * (part + 1), ROWS), :],
                    expand_w.at[
                        rows, pl.ds(pl.multiple_of(half * FF + part * 384, 128), 384)
                    ],
                    sems.at[i * 5 + 1 + part],
                )
            )
        shrink.append(
            pltpu.make_async_copy(
                pieces[i].at[pl.ds(4 * ROWS, FF_ROWS), :],
                shrink_w.at[pl.ds(pl.multiple_of(who * FF_ROWS, 16), FF_ROWS), cols],
                sems.at[i * 5 + 4],
            )
        )
    return merge, shrink, expand


def middle_kernel(x_ref, att_ref, dy_ref, gain_ref, *refs):
    pieces, refs = refs[:16], refs[16:]
    out_ref, m_ref, h_ref, dx_ref, datt_ref, dz_mine, dz_give, dob_mine, dob_give = refs[:9]
    merge_w, expand_w, shrink_w, x1, normed, inverse, z, dm, dz, dob, sems, back_sems = refs[9:]
    core = lax.axis_index("seq") % 2
    merge, shrink, expand = packed_copies(pieces, merge_w, expand_w, shrink_w, sems)
    start_all(merge)
    start_all(shrink)
    start_all(expand)
    wait_all(merge)
    for j in range(3):
        cols = slice(256 * j, 256 * (j + 1))
        x1[:, cols] = x_ref[:, cols].astype(F32) + dot(att_ref[...], merge_w[:, cols])

    step = 32
    gain = jnp.concatenate([gain_chunk(gain_ref, 8, j) for j in range(6)], 1)

    @pl.loop(0, TOKENS // step)
    def _(i):
        rows = pl.ds(pl.multiple_of(i * step, step), step)
        part, scale = normalize(x1[rows, :])
        normed[rows, :] = part
        inverse[rows, :] = scale
        h_ref[rows, :] = (part * gain).astype(BF16)

    wait_all(shrink)
    for j in range(3):
        cols = slice(384 * j, 384 * (j + 1))
        dm[:, cols] = dot_back(dy_ref[...], shrink_w[cols, :])
    wait_all(expand)
    for j in range(9):
        cols = slice(256 * j, 256 * (j + 1))
        z[:, cols] = dot(h_ref[...], expand_w[:, cols])

    @pl.loop(0, TOKENS // 16)
    def _(i):
        rows = pl.ds(pl.multiple_of(i * 16, 16), 16)
        gate = z[rows, pl.ds(0, FF)]
        up = z[rows, pl.ds(FF, FF)]
        upstream = dm[rows, :]
        below = 0.5 + 0.5 * lax.erf(gate * (0.5**0.5))
        slope = below + gate * (jnp.exp(-0.5 * gate * gate) * (2 * math.pi) ** -0.5)
        active = gate * below
        m_ref[rows, :] = (active * up).astype(BF16)
        dz[0, rows, :] = (upstream * up * slope).astype(BF16)
        dz[1, rows, :] = (upstream * active).astype(BF16)

    sends = [
        pltpu.make_async_copy(dz.at[core], dz_mine, back_sems.at[0]),
        pltpu.make_async_copy(dz.at[1 - core], dz_give, back_sems.at[1]),
    ]
    start_all(sends)
    for j in range(3):
        cols = slice(256 * j, 256 * (j + 1))
        out_ref[:, cols] = (x1[:, cols] + dot(m_ref[...], shrink_w[:, cols])).astype(BF16)
    for j in range(3):
        rows = slice(256 * j, 256 * (j + 1))
        x1[:, rows] = dot_back(dz[0], expand_w[rows, :FF]) + dot_back(dz[1], expand_w[rows, FF:])

    @pl.loop(0, TOKENS // step)
    def _(i):
        rows = pl.ds(pl.multiple_of(i * step, step), step)
        back = norm_back(x1[rows, :], normed[rows, :], inverse[rows, :], gain)
        total = dy_ref[rows, :].astype(F32) + back
        dx_ref[rows, :] = total
        dob[0, rows, :] = total[:, :384].astype(BF16)
        dob[1, rows, :] = total[:, 384:].astype(BF16)

    more = [
        pltpu.make_async_copy(dob.at[core], dob_mine, back_sems.at[2]),
        pltpu.make_async_copy(dob.at[1 - core], dob_give, back_sems.at[3]),
    ]
    start_all(more)
    for j in range(3):
        cols = slice(256 * j, 256 * (j + 1))
        datt_ref[:, cols] = (
            dot_back(dob[0], merge_w[cols, :384]) + dot_back(dob[1], merge_w[cols, 384:])
        ).astype(BF16)
    wait_all(sends)
    wait_all(more)


def middle(x, att, dy, gains, pieces):
    return call(
        middle_kernel,
        [
            ((TOKENS, D), BF16, True),
            ((TOKENS, FF), BF16, True),
            ((TOKENS, D), BF16, True),
            ((TOKENS, D), F32, True),
            ((TOKENS, D), BF16, True),
            ((TOKENS, FF), BF16, False),
            ((TOKENS, FF), BF16, False),
            ((TOKENS, D // 2), BF16, False),
            ((TOKENS, D // 2), BF16, False),
        ],
        [
            pltpu.VMEM((D, D), BF16),
            pltpu.VMEM((D, 2 * FF), BF16),
            pltpu.VMEM((FF, D), BF16),
            pltpu.VMEM((TOKENS, D), F32),
            pltpu.VMEM((TOKENS, D), F32),
            pltpu.VMEM((TOKENS, 1), F32),
            pltpu.VMEM((TOKENS, 2 * FF), F32),
            pltpu.VMEM((TOKENS, FF), F32),
            pltpu.VMEM((2, TOKENS, FF), BF16),
            pltpu.VMEM((2, TOKENS, D // 2), BF16),
            pltpu.SemaphoreType.DMA((80,)),
            pltpu.SemaphoreType.DMA((4,)),
        ],
        4 * TOKENS * (2 * D * D + 3 * FF * D),
        16 * 2**20,
        20,
        4,
    )(x, att, dy, gains, *pieces)


def paired_copies(refs, buffers, sems):
    copies = []
    for n, buffer in enumerate(buffers):
        rows = buffer.shape[0] // 2
        for side in range(2):
            copies.append(
                pltpu.make_async_copy(
                    refs[2 * n + side], buffer.at[pl.ds(side * rows, rows), :], sems.at[2 * n + side]
                )
            )
    return copies


def block_copies(blocks, outs, sems):
    x, zh, _, _ = place()
    return [
        pltpu.make_async_copy(blocks.at[owner(x, zh, dx, dz)], outs[dx].at[dz], sems.at[dx * 2 + dz])
        for dx in range(4)
        for dz in range(2)
    ]


def early_kernel(*refs):
    ins, outs, refs = refs[:12], refs[12:16], refs[16:]
    h, dz, att, dob, m, dy, blocks, sems, out_sems = refs
    copies = paired_copies(ins, (h, dz, att, dob, m, dy), sems)
    start_all(copies)
    wait_all(copies)
    for part in range(3):
        cols = slice(384 * part, 384 * (part + 1))
        grad = dot_outer(h[...], dz[:, cols]).astype(BF16)
        blocks[:, ROWS * (part + 1) : ROWS * (part + 2), :] = grad.reshape(OWNERS, ROWS, 384)
    grad = dot_outer(att[...], dob[...]).astype(BF16)
    blocks[:, :ROWS, :] = grad.reshape(OWNERS, ROWS, 384)
    grad = dot_outer(m[...], dy[...]).astype(BF16)
    blocks[:, 4 * ROWS :, :] = grad.reshape(OWNERS, FF_ROWS, 384)
    sends = block_copies(blocks, outs, out_sems)
    start_all(sends)
    wait_all(sends)


def early_grads(*args):
    return call(
        early_kernel,
        [((2, PACKED, 384), BF16, False)] * 4,
        [
            pltpu.VMEM((2 * TOKENS, D), BF16),
            pltpu.VMEM((2 * TOKENS, FF), BF16),
            pltpu.VMEM((2 * TOKENS, D), BF16),
            pltpu.VMEM((2 * TOKENS, D // 2), BF16),
            pltpu.VMEM((2 * TOKENS, FF), BF16),
            pltpu.VMEM((2 * TOKENS, D // 2), BF16),
            pltpu.VMEM((OWNERS, PACKED, 384), BF16),
            pltpu.SemaphoreType.DMA((12,)),
            pltpu.SemaphoreType.DMA((8,)),
        ],
        2 * TOKENS * (D * D + 3 * FF * D),
        12 * 2**20,
        12,
        0,
    )(*args)


def attention_back_kernel(
    q_ref, k_ref, v_ref, probs_ref, datt_ref, cos_ref, sin_ref, mine_ref, give_ref, *scratch
):
    dk, dv, dj, sems = scratch
    core = lax.axis_index("seq") % 2
    lane = lax.broadcasted_iota(jnp.int32, (TILE, 128), 1)
    own = slice(RIM, RIM + TOKENS)
    dk[...] = jnp.zeros_like(dk)
    dv[...] = jnp.zeros_like(dv)
    dj[0, :RIM, :D] = jnp.zeros((RIM, D), BF16)
    dj[0, RIM + TOKENS :, :D] = jnp.zeros((RIM, D), BF16)
    scale = HEAD_DIM**-0.5

    @pl.loop(0, PAIRS)
    def _(pair):
        lanes = pl.ds(pl.multiple_of(pair * 128, 128), 128)
        for t in range(TILES):
            rows = slice(t * TILE, (t + 1) * TILE)
            window = slice(t * TILE, (t + 2) * TILE)
            query = q_ref[rows, lanes].astype(F32) * scale
            query = jnp.concatenate(
                [jnp.where(lane < HEAD_DIM, query, 0.0), jnp.where(lane < HEAD_DIM, 0.0, query)], 0
            ).astype(BF16)
            upstream = datt_ref[rows, lanes].astype(F32)
            upstream = jnp.concatenate(
                [
                    jnp.where(lane < HEAD_DIM, upstream, 0.0),
                    jnp.where(lane < HEAD_DIM, 0.0, upstream),
                ],
                0,
            ).astype(BF16)
            probs_b = probs_ref[pair * TILES + t]
            probs = probs_b.astype(F32)
            dp = dot_back(upstream, v_ref[window, lanes])
            delta = jnp.sum(probs * dp, axis=-1, keepdims=True)
            ds = (probs * (dp - delta)).astype(BF16)
            dv[window, lanes] += dot_outer(probs_b, upstream)
            dk[window, lanes] += dot_outer(ds, query)
            dq = dot(ds, k_ref[window, lanes]) * scale
            dq = jnp.where(lane < HEAD_DIM, dq[:TILE], dq[TILE:])
            at = slice(RIM + t * TILE, RIM + (t + 1) * TILE)
            dj[0, at, lanes] = rope(dq, cos_ref[at, :], -sin_ref[at, :]).astype(BF16)

    for j in range(6):
        cols = slice(128 * j, 128 * (j + 1))
        part = rope(dk[:, cols], cos_ref[...], -sin_ref[...]).astype(BF16)
        if j < 3:
            dj[0, :, D + 128 * j : D + 128 * (j + 1)] = part
        else:
            dj[1, :, 128 * (j - 3) : 128 * (j - 2)] = part
    dj[1, :, D // 2 :] = dv[...].astype(BF16)
    sends = [
        pltpu.make_async_copy(dj.at[core], mine_ref, sems.at[0]),
        pltpu.make_async_copy(dj.at[1 - core], give_ref, sems.at[1]),
    ]
    start_all(sends)
    wait_all(sends)


def attention_back(*args):
    return call(
        attention_back_kernel,
        [((WIDE, HALF), BF16, False)] * 2,
        [
            pltpu.VMEM((WIDE, D), F32),
            pltpu.VMEM((WIDE, D), F32),
            pltpu.VMEM((2, WIDE, HALF), BF16),
            pltpu.SemaphoreType.DMA((2,)),
        ],
        10 * TOKENS * 2 * TILE * D,
        12 * 2**20,
        7,
        7,
    )(*args)


def late_kernel(*refs):
    ins, outs, refs = refs[:4], refs[4:8], refs[8:]
    h, dj, blocks, sems, out_sems = refs
    copies = paired_copies(ins, (h, dj), sems)
    start_all(copies)
    wait_all(copies)
    for part in range(3):
        cols = slice(384 * part, 384 * (part + 1))
        grad = dot_outer(h[...], dj[:, cols]).astype(BF16)
        blocks[:, :, cols] = grad.reshape(OWNERS, ROWS, 384)
    sends = block_copies(blocks, outs, out_sems)
    start_all(sends)
    wait_all(sends)


def late_grads(*args):
    return call(
        late_kernel,
        [((2, ROWS, HALF), BF16, False)] * 4,
        [
            pltpu.VMEM((2 * WIDE, D), BF16),
            pltpu.VMEM((2 * WIDE, HALF), BF16),
            pltpu.VMEM((OWNERS, ROWS, HALF), BF16),
            pltpu.SemaphoreType.DMA((4,)),
            pltpu.SemaphoreType.DMA((8,)),
        ],
        4 * WIDE * D * HALF,
        8 * 2**20,
        4,
        0,
    )(*args)


def input_kernel(normed_ref, inverse_ref, gain_ref, dx_ref, *refs):
    pieces, (mine, give), refs = refs[:16], refs[16:18], refs[18:]
    base_ref, low_ref, high_ref, joint_w, dj, upstream, sems = refs
    core = lax.axis_index("seq") % 2
    copies = joint_copies(pieces, joint_w, sems)
    copies.append(pltpu.make_async_copy(mine, dj.at[core], sems.at[16]))
    copies.append(pltpu.make_async_copy(give, dj.at[1 - core], sems.at[17]))
    start_all(copies)
    wait_all(copies)
    for j in range(3):
        cols = slice(256 * j, 256 * (j + 1))
        upstream[:, cols] = dot_back(dj[0], joint_w[cols, :HALF]) + dot_back(
            dj[1], joint_w[cols, HALF:]
        )
    gain = jnp.concatenate([gain_chunk(gain_ref, 0, j) for j in range(6)], 1)
    step = 32

    def back(rows):
        return norm_back(upstream[rows, :], normed_ref[rows, :], inverse_ref[rows, :], gain)

    @pl.loop(0, TOKENS // step)
    def _(i):
        start = pl.multiple_of(i * step, step)
        base_ref[pl.ds(start, step), :] = dx_ref[pl.ds(start, step), :] + back(
            pl.ds(start + RIM, step)
        )

    @pl.loop(0, RIM // step)
    def _(i):
        start = pl.multiple_of(i * step, step)
        low_ref[pl.ds(start, step), :] = back(pl.ds(start, step)).astype(BF16)
        high_ref[pl.ds(start, step), :] = back(pl.ds(start + RIM + TOKENS, step)).astype(BF16)


def input_back(normed, inverse, gains, dx, pieces, mine, give):
    return call(
        input_kernel,
        [((TOKENS, D), F32, True), ((RIM, D), BF16, True), ((RIM, D), BF16, True)],
        [
            pltpu.VMEM((D, 3 * D), BF16),
            pltpu.VMEM((2, WIDE, HALF), BF16),
            pltpu.VMEM((WIDE, D), F32),
            pltpu.SemaphoreType.DMA((18,)),
        ],
        2 * WIDE * D * 3 * D,
        10 * 2**20,
        22,
        4,
    )(normed, inverse, gains, dx, *pieces, mine, give)


def gather_pieces(own):
    from_low = over_fsdp(own, 1, 0)
    from_high = over_fsdp(own, -1, 0)
    across = over_fsdp(own, 0, 1)
    from_far = over_fsdp(own, 2, 0)
    across_low = over_fsdp(across, 1, 0)
    across_high = over_fsdp(across, -1, 0)
    across_far = over_fsdp(from_far, 0, 1)
    return [own, across, from_high, across_high, from_far, across_far, from_low, across_low]


def spread_sum(blocks, zh):
    got = [over_fsdp(blocks[d % 4], d, 0) for d in (1, -1, 2)]
    total = blocks[0].astype(F32) + sum(g.astype(F32) for g in got)
    keep, give = total[0], total[1].astype(BF16)
    total = (keep + over_fsdp(give, 0, 1).astype(F32)).astype(BF16)
    low, high, far = (over_seq(total, 0, d, 0) for d in (1, -1, 2))
    total = (
        (total.astype(F32) + far.astype(F32)) + (low.astype(F32) + high.astype(F32))
    ).astype(BF16)
    return (total.astype(F32) + over_seq(total, 1, 0, 0).astype(F32)).astype(BF16)


def in_order(mine, core):
    other = core_swap(mine)
    first = jnp.where(core == 0, mine, other).astype(F32)
    second = jnp.where(core == 0, other, mine).astype(F32)
    return first, second


def shards(
    inputs,
    first_gain,
    joint_weight,
    merge_weight,
    second_gain,
    expand_weight,
    shrink_weight,
    cotangent,
):
    x, zh, core, seq = place()
    fsdp = lax.axis_index("fsdp")
    source, upstream = inputs[0], cotangent[0]

    def columns(w, start, width):
        return lax.dynamic_slice_in_dim(w, start, width, 1)

    def placed_gain(gain):
        whole = lax.dynamic_update_slice_in_dim(jnp.zeros((D,), BF16), gain, fsdp * ROWS, 0)
        return jnp.pad(whole.reshape(6, 128), ((0, 2), (0, 0)))

    gain_tile = jnp.concatenate(
        [placed_gain(first_gain), placed_gain(second_gain), jnp.zeros((ROWS - 16, 128), BF16)], 0
    )
    joint_own = jnp.concatenate([columns(joint_weight, core * HALF, HALF), gain_tile], 1)
    joint_mine = gather_pieces(joint_own)
    joint_pieces = joint_mine + [core_swap(p) for p in joint_mine]
    low_halo = passed_along(source[TOKENS - RIM :], 1)
    high_halo = passed_along(source[:RIM], -1)
    packed_own = jnp.concatenate(
        [columns(merge_weight, core * 384, 384)]
        + [columns(expand_weight, core * FF + 384 * i, 384) for i in range(3)]
        + [columns(shrink_weight, core * 384, 384)],
        0,
    )
    packed_own, _ = lax.optimization_barrier((packed_own, joint_mine[1]))
    packed_mine = gather_pieces(packed_own)
    packed_pieces = packed_mine + [core_swap(p) for p in packed_mine]

    frequencies = jnp.exp(
        jnp.arange(HEAD_DIM // 2, dtype=F32) * (-2.0 * math.log(10000.0) / HEAD_DIM)
    )
    positions = (seq * TOKENS - RIM + lax.iota(jnp.int32, WIDE)).astype(F32)
    angles = positions[:, None] * frequencies[None, :]
    cosine, sine = jnp.cos(angles), jnp.sin(angles)
    cosine = jnp.concatenate([cosine] * 4, 1)
    sine = jnp.concatenate([-sine, sine] * 2, 1)
    extended = jnp.concatenate([low_halo, source, high_halo], 0).astype(F32)
    normed, inverse = normalize(extended)

    q, k, v, h_first, attended, probs, gains = joint_forward(normed, cosine, sine, joint_pieces)
    h_first_other = core_swap(h_first)
    attended_other = core_swap(attended)
    dy_mine = columns(upstream, core * 384, 384)
    dy_got = core_swap(columns(upstream, (1 - core) * 384, 384))
    result, hidden, h_second, dx, datt, dz_mine, dz_give, dob_mine, dob_give = middle(
        source, attended, upstream, gains, packed_pieces
    )
    early = early_grads(
        h_second,
        core_swap(h_second),
        dz_mine,
        core_swap(dz_give),
        attended,
        attended_other,
        dob_mine,
        core_swap(dob_give),
        hidden,
        core_swap(hidden),
        dy_mine,
        dy_got,
    )
    dj_mine, dj_give = attention_back(q, k, v, probs, datt, cosine, sine)
    late = late_grads(h_first, h_first_other, dj_mine, core_swap(dj_give))
    base, low_back, high_back = input_back(
        normed, inverse, gains, dx, joint_pieces, dj_mine, dj_give
    )
    from_high = passed_along(low_back, -1).astype(F32)
    from_low = passed_along(high_back, 1).astype(F32)
    input_grad = (
        base
        + jnp.pad(from_high, ((TOKENS - RIM, 0), (0, 0)))
        + jnp.pad(from_low, ((0, TOKENS - RIM), (0, 0)))
    ).astype(BF16)

    first, second = in_order(spread_sum(early, zh), core)
    merge_grad = jnp.concatenate([first[:ROWS], second[:ROWS]], 1)
    expand_grad = jnp.concatenate(
        [s[ROWS * (i + 1) : ROWS * (i + 2)] for s in (first, second) for i in range(3)], 1
    )
    shrink_grad = jnp.concatenate([first[4 * ROWS :], second[4 * ROWS :]], 1)
    joint_grad = jnp.concatenate(in_order(spread_sum(late, zh), core), 1)

    def gain_grad(weight, grad, gain):
        return jnp.sum(weight.astype(F32) * grad, axis=1) / gain.astype(F32)

    return (
        result[None],
        input_grad[None],
        gain_grad(joint_weight, joint_grad, first_gain),
        joint_grad,
        merge_grad,
        gain_grad(expand_weight, expand_grad, second_gain),
        expand_grad,
        shrink_grad,
    )


def solution(mesh):
    placed = (
        P("fsdp", "seq", None),
        P("fsdp"),
        P("fsdp", None),
        P("fsdp", None),
        P("fsdp"),
        P("fsdp", None),
        P("fsdp", None),
        P("fsdp", "seq", None),
    )
    return jax.shard_map(
        shards,
        mesh=mesh,
        in_specs=placed,
        out_specs=(
            P("fsdp", "seq", None),
            P("fsdp", "seq", None),
            P("fsdp"),
            P("fsdp", None),
            P("fsdp", None),
            P("fsdp"),
            P("fsdp", None),
            P("fsdp", None),
        ),
        check_vma=False,
    )
```

```python
import math

import jax
import jax.numpy as jnp
from jax import lax
from jax.experimental import pallas as pl
from jax.experimental.pallas import tpu as pltpu
from jax.sharding import PartitionSpec as P

D = 768
HEADS = 12
HEAD_DIM = 64
FF = 1152
RIM = 64
TOKENS = 384
WIDE = TOKENS + 2 * RIM
TILE = 128
TILES = TOKENS // TILE
PAIRS = HEADS // 2
OWNERS = 8
ROWS = D // OWNERS
FF_ROWS = FF // OWNERS
HALF = 3 * D // 2
PACKED = 4 * ROWS + FF_ROWS
EPSILON = 1e-05
F32 = jnp.float32
BF16 = jnp.bfloat16
MIB = 2**20


def over_fsdp(value, dx, dz):
    pairs = [
        (x * 2 + z, ((x + dx) % 4) * 2 + (z + dz) % 2) for x in range(4) for z in range(2)
    ]
    return lax.ppermute(value, "fsdp", pairs)


def over_seq(value, dz, dy, dc):
    pairs = [
        (z * 8 + y * 2 + c, ((z + dz) % 2) * 8 + ((y + dy) % 4) * 2 + (c + dc) % 2)
        for z in range(2)
        for y in range(4)
        for c in range(2)
    ]
    return lax.ppermute(value, "seq", pairs)


def core_swap(value):
    return over_seq(value, 0, 0, 1)


def passed_along(value, steps):
    first, last = (max(0, -steps), min(16, 16 - steps))
    return lax.ppermute(value, "seq", [(i, i + steps) for i in range(first, last)])


def place():
    fsdp, seq = lax.axis_index("fsdp"), lax.axis_index("seq")
    return fsdp // 2, fsdp % 2, seq % 2, seq


def owner(x, zh, dx, dz):
    return ((x + dx) % 4) * 2 + (zh + dz) % 2


def dot(left, right):
    return jnp.dot(left, right, preferred_element_type=F32)


def dot_back(left, right):
    return lax.dot_general(left, right, (((1,), (1,)), ((), ())), preferred_element_type=F32)


def dot_outer(left, right):
    return lax.dot_general(left, right, (((0,), (0,)), ((), ())), preferred_element_type=F32)


def row_mean(values):
    return jnp.sum(values, axis=-1, keepdims=True) * (1.0 / D)


def normalize(values):
    centred = values - row_mean(values)
    inverse = lax.rsqrt(row_mean(centred * centred) + EPSILON)
    return (centred * inverse, inverse)


def norm_back(upstream, normed, inverse, gain):
    scaled = upstream * gain
    centred = scaled - row_mean(scaled)
    return inverse * (centred - normed * row_mean(scaled * normed))


def rope(values, cosine, sine):
    lane = lax.broadcasted_iota(jnp.int32, values.shape, 1) % HEAD_DIM
    partner = jnp.where(
        lane < HEAD_DIM // 2,
        pltpu.roll(values, 128 - HEAD_DIM // 2, 1),
        pltpu.roll(values, HEAD_DIM // 2, 1),
    )
    return values * cosine + partner * sine


def call(kernel, outs, scratch, flops, moved, n_args, vmem_args, limit):
    vmem = pl.BlockSpec(memory_space=pltpu.VMEM)
    anywhere = pl.BlockSpec(memory_space=pl.ANY)
    return pl.pallas_call(
        kernel,
        out_shape=[jax.ShapeDtypeStruct(shape, kind) for shape, kind, _ in outs],
        in_specs=[vmem if i < vmem_args else anywhere for i in range(n_args)],
        out_specs=[vmem if inside else anywhere for _, _, inside in outs],
        scratch_shapes=scratch,
        cost_estimate=pl.CostEstimate(flops=flops, bytes_accessed=moved, transcendentals=0),
        compiler_params=pltpu.CompilerParams(vmem_limit_bytes=limit * MIB),
    )


def start_all(copies):
    for copy in copies:
        copy.start()


def wait_all(copies):
    for copy in copies:
        copy.wait()


def piece_places(pieces):
    x, zh, core, _ = place()
    return [
        (
            side * 8 + dx * 2 + dz,
            pieces[side * 4 + dx].at[dz],
            owner(x, zh, dx, dz),
            (core + side) % 2,
        )
        for side in range(2)
        for dx in range(4)
        for dz in range(2)
    ]


def joint_copies(pieces, joint_w, sems):
    return [
        pltpu.make_async_copy(
            piece.at[:, pl.ds(0, HALF)],
            joint_w.at[
                pl.ds(pl.multiple_of(who * ROWS, 16), ROWS),
                pl.ds(pl.multiple_of(half * HALF, 128), HALF),
            ],
            sems.at[i],
        )
        for i, piece, who, half in piece_places(pieces)
    ]


def gain_chunk(gain_ref, row, j):
    return gain_ref[row + j : row + j + 1, :]


def joint_kernel(normed_ref, cos_ref, sin_ref, *refs):
    pieces, refs = refs[:8], refs[8:]
    q_ref, k_ref, v_ref, h_ref, att_ref, probs_ref, gain_ref, weight_ref, joint_w, gains, sems = refs
    copies = joint_copies(pieces, joint_w, sems)
    gain_copies = [
        pltpu.make_async_copy(
            pieces[i // 2].at[i % 2, pl.ds(0, 16), pl.ds(HALF, 128)], gains.at[i], sems.at[16 + i]
        )
        for i in range(8)
    ]
    start_all(gain_copies)
    start_all(copies)
    wait_all(gain_copies)
    gain_ref[...] = jnp.sum(gains[...].astype(F32), axis=0)
    for j in range(D // 128):
        cols = slice(128 * j, 128 * (j + 1))
        h_ref[:, cols] = (normed_ref[:, cols] * gain_chunk(gain_ref, 0, j)).astype(BF16)
    wait_all(copies)
    keep = pltpu.make_async_copy(joint_w, weight_ref, sems.at[24])
    keep.start()
    own = slice(RIM, RIM + TOKENS)
    for j in range(9):
        cols = slice(256 * j, 256 * (j + 1))
        rows = own if j < 3 else slice(0, WIDE)
        got = dot(h_ref[rows, :], joint_w[:, cols])
        out = (q_ref, k_ref, v_ref)[j // 3]
        for a in range(2):
            part = got[:, 128 * a : 128 * (a + 1)]
            if j < 6:
                part = rope(part, cos_ref[rows, :], sin_ref[rows, :])
            at = 256 * (j % 3) + 128 * a
            out[:, at : at + 128] = part.astype(BF16)

    offset = lax.axis_index("seq") * TOKENS
    row = lax.broadcasted_iota(jnp.int32, (TILE, 2 * TILE), 0)
    col = lax.broadcasted_iota(jnp.int32, (TILE, 2 * TILE), 1)
    lane = lax.broadcasted_iota(jnp.int32, (TILE, 128), 1)
    band = (col >= row) & (col - row <= 2 * RIM)

    @pl.loop(0, PAIRS)
    def _(pair):
        lanes = pl.ds(pl.multiple_of(pair * 128, 128), 128)
        for t in range(TILES):
            key = col + (offset + t * TILE - RIM)
            allowed = band & (key >= 0) & (key < 16 * TOKENS)
            query = q_ref[t * TILE : (t + 1) * TILE, lanes].astype(F32) * (HEAD_DIM**-0.5)
            stacked = jnp.concatenate(
                [jnp.where(lane < HEAD_DIM, query, 0.0), jnp.where(lane < HEAD_DIM, 0.0, query)], 0
            ).astype(BF16)
            window = slice(t * TILE, (t + 2) * TILE)
            scores = dot_back(stacked, k_ref[window, lanes])
            scores = jnp.where(jnp.concatenate([allowed, allowed], 0), scores, -1e30)
            expo = jnp.exp(scores - jnp.max(scores, axis=-1, keepdims=True))
            probs = (expo / jnp.sum(expo, axis=-1, keepdims=True)).astype(BF16)
            probs_ref[pair * TILES + t] = probs
            mixed = dot(probs, v_ref[window, lanes])
            att_ref[t * TILE : (t + 1) * TILE, lanes] = jnp.where(
                lane < HEAD_DIM, mixed[:TILE], mixed[TILE:]
            ).astype(BF16)

    keep.wait()


def joint_forward(normed, cosine, sine, pieces):
    return call(
        joint_kernel,
        [
            ((TOKENS, D), BF16, True),
            ((WIDE, D), BF16, True),
            ((WIDE, D), BF16, True),
            ((WIDE, D), BF16, True),
            ((TOKENS, D), BF16, True),
            ((PAIRS * TILES, 2 * TILE, 2 * TILE), BF16, True),
            ((16, 128), F32, True),
            ((D, 3 * D), BF16, False),
        ],
        [
            pltpu.VMEM((D, 3 * D), BF16),
            pltpu.VMEM((8, 16, 128), BF16),
            pltpu.SemaphoreType.DMA((25,)),
        ],
        2 * WIDE * D * 3 * D,
        12 * 2**20,
        11,
        3,
        18,
    )(normed, cosine, sine, *pieces)


def packed_copies(pieces, merge_w, expand_w, shrink_w, sems):
    merge, shrink, expand = [], [], []
    for i, piece, who, half in piece_places(pieces):
        rows = pl.ds(pl.multiple_of(who * ROWS, 16), ROWS)
        cols = pl.ds(pl.multiple_of(half * 384, 128), 384)
        merge.append(
            pltpu.make_async_copy(
                piece.at[pl.ds(0, ROWS), :], merge_w.at[rows, cols], sems.at[i * 5]
            )
        )
        for part in range(3):
            expand.append(
                pltpu.make_async_copy(
                    piece.at[pl.ds(ROWS * (part + 1), ROWS), :],
                    expand_w.at[
                        rows, pl.ds(pl.multiple_of(half * FF + part * 384, 128), 384)
                    ],
                    sems.at[i * 5 + 1 + part],
                )
            )
        shrink.append(
            pltpu.make_async_copy(
                piece.at[pl.ds(4 * ROWS, FF_ROWS), :],
                shrink_w.at[pl.ds(pl.multiple_of(who * FF_ROWS, 16), FF_ROWS), cols],
                sems.at[i * 5 + 4],
            )
        )
    return merge, shrink, expand


def middle_kernel(x_ref, att_ref, dy_ref, gain_ref, *refs):
    pieces, refs = refs[:8], refs[8:]
    out_ref, m_ref, h_ref, dx_ref, datt_ref, dz_mine, dz_give, dob_mine, dob_give = refs[:9]
    merge_w, expand_w, shrink_w, x1, normed, inverse, z, dm, dz, dob, sems, back_sems = refs[9:]
    core = lax.axis_index("seq") % 2
    merge, shrink, expand = packed_copies(pieces, merge_w, expand_w, shrink_w, sems)
    start_all(merge)
    start_all(shrink)
    start_all(expand)
    wait_all(merge)
    for j in range(3):
        cols = slice(256 * j, 256 * (j + 1))
        x1[:, cols] = x_ref[:, cols].astype(F32) + dot(att_ref[...], merge_w[:, cols])

    step = 32
    gain = jnp.concatenate([gain_chunk(gain_ref, 8, j) for j in range(6)], 1)

    @pl.loop(0, TOKENS // step)
    def _(i):
        rows = pl.ds(pl.multiple_of(i * step, step), step)
        part, scale = normalize(x1[rows, :])
        normed[rows, :] = part
        inverse[rows, :] = scale
        h_ref[rows, :] = (part * gain).astype(BF16)

    wait_all(shrink)
    for j in range(3):
        cols = slice(384 * j, 384 * (j + 1))
        dm[:, cols] = dot_back(dy_ref[...], shrink_w[cols, :])
    wait_all(expand)
    for j in range(9):
        cols = slice(256 * j, 256 * (j + 1))
        z[:, cols] = dot(h_ref[...], expand_w[:, cols])

    @pl.loop(0, TOKENS // 16)
    def _(i):
        rows = pl.ds(pl.multiple_of(i * 16, 16), 16)
        gate = z[rows, pl.ds(0, FF)]
        up = z[rows, pl.ds(FF, FF)]
        upstream = dm[rows, :]
        below = 0.5 + 0.5 * lax.erf(gate * (0.5**0.5))
        slope = below + gate * (jnp.exp(-0.5 * gate * gate) * (2 * math.pi) ** -0.5)
        active = gate * below
        m_ref[rows, :] = (active * up).astype(BF16)
        dz[0, rows, :] = (upstream * up * slope).astype(BF16)
        dz[1, rows, :] = (upstream * active).astype(BF16)

    sends = [
        pltpu.make_async_copy(dz.at[core], dz_mine, back_sems.at[0]),
        pltpu.make_async_copy(dz.at[1 - core], dz_give, back_sems.at[1]),
    ]
    start_all(sends)
    for j in range(3):
        cols = slice(256 * j, 256 * (j + 1))
        out_ref[:, cols] = (x1[:, cols] + dot(m_ref[...], shrink_w[:, cols])).astype(BF16)
    for j in range(3):
        rows = slice(256 * j, 256 * (j + 1))
        x1[:, rows] = dot_back(dz[0], expand_w[rows, :FF]) + dot_back(dz[1], expand_w[rows, FF:])

    @pl.loop(0, TOKENS // step)
    def _(i):
        rows = pl.ds(pl.multiple_of(i * step, step), step)
        back = norm_back(x1[rows, :], normed[rows, :], inverse[rows, :], gain)
        total = dy_ref[rows, :].astype(F32) + back
        dx_ref[rows, :] = total
        dob[0, rows, :] = total[:, :384].astype(BF16)
        dob[1, rows, :] = total[:, 384:].astype(BF16)

    more = [
        pltpu.make_async_copy(dob.at[core], dob_mine, back_sems.at[2]),
        pltpu.make_async_copy(dob.at[1 - core], dob_give, back_sems.at[3]),
    ]
    start_all(more)
    for j in range(3):
        cols = slice(256 * j, 256 * (j + 1))
        datt_ref[:, cols] = (
            dot_back(dob[0], merge_w[cols, :384]) + dot_back(dob[1], merge_w[cols, 384:])
        ).astype(BF16)
    wait_all(sends)
    wait_all(more)


def middle(x, att, dy, gains, pieces):
    return call(
        middle_kernel,
        [
            ((TOKENS, D), BF16, True),
            ((TOKENS, FF), BF16, True),
            ((TOKENS, D), BF16, True),
            ((TOKENS, D), F32, True),
            ((TOKENS, D), BF16, True),
            ((TOKENS, FF), BF16, False),
            ((TOKENS, FF), BF16, False),
            ((TOKENS, D // 2), BF16, False),
            ((TOKENS, D // 2), BF16, False),
        ],
        [
            pltpu.VMEM((D, D), BF16),
            pltpu.VMEM((D, 2 * FF), BF16),
            pltpu.VMEM((FF, D), BF16),
            pltpu.VMEM((TOKENS, D), F32),
            pltpu.VMEM((TOKENS, D), F32),
            pltpu.VMEM((TOKENS, 1), F32),
            pltpu.VMEM((TOKENS, 2 * FF), F32),
            pltpu.VMEM((TOKENS, FF), F32),
            pltpu.VMEM((2, TOKENS, FF), BF16),
            pltpu.VMEM((2, TOKENS, D // 2), BF16),
            pltpu.SemaphoreType.DMA((80,)),
            pltpu.SemaphoreType.DMA((4,)),
        ],
        4 * TOKENS * (2 * D * D + 3 * FF * D),
        16 * 2**20,
        12,
        4,
        32,
    )(x, att, dy, gains, *pieces)


def paired_copies(refs, buffers, sems):
    copies = []
    for n, buffer in enumerate(buffers):
        rows = buffer.shape[0] // 2
        for side in range(2):
            copies.append(
                pltpu.make_async_copy(
                    refs[2 * n + side], buffer.at[pl.ds(side * rows, rows), :], sems.at[2 * n + side]
                )
            )
    return copies


def block_copies(blocks, outs, sems):
    x, zh, _, _ = place()
    return [
        pltpu.make_async_copy(blocks.at[owner(x, zh, dx, dz)], outs[dx].at[dz], sems.at[dx * 2 + dz])
        for dx in range(4)
        for dz in range(2)
    ]


def early_kernel(*refs):
    ins, outs, refs = refs[:12], refs[12:16], refs[16:]
    h, dz, att, dob, m, dy, blocks, sems, out_sems = refs
    copies = paired_copies(ins, (h, dz, att, dob, m, dy), sems)
    start_all(copies)
    wait_all(copies)
    for part in range(3):
        cols = slice(384 * part, 384 * (part + 1))
        grad = dot_outer(h[...], dz[:, cols]).astype(BF16)
        blocks[:, ROWS * (part + 1) : ROWS * (part + 2), :] = grad.reshape(OWNERS, ROWS, 384)
    grad = dot_outer(att[...], dob[...]).astype(BF16)
    blocks[:, :ROWS, :] = grad.reshape(OWNERS, ROWS, 384)
    grad = dot_outer(m[...], dy[...]).astype(BF16)
    blocks[:, 4 * ROWS :, :] = grad.reshape(OWNERS, FF_ROWS, 384)
    sends = block_copies(blocks, outs, out_sems)
    start_all(sends)
    wait_all(sends)


def early_grads(*args):
    return call(
        early_kernel,
        [((2, PACKED, 384), BF16, False)] * 4,
        [
            pltpu.VMEM((2 * TOKENS, D), BF16),
            pltpu.VMEM((2 * TOKENS, FF), BF16),
            pltpu.VMEM((2 * TOKENS, D), BF16),
            pltpu.VMEM((2 * TOKENS, D // 2), BF16),
            pltpu.VMEM((2 * TOKENS, FF), BF16),
            pltpu.VMEM((2 * TOKENS, D // 2), BF16),
            pltpu.VMEM((OWNERS, PACKED, 384), BF16),
            pltpu.SemaphoreType.DMA((12,)),
            pltpu.SemaphoreType.DMA((8,)),
        ],
        2 * TOKENS * (D * D + 3 * FF * D),
        12 * 2**20,
        12,
        0,
        20,
    )(*args)


def attention_back_kernel(
    q_ref, k_ref, v_ref, probs_ref, datt_ref, cos_ref, sin_ref, mine_ref, give_ref, *scratch
):
    dk, dv, dj, sems = scratch
    core = lax.axis_index("seq") % 2
    lane = lax.broadcasted_iota(jnp.int32, (TILE, 128), 1)
    own = slice(RIM, RIM + TOKENS)
    dk[...] = jnp.zeros_like(dk)
    dv[...] = jnp.zeros_like(dv)
    dj[0, :RIM, :D] = jnp.zeros((RIM, D), BF16)
    dj[0, RIM + TOKENS :, :D] = jnp.zeros((RIM, D), BF16)
    scale = HEAD_DIM**-0.5

    @pl.loop(0, PAIRS)
    def _(pair):
        lanes = pl.ds(pl.multiple_of(pair * 128, 128), 128)
        for t in range(TILES):
            rows = slice(t * TILE, (t + 1) * TILE)
            window = slice(t * TILE, (t + 2) * TILE)
            query = q_ref[rows, lanes].astype(F32) * scale
            query = jnp.concatenate(
                [jnp.where(lane < HEAD_DIM, query, 0.0), jnp.where(lane < HEAD_DIM, 0.0, query)], 0
            ).astype(BF16)
            upstream = datt_ref[rows, lanes].astype(F32)
            upstream = jnp.concatenate(
                [
                    jnp.where(lane < HEAD_DIM, upstream, 0.0),
                    jnp.where(lane < HEAD_DIM, 0.0, upstream),
                ],
                0,
            ).astype(BF16)
            probs_b = probs_ref[pair * TILES + t]
            probs = probs_b.astype(F32)
            dp = dot_back(upstream, v_ref[window, lanes])
            delta = jnp.sum(probs * dp, axis=-1, keepdims=True)
            ds = (probs * (dp - delta)).astype(BF16)
            dv[window, lanes] += dot_outer(probs_b, upstream)
            dk[window, lanes] += dot_outer(ds, query)
            dq = dot(ds, k_ref[window, lanes]) * scale
            dq = jnp.where(lane < HEAD_DIM, dq[:TILE], dq[TILE:])
            at = slice(RIM + t * TILE, RIM + (t + 1) * TILE)
            dj[0, at, lanes] = rope(dq, cos_ref[at, :], -sin_ref[at, :]).astype(BF16)

    for j in range(6):
        cols = slice(128 * j, 128 * (j + 1))
        part = rope(dk[:, cols], cos_ref[...], -sin_ref[...]).astype(BF16)
        if j < 3:
            dj[0, :, D + 128 * j : D + 128 * (j + 1)] = part
        else:
            dj[1, :, 128 * (j - 3) : 128 * (j - 2)] = part
    dj[1, :, D // 2 :] = dv[...].astype(BF16)
    sends = [
        pltpu.make_async_copy(dj.at[core], mine_ref, sems.at[0]),
        pltpu.make_async_copy(dj.at[1 - core], give_ref, sems.at[1]),
    ]
    start_all(sends)
    wait_all(sends)


def attention_back(*args):
    return call(
        attention_back_kernel,
        [((WIDE, HALF), BF16, False)] * 2,
        [
            pltpu.VMEM((WIDE, D), F32),
            pltpu.VMEM((WIDE, D), F32),
            pltpu.VMEM((2, WIDE, HALF), BF16),
            pltpu.SemaphoreType.DMA((2,)),
        ],
        10 * TOKENS * 2 * TILE * D,
        12 * 2**20,
        7,
        7,
        20,
    )(*args)


def late_kernel(*refs):
    ins, outs, refs = refs[:4], refs[4:8], refs[8:]
    h, dj, blocks, sems, out_sems = refs
    copies = paired_copies(ins, (h, dj), sems)
    start_all(copies)
    wait_all(copies)
    for part in range(3):
        cols = slice(384 * part, 384 * (part + 1))
        grad = dot_outer(h[...], dj[:, cols]).astype(BF16)
        blocks[:, :, cols] = grad.reshape(OWNERS, ROWS, 384)
    sends = block_copies(blocks, outs, out_sems)
    start_all(sends)
    wait_all(sends)


def late_grads(*args):
    return call(
        late_kernel,
        [((2, ROWS, HALF), BF16, False)] * 4,
        [
            pltpu.VMEM((2 * WIDE, D), BF16),
            pltpu.VMEM((2 * WIDE, HALF), BF16),
            pltpu.VMEM((OWNERS, ROWS, HALF), BF16),
            pltpu.SemaphoreType.DMA((4,)),
            pltpu.SemaphoreType.DMA((8,)),
        ],
        4 * WIDE * D * HALF,
        8 * 2**20,
        4,
        0,
        14,
    )(*args)


def input_kernel(normed_ref, inverse_ref, gain_ref, dx_ref, *refs):
    (weight, mine, give), refs = refs[:3], refs[3:]
    base_ref, low_ref, high_ref, joint_w, dj, upstream, sems = refs
    core = lax.axis_index("seq") % 2
    copies = [
        pltpu.make_async_copy(weight, joint_w, sems.at[0]),
        pltpu.make_async_copy(mine, dj.at[core], sems.at[1]),
        pltpu.make_async_copy(give, dj.at[1 - core], sems.at[2]),
    ]
    start_all(copies)
    wait_all(copies)
    for j in range(3):
        cols = slice(256 * j, 256 * (j + 1))
        upstream[:, cols] = dot_back(dj[0], joint_w[cols, :HALF]) + dot_back(
            dj[1], joint_w[cols, HALF:]
        )
    gain = jnp.concatenate([gain_chunk(gain_ref, 0, j) for j in range(6)], 1)
    step = 32

    def back(rows):
        return norm_back(upstream[rows, :], normed_ref[rows, :], inverse_ref[rows, :], gain)

    @pl.loop(0, TOKENS // step)
    def _(i):
        start = pl.multiple_of(i * step, step)
        base_ref[pl.ds(start, step), :] = dx_ref[pl.ds(start, step), :] + back(
            pl.ds(start + RIM, step)
        )

    @pl.loop(0, RIM // step)
    def _(i):
        start = pl.multiple_of(i * step, step)
        low_ref[pl.ds(start, step), :] = back(pl.ds(start, step)).astype(BF16)
        high_ref[pl.ds(start, step), :] = back(pl.ds(start + RIM + TOKENS, step)).astype(BF16)


def input_back(*args):
    return call(
        input_kernel,
        [((TOKENS, D), F32, True), ((RIM, D), BF16, True), ((RIM, D), BF16, True)],
        [
            pltpu.VMEM((D, 3 * D), BF16),
            pltpu.VMEM((2, WIDE, HALF), BF16),
            pltpu.VMEM((WIDE, D), F32),
            pltpu.SemaphoreType.DMA((3,)),
        ],
        2 * WIDE * D * 3 * D,
        10 * 2**20,
        7,
        4,
        18,
    )(*args)


def stack_kernel(*refs):
    *ins, out, sems = refs
    copies = [pltpu.make_async_copy(r, out.at[i], sems.at[i]) for i, r in enumerate(ins)]
    start_all(copies)
    wait_all(copies)


def stack(*parts):
    return call(
        stack_kernel,
        [((len(parts),) + parts[0].shape, parts[0].dtype, False)],
        [pltpu.SemaphoreType.DMA((len(parts),))],
        0,
        2 * len(parts) * parts[0].size * 2,
        len(parts),
        0,
        2,
    )(*parts)[0]


def gather_pairs(pair):
    from_low = over_fsdp(pair, 1, 0)
    from_high = over_fsdp(pair, -1, 0)
    from_far = over_fsdp(pair, 2, 0)
    return [pair, from_high, from_far, from_low]


def spread_sum(blocks, zh):
    got = [over_fsdp(blocks[d % 4], d, 0) for d in (1, -1, 2)]
    total = blocks[0].astype(F32) + sum(g.astype(F32) for g in got)
    keep, give = total[0], total[1].astype(BF16)
    total = (keep + over_fsdp(give, 0, 1).astype(F32)).astype(BF16)
    low, high, far = (over_seq(total, 0, d, 0) for d in (1, -1, 2))
    total = (
        (total.astype(F32) + far.astype(F32)) + (low.astype(F32) + high.astype(F32))
    ).astype(BF16)
    return (total.astype(F32) + over_seq(total, 1, 0, 0).astype(F32)).astype(BF16)


def in_order(mine, core):
    other = core_swap(mine)
    first = jnp.where(core == 0, mine, other).astype(F32)
    second = jnp.where(core == 0, other, mine).astype(F32)
    return first, second


def shards(
    inputs,
    first_gain,
    joint_weight,
    merge_weight,
    second_gain,
    expand_weight,
    shrink_weight,
    cotangent,
):
    x, zh, core, seq = place()
    fsdp = lax.axis_index("fsdp")
    source, upstream = inputs[0], cotangent[0]

    def columns(w, start, width):
        return lax.dynamic_slice_in_dim(w, start, width, 1)

    def placed_gain(gain):
        whole = lax.dynamic_update_slice_in_dim(jnp.zeros((D,), BF16), gain, fsdp * ROWS, 0)
        return jnp.pad(whole.reshape(6, 128), ((0, 2), (0, 0)))

    gain_tile = jnp.concatenate(
        [placed_gain(first_gain), placed_gain(second_gain), jnp.zeros((ROWS - 16, 128), BF16)], 0
    )
    joint_own = jnp.concatenate([columns(joint_weight, core * HALF, HALF), gain_tile], 1)
    joint_pair = stack(joint_own, over_fsdp(joint_own, 0, 1))
    joint_mine = gather_pairs(joint_pair)
    low_halo = passed_along(source[TOKENS - RIM :], 1)
    high_halo = passed_along(source[:RIM], -1)
    packed_own = jnp.concatenate(
        [columns(merge_weight, core * 384, 384)]
        + [columns(expand_weight, core * FF + 384 * i, 384) for i in range(3)]
        + [columns(shrink_weight, core * 384, 384)],
        0,
    )
    packed_own, _ = lax.optimization_barrier((packed_own, joint_pair))
    packed_mine = gather_pairs(stack(packed_own, over_fsdp(packed_own, 0, 1)))

    frequencies = jnp.exp(
        jnp.arange(HEAD_DIM // 2, dtype=F32) * (-2.0 * math.log(10000.0) / HEAD_DIM)
    )
    positions = (seq * TOKENS - RIM + lax.iota(jnp.int32, WIDE)).astype(F32)
    angles = positions[:, None] * frequencies[None, :]
    cosine, sine = jnp.cos(angles), jnp.sin(angles)
    cosine = jnp.concatenate([cosine] * 4, 1)
    sine = jnp.concatenate([-sine, sine] * 2, 1)
    extended = jnp.concatenate([low_halo, source, high_halo], 0).astype(F32)
    normed, inverse = normalize(extended)

    *joint_mine, normed, cosine, sine = lax.optimization_barrier((*joint_mine, normed, cosine, sine))
    joint_pieces = joint_mine + [core_swap(p) for p in joint_mine]
    q, k, v, h_first, attended, probs, gains, joint_w = joint_forward(
        normed, cosine, sine, joint_pieces
    )
    *packed_mine, attended = lax.optimization_barrier((*packed_mine, attended))
    packed_pieces = packed_mine + [core_swap(p) for p in packed_mine]
    h_first_other = core_swap(h_first)
    attended_other = core_swap(attended)
    dy_mine = columns(upstream, core * 384, 384)
    dy_got = core_swap(columns(upstream, (1 - core) * 384, 384))
    result, hidden, h_second, dx, datt, dz_mine, dz_give, dob_mine, dob_give = middle(
        source, attended, upstream, gains, packed_pieces
    )
    early = early_grads(
        h_second,
        core_swap(h_second),
        dz_mine,
        core_swap(dz_give),
        attended,
        attended_other,
        dob_mine,
        core_swap(dob_give),
        hidden,
        core_swap(hidden),
        dy_mine,
        dy_got,
    )
    *early, datt = lax.optimization_barrier((*early, datt))
    dj_mine, dj_give = attention_back(q, k, v, probs, datt, cosine, sine)
    late = late_grads(h_first, h_first_other, dj_mine, core_swap(dj_give))
    *late, dj_mine = lax.optimization_barrier((*late, dj_mine))
    base, low_back, high_back = input_back(normed, inverse, gains, dx, joint_w, dj_mine, dj_give)
    from_high = passed_along(low_back, -1).astype(F32)
    from_low = passed_along(high_back, 1).astype(F32)
    input_grad = (
        base
        + jnp.pad(from_high, ((TOKENS - RIM, 0), (0, 0)))
        + jnp.pad(from_low, ((0, TOKENS - RIM), (0, 0)))
    ).astype(BF16)

    first, second = in_order(spread_sum(early, zh), core)
    merge_grad = jnp.concatenate([first[:ROWS], second[:ROWS]], 1)
    expand_grad = jnp.concatenate(
        [s[ROWS * (i + 1) : ROWS * (i + 2)] for s in (first, second) for i in range(3)], 1
    )
    shrink_grad = jnp.concatenate([first[4 * ROWS :], second[4 * ROWS :]], 1)
    joint_grad = jnp.concatenate(in_order(spread_sum(late, zh), core), 1)

    def gain_grad(weight, grad, gain):
        return jnp.sum(weight.astype(F32) * grad, axis=1) / gain.astype(F32)

    return (
        result[None],
        input_grad[None],
        gain_grad(joint_weight, joint_grad, first_gain),
        joint_grad,
        merge_grad,
        gain_grad(expand_weight, expand_grad, second_gain),
        expand_grad,
        shrink_grad,
    )


def solution(mesh):
    placed = (
        P("fsdp", "seq", None),
        P("fsdp"),
        P("fsdp", None),
        P("fsdp", None),
        P("fsdp"),
        P("fsdp", None),
        P("fsdp", None),
        P("fsdp", "seq", None),
    )
    return jax.shard_map(
        shards,
        mesh=mesh,
        in_specs=placed,
        out_specs=(
            P("fsdp", "seq", None),
            P("fsdp", "seq", None),
            P("fsdp"),
            P("fsdp", None),
            P("fsdp", None),
            P("fsdp"),
            P("fsdp", None),
            P("fsdp", None),
        ),
        check_vma=False,
    )
```

```python
import math

import jax
import jax.numpy as jnp
from jax import lax
from jax.experimental import pallas as pl
from jax.experimental.pallas import tpu as pltpu
from jax.sharding import PartitionSpec as P

D = 768
HEADS = 12
HEAD_DIM = 64
FF = 1152
RIM = 64
TOKENS = 384
WIDE = TOKENS + 2 * RIM
TILE = 128
TILES = TOKENS // TILE
PAIRS = HEADS // 2
OWNERS = 8
ROWS = D // OWNERS
FF_ROWS = FF // OWNERS
HALF = 3 * D // 2
LATE_ROWS = 448
LATE_QUARTER = LATE_ROWS // 4
SIDE = 256
QUARTER = SIDE // 4
EPSILON = 1e-05
F32 = jnp.float32
BF16 = jnp.bfloat16
MIB = 2**20


def over_fsdp(value, dx, dz):
    pairs = [
        (x * 2 + z, ((x + dx) % 4) * 2 + (z + dz) % 2) for x in range(4) for z in range(2)
    ]
    return lax.ppermute(value, "fsdp", pairs)


def over_seq(value, dz, dy, dc):
    pairs = [
        (z * 8 + y * 2 + c, ((z + dz) % 2) * 8 + ((y + dy) % 4) * 2 + (c + dc) % 2)
        for z in range(2)
        for y in range(4)
        for c in range(2)
    ]
    return lax.ppermute(value, "seq", pairs)


def core_swap(value):
    return over_seq(value, 0, 0, 1)


def passed_along(value, steps):
    first, last = (max(0, -steps), min(16, 16 - steps))
    return lax.ppermute(value, "seq", [(i, i + steps) for i in range(first, last)])


def place():
    fsdp, seq = lax.axis_index("fsdp"), lax.axis_index("seq")
    return fsdp // 2, fsdp % 2, seq % 2, seq


def owner(x, zh, dx, dz):
    return ((x + dx) % 4) * 2 + (zh + dz) % 2


def dot(left, right):
    return jnp.dot(left, right, preferred_element_type=F32)


def dot_back(left, right):
    return lax.dot_general(left, right, (((1,), (1,)), ((), ())), preferred_element_type=F32)


def dot_outer(left, right):
    return lax.dot_general(left, right, (((0,), (0,)), ((), ())), preferred_element_type=F32)


def row_mean(values):
    return jnp.sum(values, axis=-1, keepdims=True) * (1.0 / D)


def normalize(values):
    centred = values - row_mean(values)
    inverse = lax.rsqrt(row_mean(centred * centred) + EPSILON)
    return (centred * inverse, inverse)


def norm_back(upstream, normed, inverse, gain):
    scaled = upstream * gain
    centred = scaled - row_mean(scaled)
    return inverse * (centred - normed * row_mean(scaled * normed))


def rope(values, cosine, sine):
    lane = lax.broadcasted_iota(jnp.int32, values.shape, 1) % HEAD_DIM
    partner = jnp.where(
        lane < HEAD_DIM // 2,
        pltpu.roll(values, 128 - HEAD_DIM // 2, 1),
        pltpu.roll(values, HEAD_DIM // 2, 1),
    )
    return values * cosine + partner * sine


def call(kernel, outs, scratch, spaces, limit):
    kinds = {"v": pltpu.VMEM, "h": pltpu.HBM, "a": pl.ANY}
    return pl.pallas_call(
        kernel,
        out_shape=[jax.ShapeDtypeStruct(shape, kind) for shape, kind in outs],
        in_specs=[pl.BlockSpec(memory_space=kinds[c]) for c in spaces],
        out_specs=[pl.BlockSpec(memory_space=pltpu.HBM) for _ in outs],
        scratch_shapes=scratch,
        compiler_params=pltpu.CompilerParams(vmem_limit_bytes=limit * MIB),
    )


def like(outs):
    return [pltpu.VMEM(shape, kind) for shape, kind in outs]


def copy_all(sources, targets, sems, first=0):
    return [
        pltpu.make_async_copy(a, b, sems.at[first + i])
        for i, (a, b) in enumerate(zip(sources, targets, strict=True))
    ]


def start_all(copies):
    for copy in copies:
        copy.start()


def wait_all(copies):
    for copy in copies:
        copy.wait()


def piece_places(pieces):
    x, zh, core, _ = place()
    return [
        (
            side * 8 + dx * 2 + dz,
            pieces[side * 4 + dx].at[dz],
            owner(x, zh, dx, dz),
            (core + side) % 2,
        )
        for side in range(2)
        for dx in range(4)
        for dz in range(2)
    ]


def joint_copies(pieces, joint_w, sems):
    return [
        pltpu.make_async_copy(
            piece.at[:, pl.ds(0, HALF)],
            joint_w.at[
                pl.ds(pl.multiple_of(who * ROWS, 16), ROWS),
                pl.ds(pl.multiple_of(half * HALF, 128), HALF),
            ],
            sems.at[i],
        )
        for i, piece, who, half in piece_places(pieces)
    ]


def gain_chunk(gain_ref, row, j):
    return gain_ref[row + j : row + j + 1, :]


JOINT_OUTS = [
    ((TOKENS, D), BF16),
    ((WIDE, D), BF16),
    ((WIDE, D), BF16),
    ((WIDE, D), BF16),
    ((TOKENS, D), BF16),
    ((PAIRS * TILES, 2 * TILE, 2 * TILE), BF16),
    ((16, 128), F32),
    ((D, 3 * D), BF16),
]


def joint_kernel(normed_ref, cos_ref, sin_ref, *refs):
    pieces, outs, refs = refs[:8], refs[8:16], refs[16:]
    q_ref, k_ref, v_ref, h_ref, att_ref, probs_ref, gain_ref, joint_w, gains, sems, out_sems = refs
    copies = joint_copies(pieces, joint_w, sems)
    gain_copies = [
        pltpu.make_async_copy(
            pieces[i // 2].at[i % 2, pl.ds(0, 16), pl.ds(HALF, 128)], gains.at[i], sems.at[16 + i]
        )
        for i in range(8)
    ]
    start_all(gain_copies)
    start_all(copies)
    wait_all(gain_copies)
    gain_ref[...] = jnp.sum(gains[...].astype(F32), axis=0)
    for j in range(D // 128):
        cols = slice(128 * j, 128 * (j + 1))
        h_ref[:, cols] = (normed_ref[:, cols] * gain_chunk(gain_ref, 0, j)).astype(BF16)
    wait_all(copies)
    sends = copy_all(refs[:5] + refs[6:8], outs[:5] + outs[6:8], out_sems)
    start_all(sends[5:])
    own = slice(RIM, RIM + TOKENS)
    for j in range(9):
        cols = slice(256 * j, 256 * (j + 1))
        rows = own if j < 3 else slice(0, WIDE)
        got = dot(h_ref[rows, :], joint_w[:, cols])
        out = (q_ref, k_ref, v_ref)[j // 3]
        for a in range(2):
            part = got[:, 128 * a : 128 * (a + 1)]
            if j < 6:
                part = rope(part, cos_ref[rows, :], sin_ref[rows, :])
            at = 256 * (j % 3) + 128 * a
            out[:, at : at + 128] = part.astype(BF16)

    start_all(sends[:4])
    offset = lax.axis_index("seq") * TOKENS
    row = lax.broadcasted_iota(jnp.int32, (TILE, 2 * TILE), 0)
    col = lax.broadcasted_iota(jnp.int32, (TILE, 2 * TILE), 1)
    lane = lax.broadcasted_iota(jnp.int32, (TILE, 128), 1)
    band = (col >= row) & (col - row <= 2 * RIM)

    @pl.loop(0, PAIRS)
    def _(pair):
        lanes = pl.ds(pl.multiple_of(pair * 128, 128), 128)
        for t in range(TILES):
            key = col + (offset + t * TILE - RIM)
            allowed = band & (key >= 0) & (key < 16 * TOKENS)
            query = q_ref[t * TILE : (t + 1) * TILE, lanes].astype(F32) * (HEAD_DIM**-0.5)
            stacked = jnp.concatenate(
                [jnp.where(lane < HEAD_DIM, query, 0.0), jnp.where(lane < HEAD_DIM, 0.0, query)], 0
            ).astype(BF16)
            window = slice(t * TILE, (t + 2) * TILE)
            scores = dot_back(stacked, k_ref[window, lanes])
            scores = jnp.where(jnp.concatenate([allowed, allowed], 0), scores, -1e30)
            expo = jnp.exp(scores - jnp.max(scores, axis=-1, keepdims=True))
            probs = (expo / jnp.sum(expo, axis=-1, keepdims=True)).astype(BF16)
            probs_ref[pair * TILES + t] = probs
            mixed = dot(probs, v_ref[window, lanes])
            att_ref[t * TILE : (t + 1) * TILE, lanes] = jnp.where(
                lane < HEAD_DIM, mixed[:TILE], mixed[TILE:]
            ).astype(BF16)
        pltpu.make_async_copy(
            probs_ref.at[pl.ds(pair * TILES, TILES)],
            outs[5].at[pl.ds(pair * TILES, TILES)],
            out_sems.at[7 + pair],
        ).start()

    sends[4].start()
    wait_all(sends)
    for pair in range(PAIRS):
        tiles = pl.ds(pair * TILES, TILES)
        pltpu.make_async_copy(probs_ref.at[tiles], outs[5].at[tiles], out_sems.at[7 + pair]).wait()


def joint_forward(normed, cosine, sine, pieces):
    return call(
        joint_kernel,
        JOINT_OUTS,
        like(JOINT_OUTS)
        + [
            pltpu.VMEM((8, 16, 128), BF16),
            pltpu.SemaphoreType.DMA((24,)),
            pltpu.SemaphoreType.DMA((13,)),
        ],
        "vvv" + "a" * 8,
        18,
    )(normed, cosine, sine, *pieces)


def expand_copies(pieces, expand_w, sems):
    return [
        pltpu.make_async_copy(
            piece,
            expand_w.at[
                pl.ds(pl.multiple_of(who * ROWS, 16), ROWS),
                pl.ds(pl.multiple_of(half * FF, 128), FF),
            ],
            sems.at[i],
        )
        for i, piece, who, half in piece_places(pieces)
    ]


def side_copies(pieces, sides, sems):
    x, zh, core, seq = place()
    y = seq % 8 // 2
    return [
        pltpu.make_async_copy(
            pieces[side * 4 + dy].at[dx * 2 + dz],
            sides.at[(core + side) % 2, (y + dy) % 4, owner(x, zh, dx, dz)],
            sems.at[((side * 4 + dy) * 4 + dx) * 2 + dz],
        )
        for side in range(2)
        for dy in range(4)
        for dx in range(4)
        for dz in range(2)
    ]


MIDDLE_OUTS = [
    ((TOKENS, D), BF16),
    ((TOKENS, FF), BF16),
    ((TOKENS, D), BF16),
    ((TOKENS, D), F32),
    ((TOKENS, D), BF16),
]
MIDDLE_HALVES = [((TOKENS, FF), BF16)] * 2 + [((TOKENS, D // 2), BF16)] * 2


def middle_kernel(gain_ref, *refs):
    ins, pieces, sides_in, refs = refs[:3], refs[3:11], refs[11:19], refs[19:]
    outs, halves, refs = refs[:5], refs[5:9], refs[9:]
    x_ref, att_ref, dy_ref, out_ref, m_ref, h_ref, dx_ref, datt_ref = refs[:8]
    merge_w, expand_w, shrink_w, sides, x1, normed, inverse, z, dm, dz, dob = refs[8:19]
    in_sems, side_sems, expand_sems, out_sems = refs[19:]
    dz_mine, dz_give, dob_mine, dob_give = halves
    core = lax.axis_index("seq") % 2
    loads = copy_all(ins, (x_ref, att_ref, dy_ref), in_sems)
    side_loads = side_copies(sides_in, sides, side_sems)
    expand = expand_copies(pieces, expand_w, expand_sems)
    start_all(loads)
    start_all(side_loads)
    start_all(expand)
    sends = copy_all(refs[3:8], outs, out_sems)
    wait_all(side_loads)
    for half in range(2):
        cols = slice(384 * half, 384 * (half + 1))
        merge_w[:, cols] = jnp.concatenate(
            [sides[half, 2, :, 16:, :], sides[half, 3, :, :48, :]], 1
        ).reshape(D, 384)
    wait_all(loads)
    for j in range(3):
        cols = slice(256 * j, 256 * (j + 1))
        x1[:, cols] = x_ref[:, cols].astype(F32) + dot(att_ref[...], merge_w[:, cols])

    step = 32
    gain = jnp.concatenate([gain_chunk(gain_ref, 8, j) for j in range(6)], 1)

    @pl.loop(0, TOKENS // step)
    def _(i):
        rows = pl.ds(pl.multiple_of(i * step, step), step)
        part, scale = normalize(x1[rows, :])
        normed[rows, :] = part
        inverse[rows, :] = scale
        h_ref[rows, :] = (part * gain).astype(BF16)

    for half in range(2):
        cols = slice(384 * half, 384 * (half + 1))
        shrink_w[:, cols] = jnp.concatenate(
            [sides[half, 0], sides[half, 1], sides[half, 2, :, :16, :]], 1
        ).reshape(FF, 384)
    for j in range(3):
        cols = slice(384 * j, 384 * (j + 1))
        dm[:, cols] = dot_back(dy_ref[...], shrink_w[cols, :])
    wait_all(expand)
    for j in range(9):
        cols = slice(256 * j, 256 * (j + 1))
        z[:, cols] = dot(h_ref[...], expand_w[:, cols])

    @pl.loop(0, TOKENS // 16)
    def _(i):
        rows = pl.ds(pl.multiple_of(i * 16, 16), 16)
        gate = z[rows, pl.ds(0, FF)]
        up = z[rows, pl.ds(FF, FF)]
        upstream = dm[rows, :]
        below = 0.5 + 0.5 * lax.erf(gate * (0.5**0.5))
        slope = below + gate * (jnp.exp(-0.5 * gate * gate) * (2 * math.pi) ** -0.5)
        active = gate * below
        m_ref[rows, :] = (active * up).astype(BF16)
        dz[0, rows, :] = (upstream * up * slope).astype(BF16)
        dz[1, rows, :] = (upstream * active).astype(BF16)

    sends += copy_all((dz.at[core], dz.at[1 - core]), (dz_mine, dz_give), out_sems, 5)
    start_all(sends[1:3])
    start_all(sends[5:])
    for j in range(3):
        cols = slice(256 * j, 256 * (j + 1))
        out_ref[:, cols] = (x1[:, cols] + dot(m_ref[...], shrink_w[:, cols])).astype(BF16)
    start_all(sends[:1])
    for j in range(3):
        rows = slice(256 * j, 256 * (j + 1))
        x1[:, rows] = dot_back(dz[0], expand_w[rows, :FF]) + dot_back(dz[1], expand_w[rows, FF:])

    @pl.loop(0, TOKENS // step)
    def _(i):
        rows = pl.ds(pl.multiple_of(i * step, step), step)
        back = norm_back(x1[rows, :], normed[rows, :], inverse[rows, :], gain)
        total = dy_ref[rows, :].astype(F32) + back
        dx_ref[rows, :] = total
        dob[0, rows, :] = total[:, :384].astype(BF16)
        dob[1, rows, :] = total[:, 384:].astype(BF16)

    sends += copy_all((dob.at[core], dob.at[1 - core]), (dob_mine, dob_give), out_sems, 7)
    start_all(sends[7:])
    start_all(sends[3:4])
    for j in range(3):
        cols = slice(256 * j, 256 * (j + 1))
        datt_ref[:, cols] = (
            dot_back(dob[0], merge_w[cols, :384]) + dot_back(dob[1], merge_w[cols, 384:])
        ).astype(BF16)
    start_all(sends[4:5])
    wait_all(sends)


def middle(gains, x, att, dy, pieces, sides):
    return call(
        middle_kernel,
        MIDDLE_OUTS + MIDDLE_HALVES,
        [pltpu.VMEM((TOKENS, D), BF16)] * 3
        + like(MIDDLE_OUTS)
        + [
            pltpu.VMEM((D, D), BF16),
            pltpu.VMEM((D, 2 * FF), BF16),
            pltpu.VMEM((FF, D), BF16),
            pltpu.VMEM((2, 4, OWNERS, QUARTER, 384), BF16),
            pltpu.VMEM((TOKENS, D), F32),
            pltpu.VMEM((TOKENS, D), F32),
            pltpu.VMEM((TOKENS, 1), F32),
            pltpu.VMEM((TOKENS, 2 * FF), F32),
            pltpu.VMEM((TOKENS, FF), F32),
            pltpu.VMEM((2, TOKENS, FF), BF16),
            pltpu.VMEM((2, TOKENS, D // 2), BF16),
            pltpu.SemaphoreType.DMA((3,)),
            pltpu.SemaphoreType.DMA((64,)),
            pltpu.SemaphoreType.DMA((16,)),
            pltpu.SemaphoreType.DMA((9,)),
        ],
        "vhhh" + "a" * 16,
        34,
    )(gains, x, att, dy, *pieces, *sides)


def paired_copies(refs, buffers, sems):
    copies = []
    for n, buffer in enumerate(buffers):
        rows = buffer.shape[0] // 2
        for side in range(2):
            copies.append(
                pltpu.make_async_copy(
                    refs[2 * n + side], buffer.at[pl.ds(side * rows, rows), :], sems.at[2 * n + side]
                )
            )
    return copies


def early_kernel(*refs):
    ins, outs, refs = refs[:8], refs[8:12], refs[12:]
    h, dz, att, dob, blocks, sems, out_sems = refs
    x, zh, _, seq = place()
    y = seq % 8 // 2
    copies = paired_copies(ins, (h, dz, att, dob), sems)
    start_all(copies)
    wait_all(copies)
    for part in range(3):
        grad = dot_outer(h[...], dz[:, 384 * part : 384 * (part + 1)]).astype(BF16)
        blocks[part] = grad.reshape(OWNERS, ROWS, 384)
    grad = dot_outer(att[...], dob[...]).astype(BF16)
    blocks[3] = grad.reshape(OWNERS, ROWS, 384)
    sends = [
        pltpu.make_async_copy(
            blocks.at[(y + dy) % 4, owner(x, zh, dx, dz)],
            outs[dy].at[dx * 2 + dz],
            out_sems.at[dy * 8 + dx * 2 + dz],
        )
        for dy in range(4)
        for dx in range(4)
        for dz in range(2)
    ]
    start_all(sends)
    wait_all(sends)


def early_grads(*args):
    return call(
        early_kernel,
        [((OWNERS, ROWS, 384), BF16)] * 4,
        [
            pltpu.VMEM((2 * TOKENS, D), BF16),
            pltpu.VMEM((2 * TOKENS, FF), BF16),
            pltpu.VMEM((2 * TOKENS, D), BF16),
            pltpu.VMEM((2 * TOKENS, D // 2), BF16),
            pltpu.VMEM((4, OWNERS, ROWS, 384), BF16),
            pltpu.SemaphoreType.DMA((8,)),
            pltpu.SemaphoreType.DMA((32,)),
        ],
        "ha" * 4,
        20,
    )(*args)


def attention_back_kernel(cos_ref, sin_ref, *refs):
    ins, probs_in, mine_ref, give_ref, scratch = refs[:4], refs[4], refs[5], refs[6], refs[7:]
    q_ref, k_ref, v_ref, datt_ref, probs_ref, dk, dv, dj, in_sems, sems = scratch
    loads = copy_all(ins, scratch[:4], in_sems)
    start_all(loads)

    def load_probs(pair):
        tiles = pl.ds(pair * TILES, TILES)
        return pltpu.make_async_copy(probs_in.at[tiles], probs_ref.at[tiles], in_sems.at[4 + pair])

    for pair in range(PAIRS):
        load_probs(pair).start()
    core = lax.axis_index("seq") % 2
    lane = lax.broadcasted_iota(jnp.int32, (TILE, 128), 1)
    own = slice(RIM, RIM + TOKENS)
    dk[...] = jnp.zeros_like(dk)
    dv[...] = jnp.zeros_like(dv)
    dj[0, :RIM, :D] = jnp.zeros((RIM, D), BF16)
    dj[0, RIM + TOKENS :, :D] = jnp.zeros((RIM, D), BF16)
    wait_all(loads)
    scale = HEAD_DIM**-0.5

    @pl.loop(0, PAIRS)
    def _(pair):
        lanes = pl.ds(pl.multiple_of(pair * 128, 128), 128)
        load_probs(pair).wait()
        for t in range(TILES):
            rows = slice(t * TILE, (t + 1) * TILE)
            window = slice(t * TILE, (t + 2) * TILE)
            query = q_ref[rows, lanes].astype(F32) * scale
            query = jnp.concatenate(
                [jnp.where(lane < HEAD_DIM, query, 0.0), jnp.where(lane < HEAD_DIM, 0.0, query)], 0
            ).astype(BF16)
            upstream = datt_ref[rows, lanes].astype(F32)
            upstream = jnp.concatenate(
                [
                    jnp.where(lane < HEAD_DIM, upstream, 0.0),
                    jnp.where(lane < HEAD_DIM, 0.0, upstream),
                ],
                0,
            ).astype(BF16)
            probs_b = probs_ref[pair * TILES + t]
            probs = probs_b.astype(F32)
            dp = dot_back(upstream, v_ref[window, lanes])
            delta = jnp.sum(probs * dp, axis=-1, keepdims=True)
            ds = (probs * (dp - delta)).astype(BF16)
            dv[window, lanes] += dot_outer(probs_b, upstream)
            dk[window, lanes] += dot_outer(ds, query)
            dq = dot(ds, k_ref[window, lanes]) * scale
            dq = jnp.where(lane < HEAD_DIM, dq[:TILE], dq[TILE:])
            at = slice(RIM + t * TILE, RIM + (t + 1) * TILE)
            dj[0, at, lanes] = rope(dq, cos_ref[at, :], -sin_ref[at, :]).astype(BF16)

    for j in range(6):
        cols = slice(128 * j, 128 * (j + 1))
        part = rope(dk[:, cols], cos_ref[...], -sin_ref[...]).astype(BF16)
        if j < 3:
            dj[0, :, D + 128 * j : D + 128 * (j + 1)] = part
        else:
            dj[1, :, 128 * (j - 3) : 128 * (j - 2)] = part
    dj[1, :, D // 2 :] = dv[...].astype(BF16)
    sends = [
        pltpu.make_async_copy(dj.at[core], mine_ref, sems.at[0]),
        pltpu.make_async_copy(dj.at[1 - core], give_ref, sems.at[1]),
    ]
    start_all(sends)
    wait_all(sends)


def attention_back(*args):
    return call(
        attention_back_kernel,
        [((WIDE, HALF), BF16)] * 2,
        [
            pltpu.VMEM((TOKENS, D), BF16),
            pltpu.VMEM((WIDE, D), BF16),
            pltpu.VMEM((WIDE, D), BF16),
            pltpu.VMEM((TOKENS, D), BF16),
            pltpu.VMEM((PAIRS * TILES, 2 * TILE, 2 * TILE), BF16),
            pltpu.VMEM((WIDE, D), F32),
            pltpu.VMEM((WIDE, D), F32),
            pltpu.VMEM((2, WIDE, HALF), BF16),
            pltpu.SemaphoreType.DMA((10,)),
            pltpu.SemaphoreType.DMA((2,)),
        ],
        "vvhhhhh",
        20,
    )(*args)


def late_kernel(*refs):
    ins, outs, refs = refs[:8], refs[8:12], refs[12:]
    m, dy, h, dj, blocks, sems, out_sems = refs
    x, zh, _, _ = place()
    copies = paired_copies(ins, (m, dy, h, dj), sems)
    start_all(copies)
    wait_all(copies)
    grad = dot_outer(m[...], dy[...]).astype(BF16)
    blocks[:, :FF_ROWS, :] = grad.reshape(OWNERS, FF_ROWS, 384)
    for part in range(3):
        grad = dot_outer(h[...], dj[:, 384 * part : 384 * (part + 1)]).astype(BF16)
        at = FF_ROWS + ROWS * part
        blocks[:, at : at + ROWS, :] = grad.reshape(OWNERS, ROWS, 384)
    blocks[:, FF_ROWS + 3 * ROWS :, :] = jnp.zeros((OWNERS, 16, 384), BF16)
    sends = [
        pltpu.make_async_copy(blocks.at[owner(x, zh, dx, dz)], outs[dx].at[dz], out_sems.at[dx * 2 + dz])
        for dx in range(4)
        for dz in range(2)
    ]
    start_all(sends)
    wait_all(sends)


def late_grads(*args):
    return call(
        late_kernel,
        [((2, LATE_ROWS, 384), BF16)] * 4,
        [
            pltpu.VMEM((2 * TOKENS, FF), BF16),
            pltpu.VMEM((2 * TOKENS, D // 2), BF16),
            pltpu.VMEM((2 * WIDE, D), BF16),
            pltpu.VMEM((2 * WIDE, HALF), BF16),
            pltpu.VMEM((OWNERS, LATE_ROWS, 384), BF16),
            pltpu.SemaphoreType.DMA((8,)),
            pltpu.SemaphoreType.DMA((8,)),
        ],
        "ha" * 4,
        20,
    )(*args)


def sum_of(parts, index):
    return sum(part[index].astype(F32) for part in parts)


def early_sum_kernel(*refs):
    ins, outs, parts, total, sems, out_sems = refs[:4], refs[4:8], refs[8:12], *refs[12:]
    copies = copy_all(ins, parts, sems)
    start_all(copies)
    wait_all(copies)
    sends = [
        pltpu.make_async_copy(total.at[pl.ds(2 * d, 2)], outs[d], out_sems.at[d]) for d in range(4)
    ]
    for d in (1, 3, 2, 0):
        for i in (2 * d, 2 * d + 1):
            total[i] = sum_of(parts, i).astype(BF16)
        sends[d].start()
    wait_all(sends)


def late_sum_kernel(*refs):
    ins, outs, parts, total, sems, out_sems = refs[:4], refs[4:8], refs[8:12], *refs[12:]
    _, _, _, seq = place()
    y = seq % 8 // 2
    copies = copy_all(ins, parts, sems)
    start_all(copies)
    wait_all(copies)
    for i in range(2):
        total[i] = sum_of(parts, i).astype(BF16)
    sends = [
        pltpu.make_async_copy(
            total.at[:, pl.ds(pl.multiple_of((y + d) % 4 * LATE_QUARTER, 16), LATE_QUARTER), :],
            outs[d],
            out_sems.at[d],
        )
        for d in range(4)
    ]
    start_all(sends)
    wait_all(sends)


def both_sum_kernel(*refs):
    ins, outs, parts, keep, give, sems, out_sems = refs[:8], refs[8:10], refs[10:18], *refs[18:]
    copies = copy_all(ins, parts, sems)
    start_all(copies)
    wait_all(copies)
    keep[:ROWS] = sum_of(parts[:4], 0)
    keep[ROWS:] = sum_of(parts[4:], 0)
    give[:ROWS] = sum_of(parts[:4], 1).astype(BF16)
    give[ROWS:] = sum_of(parts[4:], 1).astype(BF16)
    sends = copy_all((keep, give), outs, out_sems)
    start_all(sends)
    wait_all(sends)


def summed(kernel, parts, outs, scratch):
    return call(
        kernel,
        outs,
        [pltpu.VMEM(part.shape, part.dtype) for part in parts]
        + scratch
        + [pltpu.SemaphoreType.DMA((len(parts),)), pltpu.SemaphoreType.DMA((len(outs),))],
        "a" * len(parts),
        14,
    )(*parts)


def early_sum(parts):
    shape = (OWNERS, ROWS, 384)
    outs = [((2, ROWS, 384), BF16)] * 4
    return summed(early_sum_kernel, parts, outs, [pltpu.VMEM(shape, BF16)])


def late_sum(parts):
    shape = (2, LATE_ROWS, 384)
    outs = [((2, LATE_QUARTER, 384), BF16)] * 4
    return summed(late_sum_kernel, parts, outs, [pltpu.VMEM(shape, BF16)])


def both_sum(parts):
    outs = [((ROWS + LATE_QUARTER, 384), F32), ((ROWS + LATE_QUARTER, 384), BF16)]
    return summed(both_sum_kernel, parts, outs, like(outs))


INPUT_OUTS = [((TOKENS, D), F32), ((RIM, D), BF16), ((RIM, D), BF16)]


def input_kernel(inverse_ref, gain_ref, *refs):
    (normed, dx, weight, mine, give), outs, refs = refs[:5], refs[5:8], refs[8:]
    base_ref, low_ref, high_ref, joint_w, dj, upstream, normed_ref, dx_ref, sems, out_sems = refs
    core = lax.axis_index("seq") % 2
    copies = [
        pltpu.make_async_copy(weight, joint_w, sems.at[0]),
        pltpu.make_async_copy(mine, dj.at[core], sems.at[1]),
        pltpu.make_async_copy(give, dj.at[1 - core], sems.at[2]),
        pltpu.make_async_copy(normed, normed_ref, sems.at[3]),
        pltpu.make_async_copy(dx, dx_ref, sems.at[4]),
    ]
    start_all(copies)
    wait_all(copies)
    for j in range(3):
        cols = slice(256 * j, 256 * (j + 1))
        upstream[:, cols] = dot_back(dj[0], joint_w[cols, :HALF]) + dot_back(
            dj[1], joint_w[cols, HALF:]
        )
    gain = jnp.concatenate([gain_chunk(gain_ref, 0, j) for j in range(6)], 1)
    step = 32

    def back(rows):
        return norm_back(upstream[rows, :], normed_ref[rows, :], inverse_ref[rows, :], gain)

    @pl.loop(0, TOKENS // step)
    def _(i):
        start = pl.multiple_of(i * step, step)
        base_ref[pl.ds(start, step), :] = dx_ref[pl.ds(start, step), :] + back(
            pl.ds(start + RIM, step)
        )

    @pl.loop(0, RIM // step)
    def _(i):
        start = pl.multiple_of(i * step, step)
        low_ref[pl.ds(start, step), :] = back(pl.ds(start, step)).astype(BF16)
        high_ref[pl.ds(start, step), :] = back(pl.ds(start + RIM + TOKENS, step)).astype(BF16)

    sends = copy_all(refs[:3], outs, out_sems)
    start_all(sends)
    wait_all(sends)


def input_back(*args):
    return call(
        input_kernel,
        INPUT_OUTS,
        like(INPUT_OUTS)
        + [
            pltpu.VMEM((D, 3 * D), BF16),
            pltpu.VMEM((2, WIDE, HALF), BF16),
            pltpu.VMEM((WIDE, D), F32),
            pltpu.VMEM((WIDE, D), F32),
            pltpu.VMEM((TOKENS, D), F32),
            pltpu.SemaphoreType.DMA((5,)),
            pltpu.SemaphoreType.DMA((3,)),
        ],
        "vvahhhh",
        20,
    )(*args)


RESULTS = [((ROWS, 3 * D), F32), ((ROWS, D), F32), ((ROWS, 2 * FF), F32), ((FF_ROWS, D), F32)]
GAIN_RESULTS = [((ROWS, 1), F32)] * 2


def result_kernel(first_gain, second_gain, *refs):
    sums, weights, outs, refs = refs[:2], refs[2:4], refs[4:10], refs[10:]
    joint, merge, expand, shrink, first, second, early, late, joint_w, expand_w, sems = refs
    _, _, core, seq = place()
    y = seq % 8 // 2
    copies = copy_all(weights, (joint_w, expand_w), sems)
    for side in range(2):
        half = (core + side) % 2
        for dy in range(4):
            quarter = (y + dy) % 4
            rows = pl.ds(pl.multiple_of(quarter * LATE_QUARTER, 16), LATE_QUARTER)
            copies += copy_all(
                (
                    sums[side].at[dy, pl.ds(0, ROWS)],
                    sums[side].at[dy, pl.ds(ROWS, LATE_QUARTER)],
                ),
                (early.at[half, quarter], late.at[half, rows]),
                sems,
                2 + (side * 4 + dy) * 2,
            )
    start_all(copies)
    wait_all(copies)
    for half in range(2):
        cols = slice(384 * half, 384 * (half + 1))
        shrink[:, cols] = late[half, :FF_ROWS].astype(F32)
        merge[:, cols] = early[half, 3].astype(F32)
        for part in range(3):
            cols = slice(FF * half + 384 * part, FF * half + 384 * (part + 1))
            at = FF_ROWS + ROWS * part
            expand[:, cols] = early[half, part].astype(F32)
            joint[:, cols] = late[half, at : at + ROWS].astype(F32)
    sends = copy_all((joint, merge, expand, shrink, first, second), outs, sems, 18)
    start_all(sends[:4])
    for total, weight, grad, gain in (
        (first, joint_w, joint, first_gain),
        (second, expand_w, expand, second_gain),
    ):
        product = weight[...].astype(F32) * grad[...]
        total[...] = jnp.sum(product, axis=1, keepdims=True) / gain[...]
    start_all(sends[4:])
    wait_all(sends)


def results(*args):
    return call(
        result_kernel,
        RESULTS + GAIN_RESULTS,
        like(RESULTS + GAIN_RESULTS)
        + [
            pltpu.VMEM((2, 4, ROWS, 384), BF16),
            pltpu.VMEM((2, LATE_ROWS, 384), BF16),
            pltpu.VMEM((ROWS, 3 * D), BF16),
            pltpu.VMEM((ROWS, 2 * FF), BF16),
            pltpu.SemaphoreType.DMA((24,)),
        ],
        "vvaahh",
        12,
    )(*args)


def stack_kernel(*refs):
    *ins, out, sems = refs
    copies = [pltpu.make_async_copy(r, out.at[i], sems.at[i]) for i, r in enumerate(ins)]
    start_all(copies)
    wait_all(copies)


def stack(*parts):
    return call(
        stack_kernel,
        [((len(parts),) + parts[0].shape, parts[0].dtype)],
        [pltpu.SemaphoreType.DMA((len(parts),))],
        "a" * len(parts),
        2,
    )(*parts)[0]


def join_kernel(*refs):
    *ins, out, sems = refs
    copies = [
        pltpu.make_async_copy(r, out.at[pl.ds(2 * i, 2)], sems.at[i]) for i, r in enumerate(ins)
    ]
    start_all(copies)
    wait_all(copies)


def join(parts):
    return call(
        join_kernel,
        [((2 * len(parts),) + parts[0].shape[1:], parts[0].dtype)],
        [pltpu.SemaphoreType.DMA((len(parts),))],
        "a" * len(parts),
        2,
    )(*parts)[0]


def gather_pairs(pair):
    from_low = over_fsdp(pair, 1, 0)
    from_high = over_fsdp(pair, -1, 0)
    from_far = over_fsdp(pair, 2, 0)
    return [pair, from_high, from_far, from_low]


def around(blocks, shift):
    return [blocks[0]] + [shift(blocks[d % 4], d) for d in (1, -1, 2)]


def over_x(value, d):
    return over_fsdp(value, d, 0)


def over_y(value, d):
    return over_seq(value, 0, d, 0)


def over_zl(total):
    return (total.astype(F32) + over_seq(total, 1, 0, 0).astype(F32)).astype(BF16)


def gather_quarters(own):
    from_low, from_high, from_far = (over_y(own, d) for d in (1, -1, 2))
    return [own, from_high, from_far, from_low]


def shards(
    inputs,
    first_gain,
    joint_weight,
    merge_weight,
    second_gain,
    expand_weight,
    shrink_weight,
    cotangent,
):
    x, zh, core, seq = place()
    fsdp = lax.axis_index("fsdp")
    source, upstream = inputs[0], cotangent[0]

    def columns(w, start, width):
        return lax.dynamic_slice_in_dim(w, start, width, 1)

    def placed_gain(gain):
        whole = lax.dynamic_update_slice_in_dim(jnp.zeros((D,), BF16), gain, fsdp * ROWS, 0)
        return jnp.pad(whole.reshape(6, 128), ((0, 2), (0, 0)))

    gain_tile = jnp.concatenate(
        [placed_gain(first_gain), placed_gain(second_gain), jnp.zeros((ROWS - 16, 128), BF16)], 0
    )
    joint_own = jnp.concatenate([columns(joint_weight, core * HALF, HALF), gain_tile], 1)
    joint_pair = stack(joint_own, over_fsdp(joint_own, 0, 1))
    joint_mine = gather_pairs(joint_pair)
    low_halo = passed_along(source[TOKENS - RIM :], 1)
    high_halo = passed_along(source[:RIM], -1)
    expand_own = columns(expand_weight, core * FF, FF)
    side_own = jnp.concatenate(
        [
            columns(shrink_weight, core * 384, 384),
            columns(merge_weight, core * 384, 384),
            jnp.zeros((SIDE - FF_ROWS - ROWS, 384), BF16),
        ],
        0,
    )
    y = seq % 8 // 2
    side_own = lax.dynamic_slice_in_dim(side_own, y * QUARTER, QUARTER, 0)
    side_own, expand_own, _ = lax.optimization_barrier((side_own, expand_own, joint_pair))
    side_all = gather_pairs(stack(side_own, over_fsdp(side_own, 0, 1)))
    expand_pair = stack(expand_own, over_fsdp(expand_own, 0, 1))
    side_quarter = join(side_all)
    side_mine = gather_quarters(side_quarter)
    expand_pair, _ = lax.optimization_barrier((expand_pair, side_all[2]))
    expand_mine = gather_pairs(expand_pair)

    frequencies = jnp.exp(
        jnp.arange(HEAD_DIM // 2, dtype=F32) * (-2.0 * math.log(10000.0) / HEAD_DIM)
    )
    positions = (seq * TOKENS - RIM + lax.iota(jnp.int32, WIDE)).astype(F32)
    angles = positions[:, None] * frequencies[None, :]
    cosine, sine = jnp.cos(angles), jnp.sin(angles)
    cosine = jnp.concatenate([cosine] * 4, 1)
    sine = jnp.concatenate([-sine, sine] * 2, 1)
    extended = jnp.concatenate([low_halo, source, high_halo], 0).astype(F32)
    normed, inverse = normalize(extended)

    *joint_mine, normed, cosine, sine = lax.optimization_barrier((*joint_mine, normed, cosine, sine))
    joint_pieces = joint_mine + [core_swap(p) for p in joint_mine]
    q, k, v, h_first, attended, probs, gains, joint_w = joint_forward(
        normed, cosine, sine, joint_pieces
    )
    *expand_mine, attended = lax.optimization_barrier((*expand_mine, attended))
    expand_pieces = expand_mine + [core_swap(p) for p in expand_mine]
    side_pieces = side_mine + [core_swap(p) for p in side_mine]
    dy_mine = columns(upstream, core * 384, 384)
    dy_got = core_swap(columns(upstream, (1 - core) * 384, 384))
    result, hidden, h_second, dx, datt, dz_mine, dz_give, dob_mine, dob_give = middle(
        gains, source, attended, upstream, expand_pieces, side_pieces
    )
    dj_mine, dj_give = attention_back(cosine, sine, q, k, v, datt, probs)
    swaps = [core_swap(part) for part in (h_second, dz_give, attended, dob_give)]
    *swaps, dj_mine, dj_give = lax.optimization_barrier((*swaps, dj_mine, dj_give))
    early = early_grads(
        h_second, swaps[0], dz_mine, swaps[1], attended, swaps[2], dob_mine, swaps[3]
    )
    early_parts = around(early, over_y)
    swaps = [core_swap(part) for part in (hidden, h_first, dj_give)]
    *swaps, _ = lax.optimization_barrier((*swaps, early[0]))
    late = late_grads(hidden, swaps[0], dy_mine, dy_got, h_first, swaps[1], dj_mine, swaps[2])
    *late, dj_mine = lax.optimization_barrier((*late, dj_mine))
    late_parts = around(late, over_x)
    base, low_back, high_back = input_back(inverse, gains, normed, dx, joint_w, dj_mine, dj_give)
    *early_parts, base = lax.optimization_barrier((*early_parts, base))
    from_high = passed_along(low_back, -1).astype(F32)
    from_low = passed_along(high_back, 1).astype(F32)
    input_grad = (
        base
        + jnp.pad(from_high, ((TOKENS - RIM, 0), (0, 0)))
        + jnp.pad(from_low, ((0, TOKENS - RIM), (0, 0)))
    ).astype(BF16)

    keep, give = both_sum(
        around(early_sum(early_parts), over_x) + around(late_sum(late_parts), over_y)
    )
    total = (keep + over_fsdp(give, 0, 1).astype(F32)).astype(BF16)
    own = stack(*gather_quarters(over_zl(total)))
    joint_grad, merge_grad, expand_grad, shrink_grad, first_grad, second_grad = results(
        first_gain.astype(F32)[:, None],
        second_gain.astype(F32)[:, None],
        own,
        core_swap(own),
        joint_weight,
        expand_weight,
    )
    return (
        result[None],
        input_grad[None],
        first_grad[:, 0],
        joint_grad,
        merge_grad,
        second_grad[:, 0],
        expand_grad,
        shrink_grad,
    )


def solution(mesh):
    placed = (
        P("fsdp", "seq", None),
        P("fsdp"),
        P("fsdp", None),
        P("fsdp", None),
        P("fsdp"),
        P("fsdp", None),
        P("fsdp", None),
        P("fsdp", "seq", None),
    )
    return jax.shard_map(
        shards,
        mesh=mesh,
        in_specs=placed,
        out_specs=(
            P("fsdp", "seq", None),
            P("fsdp", "seq", None),
            P("fsdp"),
            P("fsdp", None),
            P("fsdp", None),
            P("fsdp"),
            P("fsdp", None),
            P("fsdp", None),
        ),
        check_vma=False,
    )
```

```python
import math

import jax
import jax.numpy as jnp
from jax import lax
from jax.experimental import pallas as pl
from jax.experimental.pallas import tpu as pltpu
from jax.sharding import PartitionSpec as P

D = 768
HEADS = 12
HEAD_DIM = 64
FF = 1152
RIM = 64
TOKENS = 384
WIDE = TOKENS + 2 * RIM
TILE = 128
TILES = TOKENS // TILE
PAIRS = HEADS // 2
OWNERS = 8
ROWS = D // OWNERS
FF_ROWS = FF // OWNERS
HALF = 3 * D // 2
LATE_ROWS = 448
LATE_QUARTER = LATE_ROWS // 4
SIDE = 256
SIDE_HALF = SIDE // 2
EPSILON = 1e-05
F32 = jnp.float32
BF16 = jnp.bfloat16
MIB = 2**20


def over_fsdp(value, dx, dz):
    pairs = [
        (x * 2 + z, ((x + dx) % 4) * 2 + (z + dz) % 2) for x in range(4) for z in range(2)
    ]
    return lax.ppermute(value, "fsdp", pairs)


def over_seq(value, dz, dy, dc):
    pairs = [
        (z * 8 + y * 2 + c, ((z + dz) % 2) * 8 + ((y + dy) % 4) * 2 + (c + dc) % 2)
        for z in range(2)
        for y in range(4)
        for c in range(2)
    ]
    return lax.ppermute(value, "seq", pairs)


def over_both_z(value):
    pairs = [
        (f * 16 + s, (f ^ 1) * 16 + (s ^ 8)) for f in range(8) for s in range(16)
    ]
    return lax.ppermute(value, ("fsdp", "seq"), pairs)


def over_y_pair(value):
    return lax.ppermute(value, "seq", [(s, s ^ 2) for s in range(16)])


def core_swap(value):
    return over_seq(value, 0, 0, 1)


def passed_along(value, steps):
    first, last = (max(0, -steps), min(16, 16 - steps))
    return lax.ppermute(value, "seq", [(i, i + steps) for i in range(first, last)])


def place():
    fsdp, seq = lax.axis_index("fsdp"), lax.axis_index("seq")
    return fsdp // 2, fsdp % 2, seq % 2, seq


def owner(x, zh, dx, dz):
    return ((x + dx) % 4) * 2 + (zh + dz) % 2


def dot(left, right):
    return jnp.dot(left, right, preferred_element_type=F32)


def dot_back(left, right):
    return lax.dot_general(left, right, (((1,), (1,)), ((), ())), preferred_element_type=F32)


def dot_outer(left, right):
    return lax.dot_general(left, right, (((0,), (0,)), ((), ())), preferred_element_type=F32)


def row_mean(values):
    return jnp.sum(values, axis=-1, keepdims=True) * (1.0 / D)


def normalize(values):
    centred = values - row_mean(values)
    inverse = lax.rsqrt(row_mean(centred * centred) + EPSILON)
    return (centred * inverse, inverse)


def norm_back(upstream, normed, inverse, gain):
    scaled = upstream * gain
    centred = scaled - row_mean(scaled)
    return inverse * (centred - normed * row_mean(scaled * normed))


def rope(values, cosine, sine):
    lane = lax.broadcasted_iota(jnp.int32, values.shape, 1) % HEAD_DIM
    partner = jnp.where(
        lane < HEAD_DIM // 2,
        pltpu.roll(values, 128 - HEAD_DIM // 2, 1),
        pltpu.roll(values, HEAD_DIM // 2, 1),
    )
    return values * cosine + partner * sine


def call(kernel, outs, scratch, spaces, limit):
    kinds = {"v": pltpu.VMEM, "h": pltpu.HBM, "a": pl.ANY}
    return pl.pallas_call(
        kernel,
        out_shape=[jax.ShapeDtypeStruct(shape, kind) for shape, kind in outs],
        in_specs=[pl.BlockSpec(memory_space=kinds[c]) for c in spaces],
        out_specs=[pl.BlockSpec(memory_space=pltpu.HBM) for _ in outs],
        scratch_shapes=scratch,
        compiler_params=pltpu.CompilerParams(vmem_limit_bytes=limit * MIB),
    )


def like(outs):
    return [pltpu.VMEM(shape, kind) for shape, kind in outs]


def copy_all(sources, targets, sems, first=0):
    return [
        pltpu.make_async_copy(a, b, sems.at[first + i])
        for i, (a, b) in enumerate(zip(sources, targets, strict=True))
    ]


def start_all(copies):
    for copy in copies:
        copy.start()


def wait_all(copies):
    for copy in copies:
        copy.wait()


def piece_places(pieces):
    x, zh, core, _ = place()
    return [
        (
            side * 8 + dx * 2 + dz,
            pieces[side * 8 + dx * 2 + dz] if len(pieces) == 16 else pieces[side * 4 + dx].at[dz],
            owner(x, zh, dx, dz),
            (core + side) % 2,
        )
        for side in range(2)
        for dx in range(4)
        for dz in range(2)
    ]


def joint_copies(pieces, joint_w, sems):
    return [
        pltpu.make_async_copy(
            piece.at[:, pl.ds(0, HALF)],
            joint_w.at[
                pl.ds(pl.multiple_of(who * ROWS, 16), ROWS),
                pl.ds(pl.multiple_of(half * HALF, 128), HALF),
            ],
            sems.at[i],
        )
        for i, piece, who, half in piece_places(pieces)
    ]


def gain_chunk(gain_ref, row, j):
    return gain_ref[row + j : row + j + 1, :]


JOINT_OUTS = [
    ((TOKENS, D), BF16),
    ((WIDE, D), BF16),
    ((WIDE, D), BF16),
    ((WIDE, D), BF16),
    ((TOKENS, D), BF16),
    ((PAIRS * TILES, 2 * TILE, 2 * TILE), BF16),
    ((16, 128), F32),
    ((D, 3 * D), BF16),
]


def joint_kernel(normed_ref, cos_ref, sin_ref, *refs):
    pieces, outs, refs = refs[:16], refs[16:24], refs[24:]
    q_ref, k_ref, v_ref, h_ref, att_ref, probs_ref, gain_ref, joint_w, gains, sems, out_sems = refs
    copies = joint_copies(pieces, joint_w, sems)
    gain_copies = [
        pltpu.make_async_copy(
            pieces[i].at[pl.ds(0, 16), pl.ds(HALF, 128)], gains.at[i], sems.at[16 + i]
        )
        for i in range(8)
    ]
    start_all(gain_copies)
    start_all(copies)
    wait_all(gain_copies)
    gain_ref[...] = jnp.sum(gains[...].astype(F32), axis=0)
    for j in range(D // 128):
        cols = slice(128 * j, 128 * (j + 1))
        h_ref[:, cols] = (normed_ref[:, cols] * gain_chunk(gain_ref, 0, j)).astype(BF16)
    wait_all(copies)
    sends = copy_all(refs[:5] + refs[6:8], outs[:5] + outs[6:8], out_sems)
    start_all(sends[5:])
    own = slice(RIM, RIM + TOKENS)
    for j in range(9):
        cols = slice(256 * j, 256 * (j + 1))
        rows = own if j < 3 else slice(0, WIDE)
        got = dot(h_ref[rows, :], joint_w[:, cols])
        out = (q_ref, k_ref, v_ref)[j // 3]
        for a in range(2):
            part = got[:, 128 * a : 128 * (a + 1)]
            if j < 6:
                part = rope(part, cos_ref[rows, :], sin_ref[rows, :])
            at = 256 * (j % 3) + 128 * a
            out[:, at : at + 128] = part.astype(BF16)

    start_all(sends[:4])
    offset = lax.axis_index("seq") * TOKENS
    row = lax.broadcasted_iota(jnp.int32, (TILE, 2 * TILE), 0)
    col = lax.broadcasted_iota(jnp.int32, (TILE, 2 * TILE), 1)
    lane = lax.broadcasted_iota(jnp.int32, (TILE, 128), 1)
    band = (col >= row) & (col - row <= 2 * RIM)

    @pl.loop(0, PAIRS)
    def _(pair):
        lanes = pl.ds(pl.multiple_of(pair * 128, 128), 128)
        for t in range(TILES):
            key = col + (offset + t * TILE - RIM)
            allowed = band & (key >= 0) & (key < 16 * TOKENS)
            query = q_ref[t * TILE : (t + 1) * TILE, lanes].astype(F32) * (HEAD_DIM**-0.5)
            stacked = jnp.concatenate(
                [jnp.where(lane < HEAD_DIM, query, 0.0), jnp.where(lane < HEAD_DIM, 0.0, query)], 0
            ).astype(BF16)
            window = slice(t * TILE, (t + 2) * TILE)
            scores = dot_back(stacked, k_ref[window, lanes])
            scores = jnp.where(jnp.concatenate([allowed, allowed], 0), scores, -1e30)
            expo = jnp.exp(scores - jnp.max(scores, axis=-1, keepdims=True))
            probs = (expo / jnp.sum(expo, axis=-1, keepdims=True)).astype(BF16)
            probs_ref[pair * TILES + t] = probs
            mixed = dot(probs, v_ref[window, lanes])
            att_ref[t * TILE : (t + 1) * TILE, lanes] = jnp.where(
                lane < HEAD_DIM, mixed[:TILE], mixed[TILE:]
            ).astype(BF16)
        pltpu.make_async_copy(
            probs_ref.at[pl.ds(pair * TILES, TILES)],
            outs[5].at[pl.ds(pair * TILES, TILES)],
            out_sems.at[7 + pair],
        ).start()

    sends[4].start()
    wait_all(sends)
    for pair in range(PAIRS):
        tiles = pl.ds(pair * TILES, TILES)
        pltpu.make_async_copy(probs_ref.at[tiles], outs[5].at[tiles], out_sems.at[7 + pair]).wait()


def joint_forward(normed, cosine, sine, pieces):
    return call(
        joint_kernel,
        JOINT_OUTS,
        like(JOINT_OUTS)
        + [
            pltpu.VMEM((8, 16, 128), BF16),
            pltpu.SemaphoreType.DMA((24,)),
            pltpu.SemaphoreType.DMA((13,)),
        ],
        "vvv" + "a" * 16,
        18,
    )(normed, cosine, sine, *pieces)


def expand_copies(pieces, expand_w, sems):
    return [
        pltpu.make_async_copy(
            piece,
            expand_w.at[
                pl.ds(pl.multiple_of(who * ROWS, 16), ROWS),
                pl.ds(pl.multiple_of(half * FF, 128), FF),
            ],
            sems.at[i],
        )
        for i, piece, who, half in piece_places(pieces)
    ]


def side_copies(pieces, sides, sems):
    _, _, core, seq = place()
    y = seq % 8 // 2
    return [
        pltpu.make_async_copy(
            pieces[side * 2 + dy],
            sides.at[(core + side) % 2, (y + dy) % 2],
            sems.at[side * 2 + dy],
        )
        for side in range(2)
        for dy in range(2)
    ]


MIDDLE_OUTS = [
    ((TOKENS, D), BF16),
    ((TOKENS, FF), BF16),
    ((TOKENS, D), BF16),
    ((TOKENS, D), F32),
    ((TOKENS, D), BF16),
]
MIDDLE_HALVES = [((TOKENS, FF), BF16)] * 2 + [((TOKENS, D // 2), BF16)] * 2


def middle_kernel(gain_ref, *refs):
    ins, pieces, sides_in, refs = refs[:3], refs[3:11], refs[11:15], refs[15:]
    outs, halves, refs = refs[:5], refs[5:9], refs[9:]
    x_ref, att_ref, dy_ref, out_ref, m_ref, h_ref, dx_ref, datt_ref = refs[:8]
    merge_w, expand_w, shrink_w, sides, x1, normed, inverse, z, dm, dz, dob = refs[8:19]
    in_sems, side_sems, expand_sems, out_sems = refs[19:]
    dz_mine, dz_give, dob_mine, dob_give = halves
    core = lax.axis_index("seq") % 2
    loads = copy_all(ins, (x_ref, att_ref, dy_ref), in_sems)
    side_loads = side_copies(sides_in, sides, side_sems)
    expand = expand_copies(pieces, expand_w, expand_sems)
    start_all(loads)
    start_all(side_loads)
    start_all(expand)
    sends = copy_all(refs[3:8], outs, out_sems)
    wait_all(side_loads)
    for half in range(2):
        cols = slice(384 * half, 384 * (half + 1))
        merge_w[:, cols] = sides[half, 1, :, 16 : 16 + ROWS, :].reshape(D, 384)
    wait_all(loads)
    for j in range(3):
        cols = slice(256 * j, 256 * (j + 1))
        x1[:, cols] = x_ref[:, cols].astype(F32) + dot(att_ref[...], merge_w[:, cols])

    step = 32
    gain = jnp.concatenate([gain_chunk(gain_ref, 8, j) for j in range(6)], 1)

    @pl.loop(0, TOKENS // step)
    def _(i):
        rows = pl.ds(pl.multiple_of(i * step, step), step)
        part, scale = normalize(x1[rows, :])
        normed[rows, :] = part
        inverse[rows, :] = scale
        h_ref[rows, :] = (part * gain).astype(BF16)

    for half in range(2):
        cols = slice(384 * half, 384 * (half + 1))
        shrink_w[:, cols] = jnp.concatenate(
            [sides[half, 0], sides[half, 1, :, :16, :]], 1
        ).reshape(FF, 384)
    for j in range(3):
        cols = slice(384 * j, 384 * (j + 1))
        dm[:, cols] = dot_back(dy_ref[...], shrink_w[cols, :])
    wait_all(expand)
    for j in range(9):
        cols = slice(256 * j, 256 * (j + 1))
        z[:, cols] = dot(h_ref[...], expand_w[:, cols])

    @pl.loop(0, TOKENS // 16)
    def _(i):
        rows = pl.ds(pl.multiple_of(i * 16, 16), 16)
        gate = z[rows, pl.ds(0, FF)]
        up = z[rows, pl.ds(FF, FF)]
        upstream = dm[rows, :]
        below = 0.5 + 0.5 * lax.erf(gate * (0.5**0.5))
        slope = below + gate * (jnp.exp(-0.5 * gate * gate) * (2 * math.pi) ** -0.5)
        active = gate * below
        m_ref[rows, :] = (active * up).astype(BF16)
        dz[0, rows, :] = (upstream * up * slope).astype(BF16)
        dz[1, rows, :] = (upstream * active).astype(BF16)

    sends += copy_all((dz.at[core], dz.at[1 - core]), (dz_mine, dz_give), out_sems, 5)
    start_all(sends[1:3])
    start_all(sends[5:])
    for j in range(3):
        cols = slice(256 * j, 256 * (j + 1))
        out_ref[:, cols] = (x1[:, cols] + dot(m_ref[...], shrink_w[:, cols])).astype(BF16)
    start_all(sends[:1])
    for j in range(3):
        rows = slice(256 * j, 256 * (j + 1))
        x1[:, rows] = dot_back(dz[0], expand_w[rows, :FF]) + dot_back(dz[1], expand_w[rows, FF:])

    @pl.loop(0, TOKENS // step)
    def _(i):
        rows = pl.ds(pl.multiple_of(i * step, step), step)
        back = norm_back(x1[rows, :], normed[rows, :], inverse[rows, :], gain)
        total = dy_ref[rows, :].astype(F32) + back
        dx_ref[rows, :] = total
        dob[0, rows, :] = total[:, :384].astype(BF16)
        dob[1, rows, :] = total[:, 384:].astype(BF16)

    sends += copy_all((dob.at[core], dob.at[1 - core]), (dob_mine, dob_give), out_sems, 7)
    start_all(sends[7:])
    start_all(sends[3:4])
    for j in range(3):
        cols = slice(256 * j, 256 * (j + 1))
        datt_ref[:, cols] = (
            dot_back(dob[0], merge_w[cols, :384]) + dot_back(dob[1], merge_w[cols, 384:])
        ).astype(BF16)
    start_all(sends[4:5])
    wait_all(sends)


def middle(gains, x, att, dy, pieces, sides):
    return call(
        middle_kernel,
        MIDDLE_OUTS + MIDDLE_HALVES,
        [pltpu.VMEM((TOKENS, D), BF16)] * 3
        + like(MIDDLE_OUTS)
        + [
            pltpu.VMEM((D, D), BF16),
            pltpu.VMEM((D, 2 * FF), BF16),
            pltpu.VMEM((FF, D), BF16),
            pltpu.VMEM((2, 2, OWNERS, SIDE_HALF, 384), BF16),
            pltpu.VMEM((TOKENS, D), F32),
            pltpu.VMEM((TOKENS, D), F32),
            pltpu.VMEM((TOKENS, 1), F32),
            pltpu.VMEM((TOKENS, 2 * FF), F32),
            pltpu.VMEM((TOKENS, FF), F32),
            pltpu.VMEM((2, TOKENS, FF), BF16),
            pltpu.VMEM((2, TOKENS, D // 2), BF16),
            pltpu.SemaphoreType.DMA((3,)),
            pltpu.SemaphoreType.DMA((4,)),
            pltpu.SemaphoreType.DMA((16,)),
            pltpu.SemaphoreType.DMA((9,)),
        ],
        "vhhh" + "a" * 12,
        34,
    )(gains, x, att, dy, *pieces, *sides)


def paired_copies(refs, buffers, sems):
    copies = []
    for n, buffer in enumerate(buffers):
        rows = buffer.shape[0] // 2
        for side in range(2):
            copies.append(
                pltpu.make_async_copy(
                    refs[2 * n + side], buffer.at[pl.ds(side * rows, rows), :], sems.at[2 * n + side]
                )
            )
    return copies


def early_kernel(*refs):
    ins, outs, refs = refs[:8], refs[8:12], refs[12:]
    h, dz, att, dob, blocks, sems, out_sems = refs
    x, zh, _, seq = place()
    y = seq % 8 // 2
    copies = paired_copies(ins, (h, dz, att, dob), sems)
    start_all(copies)
    wait_all(copies)
    for part in range(3):
        grad = dot_outer(h[...], dz[:, 384 * part : 384 * (part + 1)]).astype(BF16)
        blocks[part] = grad.reshape(OWNERS, ROWS, 384)
    grad = dot_outer(att[...], dob[...]).astype(BF16)
    blocks[3] = grad.reshape(OWNERS, ROWS, 384)
    sends = [
        pltpu.make_async_copy(
            blocks.at[(y + dy) % 4, owner(x, zh, dx, dz)],
            outs[dy].at[dx * 2 + dz],
            out_sems.at[dy * 8 + dx * 2 + dz],
        )
        for dy in range(4)
        for dx in range(4)
        for dz in range(2)
    ]
    start_all(sends)
    wait_all(sends)


def early_grads(*args):
    return call(
        early_kernel,
        [((OWNERS, ROWS, 384), BF16)] * 4,
        [
            pltpu.VMEM((2 * TOKENS, D), BF16),
            pltpu.VMEM((2 * TOKENS, FF), BF16),
            pltpu.VMEM((2 * TOKENS, D), BF16),
            pltpu.VMEM((2 * TOKENS, D // 2), BF16),
            pltpu.VMEM((4, OWNERS, ROWS, 384), BF16),
            pltpu.SemaphoreType.DMA((8,)),
            pltpu.SemaphoreType.DMA((32,)),
        ],
        "ha" * 4,
        20,
    )(*args)


def attention_back_kernel(cos_ref, sin_ref, *refs):
    ins, probs_in, mine_ref, give_ref, scratch = refs[:4], refs[4], refs[5], refs[6], refs[7:]
    q_ref, k_ref, v_ref, datt_ref, probs_ref, dk, dv, dj, in_sems, sems = scratch
    loads = copy_all(ins, scratch[:4], in_sems)
    start_all(loads)

    def load_probs(pair):
        tiles = pl.ds(pair * TILES, TILES)
        return pltpu.make_async_copy(probs_in.at[tiles], probs_ref.at[tiles], in_sems.at[4 + pair])

    for pair in range(PAIRS):
        load_probs(pair).start()
    core = lax.axis_index("seq") % 2
    lane = lax.broadcasted_iota(jnp.int32, (TILE, 128), 1)
    own = slice(RIM, RIM + TOKENS)
    dk[...] = jnp.zeros_like(dk)
    dv[...] = jnp.zeros_like(dv)
    dj[0, :RIM, :D] = jnp.zeros((RIM, D), BF16)
    dj[0, RIM + TOKENS :, :D] = jnp.zeros((RIM, D), BF16)
    wait_all(loads)
    scale = HEAD_DIM**-0.5

    @pl.loop(0, PAIRS)
    def _(pair):
        lanes = pl.ds(pl.multiple_of(pair * 128, 128), 128)
        load_probs(pair).wait()
        for t in range(TILES):
            rows = slice(t * TILE, (t + 1) * TILE)
            window = slice(t * TILE, (t + 2) * TILE)
            query = q_ref[rows, lanes].astype(F32) * scale
            query = jnp.concatenate(
                [jnp.where(lane < HEAD_DIM, query, 0.0), jnp.where(lane < HEAD_DIM, 0.0, query)], 0
            ).astype(BF16)
            upstream = datt_ref[rows, lanes].astype(F32)
            upstream = jnp.concatenate(
                [
                    jnp.where(lane < HEAD_DIM, upstream, 0.0),
                    jnp.where(lane < HEAD_DIM, 0.0, upstream),
                ],
                0,
            ).astype(BF16)
            probs_b = probs_ref[pair * TILES + t]
            probs = probs_b.astype(F32)
            dp = dot_back(upstream, v_ref[window, lanes])
            delta = jnp.sum(probs * dp, axis=-1, keepdims=True)
            ds = (probs * (dp - delta)).astype(BF16)
            dv[window, lanes] += dot_outer(probs_b, upstream)
            dk[window, lanes] += dot_outer(ds, query)
            dq = dot(ds, k_ref[window, lanes]) * scale
            dq = jnp.where(lane < HEAD_DIM, dq[:TILE], dq[TILE:])
            at = slice(RIM + t * TILE, RIM + (t + 1) * TILE)
            dj[0, at, lanes] = rope(dq, cos_ref[at, :], -sin_ref[at, :]).astype(BF16)

    for j in range(6):
        cols = slice(128 * j, 128 * (j + 1))
        part = rope(dk[:, cols], cos_ref[...], -sin_ref[...]).astype(BF16)
        if j < 3:
            dj[0, :, D + 128 * j : D + 128 * (j + 1)] = part
        else:
            dj[1, :, 128 * (j - 3) : 128 * (j - 2)] = part
    dj[1, :, D // 2 :] = dv[...].astype(BF16)
    sends = [
        pltpu.make_async_copy(dj.at[core], mine_ref, sems.at[0]),
        pltpu.make_async_copy(dj.at[1 - core], give_ref, sems.at[1]),
    ]
    start_all(sends)
    wait_all(sends)


def attention_back(*args):
    return call(
        attention_back_kernel,
        [((WIDE, HALF), BF16)] * 2,
        [
            pltpu.VMEM((TOKENS, D), BF16),
            pltpu.VMEM((WIDE, D), BF16),
            pltpu.VMEM((WIDE, D), BF16),
            pltpu.VMEM((TOKENS, D), BF16),
            pltpu.VMEM((PAIRS * TILES, 2 * TILE, 2 * TILE), BF16),
            pltpu.VMEM((WIDE, D), F32),
            pltpu.VMEM((WIDE, D), F32),
            pltpu.VMEM((2, WIDE, HALF), BF16),
            pltpu.SemaphoreType.DMA((10,)),
            pltpu.SemaphoreType.DMA((2,)),
        ],
        "vvhhhhh",
        20,
    )(*args)


def late_kernel(*refs):
    ins, outs, refs = refs[:8], refs[8:12], refs[12:]
    m, dy, h, dj, blocks, sems, out_sems = refs
    x, zh, _, _ = place()
    copies = paired_copies(ins, (m, dy, h, dj), sems)
    start_all(copies)
    wait_all(copies)
    grad = dot_outer(m[...], dy[...]).astype(BF16)
    blocks[:, :FF_ROWS, :] = grad.reshape(OWNERS, FF_ROWS, 384)
    for part in range(3):
        grad = dot_outer(h[...], dj[:, 384 * part : 384 * (part + 1)]).astype(BF16)
        at = FF_ROWS + ROWS * part
        blocks[:, at : at + ROWS, :] = grad.reshape(OWNERS, ROWS, 384)
    blocks[:, FF_ROWS + 3 * ROWS :, :] = jnp.zeros((OWNERS, 16, 384), BF16)
    sends = [
        pltpu.make_async_copy(blocks.at[owner(x, zh, dx, dz)], outs[dx].at[dz], out_sems.at[dx * 2 + dz])
        for dx in range(4)
        for dz in range(2)
    ]
    start_all(sends)
    wait_all(sends)


def late_grads(*args):
    return call(
        late_kernel,
        [((2, LATE_ROWS, 384), BF16)] * 4,
        [
            pltpu.VMEM((2 * TOKENS, FF), BF16),
            pltpu.VMEM((2 * TOKENS, D // 2), BF16),
            pltpu.VMEM((2 * WIDE, D), BF16),
            pltpu.VMEM((2 * WIDE, HALF), BF16),
            pltpu.VMEM((OWNERS, LATE_ROWS, 384), BF16),
            pltpu.SemaphoreType.DMA((8,)),
            pltpu.SemaphoreType.DMA((8,)),
        ],
        "ha" * 4,
        20,
    )(*args)


def sum_of(parts, index):
    return sum(part[index].astype(F32) for part in parts)


def early_sum_kernel(*refs):
    ins, outs, parts, total, sems, out_sems = refs[:4], refs[4:8], refs[8:12], *refs[12:]
    copies = copy_all(ins, parts, sems)
    start_all(copies)
    wait_all(copies)
    sends = [
        pltpu.make_async_copy(total.at[pl.ds(2 * d, 2)], outs[d], out_sems.at[d]) for d in range(4)
    ]
    for d in (1, 3, 2, 0):
        for i in (2 * d, 2 * d + 1):
            total[i] = sum_of(parts, i).astype(BF16)
        sends[d].start()
    wait_all(sends)


def late_sum_kernel(*refs):
    ins, outs, parts, total, sems, out_sems = refs[:4], refs[4:8], refs[8:12], *refs[12:]
    _, _, _, seq = place()
    y = seq % 8 // 2
    copies = copy_all(ins, parts, sems)
    start_all(copies)
    wait_all(copies)
    for i in range(2):
        total[i] = sum_of(parts, i).astype(BF16)
    sends = [
        pltpu.make_async_copy(
            total.at[:, pl.ds(pl.multiple_of((y + d) % 4 * LATE_QUARTER, 16), LATE_QUARTER), :],
            outs[d],
            out_sems.at[d],
        )
        for d in range(4)
    ]
    start_all(sends)
    wait_all(sends)


def both_sum_kernel(*refs):
    ins, outs, parts, keep, give, sems, out_sems = refs[:8], refs[8:10], refs[10:18], *refs[18:]
    copies = copy_all(ins, parts, sems)
    start_all(copies)
    wait_all(copies)
    keep[:ROWS] = sum_of(parts[:4], 0).astype(BF16)
    keep[ROWS:] = sum_of(parts[4:], 0).astype(BF16)
    give[:ROWS] = sum_of(parts[:4], 1).astype(BF16)
    give[ROWS:] = sum_of(parts[4:], 1).astype(BF16)
    sends = copy_all((keep, give), outs, out_sems)
    start_all(sends)
    wait_all(sends)


def summed(kernel, parts, outs, scratch):
    return call(
        kernel,
        outs,
        [pltpu.VMEM(part.shape, part.dtype) for part in parts]
        + scratch
        + [pltpu.SemaphoreType.DMA((len(parts),)), pltpu.SemaphoreType.DMA((len(outs),))],
        "a" * len(parts),
        14,
    )(*parts)


def early_sum(parts):
    shape = (OWNERS, ROWS, 384)
    outs = [((2, ROWS, 384), BF16)] * 4
    return summed(early_sum_kernel, parts, outs, [pltpu.VMEM(shape, BF16)])


def late_sum(parts):
    shape = (2, LATE_ROWS, 384)
    outs = [((2, LATE_QUARTER, 384), BF16)] * 4
    return summed(late_sum_kernel, parts, outs, [pltpu.VMEM(shape, BF16)])


def both_sum(parts):
    outs = [((ROWS + LATE_QUARTER, 384), BF16)] * 2
    return summed(both_sum_kernel, parts, outs, like(outs))


INPUT_OUTS = [((TOKENS, D), F32), ((RIM, D), BF16), ((RIM, D), BF16)]


def input_kernel(inverse_ref, gain_ref, *refs):
    (normed, dx, weight, mine, give), outs, refs = refs[:5], refs[5:8], refs[8:]
    base_ref, low_ref, high_ref, joint_w, dj, upstream, normed_ref, dx_ref, sems, out_sems = refs
    core = lax.axis_index("seq") % 2
    copies = [
        pltpu.make_async_copy(weight, joint_w, sems.at[0]),
        pltpu.make_async_copy(mine, dj.at[core], sems.at[1]),
        pltpu.make_async_copy(give, dj.at[1 - core], sems.at[2]),
        pltpu.make_async_copy(normed, normed_ref, sems.at[3]),
        pltpu.make_async_copy(dx, dx_ref, sems.at[4]),
    ]
    start_all(copies)
    wait_all(copies)
    for j in range(3):
        cols = slice(256 * j, 256 * (j + 1))
        upstream[:, cols] = dot_back(dj[0], joint_w[cols, :HALF]) + dot_back(
            dj[1], joint_w[cols, HALF:]
        )
    gain = jnp.concatenate([gain_chunk(gain_ref, 0, j) for j in range(6)], 1)
    step = 32

    def back(rows):
        return norm_back(upstream[rows, :], normed_ref[rows, :], inverse_ref[rows, :], gain)

    @pl.loop(0, TOKENS // step)
    def _(i):
        start = pl.multiple_of(i * step, step)
        base_ref[pl.ds(start, step), :] = dx_ref[pl.ds(start, step), :] + back(
            pl.ds(start + RIM, step)
        )

    @pl.loop(0, RIM // step)
    def _(i):
        start = pl.multiple_of(i * step, step)
        low_ref[pl.ds(start, step), :] = back(pl.ds(start, step)).astype(BF16)
        high_ref[pl.ds(start, step), :] = back(pl.ds(start + RIM + TOKENS, step)).astype(BF16)

    sends = copy_all(refs[:3], outs, out_sems)
    start_all(sends)
    wait_all(sends)


def input_back(*args):
    return call(
        input_kernel,
        INPUT_OUTS,
        like(INPUT_OUTS)
        + [
            pltpu.VMEM((D, 3 * D), BF16),
            pltpu.VMEM((2, WIDE, HALF), BF16),
            pltpu.VMEM((WIDE, D), F32),
            pltpu.VMEM((WIDE, D), F32),
            pltpu.VMEM((TOKENS, D), F32),
            pltpu.SemaphoreType.DMA((5,)),
            pltpu.SemaphoreType.DMA((3,)),
        ],
        "vvahhhh",
        20,
    )(*args)


RESULTS = [((ROWS, 3 * D), F32), ((ROWS, D), F32), ((ROWS, 2 * FF), F32), ((FF_ROWS, D), F32)]
GAIN_RESULTS = [((1, ROWS), F32)] * 2


def result_kernel(first_gain, second_gain, *refs):
    sums, weights, outs, refs = refs[:2], refs[2:4], refs[4:10], refs[10:]
    joint, merge, expand, shrink, first, second, early, late, joint_w, expand_w, sems = refs
    _, _, core, seq = place()
    y = seq % 8 // 2
    copies = copy_all(weights, (joint_w, expand_w), sems)
    for side in range(2):
        half = (core + side) % 2
        for dy in range(4):
            quarter = (y + dy) % 4
            rows = pl.ds(pl.multiple_of(quarter * LATE_QUARTER, 16), LATE_QUARTER)
            copies += copy_all(
                (
                    sums[side].at[dy, pl.ds(0, ROWS)],
                    sums[side].at[dy, pl.ds(ROWS, LATE_QUARTER)],
                ),
                (early.at[half, quarter], late.at[half, rows]),
                sems,
                2 + (side * 4 + dy) * 2,
            )
    start_all(copies)
    wait_all(copies)
    for half in range(2):
        cols = slice(384 * half, 384 * (half + 1))
        shrink[:, cols] = late[half, :FF_ROWS].astype(F32)
        merge[:, cols] = early[half, 3].astype(F32)
        for part in range(3):
            cols = slice(FF * half + 384 * part, FF * half + 384 * (part + 1))
            at = FF_ROWS + ROWS * part
            expand[:, cols] = early[half, part].astype(F32)
            joint[:, cols] = late[half, at : at + ROWS].astype(F32)
    sends = copy_all((joint, merge, expand, shrink, first, second), outs, sems, 18)
    start_all(sends[:4])
    for total, weight, grad, gain in (
        (first, joint_w, joint, first_gain),
        (second, expand_w, expand, second_gain),
    ):
        product = sum(
            weight[:, 128 * j : 128 * (j + 1)].astype(F32) * grad[:, 128 * j : 128 * (j + 1)]
            for j in range(3 * D // 128)
        )
        total[...] = jnp.sum(product.T, axis=0, keepdims=True) / gain[...]
    start_all(sends[4:])
    wait_all(sends)


def results(*args):
    return call(
        result_kernel,
        RESULTS + GAIN_RESULTS,
        like(RESULTS + GAIN_RESULTS)
        + [
            pltpu.VMEM((2, 4, ROWS, 384), BF16),
            pltpu.VMEM((2, LATE_ROWS, 384), BF16),
            pltpu.VMEM((ROWS, 3 * D), BF16),
            pltpu.VMEM((ROWS, 2 * FF), BF16),
            pltpu.SemaphoreType.DMA((24,)),
        ],
        "vvaahh",
        12,
    )(*args)


def stack_kernel(*refs):
    *ins, out, sems = refs
    copies = [pltpu.make_async_copy(r, out.at[i], sems.at[i]) for i, r in enumerate(ins)]
    start_all(copies)
    wait_all(copies)


def stack(*parts):
    return call(
        stack_kernel,
        [((len(parts),) + parts[0].shape, parts[0].dtype)],
        [pltpu.SemaphoreType.DMA((len(parts),))],
        "a" * len(parts),
        2,
    )(*parts)[0]


def join_kernel(*refs):
    *ins, out, sems = refs
    x, zh, _, _ = place()
    copies = [
        pltpu.make_async_copy(ins[dx].at[dz], out.at[owner(x, zh, dx, dz)], sems.at[dx * 2 + dz])
        for dx in range(4)
        for dz in range(2)
    ]
    start_all(copies)
    wait_all(copies)


def join(parts):
    return call(
        join_kernel,
        [((2 * len(parts),) + parts[0].shape[1:], parts[0].dtype)],
        [pltpu.SemaphoreType.DMA((8,))],
        "a" * len(parts),
        2,
    )(*parts)[0]


def gather_pieces(own):
    from_low = over_fsdp(own, 1, 0)
    from_high = over_fsdp(own, -1, 0)
    across = over_fsdp(own, 0, 1)
    from_far = over_fsdp(own, 2, 0)
    across_low = over_fsdp(across, 1, 0)
    across_high = over_fsdp(across, -1, 0)
    across_far = over_fsdp(from_far, 0, 1)
    return [own, across, from_high, across_high, from_far, across_far, from_low, across_low]


def gather_pairs(pair):
    from_low = over_fsdp(pair, 1, 0)
    from_high = over_fsdp(pair, -1, 0)
    from_far = over_fsdp(pair, 2, 0)
    return [pair, from_high, from_far, from_low]


def around(blocks, shift):
    return [blocks[0]] + [shift(blocks[d % 4], d) for d in (1, -1, 2)]


def over_x(value, d):
    return over_fsdp(value, d, 0)


def over_y(value, d):
    return over_seq(value, 0, d, 0)


def gather_quarters(own):
    from_low, from_high, from_far = (over_y(own, d) for d in (1, -1, 2))
    return [own, from_high, from_far, from_low]


def shards(
    inputs,
    first_gain,
    joint_weight,
    merge_weight,
    second_gain,
    expand_weight,
    shrink_weight,
    cotangent,
):
    x, zh, core, seq = place()
    fsdp = lax.axis_index("fsdp")
    source, upstream = inputs[0], cotangent[0]

    def columns(w, start, width):
        return lax.dynamic_slice_in_dim(w, start, width, 1)

    def placed_gain(gain):
        whole = lax.dynamic_update_slice_in_dim(jnp.zeros((D,), BF16), gain, fsdp * ROWS, 0)
        return jnp.pad(whole.reshape(6, 128), ((0, 2), (0, 0)))

    gain_tile = jnp.concatenate(
        [placed_gain(first_gain), placed_gain(second_gain), jnp.zeros((ROWS - 16, 128), BF16)], 0
    )
    joint_own = jnp.concatenate([columns(joint_weight, core * HALF, HALF), gain_tile], 1)
    joint_mine = gather_pieces(joint_own)
    low_halo = passed_along(source[TOKENS - RIM :], 1)
    high_halo = passed_along(source[:RIM], -1)
    expand_own = columns(expand_weight, core * FF, FF)
    side_own = jnp.concatenate(
        [
            columns(shrink_weight, core * 384, 384),
            columns(merge_weight, core * 384, 384),
            jnp.zeros((SIDE - FF_ROWS - ROWS, 384), BF16),
        ],
        0,
    )
    y = seq % 8 // 2
    side_own = lax.dynamic_slice_in_dim(side_own, y % 2 * SIDE_HALF, SIDE_HALF, 0)
    side_own, expand_own, _, _ = lax.optimization_barrier(
        (side_own, expand_own, joint_mine[2], joint_mine[6])
    )
    side_pair = stack(side_own, over_fsdp(side_own, 0, 1))
    expand_pair = stack(expand_own, over_fsdp(expand_own, 0, 1))
    side_pair, _, _ = lax.optimization_barrier((side_pair, joint_mine[3], joint_mine[7]))
    side_half = join(gather_pairs(side_pair))
    side_mine = [side_half, over_y_pair(side_half)]
    expand_pair, _ = lax.optimization_barrier((expand_pair, joint_mine[5]))
    expand_mine = gather_pairs(expand_pair)

    frequencies = jnp.exp(
        jnp.arange(HEAD_DIM // 2, dtype=F32) * (-2.0 * math.log(10000.0) / HEAD_DIM)
    )
    positions = (seq * TOKENS - RIM + lax.iota(jnp.int32, WIDE)).astype(F32)
    angles = positions[:, None] * frequencies[None, :]
    cosine, sine = jnp.cos(angles), jnp.sin(angles)
    cosine = jnp.concatenate([cosine] * 4, 1)
    sine = jnp.concatenate([-sine, sine] * 2, 1)
    extended = jnp.concatenate([low_halo, source, high_halo], 0).astype(F32)
    normed, inverse = normalize(extended)

    *joint_mine, normed, cosine, sine = lax.optimization_barrier((*joint_mine, normed, cosine, sine))
    joint_pieces = joint_mine + [core_swap(p) for p in joint_mine]
    q, k, v, h_first, attended, probs, gains, joint_w = joint_forward(
        normed, cosine, sine, joint_pieces
    )
    *expand_mine, attended = lax.optimization_barrier((*expand_mine, attended))
    expand_pieces = expand_mine + [core_swap(p) for p in expand_mine]
    side_pieces = side_mine + [core_swap(p) for p in side_mine]
    dy_mine = columns(upstream, core * 384, 384)
    dy_got = core_swap(columns(upstream, (1 - core) * 384, 384))
    result, hidden, h_second, dx, datt, dz_mine, dz_give, dob_mine, dob_give = middle(
        gains, source, attended, upstream, expand_pieces, side_pieces
    )
    dj_mine, dj_give = attention_back(cosine, sine, q, k, v, datt, probs)
    swaps = [core_swap(part) for part in (h_second, dz_give, attended, dob_give, hidden, h_first)]
    *swaps, dj_mine, dj_give = lax.optimization_barrier((*swaps, dj_mine, dj_give))
    late = late_grads(
        hidden, swaps[4], dy_mine, dy_got, h_first, swaps[5], dj_mine, core_swap(dj_give)
    )
    *swaps, late_own = lax.optimization_barrier((*swaps, late[0]))
    late = [late_own, *late[1:]]
    late_parts = around(late, over_x)
    early = early_grads(
        h_second, swaps[0], dz_mine, swaps[1], attended, swaps[2], dob_mine, swaps[3]
    )
    early_own, dj_mine = lax.optimization_barrier((early[0], dj_mine))
    early = [early_own, *early[1:]]
    early_parts = around(early, over_y)
    base, low_back, high_back = input_back(inverse, gains, normed, dx, joint_w, dj_mine, dj_give)
    from_high = passed_along(low_back, -1).astype(F32)
    from_low = passed_along(high_back, 1).astype(F32)
    input_grad = (
        base
        + jnp.pad(from_high, ((TOKENS - RIM, 0), (0, 0)))
        + jnp.pad(from_low, ((0, TOKENS - RIM), (0, 0)))
    ).astype(BF16)

    *late_parts, input_grad = lax.optimization_barrier((*late_parts, input_grad))
    late_quarters = around(late_sum(late_parts), over_y)
    keep, give = both_sum(around(early_sum(early_parts), over_x) + late_quarters)
    keeps = keep.astype(F32) + over_seq(keep, 1, 0, 0).astype(F32)
    gives = over_fsdp(give, 0, 1).astype(F32) + over_both_z(give).astype(F32)
    own = stack(*gather_quarters((keeps + gives).astype(BF16)))
    joint_grad, merge_grad, expand_grad, shrink_grad, first_grad, second_grad = results(
        first_gain.astype(F32)[None],
        second_gain.astype(F32)[None],
        own,
        core_swap(own),
        joint_weight,
        expand_weight,
    )
    return (
        result[None],
        input_grad[None],
        first_grad[0],
        joint_grad,
        merge_grad,
        second_grad[0],
        expand_grad,
        shrink_grad,
    )


def solution(mesh):
    placed = (
        P("fsdp", "seq", None),
        P("fsdp"),
        P("fsdp", None),
        P("fsdp", None),
        P("fsdp"),
        P("fsdp", None),
        P("fsdp", None),
        P("fsdp", "seq", None),
    )
    return jax.shard_map(
        shards,
        mesh=mesh,
        in_specs=placed,
        out_specs=(
            P("fsdp", "seq", None),
            P("fsdp", "seq", None),
            P("fsdp"),
            P("fsdp", None),
            P("fsdp", None),
            P("fsdp"),
            P("fsdp", None),
            P("fsdp", None),
        ),
        check_vma=False,
    )
```

```python
import math

import jax
import jax.numpy as jnp
from jax import lax
from jax.experimental import pallas as pl
from jax.experimental.pallas import tpu as pltpu
from jax.sharding import PartitionSpec as P

D = 768
HEADS = 12
HEAD_DIM = 64
FF = 1152
RIM = 64
TOKENS = 384
WIDE = TOKENS + 2 * RIM
TILE = 128
TILES = TOKENS // TILE
PAIRS = HEADS // 2
OWNERS = 8
ROWS = D // OWNERS
FF_ROWS = FF // OWNERS
HALF = 3 * D // 2
LATE_ROWS = 448
LATE_QUARTER = LATE_ROWS // 4
JOINT_ROWS = LATE_ROWS - FF_ROWS
PACKED = 4 * ROWS + FF_ROWS
EPSILON = 1e-05
F32 = jnp.float32
BF16 = jnp.bfloat16
MIB = 2**20


def over_fsdp(value, dx, dz):
    pairs = [
        (x * 2 + z, ((x + dx) % 4) * 2 + (z + dz) % 2) for x in range(4) for z in range(2)
    ]
    return lax.ppermute(value, "fsdp", pairs)


def over_seq(value, dz, dy, dc):
    pairs = [
        (z * 8 + y * 2 + c, ((z + dz) % 2) * 8 + ((y + dy) % 4) * 2 + (c + dc) % 2)
        for z in range(2)
        for y in range(4)
        for c in range(2)
    ]
    return lax.ppermute(value, "seq", pairs)


def over_both_z(value):
    pairs = [
        (f * 16 + s, (f ^ 1) * 16 + (s ^ 8)) for f in range(8) for s in range(16)
    ]
    return lax.ppermute(value, ("fsdp", "seq"), pairs)


def core_swap(value):
    return over_seq(value, 0, 0, 1)


def passed_along(value, steps):
    first, last = (max(0, -steps), min(16, 16 - steps))
    return lax.ppermute(value, "seq", [(i, i + steps) for i in range(first, last)])


def place():
    fsdp, seq = lax.axis_index("fsdp"), lax.axis_index("seq")
    return fsdp // 2, fsdp % 2, seq % 2, seq


def owner(x, zh, dx, dz):
    return ((x + dx) % 4) * 2 + (zh + dz) % 2


def dot(left, right):
    return jnp.dot(left, right, preferred_element_type=F32)


def dot_back(left, right):
    return lax.dot_general(left, right, (((1,), (1,)), ((), ())), preferred_element_type=F32)


def dot_outer(left, right):
    return lax.dot_general(left, right, (((0,), (0,)), ((), ())), preferred_element_type=F32)


def row_mean(values):
    return jnp.sum(values, axis=-1, keepdims=True) * (1.0 / D)


def normalize(values):
    centred = values - row_mean(values)
    inverse = lax.rsqrt(row_mean(centred * centred) + EPSILON)
    return (centred * inverse, inverse)


def norm_back(upstream, normed, inverse, gain):
    scaled = upstream * gain
    centred = scaled - row_mean(scaled)
    return inverse * (centred - normed * row_mean(scaled * normed))


def rope(values, cosine, sine):
    lane = lax.broadcasted_iota(jnp.int32, values.shape, 1) % HEAD_DIM
    partner = jnp.where(
        lane < HEAD_DIM // 2,
        pltpu.roll(values, 128 - HEAD_DIM // 2, 1),
        pltpu.roll(values, HEAD_DIM // 2, 1),
    )
    return values * cosine + partner * sine


def call(kernel, outs, scratch, spaces, limit):
    kinds = {"v": pltpu.VMEM, "h": pltpu.HBM, "a": pl.ANY}
    return pl.pallas_call(
        kernel,
        out_shape=[jax.ShapeDtypeStruct(shape, kind) for shape, kind in outs],
        in_specs=[pl.BlockSpec(memory_space=kinds[c]) for c in spaces],
        out_specs=[pl.BlockSpec(memory_space=pltpu.HBM) for _ in outs],
        scratch_shapes=scratch,
        compiler_params=pltpu.CompilerParams(vmem_limit_bytes=limit * MIB),
    )


def like(outs):
    return [pltpu.VMEM(shape, kind) for shape, kind in outs]


def copy_all(sources, targets, sems, first=0):
    return [
        pltpu.make_async_copy(a, b, sems.at[first + i])
        for i, (a, b) in enumerate(zip(sources, targets, strict=True))
    ]


def start_all(copies):
    for copy in copies:
        copy.start()


def wait_all(copies):
    for copy in copies:
        copy.wait()


def piece_places(pieces):
    x, zh, core, _ = place()
    return [
        (
            side * 8 + dx * 2 + dz,
            pieces[side * 8 + dx * 2 + dz] if len(pieces) == 16 else pieces[side * 4 + dx].at[dz],
            owner(x, zh, dx, dz),
            (core + side) % 2,
        )
        for side in range(2)
        for dx in range(4)
        for dz in range(2)
    ]


def joint_copies(pieces, joint_w, sems):
    return [
        pltpu.make_async_copy(
            piece.at[:, pl.ds(0, HALF)],
            joint_w.at[
                pl.ds(pl.multiple_of(who * ROWS, 16), ROWS),
                pl.ds(pl.multiple_of(half * HALF, 128), HALF),
            ],
            sems.at[i],
        )
        for i, piece, who, half in piece_places(pieces)
    ]


def gain_chunk(gain_ref, row, j):
    return gain_ref[row + j : row + j + 1, :]


JOINT_OUTS = [
    ((TOKENS, D), BF16),
    ((WIDE, D), BF16),
    ((WIDE, D), BF16),
    ((WIDE, D), BF16),
    ((TOKENS, D), BF16),
    ((PAIRS * TILES, 2 * TILE, 2 * TILE), BF16),
    ((16, 128), F32),
    ((D, 3 * D), BF16),
]


def joint_kernel(normed_ref, cos_ref, sin_ref, *refs):
    pieces, outs, refs = refs[:16], refs[16:24], refs[24:]
    q_ref, k_ref, v_ref, h_ref, att_ref, probs_ref, gain_ref, joint_w, gains, sems, out_sems = refs
    copies = joint_copies(pieces, joint_w, sems)
    gain_copies = [
        pltpu.make_async_copy(
            pieces[i].at[pl.ds(0, 16), pl.ds(HALF, 128)], gains.at[i], sems.at[16 + i]
        )
        for i in range(8)
    ]
    start_all(gain_copies)
    start_all(copies)
    wait_all(gain_copies)
    gain_ref[...] = jnp.sum(gains[...].astype(F32), axis=0)
    for j in range(D // 128):
        cols = slice(128 * j, 128 * (j + 1))
        h_ref[:, cols] = (normed_ref[:, cols] * gain_chunk(gain_ref, 0, j)).astype(BF16)
    wait_all(copies)
    sends = copy_all(refs[:5] + refs[6:8], outs[:5] + outs[6:8], out_sems)
    start_all(sends[5:])
    own = slice(RIM, RIM + TOKENS)
    for j in range(9):
        cols = slice(256 * j, 256 * (j + 1))
        rows = own if j < 3 else slice(0, WIDE)
        got = dot(h_ref[rows, :], joint_w[:, cols])
        out = (q_ref, k_ref, v_ref)[j // 3]
        for a in range(2):
            part = got[:, 128 * a : 128 * (a + 1)]
            if j < 6:
                part = rope(part, cos_ref[rows, :], sin_ref[rows, :])
            at = 256 * (j % 3) + 128 * a
            out[:, at : at + 128] = part.astype(BF16)

    start_all(sends[:4])
    offset = lax.axis_index("seq") * TOKENS
    row = lax.broadcasted_iota(jnp.int32, (TILE, 2 * TILE), 0)
    col = lax.broadcasted_iota(jnp.int32, (TILE, 2 * TILE), 1)
    lane = lax.broadcasted_iota(jnp.int32, (TILE, 128), 1)
    band = (col >= row) & (col - row <= 2 * RIM)

    @pl.loop(0, PAIRS)
    def _(pair):
        lanes = pl.ds(pl.multiple_of(pair * 128, 128), 128)
        for t in range(TILES):
            key = col + (offset + t * TILE - RIM)
            allowed = band & (key >= 0) & (key < 16 * TOKENS)
            query = q_ref[t * TILE : (t + 1) * TILE, lanes].astype(F32) * (HEAD_DIM**-0.5)
            stacked = jnp.concatenate(
                [jnp.where(lane < HEAD_DIM, query, 0.0), jnp.where(lane < HEAD_DIM, 0.0, query)], 0
            ).astype(BF16)
            window = slice(t * TILE, (t + 2) * TILE)
            scores = dot_back(stacked, k_ref[window, lanes])
            scores = jnp.where(jnp.concatenate([allowed, allowed], 0), scores, -1e30)
            expo = jnp.exp(scores - jnp.max(scores, axis=-1, keepdims=True))
            probs = (expo / jnp.sum(expo, axis=-1, keepdims=True)).astype(BF16)
            probs_ref[pair * TILES + t] = probs
            mixed = dot(probs, v_ref[window, lanes])
            att_ref[t * TILE : (t + 1) * TILE, lanes] = jnp.where(
                lane < HEAD_DIM, mixed[:TILE], mixed[TILE:]
            ).astype(BF16)
        pltpu.make_async_copy(
            probs_ref.at[pl.ds(pair * TILES, TILES)],
            outs[5].at[pl.ds(pair * TILES, TILES)],
            out_sems.at[7 + pair],
        ).start()

    sends[4].start()
    wait_all(sends)
    for pair in range(PAIRS):
        tiles = pl.ds(pair * TILES, TILES)
        pltpu.make_async_copy(probs_ref.at[tiles], outs[5].at[tiles], out_sems.at[7 + pair]).wait()


def joint_forward(normed, cosine, sine, pieces):
    return call(
        joint_kernel,
        JOINT_OUTS,
        like(JOINT_OUTS)
        + [
            pltpu.VMEM((8, 16, 128), BF16),
            pltpu.SemaphoreType.DMA((24,)),
            pltpu.SemaphoreType.DMA((13,)),
        ],
        "vvv" + "a" * 16,
        60,
    )(normed, cosine, sine, *pieces)


def packed_copies(pieces, merge_w, expand_w, shrink_w, sems):
    merge, expand, shrink = [], [], []
    for i, piece, who, half in piece_places(pieces):
        rows = pl.ds(pl.multiple_of(who * ROWS, 16), ROWS)
        cols = pl.ds(pl.multiple_of(half * 384, 128), 384)
        merge.append(
            pltpu.make_async_copy(
                piece.at[pl.ds(0, ROWS), :], merge_w.at[rows, cols], sems.at[i * 5]
            )
        )
        for part in range(3):
            expand.append(
                pltpu.make_async_copy(
                    piece.at[pl.ds(ROWS * (part + 1), ROWS), :],
                    expand_w.at[rows, pl.ds(pl.multiple_of(half * FF + part * 384, 128), 384)],
                    sems.at[i * 5 + 1 + part],
                )
            )
        shrink.append(
            pltpu.make_async_copy(
                piece.at[pl.ds(4 * ROWS, FF_ROWS), :],
                shrink_w.at[pl.ds(pl.multiple_of(who * FF_ROWS, 16), FF_ROWS), cols],
                sems.at[i * 5 + 4],
            )
        )
    return merge, expand, shrink


MIDDLE_OUTS = [
    ((TOKENS, D), BF16),
    ((TOKENS, FF), BF16),
    ((TOKENS, D), BF16),
    ((TOKENS, D), F32),
    ((TOKENS, D), BF16),
]
MIDDLE_HALVES = [((TOKENS, FF), BF16)] * 2 + [((TOKENS, D // 2), BF16)] * 2


def middle_kernel(gain_ref, *refs):
    ins, pieces, refs = refs[:3], refs[3:11], refs[11:]
    outs, halves, refs = refs[:5], refs[5:9], refs[9:]
    x_ref, att_ref, dy_ref, out_ref, m_ref, h_ref, dx_ref, datt_ref = refs[:8]
    merge_w, expand_w, shrink_w, x1, normed, inverse, z, dm, dz, dob = refs[8:18]
    in_sems, weight_sems, out_sems = refs[18:]
    dz_mine, dz_give, dob_mine, dob_give = halves
    core = lax.axis_index("seq") % 2
    loads = copy_all(ins, (x_ref, att_ref, dy_ref), in_sems)
    merge, expand, shrink = packed_copies(pieces, merge_w, expand_w, shrink_w, weight_sems)
    start_all(loads)
    start_all(merge)
    start_all(shrink)
    start_all(expand)
    sends = copy_all(refs[3:8], outs, out_sems)
    wait_all(merge)
    wait_all(loads)
    for j in range(3):
        cols = slice(256 * j, 256 * (j + 1))
        x1[:, cols] = x_ref[:, cols].astype(F32) + dot(att_ref[...], merge_w[:, cols])

    step = 32
    gain = jnp.concatenate([gain_chunk(gain_ref, 8, j) for j in range(6)], 1)

    @pl.loop(0, TOKENS // step)
    def _(i):
        rows = pl.ds(pl.multiple_of(i * step, step), step)
        part, scale = normalize(x1[rows, :])
        normed[rows, :] = part
        inverse[rows, :] = scale
        h_ref[rows, :] = (part * gain).astype(BF16)

    wait_all(shrink)
    for j in range(3):
        cols = slice(384 * j, 384 * (j + 1))
        dm[:, cols] = dot_back(dy_ref[...], shrink_w[cols, :])
    wait_all(expand)
    for j in range(9):
        cols = slice(256 * j, 256 * (j + 1))
        z[:, cols] = dot(h_ref[...], expand_w[:, cols])

    @pl.loop(0, TOKENS // 16)
    def _(i):
        rows = pl.ds(pl.multiple_of(i * 16, 16), 16)
        gate = z[rows, pl.ds(0, FF)]
        up = z[rows, pl.ds(FF, FF)]
        upstream = dm[rows, :]
        below = 0.5 + 0.5 * lax.erf(gate * (0.5**0.5))
        slope = below + gate * (jnp.exp(-0.5 * gate * gate) * (2 * math.pi) ** -0.5)
        active = gate * below
        m_ref[rows, :] = (active * up).astype(BF16)
        dz[0, rows, :] = (upstream * up * slope).astype(BF16)
        dz[1, rows, :] = (upstream * active).astype(BF16)

    sends += copy_all((dz.at[core], dz.at[1 - core]), (dz_mine, dz_give), out_sems, 5)
    start_all(sends[1:3])
    start_all(sends[5:])
    for j in range(3):
        cols = slice(256 * j, 256 * (j + 1))
        out_ref[:, cols] = (x1[:, cols] + dot(m_ref[...], shrink_w[:, cols])).astype(BF16)
    start_all(sends[:1])
    for j in range(3):
        rows = slice(256 * j, 256 * (j + 1))
        x1[:, rows] = dot_back(dz[0], expand_w[rows, :FF]) + dot_back(dz[1], expand_w[rows, FF:])

    @pl.loop(0, TOKENS // step)
    def _(i):
        rows = pl.ds(pl.multiple_of(i * step, step), step)
        back = norm_back(x1[rows, :], normed[rows, :], inverse[rows, :], gain)
        total = dy_ref[rows, :].astype(F32) + back
        dx_ref[rows, :] = total
        dob[0, rows, :] = total[:, :384].astype(BF16)
        dob[1, rows, :] = total[:, 384:].astype(BF16)

    sends += copy_all((dob.at[core], dob.at[1 - core]), (dob_mine, dob_give), out_sems, 7)
    start_all(sends[7:])
    start_all(sends[3:4])
    for j in range(3):
        cols = slice(256 * j, 256 * (j + 1))
        datt_ref[:, cols] = (
            dot_back(dob[0], merge_w[cols, :384]) + dot_back(dob[1], merge_w[cols, 384:])
        ).astype(BF16)
    start_all(sends[4:5])
    wait_all(sends)


def middle(gains, x, att, dy, pieces):
    return call(
        middle_kernel,
        MIDDLE_OUTS + MIDDLE_HALVES,
        [pltpu.VMEM((TOKENS, D), BF16)] * 3
        + like(MIDDLE_OUTS)
        + [
            pltpu.VMEM((D, D), BF16),
            pltpu.VMEM((D, 2 * FF), BF16),
            pltpu.VMEM((FF, D), BF16),
            pltpu.VMEM((TOKENS, D), F32),
            pltpu.VMEM((TOKENS, D), F32),
            pltpu.VMEM((TOKENS, 1), F32),
            pltpu.VMEM((TOKENS, 2 * FF), F32),
            pltpu.VMEM((TOKENS, FF), F32),
            pltpu.VMEM((2, TOKENS, FF), BF16),
            pltpu.VMEM((2, TOKENS, D // 2), BF16),
            pltpu.SemaphoreType.DMA((3,)),
            pltpu.SemaphoreType.DMA((80,)),
            pltpu.SemaphoreType.DMA((9,)),
        ],
        "vhhh" + "a" * 8,
        60,
    )(gains, x, att, dy, *pieces)


def paired_copies(refs, buffers, sems):
    copies = []
    for n, buffer in enumerate(buffers):
        rows = buffer.shape[0] // 2
        for side in range(2):
            copies.append(
                pltpu.make_async_copy(
                    refs[2 * n + side], buffer.at[pl.ds(side * rows, rows), :], sems.at[2 * n + side]
                )
            )
    return copies


def early_kernel(*refs):
    ins, outs, shrink_outs, refs = refs[:12], refs[12:16], refs[16:20], refs[20:]
    m, dy, h, dz, att, dob, blocks, shrink_blocks, sems, out_sems, shrink_sems = refs
    x, zh, _, seq = place()
    y = seq % 8 // 2
    copies = paired_copies(ins, (m, dy, h, dz, att, dob), sems)
    start_all(copies)
    wait_all(copies[:4])
    grad = dot_outer(m[...], dy[...]).astype(BF16)
    shrink_blocks[...] = grad.reshape(OWNERS, FF_ROWS, 384)
    sends = [
        pltpu.make_async_copy(
            shrink_blocks.at[owner(x, zh, dx, dz)], shrink_outs[dx].at[dz], shrink_sems.at[dx * 2 + dz]
        )
        for dx in range(4)
        for dz in range(2)
    ]
    start_all(sends)
    wait_all(copies[4:])
    for part in range(3):
        grad = dot_outer(h[...], dz[:, 384 * part : 384 * (part + 1)]).astype(BF16)
        blocks[part] = grad.reshape(OWNERS, ROWS, 384)
    grad = dot_outer(att[...], dob[...]).astype(BF16)
    blocks[3] = grad.reshape(OWNERS, ROWS, 384)
    more = [
        pltpu.make_async_copy(
            blocks.at[(y + dy) % 4, owner(x, zh, dx, dz)],
            outs[dy].at[dx * 2 + dz],
            out_sems.at[dy * 8 + dx * 2 + dz],
        )
        for dy in range(4)
        for dx in range(4)
        for dz in range(2)
    ]
    start_all(more)
    wait_all(sends)
    wait_all(more)


def early_grads(*args):
    return call(
        early_kernel,
        [((OWNERS, ROWS, 384), BF16)] * 4 + [((2, FF_ROWS, 384), BF16)] * 4,
        [
            pltpu.VMEM((2 * TOKENS, FF), BF16),
            pltpu.VMEM((2 * TOKENS, D // 2), BF16),
            pltpu.VMEM((2 * TOKENS, D), BF16),
            pltpu.VMEM((2 * TOKENS, FF), BF16),
            pltpu.VMEM((2 * TOKENS, D), BF16),
            pltpu.VMEM((2 * TOKENS, D // 2), BF16),
            pltpu.VMEM((4, OWNERS, ROWS, 384), BF16),
            pltpu.VMEM((OWNERS, FF_ROWS, 384), BF16),
            pltpu.SemaphoreType.DMA((12,)),
            pltpu.SemaphoreType.DMA((32,)),
            pltpu.SemaphoreType.DMA((8,)),
        ],
        "ha" * 6,
        60,
    )(*args)


def attention_back_kernel(cos_ref, sin_ref, *refs):
    ins, probs_in, mine_ref, give_ref, scratch = refs[:4], refs[4], refs[5], refs[6], refs[7:]
    q_ref, k_ref, v_ref, datt_ref, probs_ref, dk, dv, dj, in_sems, sems = scratch
    loads = copy_all(ins, scratch[:4], in_sems)
    start_all(loads)

    def load_probs(pair):
        tiles = pl.ds(pair * TILES, TILES)
        return pltpu.make_async_copy(probs_in.at[tiles], probs_ref.at[tiles], in_sems.at[4 + pair])

    for pair in range(PAIRS):
        load_probs(pair).start()
    core = lax.axis_index("seq") % 2
    lane = lax.broadcasted_iota(jnp.int32, (TILE, 128), 1)
    own = slice(RIM, RIM + TOKENS)
    dk[...] = jnp.zeros_like(dk)
    dv[...] = jnp.zeros_like(dv)
    dj[0, :RIM, :D] = jnp.zeros((RIM, D), BF16)
    dj[0, RIM + TOKENS :, :D] = jnp.zeros((RIM, D), BF16)
    wait_all(loads)
    scale = HEAD_DIM**-0.5

    @pl.loop(0, PAIRS)
    def _(pair):
        lanes = pl.ds(pl.multiple_of(pair * 128, 128), 128)
        load_probs(pair).wait()
        for t in range(TILES):
            rows = slice(t * TILE, (t + 1) * TILE)
            window = slice(t * TILE, (t + 2) * TILE)
            query = q_ref[rows, lanes].astype(F32) * scale
            query = jnp.concatenate(
                [jnp.where(lane < HEAD_DIM, query, 0.0), jnp.where(lane < HEAD_DIM, 0.0, query)], 0
            ).astype(BF16)
            upstream = datt_ref[rows, lanes].astype(F32)
            upstream = jnp.concatenate(
                [
                    jnp.where(lane < HEAD_DIM, upstream, 0.0),
                    jnp.where(lane < HEAD_DIM, 0.0, upstream),
                ],
                0,
            ).astype(BF16)
            probs_b = probs_ref[pair * TILES + t]
            probs = probs_b.astype(F32)
            dp = dot_back(upstream, v_ref[window, lanes])
            delta = jnp.sum(probs * dp, axis=-1, keepdims=True)
            ds = (probs * (dp - delta)).astype(BF16)
            dv[window, lanes] += dot_outer(probs_b, upstream)
            dk[window, lanes] += dot_outer(ds, query)
            dq = dot(ds, k_ref[window, lanes]) * scale
            dq = jnp.where(lane < HEAD_DIM, dq[:TILE], dq[TILE:])
            at = slice(RIM + t * TILE, RIM + (t + 1) * TILE)
            dj[0, at, lanes] = rope(dq, cos_ref[at, :], -sin_ref[at, :]).astype(BF16)

    for j in range(6):
        cols = slice(128 * j, 128 * (j + 1))
        part = rope(dk[:, cols], cos_ref[...], -sin_ref[...]).astype(BF16)
        if j < 3:
            dj[0, :, D + 128 * j : D + 128 * (j + 1)] = part
        else:
            dj[1, :, 128 * (j - 3) : 128 * (j - 2)] = part
    dj[1, :, D // 2 :] = dv[...].astype(BF16)
    sends = [
        pltpu.make_async_copy(dj.at[core], mine_ref, sems.at[0]),
        pltpu.make_async_copy(dj.at[1 - core], give_ref, sems.at[1]),
    ]
    start_all(sends)
    wait_all(sends)


def attention_back(*args):
    return call(
        attention_back_kernel,
        [((WIDE, HALF), BF16)] * 2,
        [
            pltpu.VMEM((TOKENS, D), BF16),
            pltpu.VMEM((WIDE, D), BF16),
            pltpu.VMEM((WIDE, D), BF16),
            pltpu.VMEM((TOKENS, D), BF16),
            pltpu.VMEM((PAIRS * TILES, 2 * TILE, 2 * TILE), BF16),
            pltpu.VMEM((WIDE, D), F32),
            pltpu.VMEM((WIDE, D), F32),
            pltpu.VMEM((2, WIDE, HALF), BF16),
            pltpu.SemaphoreType.DMA((10,)),
            pltpu.SemaphoreType.DMA((2,)),
        ],
        "vvhhhhh",
        60,
    )(*args)


def late_kernel(*refs):
    ins, outs, refs = refs[:4], refs[4:8], refs[8:]
    h, dj, blocks, sems, out_sems = refs
    x, zh, _, _ = place()
    copies = paired_copies(ins, (h, dj), sems)
    start_all(copies)
    wait_all(copies)
    for part in range(3):
        grad = dot_outer(h[...], dj[:, 384 * part : 384 * (part + 1)]).astype(BF16)
        blocks[:, ROWS * part : ROWS * (part + 1), :] = grad.reshape(OWNERS, ROWS, 384)
    blocks[:, 3 * ROWS :, :] = jnp.zeros((OWNERS, JOINT_ROWS - 3 * ROWS, 384), BF16)
    sends = [
        pltpu.make_async_copy(blocks.at[owner(x, zh, dx, dz)], outs[dx].at[dz], out_sems.at[dx * 2 + dz])
        for dx in range(4)
        for dz in range(2)
    ]
    start_all(sends)
    wait_all(sends)


def late_grads(*args):
    return call(
        late_kernel,
        [((2, JOINT_ROWS, 384), BF16)] * 4,
        [
            pltpu.VMEM((2 * WIDE, D), BF16),
            pltpu.VMEM((2 * WIDE, HALF), BF16),
            pltpu.VMEM((OWNERS, JOINT_ROWS, 384), BF16),
            pltpu.SemaphoreType.DMA((4,)),
            pltpu.SemaphoreType.DMA((8,)),
        ],
        "haha",
        60,
    )(*args)


def sum_of(parts, index):
    return sum(part[index].astype(F32) for part in parts)


def early_sum_kernel(*refs):
    ins, outs, parts, total, sems, out_sems = refs[:4], refs[4:8], refs[8:12], *refs[12:]
    copies = copy_all(ins, parts, sems)
    start_all(copies)
    wait_all(copies)
    sends = [
        pltpu.make_async_copy(total.at[pl.ds(2 * d, 2)], outs[d], out_sems.at[d]) for d in range(4)
    ]
    for d in (1, 3, 2, 0):
        for i in (2 * d, 2 * d + 1):
            total[i] = sum_of(parts, i).astype(BF16)
        sends[d].start()
    wait_all(sends)


def late_sum_kernel(*refs):
    ins, outs, parts, total, sems, out_sems = refs[:8], refs[8:12], refs[12:20], *refs[20:]
    _, _, _, seq = place()
    y = seq % 8 // 2
    copies = copy_all(ins, parts, sems)
    start_all(copies)
    wait_all(copies)
    for i in range(2):
        total[i, :FF_ROWS] = sum_of(parts[:4], i).astype(BF16)
        total[i, FF_ROWS:] = sum_of(parts[4:], i).astype(BF16)
    sends = [
        pltpu.make_async_copy(
            total.at[:, pl.ds(pl.multiple_of((y + d) % 4 * LATE_QUARTER, 16), LATE_QUARTER), :],
            outs[d],
            out_sems.at[d],
        )
        for d in range(4)
    ]
    start_all(sends)
    wait_all(sends)


def both_sum_kernel(*refs):
    ins, outs, parts, keep, give, sems, out_sems = refs[:8], refs[8:10], refs[10:18], *refs[18:]
    copies = copy_all(ins, parts, sems)
    start_all(copies)
    wait_all(copies)
    keep[:ROWS] = sum_of(parts[:4], 0).astype(BF16)
    keep[ROWS:] = sum_of(parts[4:], 0).astype(BF16)
    give[:ROWS] = sum_of(parts[:4], 1).astype(BF16)
    give[ROWS:] = sum_of(parts[4:], 1).astype(BF16)
    sends = copy_all((keep, give), outs, out_sems)
    start_all(sends)
    wait_all(sends)


def summed(kernel, parts, outs, scratch):
    return call(
        kernel,
        outs,
        [pltpu.VMEM(part.shape, part.dtype) for part in parts]
        + scratch
        + [pltpu.SemaphoreType.DMA((len(parts),)), pltpu.SemaphoreType.DMA((len(outs),))],
        "a" * len(parts),
        60,
    )(*parts)


def early_sum(parts):
    shape = (OWNERS, ROWS, 384)
    outs = [((2, ROWS, 384), BF16)] * 4
    return summed(early_sum_kernel, parts, outs, [pltpu.VMEM(shape, BF16)])


def late_sum(parts):
    shape = (2, LATE_ROWS, 384)
    outs = [((2, LATE_QUARTER, 384), BF16)] * 4
    return summed(late_sum_kernel, parts, outs, [pltpu.VMEM(shape, BF16)])


def both_sum(parts):
    outs = [((ROWS + LATE_QUARTER, 384), BF16)] * 2
    return summed(both_sum_kernel, parts, outs, like(outs))


INPUT_OUTS = [((TOKENS, D), F32), ((RIM, D), BF16), ((RIM, D), BF16)]


def input_kernel(inverse_ref, gain_ref, *refs):
    (normed, dx, weight, mine, give), outs, refs = refs[:5], refs[5:8], refs[8:]
    base_ref, low_ref, high_ref, joint_w, dj, upstream, normed_ref, dx_ref, sems, out_sems = refs
    core = lax.axis_index("seq") % 2
    copies = [
        pltpu.make_async_copy(weight, joint_w, sems.at[0]),
        pltpu.make_async_copy(mine, dj.at[core], sems.at[1]),
        pltpu.make_async_copy(give, dj.at[1 - core], sems.at[2]),
        pltpu.make_async_copy(normed, normed_ref, sems.at[3]),
        pltpu.make_async_copy(dx, dx_ref, sems.at[4]),
    ]
    start_all(copies)
    wait_all(copies)
    for j in range(3):
        cols = slice(256 * j, 256 * (j + 1))
        upstream[:, cols] = dot_back(dj[0], joint_w[cols, :HALF]) + dot_back(
            dj[1], joint_w[cols, HALF:]
        )
    gain = jnp.concatenate([gain_chunk(gain_ref, 0, j) for j in range(6)], 1)
    step = 32

    def back(rows):
        return norm_back(upstream[rows, :], normed_ref[rows, :], inverse_ref[rows, :], gain)

    @pl.loop(0, TOKENS // step)
    def _(i):
        start = pl.multiple_of(i * step, step)
        base_ref[pl.ds(start, step), :] = dx_ref[pl.ds(start, step), :] + back(
            pl.ds(start + RIM, step)
        )

    @pl.loop(0, RIM // step)
    def _(i):
        start = pl.multiple_of(i * step, step)
        low_ref[pl.ds(start, step), :] = back(pl.ds(start, step)).astype(BF16)
        high_ref[pl.ds(start, step), :] = back(pl.ds(start + RIM + TOKENS, step)).astype(BF16)

    sends = copy_all(refs[:3], outs, out_sems)
    start_all(sends)
    wait_all(sends)


def input_back(*args):
    return call(
        input_kernel,
        INPUT_OUTS,
        like(INPUT_OUTS)
        + [
            pltpu.VMEM((D, 3 * D), BF16),
            pltpu.VMEM((2, WIDE, HALF), BF16),
            pltpu.VMEM((WIDE, D), F32),
            pltpu.VMEM((WIDE, D), F32),
            pltpu.VMEM((TOKENS, D), F32),
            pltpu.SemaphoreType.DMA((5,)),
            pltpu.SemaphoreType.DMA((3,)),
        ],
        "vvahhhh",
        60,
    )(*args)


RESULTS = [((ROWS, 3 * D), F32), ((ROWS, D), F32), ((ROWS, 2 * FF), F32), ((FF_ROWS, D), F32)]
GAIN_RESULTS = [((1, ROWS), F32)] * 2


def result_kernel(first_gain, second_gain, *refs):
    sums, weights, outs, refs = refs[:2], refs[2:4], refs[4:10], refs[10:]
    joint, merge, expand, shrink, first, second, early, late, joint_w, expand_w, sems = refs
    _, _, core, seq = place()
    y = seq % 8 // 2
    copies = copy_all(weights, (joint_w, expand_w), sems)
    for side in range(2):
        half = (core + side) % 2
        for dy in range(4):
            quarter = (y + dy) % 4
            rows = pl.ds(pl.multiple_of(quarter * LATE_QUARTER, 16), LATE_QUARTER)
            copies += copy_all(
                (
                    sums[side].at[dy, pl.ds(0, ROWS)],
                    sums[side].at[dy, pl.ds(ROWS, LATE_QUARTER)],
                ),
                (early.at[half, quarter], late.at[half, rows]),
                sems,
                2 + (side * 4 + dy) * 2,
            )
    start_all(copies)
    wait_all(copies)
    for half in range(2):
        cols = slice(384 * half, 384 * (half + 1))
        shrink[:, cols] = late[half, :FF_ROWS].astype(F32)
        merge[:, cols] = early[half, 3].astype(F32)
        for part in range(3):
            cols = slice(FF * half + 384 * part, FF * half + 384 * (part + 1))
            at = FF_ROWS + ROWS * part
            expand[:, cols] = early[half, part].astype(F32)
            joint[:, cols] = late[half, at : at + ROWS].astype(F32)
    sends = copy_all((joint, merge, expand, shrink, first, second), outs, sems, 18)
    start_all(sends[:4])
    for total, weight, grad, gain in (
        (first, joint_w, joint, first_gain),
        (second, expand_w, expand, second_gain),
    ):
        product = sum(
            weight[:, 128 * j : 128 * (j + 1)].astype(F32) * grad[:, 128 * j : 128 * (j + 1)]
            for j in range(3 * D // 128)
        )
        total[...] = jnp.sum(product.T, axis=0, keepdims=True) / gain[...]
    start_all(sends[4:])
    wait_all(sends)


def results(*args):
    return call(
        result_kernel,
        RESULTS + GAIN_RESULTS,
        like(RESULTS + GAIN_RESULTS)
        + [
            pltpu.VMEM((2, 4, ROWS, 384), BF16),
            pltpu.VMEM((2, LATE_ROWS, 384), BF16),
            pltpu.VMEM((ROWS, 3 * D), BF16),
            pltpu.VMEM((ROWS, 2 * FF), BF16),
            pltpu.SemaphoreType.DMA((24,)),
        ],
        "vvaahh",
        60,
    )(*args)


def stack_kernel(*refs):
    *ins, out, sems = refs
    copies = [pltpu.make_async_copy(r, out.at[i], sems.at[i]) for i, r in enumerate(ins)]
    start_all(copies)
    wait_all(copies)


def stack(*parts):
    return call(
        stack_kernel,
        [((len(parts),) + parts[0].shape, parts[0].dtype)],
        [pltpu.SemaphoreType.DMA((len(parts),))],
        "a" * len(parts),
        2,
    )(*parts)[0]


def gather_pieces(own):
    from_low = over_fsdp(own, 1, 0)
    from_high = over_fsdp(own, -1, 0)
    across = over_fsdp(own, 0, 1)
    from_far = over_fsdp(own, 2, 0)
    across_low = over_fsdp(across, 1, 0)
    across_high = over_fsdp(across, -1, 0)
    across_far = over_fsdp(from_far, 0, 1)
    return [own, across, from_high, across_high, from_far, across_far, from_low, across_low]


def gather_pairs(pair):
    from_low = over_fsdp(pair, 1, 0)
    from_high = over_fsdp(pair, -1, 0)
    from_far = over_fsdp(pair, 2, 0)
    return [pair, from_high, from_far, from_low]


def around(blocks, shift):
    return [blocks[0]] + [shift(blocks[d % 4], d) for d in (1, -1, 2)]


def over_x(value, d):
    return over_fsdp(value, d, 0)


def over_y(value, d):
    return over_seq(value, 0, d, 0)


def gather_quarters(own):
    from_low, from_high, from_far = (over_y(own, d) for d in (1, -1, 2))
    return [own, from_high, from_far, from_low]


def shards(
    inputs,
    first_gain,
    joint_weight,
    merge_weight,
    second_gain,
    expand_weight,
    shrink_weight,
    cotangent,
):
    x, zh, core, seq = place()
    fsdp = lax.axis_index("fsdp")
    source, upstream = inputs[0], cotangent[0]

    def columns(w, start, width):
        return lax.dynamic_slice_in_dim(w, start, width, 1)

    def placed_gain(gain):
        whole = lax.dynamic_update_slice_in_dim(jnp.zeros((D,), BF16), gain, fsdp * ROWS, 0)
        return jnp.pad(whole.reshape(6, 128), ((0, 2), (0, 0)))

    gain_tile = jnp.concatenate(
        [placed_gain(first_gain), placed_gain(second_gain), jnp.zeros((ROWS - 16, 128), BF16)], 0
    )
    joint_own = jnp.concatenate([columns(joint_weight, core * HALF, HALF), gain_tile], 1)
    joint_mine = gather_pieces(joint_own)
    packed_own = jnp.concatenate(
        [columns(merge_weight, core * 384, 384)]
        + [columns(expand_weight, core * FF + 384 * i, 384) for i in range(3)]
        + [columns(shrink_weight, core * 384, 384)],
        0,
    )
    packed_own, source_halo, _ = lax.optimization_barrier((packed_own, source, joint_mine[1]))
    low_halo = passed_along(source_halo[TOKENS - RIM :], 1)
    high_halo = passed_along(source_halo[:RIM], -1)
    packed_pair = stack(packed_own, over_fsdp(packed_own, 0, 1))

    frequencies = jnp.exp(
        jnp.arange(HEAD_DIM // 2, dtype=F32) * (-2.0 * math.log(10000.0) / HEAD_DIM)
    )
    positions = (seq * TOKENS - RIM + lax.iota(jnp.int32, WIDE)).astype(F32)
    angles = positions[:, None] * frequencies[None, :]
    cosine, sine = jnp.cos(angles), jnp.sin(angles)
    cosine = jnp.concatenate([cosine] * 4, 1)
    sine = jnp.concatenate([-sine, sine] * 2, 1)
    extended = jnp.concatenate([low_halo, source, high_halo], 0).astype(F32)
    normed, inverse = normalize(extended)

    *joint_mine, normed, cosine, sine = lax.optimization_barrier((*joint_mine, normed, cosine, sine))
    joint_pieces = joint_mine + [core_swap(p) for p in joint_mine]
    packed_pair, *_ = lax.optimization_barrier((packed_pair, *joint_mine))
    packed_mine = gather_pairs(packed_pair)
    q, k, v, h_first, attended, probs, gains, joint_w = joint_forward(
        normed, cosine, sine, joint_pieces
    )
    *packed_mine, attended = lax.optimization_barrier((*packed_mine, attended))
    packed_pieces = packed_mine + [core_swap(p) for p in packed_mine]
    dy_mine = columns(upstream, core * 384, 384)
    dy_got = core_swap(columns(upstream, (1 - core) * 384, 384))
    result, hidden, h_second, dx, datt, dz_mine, dz_give, dob_mine, dob_give = middle(
        gains, source, attended, upstream, packed_pieces
    )
    *early, datt = lax.optimization_barrier(
        (
            *early_grads(
                hidden,
                core_swap(hidden),
                dy_mine,
                dy_got,
                h_second,
                core_swap(h_second),
                dz_mine,
                core_swap(dz_give),
                attended,
                core_swap(attended),
                dob_mine,
                core_swap(dob_give),
            ),
            datt,
        )
    )
    shrink_parts = around(early[4:], over_x)
    dj_mine, dj_give = attention_back(cosine, sine, q, k, v, datt, probs)
    *shrink_parts, dj_mine, dj_give = lax.optimization_barrier((*shrink_parts, dj_mine, dj_give))
    late = late_grads(h_first, core_swap(h_first), dj_mine, core_swap(dj_give))
    early_parts = around(early[:4], over_y)
    late_own, dj_mine = lax.optimization_barrier((late[0], dj_mine))
    late_parts = around([late_own, *late[1:]], over_x)
    base, low_back, high_back = input_back(inverse, gains, normed, dx, joint_w, dj_mine, dj_give)
    from_high = passed_along(low_back, -1).astype(F32)
    from_low = passed_along(high_back, 1).astype(F32)
    input_grad = (
        base
        + jnp.pad(from_high, ((TOKENS - RIM, 0), (0, 0)))
        + jnp.pad(from_low, ((0, TOKENS - RIM), (0, 0)))
    ).astype(BF16)

    *late_parts, input_grad = lax.optimization_barrier((*late_parts, input_grad))
    late_quarters = around(late_sum(shrink_parts + late_parts), over_y)
    keep, give = both_sum(around(early_sum(early_parts), over_x) + late_quarters)
    keeps = keep.astype(F32) + over_seq(keep, 1, 0, 0).astype(F32)
    gives = over_fsdp(give, 0, 1).astype(F32) + over_both_z(give).astype(F32)
    own = stack(*gather_quarters((keeps + gives).astype(BF16)))
    joint_grad, merge_grad, expand_grad, shrink_grad, first_grad, second_grad = results(
        first_gain.astype(F32)[None],
        second_gain.astype(F32)[None],
        own,
        core_swap(own),
        joint_weight,
        expand_weight,
    )
    return (
        result[None],
        input_grad[None],
        first_grad[0],
        joint_grad,
        merge_grad,
        second_grad[0],
        expand_grad,
        shrink_grad,
    )


def solution(mesh):
    placed = (
        P("fsdp", "seq", None),
        P("fsdp"),
        P("fsdp", None),
        P("fsdp", None),
        P("fsdp"),
        P("fsdp", None),
        P("fsdp", None),
        P("fsdp", "seq", None),
    )
    return jax.shard_map(
        shards,
        mesh=mesh,
        in_specs=placed,
        out_specs=(
            P("fsdp", "seq", None),
            P("fsdp", "seq", None),
            P("fsdp"),
            P("fsdp", None),
            P("fsdp", None),
            P("fsdp"),
            P("fsdp", None),
            P("fsdp", None),
        ),
        check_vma=False,
    )
```

```python
import math

import jax
import jax.numpy as jnp
from jax import lax
from jax.experimental import pallas as pl
from jax.experimental.pallas import tpu as pltpu
from jax.sharding import PartitionSpec as P

D = 768
HEADS = 12
HEAD_DIM = 64
FF = 1152
RIM = 64
TOKENS = 384
WIDE = TOKENS + 2 * RIM
TILE = 128
TILES = TOKENS // TILE
PAIRS = HEADS // 2
OWNERS = 8
ROWS = D // OWNERS
FF_ROWS = FF // OWNERS
HALF = 3 * D // 2
LATE_ROWS = 320
LATE_QUARTER = LATE_ROWS // 4
PACKED = 4 * ROWS + FF_ROWS
EPSILON = 1e-05
F32 = jnp.float32
BF16 = jnp.bfloat16
MIB = 2**20


def over_fsdp(value, dx, dz):
    pairs = [
        (x * 2 + z, ((x + dx) % 4) * 2 + (z + dz) % 2) for x in range(4) for z in range(2)
    ]
    return lax.ppermute(value, "fsdp", pairs)


def over_seq(value, dz, dy, dc):
    pairs = [
        (z * 8 + y * 2 + c, ((z + dz) % 2) * 8 + ((y + dy) % 4) * 2 + (c + dc) % 2)
        for z in range(2)
        for y in range(4)
        for c in range(2)
    ]
    return lax.ppermute(value, "seq", pairs)


def over_both_z(value):
    pairs = [
        (f * 16 + s, (f ^ 1) * 16 + (s ^ 8)) for f in range(8) for s in range(16)
    ]
    return lax.ppermute(value, ("fsdp", "seq"), pairs)


def core_swap(value):
    return over_seq(value, 0, 0, 1)


def passed_along(value, steps):
    first, last = (max(0, -steps), min(16, 16 - steps))
    return lax.ppermute(value, "seq", [(i, i + steps) for i in range(first, last)])


def place():
    fsdp, seq = lax.axis_index("fsdp"), lax.axis_index("seq")
    return fsdp // 2, fsdp % 2, seq % 2, seq


def owner(x, zh, dx, dz):
    return ((x + dx) % 4) * 2 + (zh + dz) % 2


def dot(left, right):
    return jnp.dot(left, right, preferred_element_type=F32)


def dot_back(left, right):
    return lax.dot_general(left, right, (((1,), (1,)), ((), ())), preferred_element_type=F32)


def dot_outer(left, right):
    return lax.dot_general(left, right, (((0,), (0,)), ((), ())), preferred_element_type=F32)


def row_mean(values):
    return jnp.sum(values, axis=-1, keepdims=True) * (1.0 / D)


def normalize(values):
    centred = values - row_mean(values)
    inverse = lax.rsqrt(row_mean(centred * centred) + EPSILON)
    return (centred * inverse, inverse)


def norm_back(upstream, normed, inverse, gain):
    scaled = upstream * gain
    centred = scaled - row_mean(scaled)
    return inverse * (centred - normed * row_mean(scaled * normed))


def rope(values, cosine, sine):
    lane = lax.broadcasted_iota(jnp.int32, values.shape, 1) % HEAD_DIM
    partner = jnp.where(
        lane < HEAD_DIM // 2,
        pltpu.roll(values, 128 - HEAD_DIM // 2, 1),
        pltpu.roll(values, HEAD_DIM // 2, 1),
    )
    return values * cosine + partner * sine


def call(kernel, outs, scratch, spaces, limit):
    kinds = {"v": pltpu.VMEM, "h": pltpu.HBM, "a": pl.ANY}
    return pl.pallas_call(
        kernel,
        out_shape=[jax.ShapeDtypeStruct(shape, kind) for shape, kind in outs],
        in_specs=[pl.BlockSpec(memory_space=kinds[c]) for c in spaces],
        out_specs=[pl.BlockSpec(memory_space=pltpu.HBM) for _ in outs],
        scratch_shapes=scratch,
        compiler_params=pltpu.CompilerParams(vmem_limit_bytes=limit * MIB),
    )


def like(outs):
    return [pltpu.VMEM(shape, kind) for shape, kind in outs]


def copy_all(sources, targets, sems, first=0):
    return [
        pltpu.make_async_copy(a, b, sems.at[first + i])
        for i, (a, b) in enumerate(zip(sources, targets, strict=True))
    ]


def start_all(copies):
    for copy in copies:
        copy.start()


def wait_all(copies):
    for copy in copies:
        copy.wait()


def piece_places(pieces):
    x, zh, core, _ = place()
    return [
        (
            side * 8 + dx * 2 + dz,
            pieces[side * 8 + dx * 2 + dz],
            owner(x, zh, dx, dz),
            (core + side) % 2,
        )
        for side in range(2)
        for dx in range(4)
        for dz in range(2)
    ]


def joint_copies(pieces, joint_w, sems):
    return [
        pltpu.make_async_copy(
            piece.at[:, pl.ds(0, HALF)],
            joint_w.at[
                pl.ds(pl.multiple_of(who * ROWS, 16), ROWS),
                pl.ds(pl.multiple_of(half * HALF, 128), HALF),
            ],
            sems.at[i],
        )
        for i, piece, who, half in piece_places(pieces)
    ]


def gain_chunk(gain_ref, row, j):
    return gain_ref[row + j : row + j + 1, :]


JOINT_OUTS = [
    ((TOKENS, D), BF16),
    ((WIDE, D), BF16),
    ((WIDE, D), BF16),
    ((WIDE, D), BF16),
    ((TOKENS, D), BF16),
    ((PAIRS * TILES, 2 * TILE, 2 * TILE), BF16),
    ((16, 128), F32),
    ((D, 3 * D), BF16),
]


def joint_kernel(normed_ref, cos_ref, sin_ref, *refs):
    pieces, outs, refs = refs[:16], refs[16:24], refs[24:]
    q_ref, k_ref, v_ref, h_ref, att_ref, probs_ref, gain_ref, joint_w, gains, sems, out_sems = refs
    copies = joint_copies(pieces, joint_w, sems)
    gain_copies = [
        pltpu.make_async_copy(
            pieces[i].at[pl.ds(0, 16), pl.ds(HALF, 128)], gains.at[i], sems.at[16 + i]
        )
        for i in range(8)
    ]
    start_all(gain_copies)
    start_all(copies)
    wait_all(gain_copies)
    gain_ref[...] = jnp.sum(gains[...].astype(F32), axis=0)
    for j in range(D // 128):
        cols = slice(128 * j, 128 * (j + 1))
        h_ref[:, cols] = (normed_ref[:, cols] * gain_chunk(gain_ref, 0, j)).astype(BF16)
    wait_all(copies)
    sends = copy_all(refs[:5] + refs[6:8], outs[:5] + outs[6:8], out_sems)
    start_all(sends[5:])
    own = slice(RIM, RIM + TOKENS)
    for j in range(9):
        cols = slice(256 * j, 256 * (j + 1))
        rows = own if j < 3 else slice(0, WIDE)
        got = dot(h_ref[rows, :], joint_w[:, cols])
        out = (q_ref, k_ref, v_ref)[j // 3]
        for a in range(2):
            part = got[:, 128 * a : 128 * (a + 1)]
            if j < 6:
                part = rope(part, cos_ref[rows, :], sin_ref[rows, :])
            at = 256 * (j % 3) + 128 * a
            out[:, at : at + 128] = part.astype(BF16)

    start_all(sends[:4])
    offset = lax.axis_index("seq") * TOKENS
    row = lax.broadcasted_iota(jnp.int32, (TILE, 2 * TILE), 0)
    col = lax.broadcasted_iota(jnp.int32, (TILE, 2 * TILE), 1)
    lane = lax.broadcasted_iota(jnp.int32, (TILE, 128), 1)
    band = (col >= row) & (col - row <= 2 * RIM)

    @pl.loop(0, PAIRS)
    def _(pair):
        lanes = pl.ds(pl.multiple_of(pair * 128, 128), 128)
        for t in range(TILES):
            key = col + (offset + t * TILE - RIM)
            allowed = band & (key >= 0) & (key < 16 * TOKENS)
            query = q_ref[t * TILE : (t + 1) * TILE, lanes].astype(F32) * (HEAD_DIM**-0.5)
            stacked = jnp.concatenate(
                [jnp.where(lane < HEAD_DIM, query, 0.0), jnp.where(lane < HEAD_DIM, 0.0, query)], 0
            ).astype(BF16)
            window = slice(t * TILE, (t + 2) * TILE)
            scores = dot_back(stacked, k_ref[window, lanes])
            scores = jnp.where(jnp.concatenate([allowed, allowed], 0), scores, -1e30)
            expo = jnp.exp(scores - jnp.max(scores, axis=-1, keepdims=True))
            probs = (expo / jnp.sum(expo, axis=-1, keepdims=True)).astype(BF16)
            probs_ref[pair * TILES + t] = probs
            mixed = dot(probs, v_ref[window, lanes])
            att_ref[t * TILE : (t + 1) * TILE, lanes] = jnp.where(
                lane < HEAD_DIM, mixed[:TILE], mixed[TILE:]
            ).astype(BF16)
        pltpu.make_async_copy(
            probs_ref.at[pl.ds(pair * TILES, TILES)],
            outs[5].at[pl.ds(pair * TILES, TILES)],
            out_sems.at[7 + pair],
        ).start()

    sends[4].start()
    wait_all(sends)
    for pair in range(PAIRS):
        tiles = pl.ds(pair * TILES, TILES)
        pltpu.make_async_copy(probs_ref.at[tiles], outs[5].at[tiles], out_sems.at[7 + pair]).wait()


def joint_forward(normed, cosine, sine, pieces):
    return call(
        joint_kernel,
        JOINT_OUTS,
        like(JOINT_OUTS)
        + [
            pltpu.VMEM((8, 16, 128), BF16),
            pltpu.SemaphoreType.DMA((24,)),
            pltpu.SemaphoreType.DMA((13,)),
        ],
        "vvv" + "a" * 16,
        60,
    )(normed, cosine, sine, *pieces)


def packed_copies(pieces, merge_w, expand_w, shrink_w, sems):
    merge, expand, shrink = [], [], []
    for i, piece, who, half in piece_places(pieces):
        rows = pl.ds(pl.multiple_of(who * ROWS, 16), ROWS)
        cols = pl.ds(pl.multiple_of(half * 384, 128), 384)
        merge.append(
            pltpu.make_async_copy(
                piece.at[pl.ds(0, ROWS), :], merge_w.at[rows, cols], sems.at[i * 5]
            )
        )
        for part in range(3):
            expand.append(
                pltpu.make_async_copy(
                    piece.at[pl.ds(ROWS * (part + 1), ROWS), :],
                    expand_w.at[rows, pl.ds(pl.multiple_of(half * FF + part * 384, 128), 384)],
                    sems.at[i * 5 + 1 + part],
                )
            )
        shrink.append(
            pltpu.make_async_copy(
                piece.at[pl.ds(4 * ROWS, FF_ROWS), :],
                shrink_w.at[pl.ds(pl.multiple_of(who * FF_ROWS, 16), FF_ROWS), cols],
                sems.at[i * 5 + 4],
            )
        )
    return merge, expand, shrink


MIDDLE_OUTS = [
    ((TOKENS, D), BF16),
    ((TOKENS, FF), BF16),
    ((TOKENS, D), BF16),
    ((TOKENS, D), F32),
    ((TOKENS, D), BF16),
]
MIDDLE_HALVES = [((TOKENS, FF), BF16)] * 2 + [((TOKENS, D // 2), BF16)] * 2


def middle_kernel(gain_ref, *refs):
    ins, pieces, refs = refs[:3], refs[3:19], refs[19:]
    outs, halves, refs = refs[:5], refs[5:9], refs[9:]
    x_ref, att_ref, dy_ref, out_ref, m_ref, h_ref, dx_ref, datt_ref = refs[:8]
    merge_w, expand_w, shrink_w, x1, normed, inverse, z, dm, dz, dob = refs[8:18]
    in_sems, weight_sems, out_sems = refs[18:]
    dz_mine, dz_give, dob_mine, dob_give = halves
    core = lax.axis_index("seq") % 2
    loads = copy_all(ins, (x_ref, att_ref, dy_ref), in_sems)
    merge, expand, shrink = packed_copies(pieces, merge_w, expand_w, shrink_w, weight_sems)
    start_all(loads)
    start_all(merge)
    start_all(shrink)
    start_all(expand)
    sends = copy_all(refs[3:8], outs, out_sems)
    wait_all(merge)
    wait_all(loads)
    for j in range(3):
        cols = slice(256 * j, 256 * (j + 1))
        x1[:, cols] = x_ref[:, cols].astype(F32) + dot(att_ref[...], merge_w[:, cols])

    step = 32
    gain = jnp.concatenate([gain_chunk(gain_ref, 8, j) for j in range(6)], 1)

    @pl.loop(0, TOKENS // step)
    def _(i):
        rows = pl.ds(pl.multiple_of(i * step, step), step)
        part, scale = normalize(x1[rows, :])
        normed[rows, :] = part
        inverse[rows, :] = scale
        h_ref[rows, :] = (part * gain).astype(BF16)

    wait_all(shrink)
    for j in range(3):
        cols = slice(384 * j, 384 * (j + 1))
        dm[:, cols] = dot_back(dy_ref[...], shrink_w[cols, :])
    wait_all(expand)
    for j in range(9):
        cols = slice(256 * j, 256 * (j + 1))
        z[:, cols] = dot(h_ref[...], expand_w[:, cols])

    @pl.loop(0, TOKENS // 16)
    def _(i):
        rows = pl.ds(pl.multiple_of(i * 16, 16), 16)
        gate = z[rows, pl.ds(0, FF)]
        up = z[rows, pl.ds(FF, FF)]
        upstream = dm[rows, :]
        below = 0.5 + 0.5 * lax.erf(gate * (0.5**0.5))
        slope = below + gate * (jnp.exp(-0.5 * gate * gate) * (2 * math.pi) ** -0.5)
        active = gate * below
        m_ref[rows, :] = (active * up).astype(BF16)
        dz[0, rows, :] = (upstream * up * slope).astype(BF16)
        dz[1, rows, :] = (upstream * active).astype(BF16)

    sends += copy_all((dz.at[core], dz.at[1 - core]), (dz_mine, dz_give), out_sems, 5)
    start_all(sends[1:3])
    start_all(sends[5:])
    for j in range(3):
        cols = slice(256 * j, 256 * (j + 1))
        out_ref[:, cols] = (x1[:, cols] + dot(m_ref[...], shrink_w[:, cols])).astype(BF16)
    start_all(sends[:1])
    for j in range(3):
        rows = slice(256 * j, 256 * (j + 1))
        x1[:, rows] = dot_back(dz[0], expand_w[rows, :FF]) + dot_back(dz[1], expand_w[rows, FF:])

    @pl.loop(0, TOKENS // step)
    def _(i):
        rows = pl.ds(pl.multiple_of(i * step, step), step)
        back = norm_back(x1[rows, :], normed[rows, :], inverse[rows, :], gain)
        total = dy_ref[rows, :].astype(F32) + back
        dx_ref[rows, :] = total
        dob[0, rows, :] = total[:, :384].astype(BF16)
        dob[1, rows, :] = total[:, 384:].astype(BF16)

    sends += copy_all((dob.at[core], dob.at[1 - core]), (dob_mine, dob_give), out_sems, 7)
    start_all(sends[7:])
    start_all(sends[3:4])
    for j in range(3):
        cols = slice(256 * j, 256 * (j + 1))
        datt_ref[:, cols] = (
            dot_back(dob[0], merge_w[cols, :384]) + dot_back(dob[1], merge_w[cols, 384:])
        ).astype(BF16)
    start_all(sends[4:5])
    wait_all(sends)


def middle(gains, x, att, dy, pieces):
    return call(
        middle_kernel,
        MIDDLE_OUTS + MIDDLE_HALVES,
        [pltpu.VMEM((TOKENS, D), BF16)] * 3
        + like(MIDDLE_OUTS)
        + [
            pltpu.VMEM((D, D), BF16),
            pltpu.VMEM((D, 2 * FF), BF16),
            pltpu.VMEM((FF, D), BF16),
            pltpu.VMEM((TOKENS, D), F32),
            pltpu.VMEM((TOKENS, D), F32),
            pltpu.VMEM((TOKENS, 1), F32),
            pltpu.VMEM((TOKENS, 2 * FF), F32),
            pltpu.VMEM((TOKENS, FF), F32),
            pltpu.VMEM((2, TOKENS, FF), BF16),
            pltpu.VMEM((2, TOKENS, D // 2), BF16),
            pltpu.SemaphoreType.DMA((3,)),
            pltpu.SemaphoreType.DMA((80,)),
            pltpu.SemaphoreType.DMA((9,)),
        ],
        "vhhh" + "a" * 16,
        60,
    )(gains, x, att, dy, *pieces)


def paired_copies(refs, buffers, sems):
    copies = []
    for n, buffer in enumerate(buffers):
        rows = buffer.shape[0] // 2
        for side in range(2):
            copies.append(
                pltpu.make_async_copy(
                    refs[2 * n + side], buffer.at[pl.ds(side * rows, rows), :], sems.at[2 * n + side]
                )
            )
    return copies


def early_kernel(*refs):
    ins, outs, refs = refs[:12], refs[12:16], refs[16:]
    h, dz, att, dob, m, dy, blocks, sems, out_sems = refs
    x, zh, _, seq = place()
    y = seq % 8 // 2
    copies = paired_copies(ins, (h, dz, att, dob, m, dy), sems)
    start_all(copies)
    wait_all(copies)
    grad = dot_outer(m[...], dy[...]).astype(BF16)
    blocks[0] = grad.reshape(OWNERS, FF_ROWS, 384)
    for part in range(3):
        cols = slice(384 * part, 384 * (part + 1))
        grad = dot_outer(h[...], dz[:, cols]).astype(BF16).reshape(OWNERS, ROWS, 384)
        if part == 0:
            blocks[1, :, :ROWS] = grad
        elif part == 1:
            blocks[1, :, ROWS:] = grad[:, :48]
            blocks[2, :, :48] = grad[:, 48:]
        else:
            blocks[2, :, 48:] = grad
    grad = dot_outer(att[...], dob[...]).astype(BF16)
    blocks[3, :, :ROWS] = grad.reshape(OWNERS, ROWS, 384)
    blocks[3, :, ROWS:] = jnp.zeros((OWNERS, 48, 384), BF16)
    sends = [
        pltpu.make_async_copy(
            blocks.at[(y + dy) % 4, owner(x, zh, dx, dz)],
            outs[dy].at[dx * 2 + dz],
            out_sems.at[dy * 8 + dx * 2 + dz],
        )
        for dy in range(4)
        for dx in range(4)
        for dz in range(2)
    ]
    start_all(sends)
    wait_all(sends)


def early_grads(*args):
    return call(
        early_kernel,
        [((OWNERS, FF_ROWS, 384), BF16)] * 4,
        [
            pltpu.VMEM((2 * TOKENS, D), BF16),
            pltpu.VMEM((2 * TOKENS, FF), BF16),
            pltpu.VMEM((2 * TOKENS, D), BF16),
            pltpu.VMEM((2 * TOKENS, D // 2), BF16),
            pltpu.VMEM((2 * TOKENS, FF), BF16),
            pltpu.VMEM((2 * TOKENS, D // 2), BF16),
            pltpu.VMEM((4, OWNERS, FF_ROWS, 384), BF16),
            pltpu.SemaphoreType.DMA((12,)),
            pltpu.SemaphoreType.DMA((32,)),
        ],
        "ha" * 6,
        60,
    )(*args)


def attention_back_kernel(cos_ref, sin_ref, *refs):
    ins, probs_in, mine_ref, give_ref, scratch = refs[:4], refs[4], refs[5], refs[6], refs[7:]
    q_ref, k_ref, v_ref, datt_ref, probs_ref, dk, dv, dj, in_sems, sems = scratch
    loads = copy_all(ins, scratch[:4], in_sems)
    start_all(loads)

    def load_probs(pair):
        tiles = pl.ds(pair * TILES, TILES)
        return pltpu.make_async_copy(probs_in.at[tiles], probs_ref.at[tiles], in_sems.at[4 + pair])

    for pair in range(PAIRS):
        load_probs(pair).start()
    core = lax.axis_index("seq") % 2
    lane = lax.broadcasted_iota(jnp.int32, (TILE, 128), 1)
    own = slice(RIM, RIM + TOKENS)
    dk[...] = jnp.zeros_like(dk)
    dv[...] = jnp.zeros_like(dv)
    dj[0, :RIM, :D] = jnp.zeros((RIM, D), BF16)
    dj[0, RIM + TOKENS :, :D] = jnp.zeros((RIM, D), BF16)
    wait_all(loads)
    scale = HEAD_DIM**-0.5

    @pl.loop(0, PAIRS)
    def _(pair):
        lanes = pl.ds(pl.multiple_of(pair * 128, 128), 128)
        load_probs(pair).wait()
        for t in range(TILES):
            rows = slice(t * TILE, (t + 1) * TILE)
            window = slice(t * TILE, (t + 2) * TILE)
            query = q_ref[rows, lanes].astype(F32) * scale
            query = jnp.concatenate(
                [jnp.where(lane < HEAD_DIM, query, 0.0), jnp.where(lane < HEAD_DIM, 0.0, query)], 0
            ).astype(BF16)
            upstream = datt_ref[rows, lanes].astype(F32)
            upstream = jnp.concatenate(
                [
                    jnp.where(lane < HEAD_DIM, upstream, 0.0),
                    jnp.where(lane < HEAD_DIM, 0.0, upstream),
                ],
                0,
            ).astype(BF16)
            probs_b = probs_ref[pair * TILES + t]
            probs = probs_b.astype(F32)
            dp = dot_back(upstream, v_ref[window, lanes])
            delta = jnp.sum(probs * dp, axis=-1, keepdims=True)
            ds = (probs * (dp - delta)).astype(BF16)
            dv[window, lanes] += dot_outer(probs_b, upstream)
            dk[window, lanes] += dot_outer(ds, query)
            dq = dot(ds, k_ref[window, lanes]) * scale
            dq = jnp.where(lane < HEAD_DIM, dq[:TILE], dq[TILE:])
            at = slice(RIM + t * TILE, RIM + (t + 1) * TILE)
            dj[0, at, lanes] = rope(dq, cos_ref[at, :], -sin_ref[at, :]).astype(BF16)

    for j in range(6):
        cols = slice(128 * j, 128 * (j + 1))
        part = rope(dk[:, cols], cos_ref[...], -sin_ref[...]).astype(BF16)
        if j < 3:
            dj[0, :, D + 128 * j : D + 128 * (j + 1)] = part
        else:
            dj[1, :, 128 * (j - 3) : 128 * (j - 2)] = part
    dj[1, :, D // 2 :] = dv[...].astype(BF16)
    sends = [
        pltpu.make_async_copy(dj.at[core], mine_ref, sems.at[0]),
        pltpu.make_async_copy(dj.at[1 - core], give_ref, sems.at[1]),
    ]
    start_all(sends)
    wait_all(sends)


def attention_back(*args):
    return call(
        attention_back_kernel,
        [((WIDE, HALF), BF16)] * 2,
        [
            pltpu.VMEM((TOKENS, D), BF16),
            pltpu.VMEM((WIDE, D), BF16),
            pltpu.VMEM((WIDE, D), BF16),
            pltpu.VMEM((TOKENS, D), BF16),
            pltpu.VMEM((PAIRS * TILES, 2 * TILE, 2 * TILE), BF16),
            pltpu.VMEM((WIDE, D), F32),
            pltpu.VMEM((WIDE, D), F32),
            pltpu.VMEM((2, WIDE, HALF), BF16),
            pltpu.SemaphoreType.DMA((10,)),
            pltpu.SemaphoreType.DMA((2,)),
        ],
        "vvhhhhh",
        60,
    )(*args)


def late_kernel(*refs):
    ins, outs, refs = refs[:4], refs[4:8], refs[8:]
    h, dj, blocks, sems, out_sems = refs
    x, zh, _, _ = place()
    copies = paired_copies(ins, (h, dj), sems)
    start_all(copies)
    wait_all(copies)
    for part in range(3):
        grad = dot_outer(h[...], dj[:, 384 * part : 384 * (part + 1)]).astype(BF16)
        blocks[:, ROWS * part : ROWS * (part + 1), :] = grad.reshape(OWNERS, ROWS, 384)
    blocks[:, 3 * ROWS :, :] = jnp.zeros((OWNERS, LATE_ROWS - 3 * ROWS, 384), BF16)
    sends = [
        pltpu.make_async_copy(blocks.at[owner(x, zh, dx, dz)], outs[dx].at[dz], out_sems.at[dx * 2 + dz])
        for dx in range(4)
        for dz in range(2)
    ]
    start_all(sends)
    wait_all(sends)


def late_grads(*args):
    return call(
        late_kernel,
        [((2, LATE_ROWS, 384), BF16)] * 4,
        [
            pltpu.VMEM((2 * WIDE, D), BF16),
            pltpu.VMEM((2 * WIDE, HALF), BF16),
            pltpu.VMEM((OWNERS, LATE_ROWS, 384), BF16),
            pltpu.SemaphoreType.DMA((4,)),
            pltpu.SemaphoreType.DMA((8,)),
        ],
        "haha",
        60,
    )(*args)


def sum_of(parts, index):
    return sum(part[index].astype(F32) for part in parts)


def early_sum_kernel(*refs):
    ins, outs, parts, total, sems, out_sems = refs[:4], refs[4:8], refs[8:12], *refs[12:]
    copies = copy_all(ins, parts, sems)
    start_all(copies)
    wait_all(copies)
    sends = [
        pltpu.make_async_copy(total.at[pl.ds(2 * d, 2)], outs[d], out_sems.at[d]) for d in range(4)
    ]
    for d in (1, 3, 2, 0):
        for i in (2 * d, 2 * d + 1):
            total[i] = sum_of(parts, i).astype(BF16)
        sends[d].start()
    wait_all(sends)


def late_sum_kernel(*refs):
    ins, outs, parts, total, sems, out_sems = refs[:4], refs[4:8], refs[8:12], *refs[12:]
    _, _, _, seq = place()
    y = seq % 8 // 2
    copies = copy_all(ins, parts, sems)
    start_all(copies)
    wait_all(copies)
    for i in range(2):
        total[i] = sum_of(parts, i).astype(BF16)
    sends = [
        pltpu.make_async_copy(
            total.at[:, pl.ds(pl.multiple_of((y + d) % 4 * LATE_QUARTER, 16), LATE_QUARTER), :],
            outs[d],
            out_sems.at[d],
        )
        for d in range(4)
    ]
    start_all(sends)
    wait_all(sends)


def both_sum_kernel(*refs):
    ins, outs, parts, keep, give, sems, out_sems = refs[:8], refs[8:10], refs[10:18], *refs[18:]
    copies = copy_all(ins, parts, sems)
    start_all(copies)
    wait_all(copies)
    keep[:FF_ROWS] = sum_of(parts[:4], 0).astype(BF16)
    keep[FF_ROWS:] = sum_of(parts[4:], 0).astype(BF16)
    give[:FF_ROWS] = sum_of(parts[:4], 1).astype(BF16)
    give[FF_ROWS:] = sum_of(parts[4:], 1).astype(BF16)
    sends = copy_all((keep, give), outs, out_sems)
    start_all(sends)
    wait_all(sends)


def summed(kernel, parts, outs, scratch):
    return call(
        kernel,
        outs,
        [pltpu.VMEM(part.shape, part.dtype) for part in parts]
        + scratch
        + [pltpu.SemaphoreType.DMA((len(parts),)), pltpu.SemaphoreType.DMA((len(outs),))],
        "a" * len(parts),
        60,
    )(*parts)


def early_sum(parts):
    shape = (OWNERS, FF_ROWS, 384)
    outs = [((2, FF_ROWS, 384), BF16)] * 4
    return summed(early_sum_kernel, parts, outs, [pltpu.VMEM(shape, BF16)])


def late_sum(parts):
    shape = (2, LATE_ROWS, 384)
    outs = [((2, LATE_QUARTER, 384), BF16)] * 4
    return summed(late_sum_kernel, parts, outs, [pltpu.VMEM(shape, BF16)])


def both_sum(parts):
    outs = [((FF_ROWS + LATE_QUARTER, 384), BF16)] * 2
    return summed(both_sum_kernel, parts, outs, like(outs))


INPUT_OUTS = [((TOKENS, D), F32), ((RIM, D), BF16), ((RIM, D), BF16)]


def input_kernel(inverse_ref, gain_ref, *refs):
    (normed, dx, weight, mine, give), outs, refs = refs[:5], refs[5:8], refs[8:]
    base_ref, low_ref, high_ref, joint_w, dj, upstream, normed_ref, dx_ref, sems, out_sems = refs
    core = lax.axis_index("seq") % 2
    copies = [
        pltpu.make_async_copy(weight, joint_w, sems.at[0]),
        pltpu.make_async_copy(mine, dj.at[core], sems.at[1]),
        pltpu.make_async_copy(give, dj.at[1 - core], sems.at[2]),
        pltpu.make_async_copy(normed, normed_ref, sems.at[3]),
        pltpu.make_async_copy(dx, dx_ref, sems.at[4]),
    ]
    start_all(copies)
    wait_all(copies)
    for j in range(3):
        cols = slice(256 * j, 256 * (j + 1))
        upstream[:, cols] = dot_back(dj[0], joint_w[cols, :HALF]) + dot_back(
            dj[1], joint_w[cols, HALF:]
        )
    gain = jnp.concatenate([gain_chunk(gain_ref, 0, j) for j in range(6)], 1)
    step = 32

    def back(rows):
        return norm_back(upstream[rows, :], normed_ref[rows, :], inverse_ref[rows, :], gain)

    @pl.loop(0, TOKENS // step)
    def _(i):
        start = pl.multiple_of(i * step, step)
        base_ref[pl.ds(start, step), :] = dx_ref[pl.ds(start, step), :] + back(
            pl.ds(start + RIM, step)
        )

    @pl.loop(0, RIM // step)
    def _(i):
        start = pl.multiple_of(i * step, step)
        low_ref[pl.ds(start, step), :] = back(pl.ds(start, step)).astype(BF16)
        high_ref[pl.ds(start, step), :] = back(pl.ds(start + RIM + TOKENS, step)).astype(BF16)

    sends = copy_all(refs[:3], outs, out_sems)
    start_all(sends)
    wait_all(sends)


def input_back(*args):
    return call(
        input_kernel,
        INPUT_OUTS,
        like(INPUT_OUTS)
        + [
            pltpu.VMEM((D, 3 * D), BF16),
            pltpu.VMEM((2, WIDE, HALF), BF16),
            pltpu.VMEM((WIDE, D), F32),
            pltpu.VMEM((WIDE, D), F32),
            pltpu.VMEM((TOKENS, D), F32),
            pltpu.SemaphoreType.DMA((5,)),
            pltpu.SemaphoreType.DMA((3,)),
        ],
        "vvahhhh",
        60,
    )(*args)


RESULTS = [((ROWS, 3 * D), F32), ((ROWS, D), F32), ((ROWS, 2 * FF), F32), ((FF_ROWS, D), F32)]
GAIN_RESULTS = [((1, ROWS), F32)] * 2


def result_kernel(first_gain, second_gain, *refs):
    sums, weights, outs, refs = refs[:2], refs[2:4], refs[4:10], refs[10:]
    joint, merge, expand, shrink, first, second, early, late, joint_w, expand_w, sems = refs
    _, _, core, seq = place()
    y = seq % 8 // 2
    copies = copy_all(weights, (joint_w, expand_w), sems)
    for side in range(2):
        half = (core + side) % 2
        for dy in range(4):
            quarter = (y + dy) % 4
            rows = pl.ds(pl.multiple_of(quarter * LATE_QUARTER, 16), LATE_QUARTER)
            copies += copy_all(
                (
                    sums[side].at[dy, pl.ds(0, FF_ROWS)],
                    sums[side].at[dy, pl.ds(FF_ROWS, LATE_QUARTER)],
                ),
                (early.at[half, quarter], late.at[half, rows]),
                sems,
                2 + (side * 4 + dy) * 2,
            )
    start_all(copies)
    wait_all(copies)
    for half in range(2):
        cols = slice(384 * half, 384 * (half + 1))
        shrink[:, cols] = early[half, 0].astype(F32)
        merge[:, cols] = early[half, 3, :ROWS].astype(F32)
        at = FF * half
        expand[:, at : at + 384] = early[half, 1, :ROWS].astype(F32)
        expand[:48, at + 384 : at + 768] = early[half, 1, ROWS:].astype(F32)
        expand[48:, at + 384 : at + 768] = early[half, 2, :48].astype(F32)
        expand[:, at + 768 : at + FF] = early[half, 2, 48:].astype(F32)
        for part in range(3):
            cols = slice(FF * half + 384 * part, FF * half + 384 * (part + 1))
            joint[:, cols] = late[half, ROWS * part : ROWS * (part + 1)].astype(F32)
    sends = copy_all((joint, merge, expand, shrink, first, second), outs, sems, 18)
    start_all(sends[:4])
    for total, weight, grad, gain in (
        (first, joint_w, joint, first_gain),
        (second, expand_w, expand, second_gain),
    ):
        product = sum(
            weight[:, 128 * j : 128 * (j + 1)].astype(F32) * grad[:, 128 * j : 128 * (j + 1)]
            for j in range(3 * D // 128)
        )
        total[...] = jnp.sum(product.T, axis=0, keepdims=True) / gain[...]
    start_all(sends[4:])
    wait_all(sends)


def results(*args):
    return call(
        result_kernel,
        RESULTS + GAIN_RESULTS,
        like(RESULTS + GAIN_RESULTS)
        + [
            pltpu.VMEM((2, 4, FF_ROWS, 384), BF16),
            pltpu.VMEM((2, LATE_ROWS, 384), BF16),
            pltpu.VMEM((ROWS, 3 * D), BF16),
            pltpu.VMEM((ROWS, 2 * FF), BF16),
            pltpu.SemaphoreType.DMA((24,)),
        ],
        "vvaahh",
        60,
    )(*args)


def stack_kernel(*refs):
    *ins, out, sems = refs
    copies = [pltpu.make_async_copy(r, out.at[i], sems.at[i]) for i, r in enumerate(ins)]
    start_all(copies)
    wait_all(copies)


def stack(*parts):
    return call(
        stack_kernel,
        [((len(parts),) + parts[0].shape, parts[0].dtype)],
        [pltpu.SemaphoreType.DMA((len(parts),))],
        "a" * len(parts),
        2,
    )(*parts)[0]


def gather_first(own):
    from_low, from_high = over_fsdp(own, 1, 0), over_fsdp(own, -1, 0)
    across = over_fsdp(own, 0, 1)
    return from_high, over_fsdp(own, 2, 0), from_low, across


def gather_second(own, from_high, from_far, from_low, across):
    across_low, across_high = over_fsdp(across, 1, 0), over_fsdp(across, -1, 0)
    across_far = over_fsdp(from_far, 0, 1)
    return [own, across, from_high, across_high, from_far, across_far, from_low, across_low]


def around(blocks, shift):
    return [blocks[0]] + [shift(blocks[d % 4], d) for d in (1, -1, 2)]


def over_x(value, d):
    return over_fsdp(value, d, 0)


def over_y(value, d):
    return over_seq(value, 0, d, 0)


def gather_quarters(own):
    from_low, from_high, from_far = (over_y(own, d) for d in (1, -1, 2))
    return [own, from_high, from_far, from_low]


def shards(
    inputs,
    first_gain,
    joint_weight,
    merge_weight,
    second_gain,
    expand_weight,
    shrink_weight,
    cotangent,
):
    x, zh, core, seq = place()
    fsdp = lax.axis_index("fsdp")
    source, upstream = inputs[0], cotangent[0]

    def columns(w, start, width):
        return lax.dynamic_slice_in_dim(w, start, width, 1)

    def placed_gain(gain):
        whole = lax.dynamic_update_slice_in_dim(jnp.zeros((D,), BF16), gain, fsdp * ROWS, 0)
        return jnp.pad(whole.reshape(6, 128), ((0, 2), (0, 0)))

    gain_tile = jnp.concatenate(
        [placed_gain(first_gain), placed_gain(second_gain), jnp.zeros((ROWS - 16, 128), BF16)], 0
    )
    joint_own = jnp.concatenate([columns(joint_weight, core * HALF, HALF), gain_tile], 1)
    joint_mine = gather_second(joint_own, *gather_first(joint_own))
    packed_own = jnp.concatenate(
        [columns(merge_weight, core * 384, 384)]
        + [columns(expand_weight, core * FF + 384 * i, 384) for i in range(3)]
        + [columns(shrink_weight, core * 384, 384)],
        0,
    )
    source_halo, _, _ = lax.optimization_barrier((source, joint_mine[2], joint_mine[6]))
    low_halo = passed_along(source_halo[TOKENS - RIM :], 1)
    high_halo = passed_along(source_halo[:RIM], -1)
    packed_own, _, _ = lax.optimization_barrier((packed_own, joint_mine[3], joint_mine[7]))
    packed_first = gather_first(packed_own)

    frequencies = jnp.exp(
        jnp.arange(HEAD_DIM // 2, dtype=F32) * (-2.0 * math.log(10000.0) / HEAD_DIM)
    )
    positions = (seq * TOKENS - RIM + lax.iota(jnp.int32, WIDE)).astype(F32)
    angles = positions[:, None] * frequencies[None, :]
    cosine, sine = jnp.cos(angles), jnp.sin(angles)
    cosine = jnp.concatenate([cosine] * 4, 1)
    sine = jnp.concatenate([-sine, sine] * 2, 1)
    extended = jnp.concatenate([low_halo, source, high_halo], 0).astype(F32)
    normed, inverse = normalize(extended)

    *joint_mine, normed, cosine, sine = lax.optimization_barrier((*joint_mine, normed, cosine, sine))
    joint_pieces = joint_mine + [core_swap(p) for p in joint_mine]
    q, k, v, h_first, attended, probs, gains, joint_w = joint_forward(
        normed, cosine, sine, joint_pieces
    )
    *packed_first, attended = lax.optimization_barrier((*packed_first, attended))
    packed_mine = gather_second(packed_own, *packed_first)
    packed_pieces = packed_mine + [core_swap(p) for p in packed_mine]
    dy_mine = columns(upstream, core * 384, 384)
    dy_got = core_swap(columns(upstream, (1 - core) * 384, 384))
    result, hidden, h_second, dx, datt, dz_mine, dz_give, dob_mine, dob_give = middle(
        gains, source, attended, upstream, packed_pieces
    )
    dj_mine, dj_give = attention_back(cosine, sine, q, k, v, datt, probs)
    swaps = [core_swap(part) for part in (hidden, h_second, dz_give, attended, dob_give, h_first)]
    *swaps, dj_mine, dj_give = lax.optimization_barrier((*swaps, dj_mine, dj_give))
    early = early_grads(
        h_second,
        swaps[1],
        dz_mine,
        swaps[2],
        attended,
        swaps[3],
        dob_mine,
        swaps[4],
        hidden,
        swaps[0],
        dy_mine,
        dy_got,
    )
    early_parts = around(early, over_y)
    dj_got, dj_mine, _ = lax.optimization_barrier((core_swap(dj_give), dj_mine, early[0]))
    late = late_grads(h_first, swaps[5], dj_mine, dj_got)
    late_own, dj_mine = lax.optimization_barrier((late[0], dj_mine))
    late_parts = around([late_own, *late[1:]], over_x)
    base, low_back, high_back = input_back(inverse, gains, normed, dx, joint_w, dj_mine, dj_give)
    *early_parts, base = lax.optimization_barrier((*early_parts, base))
    from_high = passed_along(low_back, -1).astype(F32)
    from_low = passed_along(high_back, 1).astype(F32)
    input_grad = (
        base
        + jnp.pad(from_high, ((TOKENS - RIM, 0), (0, 0)))
        + jnp.pad(from_low, ((0, TOKENS - RIM), (0, 0)))
    ).astype(BF16)

    *late_parts, input_grad = lax.optimization_barrier((*late_parts, input_grad))
    late_quarters = around(late_sum(late_parts), over_y)
    keep, give = both_sum(around(early_sum(early_parts), over_x) + late_quarters)
    keeps = keep.astype(F32) + over_seq(keep, 1, 0, 0).astype(F32)
    gives = over_fsdp(give, 0, 1).astype(F32) + over_both_z(give).astype(F32)
    own = stack(*gather_quarters((keeps + gives).astype(BF16)))
    joint_grad, merge_grad, expand_grad, shrink_grad, first_grad, second_grad = results(
        first_gain.astype(F32)[None],
        second_gain.astype(F32)[None],
        own,
        core_swap(own),
        joint_weight,
        expand_weight,
    )
    return (
        result[None],
        input_grad[None],
        first_grad[0],
        joint_grad,
        merge_grad,
        second_grad[0],
        expand_grad,
        shrink_grad,
    )


def solution(mesh):
    placed = (
        P("fsdp", "seq", None),
        P("fsdp"),
        P("fsdp", None),
        P("fsdp", None),
        P("fsdp"),
        P("fsdp", None),
        P("fsdp", None),
        P("fsdp", "seq", None),
    )
    return jax.shard_map(
        shards,
        mesh=mesh,
        in_specs=placed,
        out_specs=(
            P("fsdp", "seq", None),
            P("fsdp", "seq", None),
            P("fsdp"),
            P("fsdp", None),
            P("fsdp", None),
            P("fsdp"),
            P("fsdp", None),
            P("fsdp", None),
        ),
        check_vma=False,
    )
```

```python
import math

import jax
import jax.numpy as jnp
from jax import lax
from jax.experimental import pallas as pl
from jax.experimental.pallas import tpu as pltpu
from jax.sharding import PartitionSpec as P

D = 768
HEADS = 12
HEAD_DIM = 64
FF = 1152
RIM = 64
TOKENS = 384
WIDE = TOKENS + 2 * RIM
TILE = 128
TILES = TOKENS // TILE
PAIRS = HEADS // 2
OWNERS = 8
ROWS = D // OWNERS
FF_ROWS = FF // OWNERS
HALF = 3 * D // 2
LATE_ROWS = 320
LATE_QUARTER = LATE_ROWS // 4
PACKED = 4 * ROWS + FF_ROWS
EPSILON = 1e-05
F32 = jnp.float32
BF16 = jnp.bfloat16
MIB = 2**20


def over_fsdp(value, dx, dz):
    pairs = [
        (x * 2 + z, ((x + dx) % 4) * 2 + (z + dz) % 2) for x in range(4) for z in range(2)
    ]
    return lax.ppermute(value, "fsdp", pairs)


def over_seq(value, dz, dy, dc):
    pairs = [
        (z * 8 + y * 2 + c, ((z + dz) % 2) * 8 + ((y + dy) % 4) * 2 + (c + dc) % 2)
        for z in range(2)
        for y in range(4)
        for c in range(2)
    ]
    return lax.ppermute(value, "seq", pairs)


def over_x_pair(value, flip):
    pairs = [(x * 2 + z, (x ^ flip) * 2 + z) for x in range(4) for z in range(2)]
    return lax.ppermute(value, "fsdp", pairs)


def over_y_pair(value, flip):
    return lax.ppermute(value, "seq", [(s, s ^ (2 * flip)) for s in range(16)])


def over_both_z(value):
    pairs = [
        (f * 16 + s, (f ^ 1) * 16 + (s ^ 8)) for f in range(8) for s in range(16)
    ]
    return lax.ppermute(value, ("fsdp", "seq"), pairs)


def core_swap(value):
    return over_seq(value, 0, 0, 1)


def passed_along(value, steps):
    first, last = (max(0, -steps), min(16, 16 - steps))
    return lax.ppermute(value, "seq", [(i, i + steps) for i in range(first, last)])


def place():
    fsdp, seq = lax.axis_index("fsdp"), lax.axis_index("seq")
    return fsdp // 2, fsdp % 2, seq % 2, seq


def owner(x, zh, dx, dz):
    return ((x + dx) % 4) * 2 + (zh + dz) % 2


def dot(left, right):
    return jnp.dot(left, right, preferred_element_type=F32)


def dot_back(left, right):
    return lax.dot_general(left, right, (((1,), (1,)), ((), ())), preferred_element_type=F32)


def dot_outer(left, right):
    return lax.dot_general(left, right, (((0,), (0,)), ((), ())), preferred_element_type=F32)


def row_mean(values):
    return jnp.sum(values, axis=-1, keepdims=True) * (1.0 / D)


def normalize(values):
    centred = values - row_mean(values)
    inverse = lax.rsqrt(row_mean(centred * centred) + EPSILON)
    return (centred * inverse, inverse)


def norm_back(upstream, normed, inverse, gain):
    scaled = upstream * gain
    centred = scaled - row_mean(scaled)
    return inverse * (centred - normed * row_mean(scaled * normed))


def rope(values, cosine, sine):
    lane = lax.broadcasted_iota(jnp.int32, values.shape, 1) % HEAD_DIM
    partner = jnp.where(
        lane < HEAD_DIM // 2,
        pltpu.roll(values, 128 - HEAD_DIM // 2, 1),
        pltpu.roll(values, HEAD_DIM // 2, 1),
    )
    return values * cosine + partner * sine


def call(kernel, outs, scratch, spaces, limit):
    kinds = {"v": pltpu.VMEM, "h": pltpu.HBM, "a": pl.ANY}
    return pl.pallas_call(
        kernel,
        out_shape=[jax.ShapeDtypeStruct(shape, kind) for shape, kind in outs],
        in_specs=[pl.BlockSpec(memory_space=kinds[c]) for c in spaces],
        out_specs=[pl.BlockSpec(memory_space=pltpu.HBM) for _ in outs],
        scratch_shapes=scratch,
        compiler_params=pltpu.CompilerParams(vmem_limit_bytes=limit * MIB),
    )


def like(outs):
    return [pltpu.VMEM(shape, kind) for shape, kind in outs]


def copy_all(sources, targets, sems, first=0):
    return [
        pltpu.make_async_copy(a, b, sems.at[first + i])
        for i, (a, b) in enumerate(zip(sources, targets, strict=True))
    ]


def start_all(copies):
    for copy in copies:
        copy.start()


def wait_all(copies):
    for copy in copies:
        copy.wait()


def piece_places(pieces):
    x, zh, core, _ = place()
    return [
        (
            side * 8 + dx * 2 + dz,
            pieces[side * 8 + dx * 2 + dz],
            owner(x, zh, dx, dz),
            (core + side) % 2,
        )
        for side in range(2)
        for dx in range(4)
        for dz in range(2)
    ]


def joint_copies(pieces, joint_w, sems):
    return [
        pltpu.make_async_copy(
            piece.at[:, pl.ds(0, HALF)],
            joint_w.at[
                pl.ds(pl.multiple_of(who * ROWS, 16), ROWS),
                pl.ds(pl.multiple_of(half * HALF, 128), HALF),
            ],
            sems.at[i],
        )
        for i, piece, who, half in piece_places(pieces)
    ]


def gain_chunk(gain_ref, row, j):
    return gain_ref[row + j : row + j + 1, :]


JOINT_OUTS = [
    ((TOKENS, D), BF16),
    ((WIDE, D), BF16),
    ((WIDE, D), BF16),
    ((WIDE, D), BF16),
    ((TOKENS, D), BF16),
    ((PAIRS * TILES, 2 * TILE, 2 * TILE), BF16),
    ((16, 128), F32),
    ((D, 3 * D), BF16),
]


def joint_kernel(normed_ref, cos_ref, sin_ref, *refs):
    pieces, outs, refs = refs[:16], refs[16:24], refs[24:]
    q_ref, k_ref, v_ref, h_ref, att_ref, probs_ref, gain_ref, joint_w, gains, sems, out_sems = refs
    copies = joint_copies(pieces, joint_w, sems)
    gain_copies = [
        pltpu.make_async_copy(
            pieces[i].at[pl.ds(0, 16), pl.ds(HALF, 128)], gains.at[i], sems.at[16 + i]
        )
        for i in range(8)
    ]
    start_all(gain_copies)
    start_all(copies)
    wait_all(gain_copies)
    gain_ref[...] = jnp.sum(gains[...].astype(F32), axis=0)
    for j in range(D // 128):
        cols = slice(128 * j, 128 * (j + 1))
        h_ref[:, cols] = (normed_ref[:, cols] * gain_chunk(gain_ref, 0, j)).astype(BF16)
    wait_all(copies)
    sends = copy_all(refs[:5] + refs[6:8], outs[:5] + outs[6:8], out_sems)
    start_all(sends[5:])
    own = slice(RIM, RIM + TOKENS)
    for j in range(9):
        cols = slice(256 * j, 256 * (j + 1))
        rows = own if j < 3 else slice(0, WIDE)
        got = dot(h_ref[rows, :], joint_w[:, cols])
        out = (q_ref, k_ref, v_ref)[j // 3]
        for a in range(2):
            part = got[:, 128 * a : 128 * (a + 1)]
            if j < 6:
                part = rope(part, cos_ref[rows, :], sin_ref[rows, :])
            at = 256 * (j % 3) + 128 * a
            out[:, at : at + 128] = part.astype(BF16)

    start_all(sends[:4])
    offset = lax.axis_index("seq") * TOKENS
    row = lax.broadcasted_iota(jnp.int32, (TILE, 2 * TILE), 0)
    col = lax.broadcasted_iota(jnp.int32, (TILE, 2 * TILE), 1)
    lane = lax.broadcasted_iota(jnp.int32, (TILE, 128), 1)
    band = (col >= row) & (col - row <= 2 * RIM)

    @pl.loop(0, PAIRS)
    def _(pair):
        lanes = pl.ds(pl.multiple_of(pair * 128, 128), 128)
        for t in range(TILES):
            key = col + (offset + t * TILE - RIM)
            allowed = band & (key >= 0) & (key < 16 * TOKENS)
            query = q_ref[t * TILE : (t + 1) * TILE, lanes].astype(F32) * (HEAD_DIM**-0.5)
            stacked = jnp.concatenate(
                [jnp.where(lane < HEAD_DIM, query, 0.0), jnp.where(lane < HEAD_DIM, 0.0, query)], 0
            ).astype(BF16)
            window = slice(t * TILE, (t + 2) * TILE)
            scores = dot_back(stacked, k_ref[window, lanes])
            scores = jnp.where(jnp.concatenate([allowed, allowed], 0), scores, -1e30)
            expo = jnp.exp(scores - jnp.max(scores, axis=-1, keepdims=True))
            probs = (expo / jnp.sum(expo, axis=-1, keepdims=True)).astype(BF16)
            probs_ref[pair * TILES + t] = probs
            mixed = dot(probs, v_ref[window, lanes])
            att_ref[t * TILE : (t + 1) * TILE, lanes] = jnp.where(
                lane < HEAD_DIM, mixed[:TILE], mixed[TILE:]
            ).astype(BF16)
        pltpu.make_async_copy(
            probs_ref.at[pl.ds(pair * TILES, TILES)],
            outs[5].at[pl.ds(pair * TILES, TILES)],
            out_sems.at[7 + pair],
        ).start()

    sends[4].start()
    wait_all(sends)
    for pair in range(PAIRS):
        tiles = pl.ds(pair * TILES, TILES)
        pltpu.make_async_copy(probs_ref.at[tiles], outs[5].at[tiles], out_sems.at[7 + pair]).wait()


def joint_forward(normed, cosine, sine, pieces):
    return call(
        joint_kernel,
        JOINT_OUTS,
        like(JOINT_OUTS)
        + [
            pltpu.VMEM((8, 16, 128), BF16),
            pltpu.SemaphoreType.DMA((24,)),
            pltpu.SemaphoreType.DMA((13,)),
        ],
        "vvv" + "a" * 16,
        60,
    )(normed, cosine, sine, *pieces)


def packed_copies(pieces, merge_w, expand_w, shrink_w, sems):
    merge, expand, shrink = [], [], []
    for i, piece, who, half in piece_places(pieces):
        rows = pl.ds(pl.multiple_of(who * ROWS, 16), ROWS)
        cols = pl.ds(pl.multiple_of(half * 384, 128), 384)
        merge.append(
            pltpu.make_async_copy(
                piece.at[pl.ds(0, ROWS), :], merge_w.at[rows, cols], sems.at[i * 5]
            )
        )
        for part in range(3):
            expand.append(
                pltpu.make_async_copy(
                    piece.at[pl.ds(ROWS * (part + 1), ROWS), :],
                    expand_w.at[rows, pl.ds(pl.multiple_of(half * FF + part * 384, 128), 384)],
                    sems.at[i * 5 + 1 + part],
                )
            )
        shrink.append(
            pltpu.make_async_copy(
                piece.at[pl.ds(4 * ROWS, FF_ROWS), :],
                shrink_w.at[pl.ds(pl.multiple_of(who * FF_ROWS, 16), FF_ROWS), cols],
                sems.at[i * 5 + 4],
            )
        )
    return merge, expand, shrink


MIDDLE_OUTS = [
    ((TOKENS, D), BF16),
    ((TOKENS, FF), BF16),
    ((TOKENS, D), BF16),
    ((TOKENS, D), F32),
    ((TOKENS, D), BF16),
]
MIDDLE_HALVES = [((TOKENS, FF), BF16)] * 2 + [((TOKENS, D // 2), BF16)] * 2


def middle_kernel(gain_ref, *refs):
    ins, pieces, refs = refs[:3], refs[3:19], refs[19:]
    outs, halves, refs = refs[:5], refs[5:9], refs[9:]
    x_ref, att_ref, dy_ref, out_ref, m_ref, h_ref, dx_ref, datt_ref = refs[:8]
    merge_w, expand_w, shrink_w, x1, normed, inverse, z, dm, dz, dob = refs[8:18]
    in_sems, weight_sems, out_sems = refs[18:]
    dz_mine, dz_give, dob_mine, dob_give = halves
    core = lax.axis_index("seq") % 2
    loads = copy_all(ins, (x_ref, att_ref, dy_ref), in_sems)
    merge, expand, shrink = packed_copies(pieces, merge_w, expand_w, shrink_w, weight_sems)
    start_all(loads)
    start_all(merge)
    start_all(shrink)
    start_all(expand)
    sends = copy_all(refs[3:8], outs, out_sems)
    wait_all(merge)
    wait_all(loads)
    for j in range(3):
        cols = slice(256 * j, 256 * (j + 1))
        x1[:, cols] = x_ref[:, cols].astype(F32) + dot(att_ref[...], merge_w[:, cols])

    step = 32
    gain = jnp.concatenate([gain_chunk(gain_ref, 8, j) for j in range(6)], 1)

    @pl.loop(0, TOKENS // step)
    def _(i):
        rows = pl.ds(pl.multiple_of(i * step, step), step)
        part, scale = normalize(x1[rows, :])
        normed[rows, :] = part
        inverse[rows, :] = scale
        h_ref[rows, :] = (part * gain).astype(BF16)

    wait_all(shrink)
    for j in range(3):
        cols = slice(384 * j, 384 * (j + 1))
        dm[:, cols] = dot_back(dy_ref[...], shrink_w[cols, :])
    wait_all(expand)
    for j in range(9):
        cols = slice(256 * j, 256 * (j + 1))
        z[:, cols] = dot(h_ref[...], expand_w[:, cols])

    @pl.loop(0, TOKENS // 16)
    def _(i):
        rows = pl.ds(pl.multiple_of(i * 16, 16), 16)
        gate = z[rows, pl.ds(0, FF)]
        up = z[rows, pl.ds(FF, FF)]
        upstream = dm[rows, :]
        below = 0.5 + 0.5 * lax.erf(gate * (0.5**0.5))
        slope = below + gate * (jnp.exp(-0.5 * gate * gate) * (2 * math.pi) ** -0.5)
        active = gate * below
        m_ref[rows, :] = (active * up).astype(BF16)
        dz[0, rows, :] = (upstream * up * slope).astype(BF16)
        dz[1, rows, :] = (upstream * active).astype(BF16)

    sends += copy_all((dz.at[core], dz.at[1 - core]), (dz_mine, dz_give), out_sems, 5)
    start_all(sends[1:3])
    start_all(sends[5:])
    for j in range(3):
        cols = slice(256 * j, 256 * (j + 1))
        out_ref[:, cols] = (x1[:, cols] + dot(m_ref[...], shrink_w[:, cols])).astype(BF16)
    start_all(sends[:1])
    for j in range(3):
        rows = slice(256 * j, 256 * (j + 1))
        x1[:, rows] = dot_back(dz[0], expand_w[rows, :FF]) + dot_back(dz[1], expand_w[rows, FF:])

    @pl.loop(0, TOKENS // step)
    def _(i):
        rows = pl.ds(pl.multiple_of(i * step, step), step)
        back = norm_back(x1[rows, :], normed[rows, :], inverse[rows, :], gain)
        total = dy_ref[rows, :].astype(F32) + back
        dx_ref[rows, :] = total
        dob[0, rows, :] = total[:, :384].astype(BF16)
        dob[1, rows, :] = total[:, 384:].astype(BF16)

    sends += copy_all((dob.at[core], dob.at[1 - core]), (dob_mine, dob_give), out_sems, 7)
    start_all(sends[7:])
    start_all(sends[3:4])
    for j in range(3):
        cols = slice(256 * j, 256 * (j + 1))
        datt_ref[:, cols] = (
            dot_back(dob[0], merge_w[cols, :384]) + dot_back(dob[1], merge_w[cols, 384:])
        ).astype(BF16)
    start_all(sends[4:5])
    wait_all(sends)


def middle(gains, x, att, dy, pieces):
    return call(
        middle_kernel,
        MIDDLE_OUTS + MIDDLE_HALVES,
        [pltpu.VMEM((TOKENS, D), BF16)] * 3
        + like(MIDDLE_OUTS)
        + [
            pltpu.VMEM((D, D), BF16),
            pltpu.VMEM((D, 2 * FF), BF16),
            pltpu.VMEM((FF, D), BF16),
            pltpu.VMEM((TOKENS, D), F32),
            pltpu.VMEM((TOKENS, D), F32),
            pltpu.VMEM((TOKENS, 1), F32),
            pltpu.VMEM((TOKENS, 2 * FF), F32),
            pltpu.VMEM((TOKENS, FF), F32),
            pltpu.VMEM((2, TOKENS, FF), BF16),
            pltpu.VMEM((2, TOKENS, D // 2), BF16),
            pltpu.SemaphoreType.DMA((3,)),
            pltpu.SemaphoreType.DMA((80,)),
            pltpu.SemaphoreType.DMA((9,)),
        ],
        "vhhh" + "a" * 16,
        60,
    )(gains, x, att, dy, *pieces)


def paired_copies(refs, buffers, sems):
    copies = []
    for n, buffer in enumerate(buffers):
        rows = buffer.shape[0] // 2
        for side in range(2):
            copies.append(
                pltpu.make_async_copy(
                    refs[2 * n + side], buffer.at[pl.ds(side * rows, rows), :], sems.at[2 * n + side]
                )
            )
    return copies


def pair_order(i):
    near, ring, far = i + 1 - 2 * (i % 2), 3 - i, (i + 2) % 4
    return [[(i, ring), (near, far)], [(i, near), (ring, far)]]


def early_kernel(*refs):
    ins, outs, refs = refs[:12], refs[12:16], refs[16:]
    h, dz, att, dob, m, dy, blocks, sems, out_sems = refs
    x, zh, _, seq = place()
    y = seq % 8 // 2
    copies = paired_copies(ins, (h, dz, att, dob, m, dy), sems)
    start_all(copies)
    wait_all(copies)
    grad = dot_outer(m[...], dy[...]).astype(BF16)
    blocks[0] = grad.reshape(OWNERS, FF_ROWS, 384)
    for part in range(3):
        cols = slice(384 * part, 384 * (part + 1))
        grad = dot_outer(h[...], dz[:, cols]).astype(BF16).reshape(OWNERS, ROWS, 384)
        if part == 0:
            blocks[1, :, :ROWS] = grad
        elif part == 1:
            blocks[1, :, ROWS:] = grad[:, :48]
            blocks[2, :, :48] = grad[:, 48:]
        else:
            blocks[2, :, 48:] = grad
    grad = dot_outer(att[...], dob[...]).astype(BF16)
    blocks[3, :, :ROWS] = grad.reshape(OWNERS, ROWS, 384)
    blocks[3, :, ROWS:] = jnp.zeros((OWNERS, 48, 384), BF16)
    sends = [
        pltpu.make_async_copy(
            blocks.at[quarter, owner(x, zh, color * 2 + dx, dz)],
            outs[color * 2 + side].at[n, dx * 2 + dz],
            out_sems.at[((color * 2 + side) * 2 + n) * 4 + dx * 2 + dz],
        )
        for color in range(2)
        for side in range(2)
        for n, quarter in enumerate(pair_order(y)[color][side])
        for dx in range(2)
        for dz in range(2)
    ]
    start_all(sends)
    wait_all(sends)


def early_grads(*args):
    return call(
        early_kernel,
        [((2, OWNERS // 2, FF_ROWS, 384), BF16)] * 4,
        [
            pltpu.VMEM((2 * TOKENS, D), BF16),
            pltpu.VMEM((2 * TOKENS, FF), BF16),
            pltpu.VMEM((2 * TOKENS, D), BF16),
            pltpu.VMEM((2 * TOKENS, D // 2), BF16),
            pltpu.VMEM((2 * TOKENS, FF), BF16),
            pltpu.VMEM((2 * TOKENS, D // 2), BF16),
            pltpu.VMEM((4, OWNERS, FF_ROWS, 384), BF16),
            pltpu.SemaphoreType.DMA((12,)),
            pltpu.SemaphoreType.DMA((32,)),
        ],
        "ha" * 6,
        60,
    )(*args)


def attention_back_kernel(cos_ref, sin_ref, *refs):
    ins, probs_in, mine_ref, give_ref, scratch = refs[:4], refs[4], refs[5], refs[6], refs[7:]
    q_ref, k_ref, v_ref, datt_ref, probs_ref, dk, dv, dj, in_sems, sems = scratch
    loads = copy_all(ins, scratch[:4], in_sems)
    start_all(loads)

    def load_probs(pair):
        tiles = pl.ds(pair * TILES, TILES)
        return pltpu.make_async_copy(probs_in.at[tiles], probs_ref.at[tiles], in_sems.at[4 + pair])

    for pair in range(PAIRS):
        load_probs(pair).start()
    core = lax.axis_index("seq") % 2
    lane = lax.broadcasted_iota(jnp.int32, (TILE, 128), 1)
    own = slice(RIM, RIM + TOKENS)
    dk[...] = jnp.zeros_like(dk)
    dv[...] = jnp.zeros_like(dv)
    dj[0, :RIM, :D] = jnp.zeros((RIM, D), BF16)
    dj[0, RIM + TOKENS :, :D] = jnp.zeros((RIM, D), BF16)
    wait_all(loads)
    scale = HEAD_DIM**-0.5

    @pl.loop(0, PAIRS)
    def _(pair):
        lanes = pl.ds(pl.multiple_of(pair * 128, 128), 128)
        load_probs(pair).wait()
        for t in range(TILES):
            rows = slice(t * TILE, (t + 1) * TILE)
            window = slice(t * TILE, (t + 2) * TILE)
            query = q_ref[rows, lanes].astype(F32) * scale
            query = jnp.concatenate(
                [jnp.where(lane < HEAD_DIM, query, 0.0), jnp.where(lane < HEAD_DIM, 0.0, query)], 0
            ).astype(BF16)
            upstream = datt_ref[rows, lanes].astype(F32)
            upstream = jnp.concatenate(
                [
                    jnp.where(lane < HEAD_DIM, upstream, 0.0),
                    jnp.where(lane < HEAD_DIM, 0.0, upstream),
                ],
                0,
            ).astype(BF16)
            probs_b = probs_ref[pair * TILES + t]
            probs = probs_b.astype(F32)
            dp = dot_back(upstream, v_ref[window, lanes])
            delta = jnp.sum(probs * dp, axis=-1, keepdims=True)
            ds = (probs * (dp - delta)).astype(BF16)
            dv[window, lanes] += dot_outer(probs_b, upstream)
            dk[window, lanes] += dot_outer(ds, query)
            dq = dot(ds, k_ref[window, lanes]) * scale
            dq = jnp.where(lane < HEAD_DIM, dq[:TILE], dq[TILE:])
            at = slice(RIM + t * TILE, RIM + (t + 1) * TILE)
            dj[0, at, lanes] = rope(dq, cos_ref[at, :], -sin_ref[at, :]).astype(BF16)

    for j in range(6):
        cols = slice(128 * j, 128 * (j + 1))
        part = rope(dk[:, cols], cos_ref[...], -sin_ref[...]).astype(BF16)
        if j < 3:
            dj[0, :, D + 128 * j : D + 128 * (j + 1)] = part
        else:
            dj[1, :, 128 * (j - 3) : 128 * (j - 2)] = part
    dj[1, :, D // 2 :] = dv[...].astype(BF16)
    sends = [
        pltpu.make_async_copy(dj.at[core], mine_ref, sems.at[0]),
        pltpu.make_async_copy(dj.at[1 - core], give_ref, sems.at[1]),
    ]
    start_all(sends)
    wait_all(sends)


def attention_back(*args):
    return call(
        attention_back_kernel,
        [((WIDE, HALF), BF16)] * 2,
        [
            pltpu.VMEM((TOKENS, D), BF16),
            pltpu.VMEM((WIDE, D), BF16),
            pltpu.VMEM((WIDE, D), BF16),
            pltpu.VMEM((TOKENS, D), BF16),
            pltpu.VMEM((PAIRS * TILES, 2 * TILE, 2 * TILE), BF16),
            pltpu.VMEM((WIDE, D), F32),
            pltpu.VMEM((WIDE, D), F32),
            pltpu.VMEM((2, WIDE, HALF), BF16),
            pltpu.SemaphoreType.DMA((10,)),
            pltpu.SemaphoreType.DMA((2,)),
        ],
        "vvhhhhh",
        60,
    )(*args)


def late_kernel(*refs):
    ins, outs, refs = refs[:4], refs[4:8], refs[8:]
    h, dj, blocks, sems, out_sems = refs
    x, zh, _, _ = place()
    copies = paired_copies(ins, (h, dj), sems)
    start_all(copies)
    wait_all(copies)
    for part in range(3):
        grad = dot_outer(h[...], dj[:, 384 * part : 384 * (part + 1)]).astype(BF16)
        blocks[:, ROWS * part : ROWS * (part + 1), :] = grad.reshape(OWNERS, ROWS, 384)
    blocks[:, 3 * ROWS :, :] = jnp.zeros((OWNERS, LATE_ROWS - 3 * ROWS, 384), BF16)
    sends = [
        pltpu.make_async_copy(
            blocks.at[to * 2 + (zh + color) % 2],
            outs[color * 2 + side].at[n],
            out_sems.at[(color * 2 + side) * 2 + n],
        )
        for color in range(2)
        for side in range(2)
        for n, to in enumerate(pair_order(x)[color][side])
    ]
    start_all(sends)
    wait_all(sends)


def late_grads(*args):
    return call(
        late_kernel,
        [((2, LATE_ROWS, 384), BF16)] * 4,
        [
            pltpu.VMEM((2 * WIDE, D), BF16),
            pltpu.VMEM((2 * WIDE, HALF), BF16),
            pltpu.VMEM((OWNERS, LATE_ROWS, 384), BF16),
            pltpu.SemaphoreType.DMA((4,)),
            pltpu.SemaphoreType.DMA((8,)),
        ],
        "haha",
        60,
    )(*args)


def sum_of(parts, index):
    return sum(part[index].astype(F32) for part in parts)


def pair_sum_kernel(*refs):
    ins, outs, parts, totals, sems, out_sems = refs[:8], refs[8:16], refs[16:24], refs[24:32], *refs[32:]
    copies = copy_all(ins, parts, sems)
    start_all(copies)
    sends = copy_all(totals, outs, out_sems)
    for i in range(4):
        wait_all(copies[2 * i : 2 * i + 2])
        kept, came = parts[2 * i], parts[2 * i + 1]
        for n in (1, 0):
            total = totals[2 * i + n]
            if len(total.shape) == 3:
                for k in range(total.shape[0]):
                    total[k] = (kept[n, k].astype(F32) + came[n, k].astype(F32)).astype(BF16)
            else:
                total[...] = (kept[n].astype(F32) + came[n].astype(F32)).astype(BF16)
            sends[2 * i + n].start()
    wait_all(sends)


def early_sum_kernel(*refs):
    ins, outs, parts, total, sems, out_sems = refs[:4], refs[4:8], refs[8:12], *refs[12:]
    copies = copy_all(ins, parts, sems)
    start_all(copies)
    wait_all(copies)
    sends = [
        pltpu.make_async_copy(total.at[pl.ds(2 * d, 2)], outs[d], out_sems.at[d]) for d in range(4)
    ]
    for d in (1, 3, 2, 0):
        for i in (2 * d, 2 * d + 1):
            total[i] = sum_of(parts[i // 4 * 2 : i // 4 * 2 + 2], i % 4).astype(BF16)
        sends[d].start()
    wait_all(sends)


def late_sum_kernel(*refs):
    ins, outs, parts, total, sems, out_sems = refs[:4], refs[4:8], refs[8:12], *refs[12:]
    _, _, _, seq = place()
    y = seq % 8 // 2
    copies = copy_all(ins, parts, sems)
    start_all(copies)
    wait_all(copies)
    for i in range(2):
        total[i] = sum_of(parts[2 * i : 2 * i + 2], ...).astype(BF16)
    sends = [
        pltpu.make_async_copy(
            total.at[:, pl.ds(pl.multiple_of((y + d) % 4 * LATE_QUARTER, 16), LATE_QUARTER), :],
            outs[d],
            out_sems.at[d],
        )
        for d in range(4)
    ]
    start_all(sends)
    wait_all(sends)


def both_sum_kernel(*refs):
    ins, outs, parts, keep, give, sems, out_sems = refs[:8], refs[8:10], refs[10:18], *refs[18:]
    copies = copy_all(ins, parts, sems)
    start_all(copies)
    wait_all(copies)
    keep[:FF_ROWS] = sum_of(parts[:4], 0).astype(BF16)
    keep[FF_ROWS:] = sum_of(parts[4:], 0).astype(BF16)
    give[:FF_ROWS] = sum_of(parts[:4], 1).astype(BF16)
    give[FF_ROWS:] = sum_of(parts[4:], 1).astype(BF16)
    sends = copy_all((keep, give), outs, out_sems)
    start_all(sends)
    wait_all(sends)


def summed(kernel, parts, outs, scratch):
    return call(
        kernel,
        outs,
        [pltpu.VMEM(part.shape, part.dtype) for part in parts]
        + scratch
        + [pltpu.SemaphoreType.DMA((len(parts),)), pltpu.SemaphoreType.DMA((len(outs),))],
        "a" * len(parts),
        60,
    )(*parts)


def pair_sum(parts):
    outs = [(part.shape[1:], BF16) for part in parts]
    return summed(pair_sum_kernel, parts, outs, like(outs))


def early_sum(parts):
    shape = (OWNERS, FF_ROWS, 384)
    outs = [((2, FF_ROWS, 384), BF16)] * 4
    return summed(early_sum_kernel, parts, outs, [pltpu.VMEM(shape, BF16)])


def late_sum(parts):
    shape = (2, LATE_ROWS, 384)
    outs = [((2, LATE_QUARTER, 384), BF16)] * 4
    return summed(late_sum_kernel, parts, outs, [pltpu.VMEM(shape, BF16)])


def both_sum(parts):
    outs = [((FF_ROWS + LATE_QUARTER, 384), BF16)] * 2
    return summed(both_sum_kernel, parts, outs, like(outs))


INPUT_OUTS = [((TOKENS, D), F32), ((RIM, D), BF16), ((RIM, D), BF16)]


def input_kernel(inverse_ref, gain_ref, *refs):
    (normed, dx, weight, mine, give), outs, refs = refs[:5], refs[5:8], refs[8:]
    base_ref, low_ref, high_ref, joint_w, dj, upstream, normed_ref, dx_ref, sems, out_sems = refs
    core = lax.axis_index("seq") % 2
    copies = [
        pltpu.make_async_copy(weight, joint_w, sems.at[0]),
        pltpu.make_async_copy(mine, dj.at[core], sems.at[1]),
        pltpu.make_async_copy(give, dj.at[1 - core], sems.at[2]),
        pltpu.make_async_copy(normed, normed_ref, sems.at[3]),
        pltpu.make_async_copy(dx, dx_ref, sems.at[4]),
    ]
    start_all(copies)
    wait_all(copies)
    for j in range(3):
        cols = slice(256 * j, 256 * (j + 1))
        upstream[:, cols] = dot_back(dj[0], joint_w[cols, :HALF]) + dot_back(
            dj[1], joint_w[cols, HALF:]
        )
    gain = jnp.concatenate([gain_chunk(gain_ref, 0, j) for j in range(6)], 1)
    step = 32

    def back(rows):
        return norm_back(upstream[rows, :], normed_ref[rows, :], inverse_ref[rows, :], gain)

    @pl.loop(0, TOKENS // step)
    def _(i):
        start = pl.multiple_of(i * step, step)
        base_ref[pl.ds(start, step), :] = dx_ref[pl.ds(start, step), :] + back(
            pl.ds(start + RIM, step)
        )

    @pl.loop(0, RIM // step)
    def _(i):
        start = pl.multiple_of(i * step, step)
        low_ref[pl.ds(start, step), :] = back(pl.ds(start, step)).astype(BF16)
        high_ref[pl.ds(start, step), :] = back(pl.ds(start + RIM + TOKENS, step)).astype(BF16)

    sends = copy_all(refs[:3], outs, out_sems)
    start_all(sends)
    wait_all(sends)


def input_back(*args):
    return call(
        input_kernel,
        INPUT_OUTS,
        like(INPUT_OUTS)
        + [
            pltpu.VMEM((D, 3 * D), BF16),
            pltpu.VMEM((2, WIDE, HALF), BF16),
            pltpu.VMEM((WIDE, D), F32),
            pltpu.VMEM((WIDE, D), F32),
            pltpu.VMEM((TOKENS, D), F32),
            pltpu.SemaphoreType.DMA((5,)),
            pltpu.SemaphoreType.DMA((3,)),
        ],
        "vvahhhh",
        60,
    )(*args)


RESULTS = [((ROWS, 3 * D), F32), ((ROWS, D), F32), ((ROWS, 2 * FF), F32), ((FF_ROWS, D), F32)]
GAIN_RESULTS = [((1, ROWS), F32)] * 2


def result_kernel(first_gain, second_gain, *refs):
    sums, weights, outs, refs = refs[:2], refs[2:4], refs[4:10], refs[10:]
    joint, merge, expand, shrink, first, second, early, late, joint_w, expand_w, sems = refs
    _, _, core, seq = place()
    y = seq % 8 // 2
    copies = copy_all(weights, (joint_w, expand_w), sems)
    for side in range(2):
        half = (core + side) % 2
        for dy in range(4):
            quarter = (y + dy) % 4
            rows = pl.ds(pl.multiple_of(quarter * LATE_QUARTER, 16), LATE_QUARTER)
            copies += copy_all(
                (
                    sums[side].at[dy, pl.ds(0, FF_ROWS)],
                    sums[side].at[dy, pl.ds(FF_ROWS, LATE_QUARTER)],
                ),
                (early.at[half, quarter], late.at[half, rows]),
                sems,
                2 + (side * 4 + dy) * 2,
            )
    start_all(copies)
    wait_all(copies)
    for half in range(2):
        cols = slice(384 * half, 384 * (half + 1))
        shrink[:, cols] = early[half, 0].astype(F32)
        merge[:, cols] = early[half, 3, :ROWS].astype(F32)
        at = FF * half
        expand[:, at : at + 384] = early[half, 1, :ROWS].astype(F32)
        expand[:48, at + 384 : at + 768] = early[half, 1, ROWS:].astype(F32)
        expand[48:, at + 384 : at + 768] = early[half, 2, :48].astype(F32)
        expand[:, at + 768 : at + FF] = early[half, 2, 48:].astype(F32)
        for part in range(3):
            cols = slice(FF * half + 384 * part, FF * half + 384 * (part + 1))
            joint[:, cols] = late[half, ROWS * part : ROWS * (part + 1)].astype(F32)
    sends = copy_all((joint, merge, expand, shrink, first, second), outs, sems, 18)
    start_all(sends[:4])
    for total, weight, grad, gain in (
        (first, joint_w, joint, first_gain),
        (second, expand_w, expand, second_gain),
    ):
        product = sum(
            weight[:, 128 * j : 128 * (j + 1)].astype(F32) * grad[:, 128 * j : 128 * (j + 1)]
            for j in range(3 * D // 128)
        )
        total[...] = jnp.sum(product.T, axis=0, keepdims=True) / gain[...]
    start_all(sends[4:])
    wait_all(sends)


def results(*args):
    return call(
        result_kernel,
        RESULTS + GAIN_RESULTS,
        like(RESULTS + GAIN_RESULTS)
        + [
            pltpu.VMEM((2, 4, FF_ROWS, 384), BF16),
            pltpu.VMEM((2, LATE_ROWS, 384), BF16),
            pltpu.VMEM((ROWS, 3 * D), BF16),
            pltpu.VMEM((ROWS, 2 * FF), BF16),
            pltpu.SemaphoreType.DMA((24,)),
        ],
        "vvaahh",
        60,
    )(*args)


def stack_kernel(*refs):
    *ins, out, sems = refs
    copies = [pltpu.make_async_copy(r, out.at[i], sems.at[i]) for i, r in enumerate(ins)]
    start_all(copies)
    wait_all(copies)


def stack(*parts):
    return call(
        stack_kernel,
        [((len(parts),) + parts[0].shape, parts[0].dtype)],
        [pltpu.SemaphoreType.DMA((len(parts),))],
        "a" * len(parts),
        2,
    )(*parts)[0]


def gather_first(own):
    from_low, from_high = over_fsdp(own, 1, 0), over_fsdp(own, -1, 0)
    across = over_fsdp(own, 0, 1)
    return from_high, over_fsdp(own, 2, 0), from_low, across


def gather_second(own, from_high, from_far, from_low, across):
    across_low, across_high = over_fsdp(across, 1, 0), over_fsdp(across, -1, 0)
    across_far = over_fsdp(from_far, 0, 1)
    return [own, across, from_high, across_high, from_far, across_far, from_low, across_low]


def around(blocks, shift):
    return [blocks[0]] + [shift(blocks[d % 4], d) for d in (1, -1, 2)]


def over_x(value, d):
    return over_fsdp(value, d, 0)


def over_y(value, d):
    return over_seq(value, 0, d, 0)


def gather_quarters(own):
    from_low, from_high, from_far = (over_y(own, d) for d in (1, -1, 2))
    return [own, from_high, from_far, from_low]


def shards(
    inputs,
    first_gain,
    joint_weight,
    merge_weight,
    second_gain,
    expand_weight,
    shrink_weight,
    cotangent,
):
    x, zh, core, seq = place()
    fsdp = lax.axis_index("fsdp")
    source, upstream = inputs[0], cotangent[0]

    def columns(w, start, width):
        return lax.dynamic_slice_in_dim(w, start, width, 1)

    def placed_gain(gain):
        whole = lax.dynamic_update_slice_in_dim(jnp.zeros((D,), BF16), gain, fsdp * ROWS, 0)
        return jnp.pad(whole.reshape(6, 128), ((0, 2), (0, 0)))

    gain_tile = jnp.concatenate(
        [placed_gain(first_gain), placed_gain(second_gain), jnp.zeros((ROWS - 16, 128), BF16)], 0
    )
    joint_own = jnp.concatenate([columns(joint_weight, core * HALF, HALF), gain_tile], 1)
    joint_mine = gather_second(joint_own, *gather_first(joint_own))
    packed_own = jnp.concatenate(
        [columns(merge_weight, core * 384, 384)]
        + [columns(expand_weight, core * FF + 384 * i, 384) for i in range(3)]
        + [columns(shrink_weight, core * 384, 384)],
        0,
    )
    source_halo, _, _ = lax.optimization_barrier((source, joint_mine[2], joint_mine[6]))
    low_halo = passed_along(source_halo[TOKENS - RIM :], 1)
    high_halo = passed_along(source_halo[:RIM], -1)
    packed_own, _, _ = lax.optimization_barrier((packed_own, joint_mine[3], joint_mine[7]))
    packed_first = gather_first(packed_own)

    frequencies = jnp.exp(
        jnp.arange(HEAD_DIM // 2, dtype=F32) * (-2.0 * math.log(10000.0) / HEAD_DIM)
    )
    positions = (seq * TOKENS - RIM + lax.iota(jnp.int32, WIDE)).astype(F32)
    angles = positions[:, None] * frequencies[None, :]
    cosine, sine = jnp.cos(angles), jnp.sin(angles)
    cosine = jnp.concatenate([cosine] * 4, 1)
    sine = jnp.concatenate([-sine, sine] * 2, 1)
    extended = jnp.concatenate([low_halo, source, high_halo], 0).astype(F32)
    normed, inverse = normalize(extended)

    *joint_mine, normed, cosine, sine = lax.optimization_barrier((*joint_mine, normed, cosine, sine))
    joint_pieces = joint_mine + [core_swap(p) for p in joint_mine]
    q, k, v, h_first, attended, probs, gains, joint_w = joint_forward(
        normed, cosine, sine, joint_pieces
    )
    *packed_first, attended = lax.optimization_barrier((*packed_first, attended))
    packed_mine = gather_second(packed_own, *packed_first)
    packed_pieces = packed_mine + [core_swap(p) for p in packed_mine]
    dy_mine = columns(upstream, core * 384, 384)
    dy_got = core_swap(columns(upstream, (1 - core) * 384, 384))
    result, hidden, h_second, dx, datt, dz_mine, dz_give, dob_mine, dob_give = middle(
        gains, source, attended, upstream, packed_pieces
    )
    dj_mine, dj_give = attention_back(cosine, sine, q, k, v, datt, probs)
    swaps = [core_swap(part) for part in (hidden, h_second, dz_give, attended, dob_give, h_first)]
    *swaps, dj_mine, dj_give = lax.optimization_barrier((*swaps, dj_mine, dj_give))
    early = early_grads(
        h_second,
        swaps[1],
        dz_mine,
        swaps[2],
        attended,
        swaps[3],
        dob_mine,
        swaps[4],
        hidden,
        swaps[0],
        dy_mine,
        dy_got,
    )
    early_came = [over_y_pair(early[1], 1), over_y_pair(early[3], 3)]
    dj_got, dj_mine, _ = lax.optimization_barrier((core_swap(dj_give), dj_mine, early[0]))
    late = late_grads(h_first, swaps[5], dj_mine, dj_got)
    late_own, dj_mine = lax.optimization_barrier((late[0], dj_mine))
    late_came = [over_x_pair(late[1], 1), over_x_pair(late[3], 3)]
    base, low_back, high_back = input_back(inverse, gains, normed, dx, joint_w, dj_mine, dj_give)
    *came, base = lax.optimization_barrier((*early_came, *late_came, base))
    from_high = passed_along(low_back, -1).astype(F32)
    from_low = passed_along(high_back, 1).astype(F32)
    input_grad = (
        base
        + jnp.pad(from_high, ((TOKENS - RIM, 0), (0, 0)))
        + jnp.pad(from_low, ((0, TOKENS - RIM), (0, 0)))
    ).astype(BF16)

    early_a, early_a_give, early_b, early_b_give, late_a, late_a_give, late_b, late_b_give = pair_sum(
        [early[0], came[0], early[2], came[1], late_own, came[2], late[2], came[3]]
    )
    early_parts = [early_a, over_y_pair(early_a_give, 3), early_b, over_y_pair(early_b_give, 1)]
    late_parts = [late_a, over_x_pair(late_a_give, 3), late_b, over_x_pair(late_b_give, 1)]
    *late_parts, input_grad = lax.optimization_barrier((*late_parts, input_grad))
    late_quarters = around(late_sum(late_parts), over_y)
    keep, give = both_sum(around(early_sum(early_parts), over_x) + late_quarters)
    keeps = keep.astype(F32) + over_seq(keep, 1, 0, 0).astype(F32)
    gives = over_fsdp(give, 0, 1).astype(F32) + over_both_z(give).astype(F32)
    own = stack(*gather_quarters((keeps + gives).astype(BF16)))
    joint_grad, merge_grad, expand_grad, shrink_grad, first_grad, second_grad = results(
        first_gain.astype(F32)[None],
        second_gain.astype(F32)[None],
        own,
        core_swap(own),
        joint_weight,
        expand_weight,
    )
    return (
        result[None],
        input_grad[None],
        first_grad[0],
        joint_grad,
        merge_grad,
        second_grad[0],
        expand_grad,
        shrink_grad,
    )


def solution(mesh):
    placed = (
        P("fsdp", "seq", None),
        P("fsdp"),
        P("fsdp", None),
        P("fsdp", None),
        P("fsdp"),
        P("fsdp", None),
        P("fsdp", None),
        P("fsdp", "seq", None),
    )
    return jax.shard_map(
        shards,
        mesh=mesh,
        in_specs=placed,
        out_specs=(
            P("fsdp", "seq", None),
            P("fsdp", "seq", None),
            P("fsdp"),
            P("fsdp", None),
            P("fsdp", None),
            P("fsdp"),
            P("fsdp", None),
            P("fsdp", None),
        ),
        check_vma=False,
    )
```

```python
import math

import jax
import jax.numpy as jnp
from jax import lax
from jax.experimental import pallas as pl
from jax.experimental.pallas import tpu as pltpu
from jax.sharding import PartitionSpec as P

D = 768
HEADS = 12
HEAD_DIM = 64
FF = 1152
RIM = 64
TOKENS = 384
WIDE = TOKENS + 2 * RIM
TILE = 128
TILES = TOKENS // TILE
PAIRS = HEADS // 2
OWNERS = 8
ROWS = D // OWNERS
FF_ROWS = FF // OWNERS
HALF = 3 * D // 2
LATE_ROWS = 320
LATE_QUARTER = LATE_ROWS // 4
PACKED = 4 * ROWS + FF_ROWS
EPSILON = 1e-05
F32 = jnp.float32
BF16 = jnp.bfloat16
MIB = 2**20


def over_fsdp(value, dx, dz):
    pairs = [
        (x * 2 + z, ((x + dx) % 4) * 2 + (z + dz) % 2) for x in range(4) for z in range(2)
    ]
    return lax.ppermute(value, "fsdp", pairs)


def over_seq(value, dz, dy, dc):
    pairs = [
        (z * 8 + y * 2 + c, ((z + dz) % 2) * 8 + ((y + dy) % 4) * 2 + (c + dc) % 2)
        for z in range(2)
        for y in range(4)
        for c in range(2)
    ]
    return lax.ppermute(value, "seq", pairs)


def over_x_pair(value, flip):
    pairs = [(x * 2 + z, (x ^ flip) * 2 + z) for x in range(4) for z in range(2)]
    return lax.ppermute(value, "fsdp", pairs)


def over_y_pair(value, flip):
    return lax.ppermute(value, "seq", [(s, s ^ (2 * flip)) for s in range(16)])


def over_both_z(value):
    pairs = [
        (f * 16 + s, (f ^ 1) * 16 + (s ^ 8)) for f in range(8) for s in range(16)
    ]
    return lax.ppermute(value, ("fsdp", "seq"), pairs)


def core_swap(value):
    return over_seq(value, 0, 0, 1)


def passed_along(value, steps):
    first, last = (max(0, -steps), min(16, 16 - steps))
    return lax.ppermute(value, "seq", [(i, i + steps) for i in range(first, last)])


def place():
    fsdp, seq = lax.axis_index("fsdp"), lax.axis_index("seq")
    return fsdp // 2, fsdp % 2, seq % 2, seq


def owner(x, zh, dx, dz):
    return ((x + dx) % 4) * 2 + (zh + dz) % 2


def dot(left, right):
    return jnp.dot(left, right, preferred_element_type=F32)


def dot_back(left, right):
    return lax.dot_general(left, right, (((1,), (1,)), ((), ())), preferred_element_type=F32)


def dot_outer(left, right):
    return lax.dot_general(left, right, (((0,), (0,)), ((), ())), preferred_element_type=F32)


def row_mean(values):
    return jnp.sum(values, axis=-1, keepdims=True) * (1.0 / D)


def normalize(values):
    centred = values - row_mean(values)
    inverse = lax.rsqrt(row_mean(centred * centred) + EPSILON)
    return (centred * inverse, inverse)


def norm_back(upstream, normed, inverse, gain):
    scaled = upstream * gain
    centred = scaled - row_mean(scaled)
    return inverse * (centred - normed * row_mean(scaled * normed))


def rope(values, cosine, sine):
    lane = lax.broadcasted_iota(jnp.int32, values.shape, 1) % HEAD_DIM
    partner = jnp.where(
        lane < HEAD_DIM // 2,
        pltpu.roll(values, 128 - HEAD_DIM // 2, 1),
        pltpu.roll(values, HEAD_DIM // 2, 1),
    )
    return values * cosine + partner * sine


def call(kernel, outs, scratch, spaces, limit, place_outs="h"):
    kinds = {"v": pltpu.VMEM, "h": pltpu.HBM, "a": pl.ANY}
    return pl.pallas_call(
        kernel,
        out_shape=[jax.ShapeDtypeStruct(shape, kind) for shape, kind in outs],
        in_specs=[pl.BlockSpec(memory_space=kinds[c]) for c in spaces],
        out_specs=[pl.BlockSpec(memory_space=kinds[place_outs]) for _ in outs],
        scratch_shapes=scratch,
        compiler_params=pltpu.CompilerParams(vmem_limit_bytes=limit * MIB),
    )


def like(outs):
    return [pltpu.VMEM(shape, kind) for shape, kind in outs]


def copy_all(sources, targets, sems, first=0):
    return [
        pltpu.make_async_copy(a, b, sems.at[first + i])
        for i, (a, b) in enumerate(zip(sources, targets, strict=True))
    ]


def start_all(copies):
    for copy in copies:
        copy.start()


def wait_all(copies):
    for copy in copies:
        copy.wait()


def piece_places(pieces):
    x, zh, core, _ = place()
    return [
        (
            side * 8 + dx * 2 + dz,
            pieces[side * 8 + dx * 2 + dz],
            owner(x, zh, dx, dz),
            (core + side) % 2,
        )
        for side in range(2)
        for dx in range(4)
        for dz in range(2)
    ]


def joint_copies(pieces, joint_w, sems):
    return [
        pltpu.make_async_copy(
            piece.at[:, pl.ds(0, HALF)],
            joint_w.at[
                pl.ds(pl.multiple_of(who * ROWS, 16), ROWS),
                pl.ds(pl.multiple_of(half * HALF, 128), HALF),
            ],
            sems.at[i],
        )
        for i, piece, who, half in piece_places(pieces)
    ]


def gain_chunk(gain_ref, row, j):
    return gain_ref[row + j : row + j + 1, :]


JOINT_OUTS = [
    ((TOKENS, D), BF16),
    ((WIDE, D), BF16),
    ((WIDE, D), BF16),
    ((WIDE, D), BF16),
    ((TOKENS, D), BF16),
    ((PAIRS * TILES, 2 * TILE, 2 * TILE), BF16),
    ((16, 128), F32),
    ((D, 3 * D), BF16),
]


def joint_kernel(normed_ref, cos_ref, sin_ref, *refs):
    pieces, outs, refs = refs[:16], refs[16:24], refs[24:]
    q_ref, k_ref, v_ref, h_ref, att_ref, probs_ref, gain_ref, joint_w, gains, sems, out_sems = refs
    copies = joint_copies(pieces, joint_w, sems)
    gain_copies = [
        pltpu.make_async_copy(
            pieces[i].at[pl.ds(0, 16), pl.ds(HALF, 128)], gains.at[i], sems.at[16 + i]
        )
        for i in range(8)
    ]
    start_all(gain_copies)
    start_all(copies)
    wait_all(gain_copies)
    gain_ref[...] = jnp.sum(gains[...].astype(F32), axis=0)
    for j in range(D // 128):
        cols = slice(128 * j, 128 * (j + 1))
        h_ref[:, cols] = (normed_ref[:, cols] * gain_chunk(gain_ref, 0, j)).astype(BF16)
    wait_all(copies)
    sends = copy_all(refs[:5] + refs[6:8], outs[:5] + outs[6:8], out_sems)
    start_all(sends[5:])
    own = slice(RIM, RIM + TOKENS)
    for j in range(9):
        cols = slice(256 * j, 256 * (j + 1))
        rows = own if j < 3 else slice(0, WIDE)
        got = dot(h_ref[rows, :], joint_w[:, cols])
        out = (q_ref, k_ref, v_ref)[j // 3]
        for a in range(2):
            part = got[:, 128 * a : 128 * (a + 1)]
            if j < 6:
                part = rope(part, cos_ref[rows, :], sin_ref[rows, :])
            at = 256 * (j % 3) + 128 * a
            out[:, at : at + 128] = part.astype(BF16)

    start_all(sends[:4])
    offset = lax.axis_index("seq") * TOKENS
    row = lax.broadcasted_iota(jnp.int32, (TILE, 2 * TILE), 0)
    col = lax.broadcasted_iota(jnp.int32, (TILE, 2 * TILE), 1)
    lane = lax.broadcasted_iota(jnp.int32, (TILE, 128), 1)
    band = (col >= row) & (col - row <= 2 * RIM)

    @pl.loop(0, PAIRS)
    def _(pair):
        lanes = pl.ds(pl.multiple_of(pair * 128, 128), 128)
        for t in range(TILES):
            key = col + (offset + t * TILE - RIM)
            allowed = band & (key >= 0) & (key < 16 * TOKENS)
            query = q_ref[t * TILE : (t + 1) * TILE, lanes].astype(F32) * (HEAD_DIM**-0.5)
            stacked = jnp.concatenate(
                [jnp.where(lane < HEAD_DIM, query, 0.0), jnp.where(lane < HEAD_DIM, 0.0, query)], 0
            ).astype(BF16)
            window = slice(t * TILE, (t + 2) * TILE)
            scores = dot_back(stacked, k_ref[window, lanes])
            scores = jnp.where(jnp.concatenate([allowed, allowed], 0), scores, -1e30)
            expo = jnp.exp(scores - jnp.max(scores, axis=-1, keepdims=True))
            probs = (expo / jnp.sum(expo, axis=-1, keepdims=True)).astype(BF16)
            probs_ref[pair * TILES + t] = probs
            mixed = dot(probs, v_ref[window, lanes])
            att_ref[t * TILE : (t + 1) * TILE, lanes] = jnp.where(
                lane < HEAD_DIM, mixed[:TILE], mixed[TILE:]
            ).astype(BF16)
        pltpu.make_async_copy(
            probs_ref.at[pl.ds(pair * TILES, TILES)],
            outs[5].at[pl.ds(pair * TILES, TILES)],
            out_sems.at[7 + pair],
        ).start()

    sends[4].start()
    wait_all(sends)
    for pair in range(PAIRS):
        tiles = pl.ds(pair * TILES, TILES)
        pltpu.make_async_copy(probs_ref.at[tiles], outs[5].at[tiles], out_sems.at[7 + pair]).wait()


def joint_forward(normed, cosine, sine, pieces):
    return call(
        joint_kernel,
        JOINT_OUTS,
        like(JOINT_OUTS)
        + [
            pltpu.VMEM((8, 16, 128), BF16),
            pltpu.SemaphoreType.DMA((24,)),
            pltpu.SemaphoreType.DMA((13,)),
        ],
        "vvv" + "a" * 16,
        60,
    )(normed, cosine, sine, *pieces)


def packed_copies(pieces, merge_w, expand_w, shrink_w, sems):
    merge, expand, shrink = [], [], []
    for i, piece, who, half in piece_places(pieces):
        rows = pl.ds(pl.multiple_of(who * ROWS, 16), ROWS)
        cols = pl.ds(pl.multiple_of(half * 384, 128), 384)
        merge.append(
            pltpu.make_async_copy(
                piece.at[pl.ds(0, ROWS), :], merge_w.at[rows, cols], sems.at[i * 5]
            )
        )
        for part in range(3):
            expand.append(
                pltpu.make_async_copy(
                    piece.at[pl.ds(ROWS * (part + 1), ROWS), :],
                    expand_w.at[rows, pl.ds(pl.multiple_of(half * FF + part * 384, 128), 384)],
                    sems.at[i * 5 + 1 + part],
                )
            )
        shrink.append(
            pltpu.make_async_copy(
                piece.at[pl.ds(4 * ROWS, FF_ROWS), :],
                shrink_w.at[pl.ds(pl.multiple_of(who * FF_ROWS, 16), FF_ROWS), cols],
                sems.at[i * 5 + 4],
            )
        )
    return merge, expand, shrink


MIDDLE_OUTS = [
    ((TOKENS, D), BF16),
    ((TOKENS, FF), BF16),
    ((TOKENS, D), BF16),
    ((TOKENS, D), F32),
    ((TOKENS, D), BF16),
]
MIDDLE_HALVES = [((TOKENS, FF), BF16)] * 2 + [((TOKENS, D // 2), BF16)] * 2


def middle_kernel(gain_ref, *refs):
    ins, pieces, refs = refs[:3], refs[3:19], refs[19:]
    outs, halves, refs = refs[:5], refs[5:9], refs[9:]
    x_ref, att_ref, dy_ref, out_ref, m_ref, h_ref, dx_ref, datt_ref = refs[:8]
    merge_w, expand_w, shrink_w, x1, normed, inverse, z, dm, dz, dob = refs[8:18]
    in_sems, weight_sems, out_sems = refs[18:]
    dz_mine, dz_give, dob_mine, dob_give = halves
    core = lax.axis_index("seq") % 2
    loads = copy_all(ins, (x_ref, att_ref, dy_ref), in_sems)
    merge, expand, shrink = packed_copies(pieces, merge_w, expand_w, shrink_w, weight_sems)
    start_all(loads)
    start_all(merge)
    start_all(shrink)
    start_all(expand)
    sends = copy_all(refs[3:8], outs, out_sems)
    wait_all(merge)
    wait_all(loads)
    for j in range(3):
        cols = slice(256 * j, 256 * (j + 1))
        x1[:, cols] = x_ref[:, cols].astype(F32) + dot(att_ref[...], merge_w[:, cols])

    step = 32
    gain = jnp.concatenate([gain_chunk(gain_ref, 8, j) for j in range(6)], 1)

    @pl.loop(0, TOKENS // step)
    def _(i):
        rows = pl.ds(pl.multiple_of(i * step, step), step)
        part, scale = normalize(x1[rows, :])
        normed[rows, :] = part
        inverse[rows, :] = scale
        h_ref[rows, :] = (part * gain).astype(BF16)

    wait_all(shrink)
    for j in range(3):
        cols = slice(384 * j, 384 * (j + 1))
        dm[:, cols] = dot_back(dy_ref[...], shrink_w[cols, :])
    wait_all(expand)
    for j in range(9):
        cols = slice(256 * j, 256 * (j + 1))
        z[:, cols] = dot(h_ref[...], expand_w[:, cols])

    @pl.loop(0, TOKENS // 16)
    def _(i):
        rows = pl.ds(pl.multiple_of(i * 16, 16), 16)
        gate = z[rows, pl.ds(0, FF)]
        up = z[rows, pl.ds(FF, FF)]
        upstream = dm[rows, :]
        below = 0.5 + 0.5 * lax.erf(gate * (0.5**0.5))
        slope = below + gate * (jnp.exp(-0.5 * gate * gate) * (2 * math.pi) ** -0.5)
        active = gate * below
        m_ref[rows, :] = (active * up).astype(BF16)
        dz[0, rows, :] = (upstream * up * slope).astype(BF16)
        dz[1, rows, :] = (upstream * active).astype(BF16)

    sends += copy_all((dz.at[core], dz.at[1 - core]), (dz_mine, dz_give), out_sems, 5)
    start_all(sends[1:3])
    start_all(sends[5:])
    for j in range(3):
        cols = slice(256 * j, 256 * (j + 1))
        out_ref[:, cols] = (x1[:, cols] + dot(m_ref[...], shrink_w[:, cols])).astype(BF16)
    start_all(sends[:1])
    for j in range(3):
        rows = slice(256 * j, 256 * (j + 1))
        x1[:, rows] = dot_back(dz[0], expand_w[rows, :FF]) + dot_back(dz[1], expand_w[rows, FF:])

    @pl.loop(0, TOKENS // step)
    def _(i):
        rows = pl.ds(pl.multiple_of(i * step, step), step)
        back = norm_back(x1[rows, :], normed[rows, :], inverse[rows, :], gain)
        total = dy_ref[rows, :].astype(F32) + back
        dx_ref[rows, :] = total
        dob[0, rows, :] = total[:, :384].astype(BF16)
        dob[1, rows, :] = total[:, 384:].astype(BF16)

    sends += copy_all((dob.at[core], dob.at[1 - core]), (dob_mine, dob_give), out_sems, 7)
    start_all(sends[7:])
    start_all(sends[3:4])
    for j in range(3):
        cols = slice(256 * j, 256 * (j + 1))
        datt_ref[:, cols] = (
            dot_back(dob[0], merge_w[cols, :384]) + dot_back(dob[1], merge_w[cols, 384:])
        ).astype(BF16)
    start_all(sends[4:5])
    wait_all(sends)


def middle(gains, x, att, dy, pieces):
    return call(
        middle_kernel,
        MIDDLE_OUTS + MIDDLE_HALVES,
        [pltpu.VMEM((TOKENS, D), BF16)] * 3
        + like(MIDDLE_OUTS)
        + [
            pltpu.VMEM((D, D), BF16),
            pltpu.VMEM((D, 2 * FF), BF16),
            pltpu.VMEM((FF, D), BF16),
            pltpu.VMEM((TOKENS, D), F32),
            pltpu.VMEM((TOKENS, D), F32),
            pltpu.VMEM((TOKENS, 1), F32),
            pltpu.VMEM((TOKENS, 2 * FF), F32),
            pltpu.VMEM((TOKENS, FF), F32),
            pltpu.VMEM((2, TOKENS, FF), BF16),
            pltpu.VMEM((2, TOKENS, D // 2), BF16),
            pltpu.SemaphoreType.DMA((3,)),
            pltpu.SemaphoreType.DMA((80,)),
            pltpu.SemaphoreType.DMA((9,)),
        ],
        "vhhh" + "a" * 16,
        60,
    )(gains, x, att, dy, *pieces)


def paired_copies(refs, buffers, sems):
    copies = []
    for n, buffer in enumerate(buffers):
        rows = buffer.shape[0] // 2
        for side in range(2):
            copies.append(
                pltpu.make_async_copy(
                    refs[2 * n + side], buffer.at[pl.ds(side * rows, rows), :], sems.at[2 * n + side]
                )
            )
    return copies


def pair_order(i):
    near, ring, far = i + 1 - 2 * (i % 2), 3 - i, (i + 2) % 4
    return [[(i, ring), (near, far)], [(i, near), (ring, far)]]


def early_kernel(*refs):
    ins, outs, refs = refs[:12], refs[12:16], refs[16:]
    h, dz, att, dob, m, dy, blocks, sems, out_sems = refs
    x, zh, _, seq = place()
    y = seq % 8 // 2
    copies = paired_copies(ins, (h, dz, att, dob, m, dy), sems)
    start_all(copies)
    wait_all(copies)
    grad = dot_outer(m[...], dy[...]).astype(BF16)
    blocks[0] = grad.reshape(OWNERS, FF_ROWS, 384)
    for part in range(3):
        cols = slice(384 * part, 384 * (part + 1))
        grad = dot_outer(h[...], dz[:, cols]).astype(BF16).reshape(OWNERS, ROWS, 384)
        if part == 0:
            blocks[1, :, :ROWS] = grad
        elif part == 1:
            blocks[1, :, ROWS:] = grad[:, :48]
            blocks[2, :, :48] = grad[:, 48:]
        else:
            blocks[2, :, 48:] = grad
    grad = dot_outer(att[...], dob[...]).astype(BF16)
    blocks[3, :, :ROWS] = grad.reshape(OWNERS, ROWS, 384)
    blocks[3, :, ROWS:] = jnp.zeros((OWNERS, 48, 384), BF16)
    sends = [
        pltpu.make_async_copy(
            blocks.at[quarter, owner(x, zh, color * 2 + dx, dz)],
            outs[color * 2 + side].at[n, dx * 2 + dz],
            out_sems.at[((color * 2 + side) * 2 + n) * 4 + dx * 2 + dz],
        )
        for color in range(2)
        for side in range(2)
        for n, quarter in enumerate(pair_order(y)[color][side])
        for dx in range(2)
        for dz in range(2)
    ]
    start_all(sends)
    wait_all(sends)


def early_grads(*args):
    return call(
        early_kernel,
        [((2, OWNERS // 2, FF_ROWS, 384), BF16)] * 4,
        [
            pltpu.VMEM((2 * TOKENS, D), BF16),
            pltpu.VMEM((2 * TOKENS, FF), BF16),
            pltpu.VMEM((2 * TOKENS, D), BF16),
            pltpu.VMEM((2 * TOKENS, D // 2), BF16),
            pltpu.VMEM((2 * TOKENS, FF), BF16),
            pltpu.VMEM((2 * TOKENS, D // 2), BF16),
            pltpu.VMEM((4, OWNERS, FF_ROWS, 384), BF16),
            pltpu.SemaphoreType.DMA((12,)),
            pltpu.SemaphoreType.DMA((32,)),
        ],
        "ha" * 6,
        60,
    )(*args)


def attention_back_kernel(cos_ref, sin_ref, *refs):
    ins, probs_in, mine_ref, give_ref, scratch = refs[:4], refs[4], refs[5], refs[6], refs[7:]
    q_ref, k_ref, v_ref, datt_ref, probs_ref, dk, dv, dj, in_sems, sems = scratch
    loads = copy_all(ins, scratch[:4], in_sems)
    start_all(loads)

    def load_probs(pair):
        tiles = pl.ds(pair * TILES, TILES)
        return pltpu.make_async_copy(probs_in.at[tiles], probs_ref.at[tiles], in_sems.at[4 + pair])

    for pair in range(PAIRS):
        load_probs(pair).start()
    core = lax.axis_index("seq") % 2
    lane = lax.broadcasted_iota(jnp.int32, (TILE, 128), 1)
    own = slice(RIM, RIM + TOKENS)
    dk[...] = jnp.zeros_like(dk)
    dv[...] = jnp.zeros_like(dv)
    dj[0, :RIM, :D] = jnp.zeros((RIM, D), BF16)
    dj[0, RIM + TOKENS :, :D] = jnp.zeros((RIM, D), BF16)
    wait_all(loads)
    scale = HEAD_DIM**-0.5

    @pl.loop(0, PAIRS)
    def _(pair):
        lanes = pl.ds(pl.multiple_of(pair * 128, 128), 128)
        load_probs(pair).wait()
        for t in range(TILES):
            rows = slice(t * TILE, (t + 1) * TILE)
            window = slice(t * TILE, (t + 2) * TILE)
            query = q_ref[rows, lanes].astype(F32) * scale
            query = jnp.concatenate(
                [jnp.where(lane < HEAD_DIM, query, 0.0), jnp.where(lane < HEAD_DIM, 0.0, query)], 0
            ).astype(BF16)
            upstream = datt_ref[rows, lanes].astype(F32)
            upstream = jnp.concatenate(
                [
                    jnp.where(lane < HEAD_DIM, upstream, 0.0),
                    jnp.where(lane < HEAD_DIM, 0.0, upstream),
                ],
                0,
            ).astype(BF16)
            probs_b = probs_ref[pair * TILES + t]
            probs = probs_b.astype(F32)
            dp = dot_back(upstream, v_ref[window, lanes])
            delta = jnp.sum(probs * dp, axis=-1, keepdims=True)
            ds = (probs * (dp - delta)).astype(BF16)
            dv[window, lanes] += dot_outer(probs_b, upstream)
            dk[window, lanes] += dot_outer(ds, query)
            dq = dot(ds, k_ref[window, lanes]) * scale
            dq = jnp.where(lane < HEAD_DIM, dq[:TILE], dq[TILE:])
            at = slice(RIM + t * TILE, RIM + (t + 1) * TILE)
            dj[0, at, lanes] = rope(dq, cos_ref[at, :], -sin_ref[at, :]).astype(BF16)

    for j in range(6):
        cols = slice(128 * j, 128 * (j + 1))
        part = rope(dk[:, cols], cos_ref[...], -sin_ref[...]).astype(BF16)
        if j < 3:
            dj[0, :, D + 128 * j : D + 128 * (j + 1)] = part
        else:
            dj[1, :, 128 * (j - 3) : 128 * (j - 2)] = part
    dj[1, :, D // 2 :] = dv[...].astype(BF16)
    sends = [
        pltpu.make_async_copy(dj.at[core], mine_ref, sems.at[0]),
        pltpu.make_async_copy(dj.at[1 - core], give_ref, sems.at[1]),
    ]
    start_all(sends)
    wait_all(sends)


def attention_back(*args):
    return call(
        attention_back_kernel,
        [((WIDE, HALF), BF16)] * 2,
        [
            pltpu.VMEM((TOKENS, D), BF16),
            pltpu.VMEM((WIDE, D), BF16),
            pltpu.VMEM((WIDE, D), BF16),
            pltpu.VMEM((TOKENS, D), BF16),
            pltpu.VMEM((PAIRS * TILES, 2 * TILE, 2 * TILE), BF16),
            pltpu.VMEM((WIDE, D), F32),
            pltpu.VMEM((WIDE, D), F32),
            pltpu.VMEM((2, WIDE, HALF), BF16),
            pltpu.SemaphoreType.DMA((10,)),
            pltpu.SemaphoreType.DMA((2,)),
        ],
        "vvhhhhh",
        60,
    )(*args)


def late_kernel(*refs):
    ins, outs, refs = refs[:4], refs[4:8], refs[8:]
    h, dj, blocks, sems, out_sems = refs
    x, zh, _, _ = place()
    copies = paired_copies(ins, (h, dj), sems)
    start_all(copies)
    wait_all(copies)
    for part in range(3):
        grad = dot_outer(h[...], dj[:, 384 * part : 384 * (part + 1)]).astype(BF16)
        blocks[:, ROWS * part : ROWS * (part + 1), :] = grad.reshape(OWNERS, ROWS, 384)
    blocks[:, 3 * ROWS :, :] = jnp.zeros((OWNERS, LATE_ROWS - 3 * ROWS, 384), BF16)
    sends = [
        pltpu.make_async_copy(
            blocks.at[to * 2 + (zh + color) % 2],
            outs[color * 2 + side].at[n],
            out_sems.at[(color * 2 + side) * 2 + n],
        )
        for color in range(2)
        for side in range(2)
        for n, to in enumerate(pair_order(x)[color][side])
    ]
    start_all(sends)
    wait_all(sends)


def late_grads(*args):
    return call(
        late_kernel,
        [((2, LATE_ROWS, 384), BF16)] * 4,
        [
            pltpu.VMEM((2 * WIDE, D), BF16),
            pltpu.VMEM((2 * WIDE, HALF), BF16),
            pltpu.VMEM((OWNERS, LATE_ROWS, 384), BF16),
            pltpu.SemaphoreType.DMA((4,)),
            pltpu.SemaphoreType.DMA((8,)),
        ],
        "haha",
        60,
    )(*args)


def sum_of(parts, index):
    return sum(part[index].astype(F32) for part in parts)


def pair_sum_kernel(*refs):
    ins, totals, parts, sems = refs[:8], refs[8:16], refs[16:24], refs[24]
    copies = copy_all(ins, parts, sems)
    start_all(copies)
    for i in range(4):
        wait_all(copies[2 * i : 2 * i + 2])
        kept, came = parts[2 * i], parts[2 * i + 1]
        for n in range(2):
            total = totals[2 * i + n]
            if len(total.shape) == 3:
                for k in range(total.shape[0]):
                    total[k] = (kept[n, k].astype(F32) + came[n, k].astype(F32)).astype(BF16)
            else:
                total[...] = (kept[n].astype(F32) + came[n].astype(F32)).astype(BF16)


def early_sum_kernel(*refs):
    parts, outs = refs[:4], refs[4:]
    for i in range(OWNERS):
        outs[i // 2][i % 2] = sum_of(parts[i // 4 * 2 : i // 4 * 2 + 2], i % 4).astype(BF16)


def late_sum_kernel(*refs):
    parts, outs = refs[:4], refs[4:]
    _, _, _, seq = place()
    y = seq % 8 // 2
    for d in range(4):
        rows = pl.ds(pl.multiple_of((y + d) % 4 * LATE_QUARTER, 16), LATE_QUARTER)
        for i in range(2):
            outs[d][i] = sum_of([part.at[rows] for part in parts[2 * i : 2 * i + 2]], ...).astype(BF16)


def both_sum_kernel(*refs):
    parts, outs = refs[:8], refs[8:]
    for i in range(2):
        outs[i][:FF_ROWS] = sum_of(parts[:4], i).astype(BF16)
        outs[i][FF_ROWS:] = sum_of(parts[4:], i).astype(BF16)


def pair_sum(parts):
    return call(
        pair_sum_kernel,
        [(part.shape[1:], BF16) for part in parts],
        [pltpu.VMEM(part.shape, part.dtype) for part in parts]
        + [pltpu.SemaphoreType.DMA((len(parts),))],
        "a" * len(parts),
        24,
        "v",
    )(*parts)


def summed(kernel, parts, shapes):
    outs = [(shape, BF16) for shape in shapes]
    return call(kernel, outs, [], "v" * len(parts), 12, "v")(*parts)


def early_sum(parts):
    return summed(early_sum_kernel, parts, [(2, FF_ROWS, 384)] * 4)


def late_sum(parts):
    return summed(late_sum_kernel, parts, [(2, LATE_QUARTER, 384)] * 4)


def both_sum(parts):
    return summed(both_sum_kernel, parts, [(FF_ROWS + LATE_QUARTER, 384)] * 2)


INPUT_OUTS = [((TOKENS, D), F32), ((RIM, D), BF16), ((RIM, D), BF16)]


def input_kernel(inverse_ref, gain_ref, *refs):
    (normed, dx, weight, mine, give), outs, refs = refs[:5], refs[5:8], refs[8:]
    base_ref, low_ref, high_ref, joint_w, dj, upstream, normed_ref, dx_ref, sems, out_sems = refs
    core = lax.axis_index("seq") % 2
    copies = [
        pltpu.make_async_copy(weight, joint_w, sems.at[0]),
        pltpu.make_async_copy(mine, dj.at[core], sems.at[1]),
        pltpu.make_async_copy(give, dj.at[1 - core], sems.at[2]),
        pltpu.make_async_copy(normed, normed_ref, sems.at[3]),
        pltpu.make_async_copy(dx, dx_ref, sems.at[4]),
    ]
    start_all(copies)
    wait_all(copies)
    for j in range(3):
        cols = slice(256 * j, 256 * (j + 1))
        upstream[:, cols] = dot_back(dj[0], joint_w[cols, :HALF]) + dot_back(
            dj[1], joint_w[cols, HALF:]
        )
    gain = jnp.concatenate([gain_chunk(gain_ref, 0, j) for j in range(6)], 1)
    step = 32

    def back(rows):
        return norm_back(upstream[rows, :], normed_ref[rows, :], inverse_ref[rows, :], gain)

    @pl.loop(0, TOKENS // step)
    def _(i):
        start = pl.multiple_of(i * step, step)
        base_ref[pl.ds(start, step), :] = dx_ref[pl.ds(start, step), :] + back(
            pl.ds(start + RIM, step)
        )

    @pl.loop(0, RIM // step)
    def _(i):
        start = pl.multiple_of(i * step, step)
        low_ref[pl.ds(start, step), :] = back(pl.ds(start, step)).astype(BF16)
        high_ref[pl.ds(start, step), :] = back(pl.ds(start + RIM + TOKENS, step)).astype(BF16)

    sends = copy_all(refs[:3], outs, out_sems)
    start_all(sends)
    wait_all(sends)


def input_back(*args):
    return call(
        input_kernel,
        INPUT_OUTS,
        like(INPUT_OUTS)
        + [
            pltpu.VMEM((D, 3 * D), BF16),
            pltpu.VMEM((2, WIDE, HALF), BF16),
            pltpu.VMEM((WIDE, D), F32),
            pltpu.VMEM((WIDE, D), F32),
            pltpu.VMEM((TOKENS, D), F32),
            pltpu.SemaphoreType.DMA((5,)),
            pltpu.SemaphoreType.DMA((3,)),
        ],
        "vvahhhh",
        60,
    )(*args)


RESULTS = [((ROWS, 3 * D), F32), ((ROWS, D), F32), ((ROWS, 2 * FF), F32), ((FF_ROWS, D), F32)]
GAIN_RESULTS = [((1, ROWS), F32)] * 2


def result_kernel(first_gain, second_gain, *refs):
    sums, weights, outs, refs = refs[:8], refs[8:10], refs[10:16], refs[16:]
    joint, merge, expand, shrink, first, second, early, late, sems = refs
    joint_w, expand_w = weights
    _, _, core, seq = place()
    y = seq % 8 // 2
    for side in range(2):
        half = (core + side) % 2
        for dy in range(4):
            quarter = (y + dy) % 4
            rows = pl.ds(pl.multiple_of(quarter * LATE_QUARTER, 16), LATE_QUARTER)
            early[half, quarter] = sums[side * 4 + dy][:FF_ROWS]
            late[half, rows] = sums[side * 4 + dy][FF_ROWS:]
    for half in range(2):
        cols = slice(384 * half, 384 * (half + 1))
        shrink[:, cols] = early[half, 0].astype(F32)
        merge[:, cols] = early[half, 3, :ROWS].astype(F32)
        at = FF * half
        expand[:, at : at + 384] = early[half, 1, :ROWS].astype(F32)
        expand[:48, at + 384 : at + 768] = early[half, 1, ROWS:].astype(F32)
        expand[48:, at + 384 : at + 768] = early[half, 2, :48].astype(F32)
        expand[:, at + 768 : at + FF] = early[half, 2, 48:].astype(F32)
        for part in range(3):
            cols = slice(FF * half + 384 * part, FF * half + 384 * (part + 1))
            joint[:, cols] = late[half, ROWS * part : ROWS * (part + 1)].astype(F32)
    sends = copy_all((joint, merge, expand, shrink, first, second), outs, sems)
    start_all(sends[:4])
    for total, weight, grad, gain in (
        (first, joint_w, joint, first_gain),
        (second, expand_w, expand, second_gain),
    ):
        product = sum(
            weight[:, 128 * j : 128 * (j + 1)].astype(F32) * grad[:, 128 * j : 128 * (j + 1)]
            for j in range(3 * D // 128)
        )
        total[...] = jnp.sum(product.T, axis=0, keepdims=True) / gain[...]
    start_all(sends[4:])
    wait_all(sends)


def results(*args):
    return call(
        result_kernel,
        RESULTS + GAIN_RESULTS,
        like(RESULTS + GAIN_RESULTS)
        + [
            pltpu.VMEM((2, 4, FF_ROWS, 384), BF16),
            pltpu.VMEM((2, LATE_ROWS, 384), BF16),
            pltpu.SemaphoreType.DMA((6,)),
        ],
        "v" * 12,
        60,
    )(*args)


def joint_part_kernel(gains, weight, out, tile, sems):
    fsdp = lax.axis_index("fsdp")
    _, _, core, _ = place()
    start = pl.multiple_of(core * HALF, 128)
    copies = [
        pltpu.make_async_copy(weight.at[:, pl.ds(start, HALF)], out.at[:, pl.ds(0, HALF)], sems.at[0]),
        pltpu.make_async_copy(tile, out.at[:, pl.ds(HALF, 128)], sems.at[1]),
    ]
    copies[0].start()
    placed = pltpu.roll(gains[...], fsdp * ROWS, 1)
    rows = []
    for i in range(2):
        rows += [placed[i : i + 1, 128 * j : 128 * (j + 1)] for j in range(6)]
        rows += [jnp.zeros((2, 128), F32)]
    tile[...] = jnp.concatenate([*rows, jnp.zeros((ROWS - 16, 128), F32)], 0).astype(BF16)
    copies[1].start()
    wait_all(copies)


def joint_part(gains, weight):
    return call(
        joint_part_kernel,
        [((ROWS, HALF + 128), BF16)],
        [pltpu.VMEM((ROWS, 128), BF16), pltpu.SemaphoreType.DMA((2,))],
        "vh",
        4,
    )(gains, weight)[0]


def other_parts_kernel(merge, expand, shrink, x, dy, *refs):
    packed, low, high, mine, give, sems = refs
    _, _, core, _ = place()
    half = pl.ds(pl.multiple_of(core * 384, 128), 384)
    rest = pl.ds(pl.multiple_of((1 - core) * 384, 128), 384)
    sources = [merge.at[:, half]]
    targets = [packed.at[pl.ds(0, ROWS)]]
    for i in range(3):
        sources.append(expand.at[:, pl.ds(pl.multiple_of(core * FF + 384 * i, 128), 384)])
        targets.append(packed.at[pl.ds(ROWS * (i + 1), ROWS)])
    sources += [shrink.at[:, half], x.at[pl.ds(TOKENS - RIM, RIM)], x.at[pl.ds(0, RIM)]]
    targets += [packed.at[pl.ds(4 * ROWS, FF_ROWS)], low, high]
    copies = copy_all(sources + [dy.at[:, half], dy.at[:, rest]], targets + [mine, give], sems)
    start_all(copies)
    wait_all(copies)


def other_parts(*args):
    return call(
        other_parts_kernel,
        [((PACKED, 384), BF16)] + [((RIM, D), BF16)] * 2 + [((TOKENS, D // 2), BF16)] * 2,
        [pltpu.SemaphoreType.DMA((9,))],
        "hhhhh",
        2,
    )(*args)


def gather_first(own):
    from_low, from_high = over_fsdp(own, 1, 0), over_fsdp(own, -1, 0)
    across = over_fsdp(own, 0, 1)
    return from_high, over_fsdp(own, 2, 0), from_low, across


def gather_second(own, from_high, from_far, from_low, across):
    across_low, across_high = over_fsdp(across, 1, 0), over_fsdp(across, -1, 0)
    across_far = over_fsdp(from_far, 0, 1)
    return [own, across, from_high, across_high, from_far, across_far, from_low, across_low]


def around(blocks, shift):
    return [blocks[0]] + [shift(blocks[d % 4], d) for d in (1, -1, 2)]


def over_x(value, d):
    return over_fsdp(value, d, 0)


def over_y(value, d):
    return over_seq(value, 0, d, 0)


def gather_quarters(own):
    from_low, from_high, from_far = (over_y(own, d) for d in (1, -1, 2))
    return [own, from_high, from_far, from_low]


def shards(
    inputs,
    first_gain,
    joint_weight,
    merge_weight,
    second_gain,
    expand_weight,
    shrink_weight,
    cotangent,
):
    x, zh, core, seq = place()
    fsdp = lax.axis_index("fsdp")
    source, upstream = inputs[0], cotangent[0]

    gains = jnp.pad(jnp.stack([first_gain, second_gain]), ((0, 6), (0, D - ROWS)))
    joint_own = joint_part(gains.astype(F32), joint_weight)
    packed_own, low_own, high_own, dy_mine, dy_give = other_parts(
        merge_weight, expand_weight, shrink_weight, source, upstream
    )
    joint_first = gather_first(joint_own)
    joint_mine = gather_second(joint_own, *joint_first)
    low_own, high_own, _ = lax.optimization_barrier((low_own, high_own, joint_first[3]))
    packed_own, _, _ = lax.optimization_barrier((packed_own, joint_mine[3], joint_mine[7]))
    low_halo = passed_along(low_own, 1)
    high_halo = passed_along(high_own, -1)
    packed_first = gather_first(packed_own)
    soon = [joint_mine[i] for i in (0, 1, 2, 4, 6)]
    *swapped, last = lax.optimization_barrier((*[core_swap(p) for p in soon], joint_mine[5]))
    joint_mine[5] = last

    frequencies = jnp.exp(
        jnp.arange(HEAD_DIM // 2, dtype=F32) * (-2.0 * math.log(10000.0) / HEAD_DIM)
    )
    positions = (seq * TOKENS - RIM + lax.iota(jnp.int32, WIDE)).astype(F32)
    angles = positions[:, None] * frequencies[None, :]
    cosine, sine = jnp.cos(angles), jnp.sin(angles)
    cosine = jnp.concatenate([cosine] * 4, 1)
    sine = jnp.concatenate([-sine, sine] * 2, 1)
    extended = jnp.concatenate([low_halo, source, high_halo], 0).astype(F32)
    normed, inverse = normalize(extended)

    *joint_mine, normed, cosine, sine = lax.optimization_barrier((*joint_mine, normed, cosine, sine))
    joint_swapped = [core_swap(joint_mine[i]) for i in (3, 5, 7)]
    joint_other = [swapped[0], swapped[1], swapped[2], joint_swapped[0], swapped[3]]
    joint_other += [joint_swapped[1], swapped[4], joint_swapped[2]]
    joint_pieces = joint_mine + joint_other
    q, k, v, h_first, attended, probs, gains, joint_w = joint_forward(
        normed, cosine, sine, joint_pieces
    )
    *packed_first, attended = lax.optimization_barrier((*packed_first, attended))
    packed_mine = gather_second(packed_own, *packed_first)
    packed_pieces = packed_mine + [core_swap(p) for p in packed_mine]
    dy_got = core_swap(dy_give)
    result, hidden, h_second, dx, datt, dz_mine, dz_give, dob_mine, dob_give = middle(
        gains, source, attended, upstream, packed_pieces
    )
    dj_mine, dj_give = attention_back(cosine, sine, q, k, v, datt, probs)
    swaps = [core_swap(part) for part in (hidden, h_second, dz_give, attended, dob_give, h_first)]
    *swaps, dj_mine, dj_give = lax.optimization_barrier((*swaps, dj_mine, dj_give))
    early = early_grads(
        h_second,
        swaps[1],
        dz_mine,
        swaps[2],
        attended,
        swaps[3],
        dob_mine,
        swaps[4],
        hidden,
        swaps[0],
        dy_mine,
        dy_got,
    )
    early_came = [over_y_pair(early[1], 1), over_y_pair(early[3], 3)]
    dj_got, dj_mine, _ = lax.optimization_barrier((core_swap(dj_give), dj_mine, early[0]))
    late = late_grads(h_first, swaps[5], dj_mine, dj_got)
    late_own, dj_mine = lax.optimization_barrier((late[0], dj_mine))
    late_came = [over_x_pair(late[1], 1), over_x_pair(late[3], 3)]
    base, low_back, high_back = input_back(inverse, gains, normed, dx, joint_w, dj_mine, dj_give)
    *came, base = lax.optimization_barrier((*early_came, *late_came, base))
    from_high = passed_along(low_back, -1).astype(F32)
    from_low = passed_along(high_back, 1).astype(F32)
    input_grad = (
        base
        + jnp.pad(from_high, ((TOKENS - RIM, 0), (0, 0)))
        + jnp.pad(from_low, ((0, TOKENS - RIM), (0, 0)))
    ).astype(BF16)

    early_a, early_a_give, early_b, early_b_give, late_a, late_a_give, late_b, late_b_give = pair_sum(
        [early[0], came[0], early[2], came[1], late_own, came[2], late[2], came[3]]
    )
    early_parts = [early_a, over_y_pair(early_a_give, 3), early_b, over_y_pair(early_b_give, 1)]
    late_parts = [late_a, over_x_pair(late_a_give, 3), late_b, over_x_pair(late_b_give, 1)]
    *late_parts, input_grad = lax.optimization_barrier((*late_parts, input_grad))
    late_quarters = around(late_sum(late_parts), over_y)
    keep, give = both_sum(around(early_sum(early_parts), over_x) + late_quarters)
    keeps = keep.astype(F32) + over_seq(keep, 1, 0, 0).astype(F32)
    gives = over_fsdp(give, 0, 1).astype(F32) + over_both_z(give).astype(F32)
    own = gather_quarters((keeps + gives).astype(BF16))
    joint_grad, merge_grad, expand_grad, shrink_grad, first_grad, second_grad = results(
        first_gain.astype(F32)[None],
        second_gain.astype(F32)[None],
        *own,
        *[core_swap(part) for part in own],
        joint_weight,
        expand_weight,
    )
    return (
        result[None],
        input_grad[None],
        first_grad[0],
        joint_grad,
        merge_grad,
        second_grad[0],
        expand_grad,
        shrink_grad,
    )


def solution(mesh):
    placed = (
        P("fsdp", "seq", None),
        P("fsdp"),
        P("fsdp", None),
        P("fsdp", None),
        P("fsdp"),
        P("fsdp", None),
        P("fsdp", None),
        P("fsdp", "seq", None),
    )
    return jax.shard_map(
        shards,
        mesh=mesh,
        in_specs=placed,
        out_specs=(
            P("fsdp", "seq", None),
            P("fsdp", "seq", None),
            P("fsdp"),
            P("fsdp", None),
            P("fsdp", None),
            P("fsdp"),
            P("fsdp", None),
            P("fsdp", None),
        ),
        check_vma=False,
    )
```

```python
import math

import jax
import jax.numpy as jnp
from jax import lax
from jax.experimental import pallas as pl
from jax.experimental.pallas import tpu as pltpu
from jax.sharding import PartitionSpec as P

D = 768
HEADS = 12
HEAD_DIM = 64
FF = 1152
RIM = 64
TOKENS = 384
WIDE = TOKENS + 2 * RIM
TILE = 128
TILES = TOKENS // TILE
PAIRS = HEADS // 2
OWNERS = 8
ROWS = D // OWNERS
FF_ROWS = FF // OWNERS
HALF = 3 * D // 2
LATE_ROWS = 320
LATE_QUARTER = LATE_ROWS // 4
PACKED = 4 * ROWS + FF_ROWS
EPSILON = 1e-05
F32 = jnp.float32
BF16 = jnp.bfloat16
MIB = 2**20


def over_fsdp(value, dx, dz):
    pairs = [
        (x * 2 + z, ((x + dx) % 4) * 2 + (z + dz) % 2) for x in range(4) for z in range(2)
    ]
    return lax.ppermute(value, "fsdp", pairs)


def over_seq(value, dz, dy, dc):
    pairs = [
        (z * 8 + y * 2 + c, ((z + dz) % 2) * 8 + ((y + dy) % 4) * 2 + (c + dc) % 2)
        for z in range(2)
        for y in range(4)
        for c in range(2)
    ]
    return lax.ppermute(value, "seq", pairs)


def over_x_pair(value, flip):
    pairs = [(x * 2 + z, (x ^ flip) * 2 + z) for x in range(4) for z in range(2)]
    return lax.ppermute(value, "fsdp", pairs)


def over_y_pair(value, flip):
    return lax.ppermute(value, "seq", [(s, s ^ (2 * flip)) for s in range(16)])


def over_both_z(value):
    pairs = [
        (f * 16 + s, (f ^ 1) * 16 + (s ^ 8)) for f in range(8) for s in range(16)
    ]
    return lax.ppermute(value, ("fsdp", "seq"), pairs)


def core_swap(value):
    return over_seq(value, 0, 0, 1)


def passed_along(value, steps):
    first, last = (max(0, -steps), min(16, 16 - steps))
    return lax.ppermute(value, "seq", [(i, i + steps) for i in range(first, last)])


def place():
    fsdp, seq = lax.axis_index("fsdp"), lax.axis_index("seq")
    return fsdp // 2, fsdp % 2, seq % 2, seq


def owner(x, zh, dx, dz):
    return ((x + dx) % 4) * 2 + (zh + dz) % 2


def dot(left, right):
    return jnp.dot(left, right, preferred_element_type=F32)


def dot_back(left, right):
    return lax.dot_general(left, right, (((1,), (1,)), ((), ())), preferred_element_type=F32)


def dot_outer(left, right):
    return lax.dot_general(left, right, (((0,), (0,)), ((), ())), preferred_element_type=F32)


def row_mean(values):
    return jnp.sum(values, axis=-1, keepdims=True) * (1.0 / D)


def normalize(values):
    centred = values - row_mean(values)
    inverse = lax.rsqrt(row_mean(centred * centred) + EPSILON)
    return (centred * inverse, inverse)


def norm_back(upstream, normed, inverse, gain):
    scaled = upstream * gain
    centred = scaled - row_mean(scaled)
    return inverse * (centred - normed * row_mean(scaled * normed))


def rope(values, cosine, sine):
    lane = lax.broadcasted_iota(jnp.int32, values.shape, 1) % HEAD_DIM
    partner = jnp.where(
        lane < HEAD_DIM // 2,
        pltpu.roll(values, 128 - HEAD_DIM // 2, 1),
        pltpu.roll(values, HEAD_DIM // 2, 1),
    )
    return values * cosine + partner * sine


def call(kernel, outs, scratch, spaces, limit, place_outs="h"):
    kinds = {"v": pltpu.VMEM, "h": pltpu.HBM, "a": pl.ANY}
    return pl.pallas_call(
        kernel,
        out_shape=[jax.ShapeDtypeStruct(shape, kind) for shape, kind in outs],
        in_specs=[pl.BlockSpec(memory_space=kinds[c]) for c in spaces],
        out_specs=[pl.BlockSpec(memory_space=kinds[place_outs]) for _ in outs],
        scratch_shapes=scratch,
        compiler_params=pltpu.CompilerParams(vmem_limit_bytes=limit * MIB),
    )


def like(outs):
    return [pltpu.VMEM(shape, kind) for shape, kind in outs]


def copy_all(sources, targets, sems, first=0):
    return [
        pltpu.make_async_copy(a, b, sems.at[first + i])
        for i, (a, b) in enumerate(zip(sources, targets, strict=True))
    ]


def start_all(copies):
    for copy in copies:
        copy.start()


def wait_all(copies):
    for copy in copies:
        copy.wait()


def piece_places(pieces):
    x, zh, core, _ = place()
    return [
        (
            side * 8 + dx * 2 + dz,
            pieces[side * 8 + dx * 2 + dz],
            owner(x, zh, dx, dz),
            (core + side) % 2,
        )
        for side in range(2)
        for dx in range(4)
        for dz in range(2)
    ]


def joint_copies(pieces, joint_w, sems):
    return [
        pltpu.make_async_copy(
            piece.at[:, pl.ds(0, HALF)],
            joint_w.at[
                pl.ds(pl.multiple_of(who * ROWS, 16), ROWS),
                pl.ds(pl.multiple_of(half * HALF, 128), HALF),
            ],
            sems.at[i],
        )
        for i, piece, who, half in piece_places(pieces)
    ]


def gain_chunk(gain_ref, row, j):
    return gain_ref[row + j : row + j + 1, :]


def own_halves(value):
    return jnp.concatenate([value[:HEAD_DIM, :TILE], value[HEAD_DIM:, TILE:]], 0).T


JOINT_OUTS = [
    ((TOKENS, D), BF16),
    ((WIDE, D), BF16),
    ((WIDE, D), BF16),
    ((WIDE, D), BF16),
    ((TOKENS, D), BF16),
    ((PAIRS * TILES, 2 * TILE, 2 * TILE), BF16),
    ((16, 128), F32),
    ((D, 3 * D), BF16),
]


def joint_kernel(normed_ref, cos_ref, sin_ref, *refs):
    pieces, outs, refs = refs[:16], refs[16:24], refs[24:]
    q_ref, k_ref, v_ref, h_ref, att_ref, probs_ref, gain_ref, joint_w, gains, sems, out_sems = refs
    copies = joint_copies(pieces, joint_w, sems)
    gain_copies = [
        pltpu.make_async_copy(
            pieces[i].at[pl.ds(0, 16), pl.ds(HALF, 128)], gains.at[i], sems.at[16 + i]
        )
        for i in range(8)
    ]
    start_all(gain_copies)
    start_all(copies)
    wait_all(gain_copies)
    gain_ref[...] = jnp.sum(gains[...].astype(F32), axis=0)
    for j in range(D // 128):
        cols = slice(128 * j, 128 * (j + 1))
        h_ref[:, cols] = (normed_ref[:, cols] * gain_chunk(gain_ref, 0, j)).astype(BF16)
    wait_all(copies)
    sends = copy_all(refs[:5] + refs[6:8], outs[:5] + outs[6:8], out_sems)
    start_all(sends[5:])
    own = slice(RIM, RIM + TOKENS)
    for j in range(9):
        cols = slice(256 * j, 256 * (j + 1))
        rows = own if j < 3 else slice(0, WIDE)
        got = dot(h_ref[rows, :], joint_w[:, cols])
        out = (q_ref, k_ref, v_ref)[j // 3]
        for a in range(2):
            part = got[:, 128 * a : 128 * (a + 1)]
            if j < 6:
                part = rope(part, cos_ref[rows, :], sin_ref[rows, :])
            at = 256 * (j % 3) + 128 * a
            out[:, at : at + 128] = part.astype(BF16)

    start_all(sends[:4])
    offset = lax.axis_index("seq") * TOKENS
    place_of_key = lax.broadcasted_iota(jnp.int32, (2 * TILE, 2 * TILE), 0)
    place_of_query = lax.broadcasted_iota(jnp.int32, (2 * TILE, 2 * TILE), 1) % TILE
    lane = lax.broadcasted_iota(jnp.int32, (TILE, 128), 1)
    apart = place_of_key - place_of_query
    band = (apart >= 0) & (apart <= 2 * RIM)

    @pl.loop(0, PAIRS)
    def _(pair):
        lanes = pl.ds(pl.multiple_of(pair * 128, 128), 128)
        for t in range(TILES):
            key = place_of_key + (offset + t * TILE - RIM)
            allowed = band & (key >= 0) & (key < 16 * TOKENS)
            query = q_ref[t * TILE : (t + 1) * TILE, lanes].astype(F32) * (HEAD_DIM**-0.5)
            stacked = jnp.concatenate(
                [jnp.where(lane < HEAD_DIM, query, 0.0), jnp.where(lane < HEAD_DIM, 0.0, query)], 0
            ).astype(BF16)
            window = slice(t * TILE, (t + 2) * TILE)
            scores = jnp.where(allowed, dot_back(k_ref[window, lanes], stacked), -1e30)
            expo = jnp.exp(scores - jnp.max(scores, axis=0, keepdims=True))
            probs = (expo * (1.0 / jnp.sum(expo, axis=0, keepdims=True))).astype(BF16)
            probs_ref[pair * TILES + t] = probs
            mixed = dot_outer(v_ref[window, lanes], probs)
            att_ref[t * TILE : (t + 1) * TILE, lanes] = own_halves(mixed).astype(BF16)
        pltpu.make_async_copy(
            probs_ref.at[pl.ds(pair * TILES, TILES)],
            outs[5].at[pl.ds(pair * TILES, TILES)],
            out_sems.at[7 + pair],
        ).start()

    sends[4].start()
    wait_all(sends)
    for pair in range(PAIRS):
        tiles = pl.ds(pair * TILES, TILES)
        pltpu.make_async_copy(probs_ref.at[tiles], outs[5].at[tiles], out_sems.at[7 + pair]).wait()


def joint_forward(normed, cosine, sine, pieces):
    return call(
        joint_kernel,
        JOINT_OUTS,
        like(JOINT_OUTS)
        + [
            pltpu.VMEM((8, 16, 128), BF16),
            pltpu.SemaphoreType.DMA((24,)),
            pltpu.SemaphoreType.DMA((13,)),
        ],
        "vvv" + "a" * 16,
        20,
    )(normed, cosine, sine, *pieces)


def packed_copies(pieces, merge_w, expand_w, shrink_w, sems):
    merge, expand, shrink = [], [], []
    for i, piece, who, half in piece_places(pieces):
        rows = pl.ds(pl.multiple_of(who * ROWS, 16), ROWS)
        cols = pl.ds(pl.multiple_of(half * 384, 128), 384)
        merge.append(
            pltpu.make_async_copy(
                piece.at[pl.ds(0, ROWS), :], merge_w.at[rows, cols], sems.at[i * 5]
            )
        )
        for part in range(3):
            expand.append(
                pltpu.make_async_copy(
                    piece.at[pl.ds(ROWS * (part + 1), ROWS), :],
                    expand_w.at[rows, pl.ds(pl.multiple_of(half * FF + part * 384, 128), 384)],
                    sems.at[i * 5 + 1 + part],
                )
            )
        shrink.append(
            pltpu.make_async_copy(
                piece.at[pl.ds(4 * ROWS, FF_ROWS), :],
                shrink_w.at[pl.ds(pl.multiple_of(who * FF_ROWS, 16), FF_ROWS), cols],
                sems.at[i * 5 + 4],
            )
        )
    return merge, expand, shrink


MIDDLE_OUTS = [
    ((TOKENS, D), BF16),
    ((TOKENS, FF), BF16),
    ((TOKENS, D), BF16),
    ((TOKENS, D), F32),
    ((TOKENS, D), BF16),
]
MIDDLE_HALVES = [((TOKENS, FF), BF16)] * 2 + [((TOKENS, D // 2), BF16)] * 2


def middle_kernel(gain_ref, *refs):
    ins, pieces, refs = refs[:3], refs[3:19], refs[19:]
    outs, halves, refs = refs[:5], refs[5:9], refs[9:]
    x_ref, att_ref, dy_ref, out_ref, m_ref, h_ref, dx_ref, datt_ref = refs[:8]
    merge_w, expand_w, shrink_w, x1, normed, inverse, z, dm, dz, dob = refs[8:18]
    in_sems, weight_sems, out_sems = refs[18:]
    dz_mine, dz_give, dob_mine, dob_give = halves
    core = lax.axis_index("seq") % 2
    loads = copy_all(ins, (x_ref, att_ref, dy_ref), in_sems)
    merge, expand, shrink = packed_copies(pieces, merge_w, expand_w, shrink_w, weight_sems)
    start_all(loads)
    start_all(merge)
    start_all(shrink)
    start_all(expand)
    sends = copy_all(refs[3:8], outs, out_sems)
    wait_all(merge)
    wait_all(loads)
    for j in range(3):
        cols = slice(256 * j, 256 * (j + 1))
        x1[:, cols] = x_ref[:, cols].astype(F32) + dot(att_ref[...], merge_w[:, cols])

    step = 128
    gain = jnp.concatenate([gain_chunk(gain_ref, 8, j) for j in range(6)], 1)

    @pl.loop(0, TOKENS // step)
    def _(i):
        rows = pl.ds(pl.multiple_of(i * step, step), step)
        part, scale = normalize(x1[rows, :])
        normed[rows, :] = part
        inverse[rows, :] = scale
        h_ref[rows, :] = (part * gain).astype(BF16)

    wait_all(shrink)
    for j in range(3):
        cols = slice(384 * j, 384 * (j + 1))
        dm[:, cols] = dot_back(dy_ref[...], shrink_w[cols, :])
    wait_all(expand)
    for j in range(9):
        cols = slice(256 * j, 256 * (j + 1))
        z[:, cols] = dot(h_ref[...], expand_w[:, cols])

    @pl.loop(0, TOKENS // 16)
    def _(i):
        rows = pl.ds(pl.multiple_of(i * 16, 16), 16)
        gate = z[rows, pl.ds(0, FF)]
        up = z[rows, pl.ds(FF, FF)]
        upstream = dm[rows, :]
        below = 0.5 + 0.5 * lax.erf(gate * (0.5**0.5))
        slope = below + gate * (jnp.exp(-0.5 * gate * gate) * (2 * math.pi) ** -0.5)
        active = gate * below
        m_ref[rows, :] = (active * up).astype(BF16)
        dz[0, rows, :] = (upstream * up * slope).astype(BF16)
        dz[1, rows, :] = (upstream * active).astype(BF16)

    sends += copy_all((dz.at[core], dz.at[1 - core]), (dz_mine, dz_give), out_sems, 5)
    start_all(sends[1:3])
    start_all(sends[5:])
    for j in range(3):
        cols = slice(256 * j, 256 * (j + 1))
        out_ref[:, cols] = (x1[:, cols] + dot(m_ref[...], shrink_w[:, cols])).astype(BF16)
    start_all(sends[:1])
    for j in range(3):
        rows = slice(256 * j, 256 * (j + 1))
        x1[:, rows] = dot_back(dz[0], expand_w[rows, :FF]) + dot_back(dz[1], expand_w[rows, FF:])

    @pl.loop(0, TOKENS // step)
    def _(i):
        rows = pl.ds(pl.multiple_of(i * step, step), step)
        back = norm_back(x1[rows, :], normed[rows, :], inverse[rows, :], gain)
        total = dy_ref[rows, :].astype(F32) + back
        dx_ref[rows, :] = total
        dob[0, rows, :] = total[:, :384].astype(BF16)
        dob[1, rows, :] = total[:, 384:].astype(BF16)

    sends += copy_all((dob.at[core], dob.at[1 - core]), (dob_mine, dob_give), out_sems, 7)
    start_all(sends[7:])
    start_all(sends[3:4])
    for j in range(3):
        cols = slice(256 * j, 256 * (j + 1))
        datt_ref[:, cols] = (
            dot_back(dob[0], merge_w[cols, :384]) + dot_back(dob[1], merge_w[cols, 384:])
        ).astype(BF16)
    start_all(sends[4:5])
    wait_all(sends)


def middle(gains, x, att, dy, pieces):
    return call(
        middle_kernel,
        MIDDLE_OUTS + MIDDLE_HALVES,
        [pltpu.VMEM((TOKENS, D), BF16)] * 3
        + like(MIDDLE_OUTS)
        + [
            pltpu.VMEM((D, D), BF16),
            pltpu.VMEM((D, 2 * FF), BF16),
            pltpu.VMEM((FF, D), BF16),
            pltpu.VMEM((TOKENS, D), F32),
            pltpu.VMEM((TOKENS, D), F32),
            pltpu.VMEM((TOKENS, 1), F32),
            pltpu.VMEM((TOKENS, 2 * FF), F32),
            pltpu.VMEM((TOKENS, FF), F32),
            pltpu.VMEM((2, TOKENS, FF), BF16),
            pltpu.VMEM((2, TOKENS, D // 2), BF16),
            pltpu.SemaphoreType.DMA((3,)),
            pltpu.SemaphoreType.DMA((80,)),
            pltpu.SemaphoreType.DMA((9,)),
        ],
        "vaaa" + "a" * 16,
        32,
    )(gains, x, att, dy, *pieces)


def paired_copies(refs, buffers, sems):
    copies = []
    for n, buffer in enumerate(buffers):
        rows = buffer.shape[0] // 2
        for side in range(2):
            copies.append(
                pltpu.make_async_copy(
                    refs[2 * n + side], buffer.at[pl.ds(side * rows, rows), :], sems.at[2 * n + side]
                )
            )
    return copies


def pair_order(i):
    near, ring, far = i + 1 - 2 * (i % 2), 3 - i, (i + 2) % 4
    return [[(i, ring), (near, far)], [(i, near), (ring, far)]]


def early_kernel(*refs):
    ins, outs, refs = refs[:12], refs[12:16], refs[16:]
    h, dz, att, dob, m, dy, blocks, sems, out_sems = refs
    x, zh, _, seq = place()
    y = seq % 8 // 2
    copies = paired_copies(ins, (h, dz, att, dob, m, dy), sems)
    start_all(copies)
    blocks[3, :, ROWS:] = jnp.zeros((OWNERS, 48, 384), BF16)
    wait_all(copies[:4])
    for part in range(3):
        cols = slice(384 * part, 384 * (part + 1))
        grad = dot_outer(h[...], dz[:, cols]).astype(BF16).reshape(OWNERS, ROWS, 384)
        if part == 0:
            blocks[1, :, :ROWS] = grad
        elif part == 1:
            blocks[1, :, ROWS:] = grad[:, :48]
            blocks[2, :, :48] = grad[:, 48:]
        else:
            blocks[2, :, 48:] = grad
    wait_all(copies[4:8])
    grad = dot_outer(att[...], dob[...]).astype(BF16)
    blocks[3, :, :ROWS] = grad.reshape(OWNERS, ROWS, 384)
    wait_all(copies[8:])
    grad = dot_outer(m[...], dy[...]).astype(BF16)
    blocks[0] = grad.reshape(OWNERS, FF_ROWS, 384)
    sends = [
        pltpu.make_async_copy(
            blocks.at[quarter, owner(x, zh, color * 2 + dx, dz)],
            outs[color * 2 + side].at[n, dx * 2 + dz],
            out_sems.at[((color * 2 + side) * 2 + n) * 4 + dx * 2 + dz],
        )
        for color in range(2)
        for side in range(2)
        for n, quarter in enumerate(pair_order(y)[color][side])
        for dx in range(2)
        for dz in range(2)
    ]
    start_all(sends)
    wait_all(sends)


def early_grads(*args):
    return call(
        early_kernel,
        [((2, OWNERS // 2, FF_ROWS, 384), BF16)] * 4,
        [
            pltpu.VMEM((2 * TOKENS, D), BF16),
            pltpu.VMEM((2 * TOKENS, FF), BF16),
            pltpu.VMEM((2 * TOKENS, D), BF16),
            pltpu.VMEM((2 * TOKENS, D // 2), BF16),
            pltpu.VMEM((2 * TOKENS, FF), BF16),
            pltpu.VMEM((2 * TOKENS, D // 2), BF16),
            pltpu.VMEM((4, OWNERS, FF_ROWS, 384), BF16),
            pltpu.SemaphoreType.DMA((12,)),
            pltpu.SemaphoreType.DMA((32,)),
        ],
        "aa" * 6,
        18,
    )(*args)


def attention_back_kernel(cos_ref, sin_ref, *refs):
    ins, probs_in, mine_ref, give_ref, scratch = refs[:4], refs[4], refs[5], refs[6], refs[7:]
    q_ref, k_ref, v_ref, datt_ref, probs_ref, dk, dv, dj, in_sems, sems = scratch
    loads = copy_all(ins, scratch[:4], in_sems)
    start_all(loads)

    def load_probs(pair):
        tiles = pl.ds(pair * TILES, TILES)
        return pltpu.make_async_copy(probs_in.at[tiles], probs_ref.at[tiles], in_sems.at[4 + pair])

    for pair in range(PAIRS):
        load_probs(pair).start()
    core = lax.axis_index("seq") % 2
    lane = lax.broadcasted_iota(jnp.int32, (TILE, 128), 1)
    own = slice(RIM, RIM + TOKENS)
    dk[...] = jnp.zeros_like(dk)
    dv[...] = jnp.zeros_like(dv)
    dj[0, :RIM, :D] = jnp.zeros((RIM, D), BF16)
    dj[0, RIM + TOKENS :, :D] = jnp.zeros((RIM, D), BF16)
    wait_all(loads)
    scale = HEAD_DIM**-0.5

    @pl.loop(0, PAIRS)
    def _(pair):
        lanes = pl.ds(pl.multiple_of(pair * 128, 128), 128)
        load_probs(pair).wait()
        for t in range(TILES):
            rows = slice(t * TILE, (t + 1) * TILE)
            window = slice(t * TILE, (t + 2) * TILE)
            query = q_ref[rows, lanes].astype(F32) * scale
            query = jnp.concatenate(
                [jnp.where(lane < HEAD_DIM, query, 0.0), jnp.where(lane < HEAD_DIM, 0.0, query)], 0
            ).astype(BF16)
            upstream = datt_ref[rows, lanes].astype(F32)
            upstream = jnp.concatenate(
                [
                    jnp.where(lane < HEAD_DIM, upstream, 0.0),
                    jnp.where(lane < HEAD_DIM, 0.0, upstream),
                ],
                0,
            ).astype(BF16)
            probs_b = probs_ref[pair * TILES + t]
            probs = probs_b.astype(F32)
            dp = dot_back(v_ref[window, lanes], upstream)
            delta = jnp.sum(probs * dp, axis=0, keepdims=True)
            ds = (probs * (dp - delta)).astype(BF16)
            dv[window, lanes] += dot(probs_b, upstream)
            dk[window, lanes] += dot(ds, query)
            dq = own_halves(dot_outer(k_ref[window, lanes], ds)) * scale
            at = slice(RIM + t * TILE, RIM + (t + 1) * TILE)
            dj[0, at, lanes] = rope(dq, cos_ref[at, :], -sin_ref[at, :]).astype(BF16)

    for j in range(6):
        cols = slice(128 * j, 128 * (j + 1))
        part = rope(dk[:, cols], cos_ref[...], -sin_ref[...]).astype(BF16)
        if j < 3:
            dj[0, :, D + 128 * j : D + 128 * (j + 1)] = part
        else:
            dj[1, :, 128 * (j - 3) : 128 * (j - 2)] = part
    dj[1, :, D // 2 :] = dv[...].astype(BF16)
    sends = [
        pltpu.make_async_copy(dj.at[core], mine_ref, sems.at[0]),
        pltpu.make_async_copy(dj.at[1 - core], give_ref, sems.at[1]),
    ]
    start_all(sends)
    wait_all(sends)


def attention_back(*args):
    return call(
        attention_back_kernel,
        [((WIDE, HALF), BF16)] * 2,
        [
            pltpu.VMEM((TOKENS, D), BF16),
            pltpu.VMEM((WIDE, D), BF16),
            pltpu.VMEM((WIDE, D), BF16),
            pltpu.VMEM((TOKENS, D), BF16),
            pltpu.VMEM((PAIRS * TILES, 2 * TILE, 2 * TILE), BF16),
            pltpu.VMEM((WIDE, D), F32),
            pltpu.VMEM((WIDE, D), F32),
            pltpu.VMEM((2, WIDE, HALF), BF16),
            pltpu.SemaphoreType.DMA((10,)),
            pltpu.SemaphoreType.DMA((2,)),
        ],
        "vvaaaaa",
        18,
    )(*args)


def late_kernel(*refs):
    ins, outs, refs = refs[:4], refs[4:8], refs[8:]
    h, dj, blocks, sems, out_sems = refs
    x, zh, _, _ = place()
    copies = paired_copies(ins, (h, dj), sems)
    start_all(copies)
    wait_all(copies)
    for part in range(3):
        grad = dot_outer(h[...], dj[:, 384 * part : 384 * (part + 1)]).astype(BF16)
        blocks[:, ROWS * part : ROWS * (part + 1), :] = grad.reshape(OWNERS, ROWS, 384)
    blocks[:, 3 * ROWS :, :] = jnp.zeros((OWNERS, LATE_ROWS - 3 * ROWS, 384), BF16)
    sends = [
        pltpu.make_async_copy(
            blocks.at[to * 2 + (zh + color) % 2],
            outs[color * 2 + side].at[n],
            out_sems.at[(color * 2 + side) * 2 + n],
        )
        for color in range(2)
        for side in range(2)
        for n, to in enumerate(pair_order(x)[color][side])
    ]
    start_all(sends)
    wait_all(sends)


def late_grads(*args):
    return call(
        late_kernel,
        [((2, LATE_ROWS, 384), BF16)] * 4,
        [
            pltpu.VMEM((2 * WIDE, D), BF16),
            pltpu.VMEM((2 * WIDE, HALF), BF16),
            pltpu.VMEM((OWNERS, LATE_ROWS, 384), BF16),
            pltpu.SemaphoreType.DMA((4,)),
            pltpu.SemaphoreType.DMA((8,)),
        ],
        "aaaa",
        12,
    )(*args)


def sum_of(parts, index):
    return sum(part[index].astype(F32) for part in parts)


def pair_sum_kernel(*refs):
    ins, totals, parts, sems = refs[:8], refs[8:16], refs[16:24], refs[24]
    copies = copy_all(ins, parts, sems)
    start_all(copies)
    for i in range(4):
        wait_all(copies[2 * i : 2 * i + 2])
        kept, came = parts[2 * i], parts[2 * i + 1]
        for n in range(2):
            total = totals[2 * i + n]
            if len(total.shape) == 3:
                for k in range(total.shape[0]):
                    total[k] = (kept[n, k].astype(F32) + came[n, k].astype(F32)).astype(BF16)
            else:
                total[...] = (kept[n].astype(F32) + came[n].astype(F32)).astype(BF16)


def early_sum_kernel(*refs):
    parts, outs = refs[:4], refs[4:]
    for i in range(OWNERS):
        outs[i // 2][i % 2] = sum_of(parts[i // 4 * 2 : i // 4 * 2 + 2], i % 4).astype(BF16)


def late_sum_kernel(*refs):
    parts, outs = refs[:4], refs[4:]
    _, _, _, seq = place()
    y = seq % 8 // 2
    for d in range(4):
        rows = pl.ds(pl.multiple_of((y + d) % 4 * LATE_QUARTER, 16), LATE_QUARTER)
        for i in range(2):
            outs[d][i] = sum_of([part.at[rows] for part in parts[2 * i : 2 * i + 2]], ...).astype(BF16)


def both_sum_kernel(*refs):
    parts, outs = refs[:8], refs[8:]
    for i in range(2):
        outs[i][:FF_ROWS] = sum_of(parts[:4], i).astype(BF16)
        outs[i][FF_ROWS:] = sum_of(parts[4:], i).astype(BF16)


def pair_sum(parts):
    return call(
        pair_sum_kernel,
        [(part.shape[1:], BF16) for part in parts],
        [pltpu.VMEM(part.shape, part.dtype) for part in parts]
        + [pltpu.SemaphoreType.DMA((len(parts),))],
        "a" * len(parts),
        24,
        "v",
    )(*parts)


def summed(kernel, parts, shapes):
    outs = [(shape, BF16) for shape in shapes]
    return call(kernel, outs, [], "v" * len(parts), 12, "v")(*parts)


def early_sum(parts):
    return summed(early_sum_kernel, parts, [(2, FF_ROWS, 384)] * 4)


def late_sum(parts):
    return summed(late_sum_kernel, parts, [(2, LATE_QUARTER, 384)] * 4)


def both_sum(parts):
    return summed(both_sum_kernel, parts, [(FF_ROWS + LATE_QUARTER, 384)] * 2)


INPUT_OUTS = [((TOKENS, D), F32), ((RIM, D), BF16), ((RIM, D), BF16)]


def input_kernel(inverse_ref, gain_ref, *refs):
    (normed, dx, weight, mine, give), outs, refs = refs[:5], refs[5:8], refs[8:]
    base_ref, low_ref, high_ref, joint_w, dj, upstream, normed_ref, dx_ref, sems, out_sems = refs
    core = lax.axis_index("seq") % 2
    copies = [
        pltpu.make_async_copy(weight, joint_w, sems.at[0]),
        pltpu.make_async_copy(mine, dj.at[core], sems.at[1]),
        pltpu.make_async_copy(give, dj.at[1 - core], sems.at[2]),
        pltpu.make_async_copy(normed, normed_ref, sems.at[3]),
        pltpu.make_async_copy(dx, dx_ref, sems.at[4]),
    ]
    start_all(copies)
    wait_all(copies)
    for j in range(3):
        cols = slice(256 * j, 256 * (j + 1))
        upstream[:, cols] = dot_back(dj[0], joint_w[cols, :HALF]) + dot_back(
            dj[1], joint_w[cols, HALF:]
        )
    gain = jnp.concatenate([gain_chunk(gain_ref, 0, j) for j in range(6)], 1)
    step = 128

    def back(rows):
        return norm_back(upstream[rows, :], normed_ref[rows, :], inverse_ref[rows, :], gain)

    @pl.loop(0, TOKENS // step)
    def _(i):
        start = pl.multiple_of(i * step, step)
        base_ref[pl.ds(start, step), :] = dx_ref[pl.ds(start, step), :] + back(
            pl.ds(start + RIM, step)
        )

    low_ref[...] = back(pl.ds(0, RIM)).astype(BF16)
    high_ref[...] = back(pl.ds(RIM + TOKENS, RIM)).astype(BF16)
    sends = copy_all(refs[:3], outs, out_sems)
    start_all(sends)
    wait_all(sends)


def input_back(*args):
    return call(
        input_kernel,
        INPUT_OUTS,
        like(INPUT_OUTS)
        + [
            pltpu.VMEM((D, 3 * D), BF16),
            pltpu.VMEM((2, WIDE, HALF), BF16),
            pltpu.VMEM((WIDE, D), F32),
            pltpu.VMEM((WIDE, D), F32),
            pltpu.VMEM((TOKENS, D), F32),
            pltpu.SemaphoreType.DMA((5,)),
            pltpu.SemaphoreType.DMA((3,)),
        ],
        "vvaaaaa",
        20,
    )(*args)


RESULTS = [((ROWS, 3 * D), F32), ((ROWS, D), F32), ((ROWS, 2 * FF), F32), ((FF_ROWS, D), F32)]
GAIN_RESULTS = [((1, ROWS), F32)] * 2


def result_kernel(first_gain, second_gain, *refs):
    sums, weights, outs, refs = refs[:8], refs[8:10], refs[10:16], refs[16:]
    joint, merge, expand, shrink, first, second, early, late, sems = refs
    joint_w, expand_w = weights
    _, _, core, seq = place()
    y = seq % 8 // 2
    for side in range(2):
        half = (core + side) % 2
        for dy in range(4):
            quarter = (y + dy) % 4
            rows = pl.ds(pl.multiple_of(quarter * LATE_QUARTER, 16), LATE_QUARTER)
            early[half, quarter] = sums[side * 4 + dy][:FF_ROWS]
            late[half, rows] = sums[side * 4 + dy][FF_ROWS:]
    for half in range(2):
        cols = slice(384 * half, 384 * (half + 1))
        shrink[:, cols] = early[half, 0].astype(F32)
        merge[:, cols] = early[half, 3, :ROWS].astype(F32)
        at = FF * half
        expand[:, at : at + 384] = early[half, 1, :ROWS].astype(F32)
        expand[:48, at + 384 : at + 768] = early[half, 1, ROWS:].astype(F32)
        expand[48:, at + 384 : at + 768] = early[half, 2, :48].astype(F32)
        expand[:, at + 768 : at + FF] = early[half, 2, 48:].astype(F32)
        for part in range(3):
            cols = slice(FF * half + 384 * part, FF * half + 384 * (part + 1))
            joint[:, cols] = late[half, ROWS * part : ROWS * (part + 1)].astype(F32)
    sends = copy_all((joint, merge, expand, shrink, first, second), outs, sems)
    start_all(sends[:4])
    for total, weight, grad, gain in (
        (first, joint_w, joint, first_gain),
        (second, expand_w, expand, second_gain),
    ):
        product = sum(
            weight[:, 128 * j : 128 * (j + 1)].astype(F32) * grad[:, 128 * j : 128 * (j + 1)]
            for j in range(3 * D // 128)
        )
        total[...] = jnp.sum(product.T, axis=0, keepdims=True) / gain[...]
    start_all(sends[4:])
    wait_all(sends)


def results(*args):
    return call(
        result_kernel,
        RESULTS + GAIN_RESULTS,
        like(RESULTS + GAIN_RESULTS)
        + [
            pltpu.VMEM((2, 4, FF_ROWS, 384), BF16),
            pltpu.VMEM((2, LATE_ROWS, 384), BF16),
            pltpu.SemaphoreType.DMA((6,)),
        ],
        "v" * 12,
        12,
    )(*args)


def joint_part_kernel(gains, weight, out, tile, sems):
    fsdp = lax.axis_index("fsdp")
    _, _, core, _ = place()
    start = pl.multiple_of(core * HALF, 128)
    copies = [
        pltpu.make_async_copy(weight.at[:, pl.ds(start, HALF)], out.at[:, pl.ds(0, HALF)], sems.at[0]),
        pltpu.make_async_copy(tile, out.at[:, pl.ds(HALF, 128)], sems.at[1]),
    ]
    copies[0].start()
    placed = pltpu.roll(gains[...], fsdp * ROWS, 1)
    rows = []
    for i in range(2):
        rows += [placed[i : i + 1, 128 * j : 128 * (j + 1)] for j in range(6)]
        rows += [jnp.zeros((2, 128), F32)]
    tile[...] = jnp.concatenate([*rows, jnp.zeros((ROWS - 16, 128), F32)], 0).astype(BF16)
    copies[1].start()
    wait_all(copies)


def joint_part(gains, weight):
    return call(
        joint_part_kernel,
        [((ROWS, HALF + 128), BF16)],
        [pltpu.VMEM((ROWS, 128), BF16), pltpu.SemaphoreType.DMA((2,))],
        "vh",
        4,
    )(gains, weight)[0]


def other_parts_kernel(merge, expand, shrink, x, dy, *refs):
    packed, low, high, mine, give, sems = refs
    _, _, core, _ = place()
    half = pl.ds(pl.multiple_of(core * 384, 128), 384)
    rest = pl.ds(pl.multiple_of((1 - core) * 384, 128), 384)
    sources = [merge.at[:, half]]
    targets = [packed.at[pl.ds(0, ROWS)]]
    for i in range(3):
        sources.append(expand.at[:, pl.ds(pl.multiple_of(core * FF + 384 * i, 128), 384)])
        targets.append(packed.at[pl.ds(ROWS * (i + 1), ROWS)])
    sources += [shrink.at[:, half], x.at[pl.ds(TOKENS - RIM, RIM)], x.at[pl.ds(0, RIM)]]
    targets += [packed.at[pl.ds(4 * ROWS, FF_ROWS)], low, high]
    copies = copy_all(sources + [dy.at[:, half], dy.at[:, rest]], targets + [mine, give], sems)
    start_all(copies)
    wait_all(copies)


def other_parts(*args):
    return call(
        other_parts_kernel,
        [((PACKED, 384), BF16)] + [((RIM, D), BF16)] * 2 + [((TOKENS, D // 2), BF16)] * 2,
        [pltpu.SemaphoreType.DMA((9,))],
        "hhhhh",
        2,
    )(*args)


def gather_first(own):
    from_low, from_high = over_fsdp(own, 1, 0), over_fsdp(own, -1, 0)
    across = over_fsdp(own, 0, 1)
    return from_high, over_fsdp(own, 2, 0), from_low, across


def gather_second(own, from_high, from_far, from_low, across):
    across_low, across_high = over_fsdp(across, 1, 0), over_fsdp(across, -1, 0)
    across_far = over_fsdp(from_far, 0, 1)
    return [own, across, from_high, across_high, from_far, across_far, from_low, across_low]


def around(blocks, shift):
    return [blocks[0]] + [shift(blocks[d % 4], d) for d in (1, -1, 2)]


def over_x(value, d):
    return over_fsdp(value, d, 0)


def over_y(value, d):
    return over_seq(value, 0, d, 0)


def gather_quarters(own):
    from_low, from_high, from_far = (over_y(own, d) for d in (1, -1, 2))
    return [own, from_high, from_far, from_low]


def shards(
    inputs,
    first_gain,
    joint_weight,
    merge_weight,
    second_gain,
    expand_weight,
    shrink_weight,
    cotangent,
):
    x, zh, core, seq = place()
    fsdp = lax.axis_index("fsdp")
    source, upstream = inputs[0], cotangent[0]

    gains = jnp.pad(jnp.stack([first_gain, second_gain]), ((0, 6), (0, D - ROWS)))
    joint_own = joint_part(gains.astype(F32), joint_weight)
    packed_own, low_own, high_own, dy_mine, dy_give = other_parts(
        merge_weight, expand_weight, shrink_weight, source, upstream
    )
    joint_first = gather_first(joint_own)
    joint_mine = gather_second(joint_own, *joint_first)
    low_own, high_own, _ = lax.optimization_barrier((low_own, high_own, joint_first[3]))
    packed_own, _, _ = lax.optimization_barrier((packed_own, joint_mine[3], joint_mine[7]))
    low_halo = passed_along(low_own, 1)
    high_halo = passed_along(high_own, -1)
    packed_first = gather_first(packed_own)
    soon = [joint_mine[i] for i in (0, 1, 2, 4, 6)]
    *swapped, last = lax.optimization_barrier((*[core_swap(p) for p in soon], joint_mine[5]))
    joint_mine[5] = last

    frequencies = jnp.exp(
        jnp.arange(HEAD_DIM // 2, dtype=F32) * (-2.0 * math.log(10000.0) / HEAD_DIM)
    )
    positions = (seq * TOKENS - RIM + lax.iota(jnp.int32, WIDE)).astype(F32)
    angles = positions[:, None] * frequencies[None, :]
    cosine, sine = jnp.cos(angles), jnp.sin(angles)
    cosine = jnp.concatenate([cosine] * 4, 1)
    sine = jnp.concatenate([-sine, sine] * 2, 1)
    extended = jnp.concatenate([low_halo, source, high_halo], 0).astype(F32)
    normed, inverse = normalize(extended)

    *joint_mine, normed, cosine, sine = lax.optimization_barrier((*joint_mine, normed, cosine, sine))
    joint_swapped = [core_swap(joint_mine[i]) for i in (3, 5, 7)]
    joint_other = [swapped[0], swapped[1], swapped[2], joint_swapped[0], swapped[3]]
    joint_other += [joint_swapped[1], swapped[4], joint_swapped[2]]
    joint_pieces = joint_mine + joint_other
    q, k, v, h_first, attended, probs, gains, joint_w = joint_forward(
        normed, cosine, sine, joint_pieces
    )
    *packed_first, attended = lax.optimization_barrier((*packed_first, attended))
    packed_mine = gather_second(packed_own, *packed_first)
    packed_pieces = packed_mine + [core_swap(p) for p in packed_mine]
    dy_give, attended = lax.optimization_barrier((dy_give, attended))
    result, hidden, h_second, dx, datt, dz_mine, dz_give, dob_mine, dob_give = middle(
        gains, source, attended, upstream, packed_pieces
    )
    dj_mine, dj_give = attention_back(cosine, sine, q, k, v, datt, probs)
    swaps = [hidden, h_second, dz_give, attended, dob_give, h_first, dy_give]
    swaps = [core_swap(part) for part in swaps]
    *swaps, dj_mine, dj_give = lax.optimization_barrier((*swaps, dj_mine, dj_give))
    early = early_grads(
        h_second,
        swaps[1],
        dz_mine,
        swaps[2],
        attended,
        swaps[3],
        dob_mine,
        swaps[4],
        hidden,
        swaps[0],
        dy_mine,
        swaps[6],
    )
    early_came = [over_y_pair(early[1], 1), over_y_pair(early[3], 3)]
    dj_got, dj_mine, _ = lax.optimization_barrier((core_swap(dj_give), dj_mine, early[0]))
    late = late_grads(h_first, swaps[5], dj_mine, dj_got)
    late_own, dj_mine = lax.optimization_barrier((late[0], dj_mine))
    late_came = [over_x_pair(late[1], 1), over_x_pair(late[3], 3)]
    base, low_back, high_back = input_back(inverse, gains, normed, dx, joint_w, dj_mine, dj_give)
    *came, base = lax.optimization_barrier((*early_came, *late_came, base))
    from_high, from_low = passed_along(low_back, -1), passed_along(high_back, 1)
    *came, base, from_high, from_low = lax.optimization_barrier(
        (*early_came, *late_came, base, from_high, from_low)
    )
    input_grad = (
        base
        + jnp.pad(from_high.astype(F32), ((TOKENS - RIM, 0), (0, 0)))
        + jnp.pad(from_low.astype(F32), ((0, TOKENS - RIM), (0, 0)))
    ).astype(BF16)
    early_a, early_a_give, early_b, early_b_give, late_a, late_a_give, late_b, late_b_give = pair_sum(
        [early[0], came[0], early[2], came[1], late_own, came[2], late[2], came[3]]
    )
    early_parts = [early_a, over_y_pair(early_a_give, 3), early_b, over_y_pair(early_b_give, 1)]
    late_parts = [late_a, over_x_pair(late_a_give, 3), late_b, over_x_pair(late_b_give, 1)]
    *late_parts, input_grad = lax.optimization_barrier((*late_parts, input_grad))
    late_quarters = around(late_sum(late_parts), over_y)
    keep, give = both_sum(around(early_sum(early_parts), over_x) + late_quarters)
    keeps = keep.astype(F32) + over_seq(keep, 1, 0, 0).astype(F32)
    gives = over_fsdp(give, 0, 1).astype(F32) + over_both_z(give).astype(F32)
    own = gather_quarters((keeps + gives).astype(BF16))
    joint_grad, merge_grad, expand_grad, shrink_grad, first_grad, second_grad = results(
        first_gain.astype(F32)[None],
        second_gain.astype(F32)[None],
        *own,
        *[core_swap(part) for part in own],
        joint_weight,
        expand_weight,
    )
    return (
        result[None],
        input_grad[None],
        first_grad[0],
        joint_grad,
        merge_grad,
        second_grad[0],
        expand_grad,
        shrink_grad,
    )


def solution(mesh):
    placed = (
        P("fsdp", "seq", None),
        P("fsdp"),
        P("fsdp", None),
        P("fsdp", None),
        P("fsdp"),
        P("fsdp", None),
        P("fsdp", None),
        P("fsdp", "seq", None),
    )
    return jax.shard_map(
        shards,
        mesh=mesh,
        in_specs=placed,
        out_specs=(
            P("fsdp", "seq", None),
            P("fsdp", "seq", None),
            P("fsdp"),
            P("fsdp", None),
            P("fsdp", None),
            P("fsdp"),
            P("fsdp", None),
            P("fsdp", None),
        ),
        check_vma=False,
    )
```

```python
import math

import jax
import jax.numpy as jnp
from jax import lax
from jax.experimental import pallas as pl
from jax.experimental.pallas import tpu as pltpu
from jax.sharding import PartitionSpec as P

D = 768
HEADS = 12
HEAD_DIM = 64
FF = 1152
RIM = 64
TOKENS = 384
WIDE = TOKENS + 2 * RIM
TILE = 128
TILES = TOKENS // TILE
PAIRS = HEADS // 2
OWNERS = 8
ROWS = D // OWNERS
FF_ROWS = FF // OWNERS
HALF = 3 * D // 2
EARLY_ROWS = 448
EARLY_QUARTER = EARLY_ROWS // 4
LATE_ROWS = 384
LATE_QUARTER = LATE_ROWS // 4
PACKED = 4 * ROWS + FF_ROWS
EPSILON = 1e-05
F32 = jnp.float32
BF16 = jnp.bfloat16
MIB = 2**20


def over_fsdp(value, dx, dz):
    pairs = [
        (x * 2 + z, ((x + dx) % 4) * 2 + (z + dz) % 2) for x in range(4) for z in range(2)
    ]
    return lax.ppermute(value, "fsdp", pairs)


def over_seq(value, dz, dy, dc):
    pairs = [
        (z * 8 + y * 2 + c, ((z + dz) % 2) * 8 + ((y + dy) % 4) * 2 + (c + dc) % 2)
        for z in range(2)
        for y in range(4)
        for c in range(2)
    ]
    return lax.ppermute(value, "seq", pairs)


def over_x_pair(value, flip):
    pairs = [(x * 2 + z, (x ^ flip) * 2 + z) for x in range(4) for z in range(2)]
    return lax.ppermute(value, "fsdp", pairs)


def over_y_pair(value, flip):
    return lax.ppermute(value, "seq", [(s, s ^ (2 * flip)) for s in range(16)])


def over_both_z(value):
    pairs = [
        (f * 16 + s, (f ^ 1) * 16 + (s ^ 8)) for f in range(8) for s in range(16)
    ]
    return lax.ppermute(value, ("fsdp", "seq"), pairs)


def core_swap(value):
    return over_seq(value, 0, 0, 1)


def passed_along(value, steps):
    first, last = (max(0, -steps), min(16, 16 - steps))
    return lax.ppermute(value, "seq", [(i, i + steps) for i in range(first, last)])


def place():
    fsdp, seq = lax.axis_index("fsdp"), lax.axis_index("seq")
    return fsdp // 2, fsdp % 2, seq % 2, seq


def owner(x, zh, dx, dz):
    return ((x + dx) % 4) * 2 + (zh + dz) % 2


def dot(left, right):
    return jnp.dot(left, right, preferred_element_type=F32)


def dot_back(left, right):
    return lax.dot_general(left, right, (((1,), (1,)), ((), ())), preferred_element_type=F32)


def dot_outer(left, right):
    return lax.dot_general(left, right, (((0,), (0,)), ((), ())), preferred_element_type=F32)


def row_mean(values):
    return jnp.sum(values, axis=-1, keepdims=True) * (1.0 / D)


def normalize(values):
    centred = values - row_mean(values)
    inverse = lax.rsqrt(row_mean(centred * centred) + EPSILON)
    return (centred * inverse, inverse)


def norm_back(upstream, normed, inverse, gain):
    scaled = upstream * gain
    centred = scaled - row_mean(scaled)
    return inverse * (centred - normed * row_mean(scaled * normed))


def rope(values, cosine, sine):
    lane = lax.broadcasted_iota(jnp.int32, values.shape, 1) % HEAD_DIM
    partner = jnp.where(
        lane < HEAD_DIM // 2,
        pltpu.roll(values, 128 - HEAD_DIM // 2, 1),
        pltpu.roll(values, HEAD_DIM // 2, 1),
    )
    return values * cosine + partner * sine


def call(kernel, outs, scratch, spaces, limit, place_outs="h"):
    kinds = {"v": pltpu.VMEM, "h": pltpu.HBM, "a": pl.ANY}
    return pl.pallas_call(
        kernel,
        out_shape=[jax.ShapeDtypeStruct(shape, kind) for shape, kind in outs],
        in_specs=[pl.BlockSpec(memory_space=kinds[c]) for c in spaces],
        out_specs=[pl.BlockSpec(memory_space=kinds[place_outs]) for _ in outs],
        scratch_shapes=scratch,
        compiler_params=pltpu.CompilerParams(vmem_limit_bytes=limit * MIB),
    )


def like(outs):
    return [pltpu.VMEM(shape, kind) for shape, kind in outs]


def copy_all(sources, targets, sems, first=0):
    return [
        pltpu.make_async_copy(a, b, sems.at[first + i])
        for i, (a, b) in enumerate(zip(sources, targets, strict=True))
    ]


def start_all(copies):
    for copy in copies:
        copy.start()


def wait_all(copies):
    for copy in copies:
        copy.wait()


def piece_places(pieces):
    x, zh, core, _ = place()
    return [
        (
            side * 8 + dx * 2 + dz,
            pieces[side * 8 + dx * 2 + dz],
            owner(x, zh, dx, dz),
            (core + side) % 2,
        )
        for side in range(2)
        for dx in range(4)
        for dz in range(2)
    ]


def joint_copies(pieces, joint_w, sems):
    return [
        pltpu.make_async_copy(
            piece.at[:, pl.ds(0, HALF)],
            joint_w.at[
                pl.ds(pl.multiple_of(who * ROWS, 16), ROWS),
                pl.ds(pl.multiple_of(half * HALF, 128), HALF),
            ],
            sems.at[i],
        )
        for i, piece, who, half in piece_places(pieces)
    ]


def gain_chunk(gain_ref, row, j):
    return gain_ref[row + j : row + j + 1, :]


def own_halves(value):
    return jnp.concatenate([value[:HEAD_DIM, :TILE], value[HEAD_DIM:, TILE:]], 0).T


JOINT_OUTS = [
    ((TOKENS, D), BF16),
    ((WIDE, D), BF16),
    ((WIDE, D), BF16),
    ((WIDE, D), BF16),
    ((TOKENS, D), BF16),
    ((PAIRS * TILES, 2 * TILE, 2 * TILE), BF16),
    ((16, 128), F32),
    ((D, 3 * D), BF16),
]


def joint_kernel(normed_ref, cos_ref, sin_ref, *refs):
    pieces, outs, refs = refs[:16], refs[16:24], refs[24:]
    q_ref, k_ref, v_ref, h_ref, att_ref, probs_ref, gain_ref, joint_w, gains, sems, out_sems = refs
    copies = joint_copies(pieces, joint_w, sems)
    gain_copies = [
        pltpu.make_async_copy(
            pieces[i].at[pl.ds(0, 16), pl.ds(HALF, 128)], gains.at[i], sems.at[16 + i]
        )
        for i in range(8)
    ]
    start_all(gain_copies)
    start_all(copies)
    wait_all(gain_copies)
    gain_ref[...] = jnp.sum(gains[...].astype(F32), axis=0)
    for j in range(D // 128):
        cols = slice(128 * j, 128 * (j + 1))
        h_ref[:, cols] = (normed_ref[:, cols] * gain_chunk(gain_ref, 0, j)).astype(BF16)
    wait_all(copies)
    sends = copy_all(refs[:5] + refs[6:8], outs[:5] + outs[6:8], out_sems)
    start_all(sends[5:])
    own = slice(RIM, RIM + TOKENS)
    for j in range(9):
        cols = slice(256 * j, 256 * (j + 1))
        rows = own if j < 3 else slice(0, WIDE)
        got = dot(h_ref[rows, :], joint_w[:, cols])
        out = (q_ref, k_ref, v_ref)[j // 3]
        for a in range(2):
            part = got[:, 128 * a : 128 * (a + 1)]
            if j < 6:
                part = rope(part, cos_ref[rows, :], sin_ref[rows, :])
            at = 256 * (j % 3) + 128 * a
            out[:, at : at + 128] = part.astype(BF16)

    start_all(sends[:4])
    offset = lax.axis_index("seq") * TOKENS
    place_of_key = lax.broadcasted_iota(jnp.int32, (2 * TILE, 2 * TILE), 0)
    place_of_query = lax.broadcasted_iota(jnp.int32, (2 * TILE, 2 * TILE), 1) % TILE
    lane = lax.broadcasted_iota(jnp.int32, (TILE, 128), 1)
    apart = place_of_key - place_of_query
    band = (apart >= 0) & (apart <= 2 * RIM)

    @pl.loop(0, PAIRS)
    def _(pair):
        lanes = pl.ds(pl.multiple_of(pair * 128, 128), 128)
        for t in range(TILES):
            key = place_of_key + (offset + t * TILE - RIM)
            allowed = band & (key >= 0) & (key < 16 * TOKENS)
            query = q_ref[t * TILE : (t + 1) * TILE, lanes].astype(F32) * (HEAD_DIM**-0.5)
            stacked = jnp.concatenate(
                [jnp.where(lane < HEAD_DIM, query, 0.0), jnp.where(lane < HEAD_DIM, 0.0, query)], 0
            ).astype(BF16)
            window = slice(t * TILE, (t + 2) * TILE)
            scores = jnp.where(allowed, dot_back(k_ref[window, lanes], stacked), -1e30)
            expo = jnp.exp(scores - jnp.max(scores, axis=0, keepdims=True))
            probs = (expo * (1.0 / jnp.sum(expo, axis=0, keepdims=True))).astype(BF16)
            probs_ref[pair * TILES + t] = probs
            mixed = dot_outer(v_ref[window, lanes], probs)
            att_ref[t * TILE : (t + 1) * TILE, lanes] = own_halves(mixed).astype(BF16)
        pltpu.make_async_copy(
            probs_ref.at[pl.ds(pair * TILES, TILES)],
            outs[5].at[pl.ds(pair * TILES, TILES)],
            out_sems.at[7 + pair],
        ).start()

    sends[4].start()
    wait_all(sends)
    for pair in range(PAIRS):
        tiles = pl.ds(pair * TILES, TILES)
        pltpu.make_async_copy(probs_ref.at[tiles], outs[5].at[tiles], out_sems.at[7 + pair]).wait()


def joint_forward(normed, cosine, sine, pieces):
    return call(
        joint_kernel,
        JOINT_OUTS,
        like(JOINT_OUTS)
        + [
            pltpu.VMEM((8, 16, 128), BF16),
            pltpu.SemaphoreType.DMA((24,)),
            pltpu.SemaphoreType.DMA((13,)),
        ],
        "vvv" + "a" * 16,
        20,
    )(normed, cosine, sine, *pieces)


def packed_copies(pieces, merge_w, expand_w, shrink_w, sems):
    merge, expand, shrink = [], [], []
    for i, piece, who, half in piece_places(pieces):
        rows = pl.ds(pl.multiple_of(who * ROWS, 16), ROWS)
        cols = pl.ds(pl.multiple_of(half * 384, 128), 384)
        merge.append(
            pltpu.make_async_copy(
                piece.at[pl.ds(0, ROWS), :], merge_w.at[rows, cols], sems.at[i * 5]
            )
        )
        for part in range(3):
            expand.append(
                pltpu.make_async_copy(
                    piece.at[pl.ds(ROWS * (part + 1), ROWS), :],
                    expand_w.at[rows, pl.ds(pl.multiple_of(half * FF + part * 384, 128), 384)],
                    sems.at[i * 5 + 1 + part],
                )
            )
        shrink.append(
            pltpu.make_async_copy(
                piece.at[pl.ds(4 * ROWS, FF_ROWS), :],
                shrink_w.at[pl.ds(pl.multiple_of(who * FF_ROWS, 16), FF_ROWS), cols],
                sems.at[i * 5 + 4],
            )
        )
    return merge, expand, shrink


MIDDLE_OUTS = [
    ((TOKENS, D), BF16),
    ((TOKENS, FF), BF16),
    ((TOKENS, D), BF16),
    ((TOKENS, D), F32),
    ((TOKENS, D), BF16),
]
MIDDLE_HALVES = [((TOKENS, FF), BF16)] * 2 + [((TOKENS, D // 2), BF16)] * 2


def middle_kernel(gain_ref, *refs):
    ins, pieces, refs = refs[:3], refs[3:19], refs[19:]
    outs, halves, refs = refs[:5], refs[5:9], refs[9:]
    x_ref, att_ref, dy_ref, out_ref, m_ref, h_ref, dx_ref, datt_ref = refs[:8]
    merge_w, expand_w, shrink_w, x1, normed, inverse, z, dm, dz, dob = refs[8:18]
    in_sems, weight_sems, out_sems = refs[18:]
    dz_mine, dz_give, dob_mine, dob_give = halves
    core = lax.axis_index("seq") % 2
    loads = copy_all(ins, (x_ref, att_ref, dy_ref), in_sems)
    merge, expand, shrink = packed_copies(pieces, merge_w, expand_w, shrink_w, weight_sems)
    start_all(loads)
    start_all(merge)
    start_all(shrink)
    start_all(expand)
    sends = copy_all(refs[3:8], outs, out_sems)
    wait_all(merge)
    wait_all(loads)
    for j in range(3):
        cols = slice(256 * j, 256 * (j + 1))
        x1[:, cols] = x_ref[:, cols].astype(F32) + dot(att_ref[...], merge_w[:, cols])

    step = 128
    gain = jnp.concatenate([gain_chunk(gain_ref, 8, j) for j in range(6)], 1)

    @pl.loop(0, TOKENS // step)
    def _(i):
        rows = pl.ds(pl.multiple_of(i * step, step), step)
        part, scale = normalize(x1[rows, :])
        normed[rows, :] = part
        inverse[rows, :] = scale
        h_ref[rows, :] = (part * gain).astype(BF16)

    wait_all(shrink)
    for j in range(3):
        cols = slice(384 * j, 384 * (j + 1))
        dm[:, cols] = dot_back(dy_ref[...], shrink_w[cols, :])
    wait_all(expand)
    for j in range(9):
        cols = slice(256 * j, 256 * (j + 1))
        z[:, cols] = dot(h_ref[...], expand_w[:, cols])

    @pl.loop(0, TOKENS // 16)
    def _(i):
        rows = pl.ds(pl.multiple_of(i * 16, 16), 16)
        gate = z[rows, pl.ds(0, FF)]
        up = z[rows, pl.ds(FF, FF)]
        upstream = dm[rows, :]
        below = 0.5 + 0.5 * lax.erf(gate * (0.5**0.5))
        slope = below + gate * (jnp.exp(-0.5 * gate * gate) * (2 * math.pi) ** -0.5)
        active = gate * below
        m_ref[rows, :] = (active * up).astype(BF16)
        dz[0, rows, :] = (upstream * up * slope).astype(BF16)
        dz[1, rows, :] = (upstream * active).astype(BF16)

    sends += copy_all((dz.at[core], dz.at[1 - core]), (dz_mine, dz_give), out_sems, 5)
    start_all(sends[1:3])
    start_all(sends[5:])
    for j in range(3):
        cols = slice(256 * j, 256 * (j + 1))
        out_ref[:, cols] = (x1[:, cols] + dot(m_ref[...], shrink_w[:, cols])).astype(BF16)
    start_all(sends[:1])
    for j in range(3):
        rows = slice(256 * j, 256 * (j + 1))
        x1[:, rows] = dot_back(dz[0], expand_w[rows, :FF]) + dot_back(dz[1], expand_w[rows, FF:])

    @pl.loop(0, TOKENS // step)
    def _(i):
        rows = pl.ds(pl.multiple_of(i * step, step), step)
        back = norm_back(x1[rows, :], normed[rows, :], inverse[rows, :], gain)
        total = dy_ref[rows, :].astype(F32) + back
        dx_ref[rows, :] = total
        dob[0, rows, :] = total[:, :384].astype(BF16)
        dob[1, rows, :] = total[:, 384:].astype(BF16)

    sends += copy_all((dob.at[core], dob.at[1 - core]), (dob_mine, dob_give), out_sems, 7)
    start_all(sends[7:])
    start_all(sends[3:4])
    for j in range(3):
        cols = slice(256 * j, 256 * (j + 1))
        datt_ref[:, cols] = (
            dot_back(dob[0], merge_w[cols, :384]) + dot_back(dob[1], merge_w[cols, 384:])
        ).astype(BF16)
    start_all(sends[4:5])
    wait_all(sends)


def middle(gains, x, att, dy, pieces):
    return call(
        middle_kernel,
        MIDDLE_OUTS + MIDDLE_HALVES,
        [pltpu.VMEM((TOKENS, D), BF16)] * 3
        + like(MIDDLE_OUTS)
        + [
            pltpu.VMEM((D, D), BF16),
            pltpu.VMEM((D, 2 * FF), BF16),
            pltpu.VMEM((FF, D), BF16),
            pltpu.VMEM((TOKENS, D), F32),
            pltpu.VMEM((TOKENS, D), F32),
            pltpu.VMEM((TOKENS, 1), F32),
            pltpu.VMEM((TOKENS, 2 * FF), F32),
            pltpu.VMEM((TOKENS, FF), F32),
            pltpu.VMEM((2, TOKENS, FF), BF16),
            pltpu.VMEM((2, TOKENS, D // 2), BF16),
            pltpu.SemaphoreType.DMA((3,)),
            pltpu.SemaphoreType.DMA((80,)),
            pltpu.SemaphoreType.DMA((9,)),
        ],
        "vaaa" + "a" * 16,
        32,
    )(gains, x, att, dy, *pieces)


def paired_copies(refs, buffers, sems):
    copies = []
    for n, buffer in enumerate(buffers):
        rows = buffer.shape[0] // 2
        for side in range(2):
            copies.append(
                pltpu.make_async_copy(
                    refs[2 * n + side], buffer.at[pl.ds(side * rows, rows), :], sems.at[2 * n + side]
                )
            )
    return copies


def pair_order(i):
    near, ring, far = i + 1 - 2 * (i % 2), 3 - i, (i + 2) % 4
    return [[(i, ring), (near, far)], [(i, near), (ring, far)]]


def pair_outer(left, right, cols=slice(None)):
    return sum(dot_outer(a[...], b[:, cols]) for a, b in zip(left, right, strict=True))


def early_kernel(*refs):
    ins, outs, (blocks, out_sems) = refs[:8], refs[8:12], refs[12:]
    h, dz, m, dy = [ins[2 * i : 2 * i + 2] for i in range(4)]
    x, zh, _, seq = place()
    y = seq % 8 // 2
    for part in range(3):
        grad = pair_outer(h, dz, slice(384 * part, 384 * (part + 1))).astype(BF16)
        at = FF_ROWS + ROWS * part
        blocks[:, at : at + ROWS, :] = grad.reshape(OWNERS, ROWS, 384)
    blocks[:, :FF_ROWS, :] = pair_outer(m, dy).astype(BF16).reshape(OWNERS, FF_ROWS, 384)
    blocks[:, FF_ROWS + 3 * ROWS :, :] = jnp.zeros((OWNERS, 16, 384), BF16)
    sends = [
        pltpu.make_async_copy(
            blocks.at[
                owner(x, zh, color * 2 + dx, dz),
                pl.ds(pl.multiple_of(quarter * EARLY_QUARTER, 16), EARLY_QUARTER),
            ],
            outs[color * 2 + side].at[n, dx * 2 + dz],
            out_sems.at[((color * 2 + side) * 2 + n) * 4 + dx * 2 + dz],
        )
        for color in range(2)
        for side in range(2)
        for n, quarter in enumerate(pair_order(y)[color][side])
        for dx in range(2)
        for dz in range(2)
    ]
    start_all(sends)
    wait_all(sends)


def early_grads(*args):
    return call(
        early_kernel,
        [((2, OWNERS // 2, EARLY_QUARTER, 384), BF16)] * 4,
        [
            pltpu.VMEM((OWNERS, EARLY_ROWS, 384), BF16),
            pltpu.SemaphoreType.DMA((32,)),
        ],
        "vv" * 4,
        18,
    )(*args)


def attention_back_kernel(cos_ref, sin_ref, *refs):
    ins, probs_in, mine_ref, give_ref, scratch = refs[:4], refs[4], refs[5], refs[6], refs[7:]
    q_ref, k_ref, v_ref, datt_ref, probs_ref = *ins, probs_in
    dk, dv, dj, sems = scratch
    core = lax.axis_index("seq") % 2
    lane = lax.broadcasted_iota(jnp.int32, (TILE, 128), 1)
    own = slice(RIM, RIM + TOKENS)
    dk[...] = jnp.zeros_like(dk)
    dv[...] = jnp.zeros_like(dv)
    dj[0, :RIM, :D] = jnp.zeros((RIM, D), BF16)
    dj[0, RIM + TOKENS :, :D] = jnp.zeros((RIM, D), BF16)
    scale = HEAD_DIM**-0.5

    @pl.loop(0, PAIRS)
    def _(pair):
        lanes = pl.ds(pl.multiple_of(pair * 128, 128), 128)
        for t in range(TILES):
            rows = slice(t * TILE, (t + 1) * TILE)
            window = slice(t * TILE, (t + 2) * TILE)
            query = q_ref[rows, lanes].astype(F32) * scale
            query = jnp.concatenate(
                [jnp.where(lane < HEAD_DIM, query, 0.0), jnp.where(lane < HEAD_DIM, 0.0, query)], 0
            ).astype(BF16)
            upstream = datt_ref[rows, lanes].astype(F32)
            upstream = jnp.concatenate(
                [
                    jnp.where(lane < HEAD_DIM, upstream, 0.0),
                    jnp.where(lane < HEAD_DIM, 0.0, upstream),
                ],
                0,
            ).astype(BF16)
            probs_b = probs_ref[pair * TILES + t]
            probs = probs_b.astype(F32)
            dp = dot_back(v_ref[window, lanes], upstream)
            delta = jnp.sum(probs * dp, axis=0, keepdims=True)
            ds = (probs * (dp - delta)).astype(BF16)
            dv[window, lanes] += dot(probs_b, upstream)
            dk[window, lanes] += dot(ds, query)
            dq = own_halves(dot_outer(k_ref[window, lanes], ds)) * scale
            at = slice(RIM + t * TILE, RIM + (t + 1) * TILE)
            dj[0, at, lanes] = rope(dq, cos_ref[at, :], -sin_ref[at, :]).astype(BF16)

    for j in range(6):
        cols = slice(128 * j, 128 * (j + 1))
        part = rope(dk[:, cols], cos_ref[...], -sin_ref[...]).astype(BF16)
        if j < 3:
            dj[0, :, D + 128 * j : D + 128 * (j + 1)] = part
        else:
            dj[1, :, 128 * (j - 3) : 128 * (j - 2)] = part
    dj[1, :, D // 2 :] = dv[...].astype(BF16)
    sends = [
        pltpu.make_async_copy(dj.at[core], mine_ref, sems.at[0]),
        pltpu.make_async_copy(dj.at[1 - core], give_ref, sems.at[1]),
    ]
    start_all(sends)
    wait_all(sends)


def attention_back(*args):
    return call(
        attention_back_kernel,
        [((WIDE, HALF), BF16)] * 2,
        [
            pltpu.VMEM((WIDE, D), F32),
            pltpu.VMEM((WIDE, D), F32),
            pltpu.VMEM((2, WIDE, HALF), BF16),
            pltpu.SemaphoreType.DMA((2,)),
        ],
        "vvvvvvv",
        18,
    )(*args)


def late_kernel(*refs):
    ins, outs, (blocks, out_sems) = refs[:8], refs[8:12], refs[12:]
    h, dj, att, dob = [ins[2 * i : 2 * i + 2] for i in range(4)]
    x, zh, _, _ = place()
    for part in range(3):
        grad = pair_outer(h, dj, slice(384 * part, 384 * (part + 1))).astype(BF16)
        blocks[:, ROWS * part : ROWS * (part + 1), :] = grad.reshape(OWNERS, ROWS, 384)
    blocks[:, 3 * ROWS :, :] = pair_outer(att, dob).astype(BF16).reshape(OWNERS, ROWS, 384)
    sends = [
        pltpu.make_async_copy(
            blocks.at[to * 2 + (zh + color) % 2],
            outs[color * 2 + side].at[n],
            out_sems.at[(color * 2 + side) * 2 + n],
        )
        for color in range(2)
        for side in range(2)
        for n, to in enumerate(pair_order(x)[color][side])
    ]
    start_all(sends)
    wait_all(sends)


def late_grads(*args):
    return call(
        late_kernel,
        [((2, LATE_ROWS, 384), BF16)] * 4,
        [
            pltpu.VMEM((OWNERS, LATE_ROWS, 384), BF16),
            pltpu.SemaphoreType.DMA((8,)),
        ],
        "vvvvvvvv",
        14,
    )(*args)


def sum_of(parts, index):
    return sum(part[index].astype(F32) for part in parts)


def pair_sum_kernel(*refs):
    ins, totals, parts, sems = refs[:8], refs[8:16], refs[16:24], refs[24]
    copies = copy_all(ins, parts, sems)
    start_all(copies)
    for i in range(4):
        wait_all(copies[2 * i : 2 * i + 2])
        kept, came = parts[2 * i], parts[2 * i + 1]
        for n in range(2):
            total = totals[2 * i + n]
            if len(total.shape) == 3:
                for k in range(total.shape[0]):
                    total[k] = (kept[n, k].astype(F32) + came[n, k].astype(F32)).astype(BF16)
            else:
                total[...] = (kept[n].astype(F32) + came[n].astype(F32)).astype(BF16)


def early_sum_kernel(*refs):
    parts, outs = refs[:4], refs[4:]
    for i in range(OWNERS):
        outs[i // 2][i % 2] = sum_of(parts[i // 4 * 2 : i // 4 * 2 + 2], i % 4).astype(BF16)


def late_sum_kernel(*refs):
    parts, outs = refs[:4], refs[4:]
    _, _, _, seq = place()
    y = seq % 8 // 2
    for d in range(4):
        rows = pl.ds(pl.multiple_of((y + d) % 4 * LATE_QUARTER, 16), LATE_QUARTER)
        for i in range(2):
            outs[d][i] = sum_of([part.at[rows] for part in parts[2 * i : 2 * i + 2]], ...).astype(BF16)


def both_sum_kernel(*refs):
    parts, outs = refs[:8], refs[8:]
    for i in range(2):
        outs[i][:EARLY_QUARTER] = sum_of(parts[:4], i).astype(BF16)
        outs[i][EARLY_QUARTER:] = sum_of(parts[4:], i).astype(BF16)


def pair_sum(parts):
    return call(
        pair_sum_kernel,
        [(part.shape[1:], BF16) for part in parts],
        [pltpu.VMEM(part.shape, part.dtype) for part in parts]
        + [pltpu.SemaphoreType.DMA((len(parts),))],
        "a" * len(parts),
        24,
        "v",
    )(*parts)


def summed(kernel, parts, shapes):
    outs = [(shape, BF16) for shape in shapes]
    return call(kernel, outs, [], "v" * len(parts), 12, "v")(*parts)


def early_sum(parts):
    return summed(early_sum_kernel, parts, [(2, EARLY_QUARTER, 384)] * 4)


def late_sum(parts):
    return summed(late_sum_kernel, parts, [(2, LATE_QUARTER, 384)] * 4)


def both_sum(parts):
    return summed(both_sum_kernel, parts, [(EARLY_QUARTER + LATE_QUARTER, 384)] * 2)


INPUT_OUTS = [((TOKENS, D), F32), ((RIM, D), BF16), ((RIM, D), BF16)]


def input_kernel(inverse_ref, gain_ref, *refs):
    (normed, dx, weight, mine, give), outs, refs = refs[:5], refs[5:8], refs[8:]
    base_ref, low_ref, high_ref, joint_w, dj, upstream, normed_ref, dx_ref, sems, out_sems = refs
    core = lax.axis_index("seq") % 2
    copies = [
        pltpu.make_async_copy(weight, joint_w, sems.at[0]),
        pltpu.make_async_copy(mine, dj.at[core], sems.at[1]),
        pltpu.make_async_copy(give, dj.at[1 - core], sems.at[2]),
        pltpu.make_async_copy(normed, normed_ref, sems.at[3]),
        pltpu.make_async_copy(dx, dx_ref, sems.at[4]),
    ]
    start_all(copies)
    wait_all(copies)
    for j in range(3):
        cols = slice(256 * j, 256 * (j + 1))
        upstream[:, cols] = dot_back(dj[0], joint_w[cols, :HALF]) + dot_back(
            dj[1], joint_w[cols, HALF:]
        )
    gain = jnp.concatenate([gain_chunk(gain_ref, 0, j) for j in range(6)], 1)
    step = 128

    def back(rows):
        return norm_back(upstream[rows, :], normed_ref[rows, :], inverse_ref[rows, :], gain)

    @pl.loop(0, TOKENS // step)
    def _(i):
        start = pl.multiple_of(i * step, step)
        base_ref[pl.ds(start, step), :] = dx_ref[pl.ds(start, step), :] + back(
            pl.ds(start + RIM, step)
        )

    low_ref[...] = back(pl.ds(0, RIM)).astype(BF16)
    high_ref[...] = back(pl.ds(RIM + TOKENS, RIM)).astype(BF16)
    sends = copy_all(refs[:3], outs, out_sems)
    start_all(sends)
    wait_all(sends)


def input_back(*args):
    return call(
        input_kernel,
        INPUT_OUTS,
        like(INPUT_OUTS)
        + [
            pltpu.VMEM((D, 3 * D), BF16),
            pltpu.VMEM((2, WIDE, HALF), BF16),
            pltpu.VMEM((WIDE, D), F32),
            pltpu.VMEM((WIDE, D), F32),
            pltpu.VMEM((TOKENS, D), F32),
            pltpu.SemaphoreType.DMA((5,)),
            pltpu.SemaphoreType.DMA((3,)),
        ],
        "vvaaaaa",
        20,
    )(*args)


RESULTS = [((ROWS, 3 * D), F32), ((ROWS, D), F32), ((ROWS, 2 * FF), F32), ((FF_ROWS, D), F32)]
GAIN_RESULTS = [((1, ROWS), F32)] * 2


def result_kernel(first_gain, second_gain, *refs):
    sums, weights, outs, refs = refs[:8], refs[8:10], refs[10:16], refs[16:]
    joint, merge, expand, shrink, first, second, early, late, sems = refs
    joint_w, expand_w = weights
    _, _, core, seq = place()
    y = seq % 8 // 2
    for side in range(2):
        half = (core + side) % 2
        for dy in range(4):
            quarter = (y + dy) % 4
            rows = pl.ds(pl.multiple_of(quarter * EARLY_QUARTER, 16), EARLY_QUARTER)
            early[half, rows] = sums[side * 4 + dy][:EARLY_QUARTER]
            rows = pl.ds(pl.multiple_of(quarter * LATE_QUARTER, 16), LATE_QUARTER)
            late[half, rows] = sums[side * 4 + dy][EARLY_QUARTER:]
    for half in range(2):
        cols = slice(384 * half, 384 * (half + 1))
        shrink[:, cols] = early[half, :FF_ROWS].astype(F32)
        merge[:, cols] = late[half, 3 * ROWS :].astype(F32)
        for part in range(3):
            cols = slice(FF * half + 384 * part, FF * half + 384 * (part + 1))
            at = FF_ROWS + ROWS * part
            expand[:, cols] = early[half, at : at + ROWS].astype(F32)
            joint[:, cols] = late[half, ROWS * part : ROWS * (part + 1)].astype(F32)
    sends = copy_all((joint, merge, expand, shrink, first, second), outs, sems)
    start_all(sends[:4])
    for total, weight, grad, gain in (
        (first, joint_w, joint, first_gain),
        (second, expand_w, expand, second_gain),
    ):
        product = sum(
            weight[:, 128 * j : 128 * (j + 1)].astype(F32) * grad[:, 128 * j : 128 * (j + 1)]
            for j in range(3 * D // 128)
        )
        total[...] = jnp.sum(product.T, axis=0, keepdims=True) / gain[...]
    start_all(sends[4:])
    wait_all(sends)


def results(*args):
    return call(
        result_kernel,
        RESULTS + GAIN_RESULTS,
        like(RESULTS + GAIN_RESULTS)
        + [
            pltpu.VMEM((2, EARLY_ROWS, 384), BF16),
            pltpu.VMEM((2, LATE_ROWS, 384), BF16),
            pltpu.SemaphoreType.DMA((6,)),
        ],
        "v" * 12,
        12,
    )(*args)


def joint_part_kernel(gains, weight, out, tile, sems):
    fsdp = lax.axis_index("fsdp")
    _, _, core, _ = place()
    start = pl.multiple_of(core * HALF, 128)
    copies = [
        pltpu.make_async_copy(weight.at[:, pl.ds(start, HALF)], out.at[:, pl.ds(0, HALF)], sems.at[0]),
        pltpu.make_async_copy(tile, out.at[:, pl.ds(HALF, 128)], sems.at[1]),
    ]
    copies[0].start()
    placed = pltpu.roll(gains[...], fsdp * ROWS, 1)
    rows = []
    for i in range(2):
        rows += [placed[i : i + 1, 128 * j : 128 * (j + 1)] for j in range(6)]
        rows += [jnp.zeros((2, 128), F32)]
    tile[...] = jnp.concatenate([*rows, jnp.zeros((ROWS - 16, 128), F32)], 0).astype(BF16)
    copies[1].start()
    wait_all(copies)


def joint_part(gains, weight):
    return call(
        joint_part_kernel,
        [((ROWS, HALF + 128), BF16)],
        [pltpu.VMEM((ROWS, 128), BF16), pltpu.SemaphoreType.DMA((2,))],
        "vh",
        4,
    )(gains, weight)[0]


def other_parts_kernel(merge, expand, shrink, x, dy, *refs):
    packed, low, high, mine, give, sems = refs
    _, _, core, _ = place()
    half = pl.ds(pl.multiple_of(core * 384, 128), 384)
    rest = pl.ds(pl.multiple_of((1 - core) * 384, 128), 384)
    sources = [merge.at[:, half]]
    targets = [packed.at[pl.ds(0, ROWS)]]
    for i in range(3):
        sources.append(expand.at[:, pl.ds(pl.multiple_of(core * FF + 384 * i, 128), 384)])
        targets.append(packed.at[pl.ds(ROWS * (i + 1), ROWS)])
    sources += [shrink.at[:, half], x.at[pl.ds(TOKENS - RIM, RIM)], x.at[pl.ds(0, RIM)]]
    targets += [packed.at[pl.ds(4 * ROWS, FF_ROWS)], low, high]
    copies = copy_all(sources + [dy.at[:, half], dy.at[:, rest]], targets + [mine, give], sems)
    start_all(copies)
    wait_all(copies)


def other_parts(*args):
    return call(
        other_parts_kernel,
        [((PACKED, 384), BF16)] + [((RIM, D), BF16)] * 2 + [((TOKENS, D // 2), BF16)] * 2,
        [pltpu.SemaphoreType.DMA((9,))],
        "hhhhh",
        2,
    )(*args)


def gather_first(own):
    from_low, from_high = over_fsdp(own, 1, 0), over_fsdp(own, -1, 0)
    across = over_fsdp(own, 0, 1)
    return from_high, over_fsdp(own, 2, 0), from_low, across


def gather_second(own, from_high, from_far, from_low, across):
    across_low, across_high = over_fsdp(across, 1, 0), over_fsdp(across, -1, 0)
    across_far = over_fsdp(from_far, 0, 1)
    return [own, across, from_high, across_high, from_far, across_far, from_low, across_low]


def around(blocks, shift):
    return [blocks[0]] + [shift(blocks[d % 4], d) for d in (1, -1, 2)]


def over_x(value, d):
    return over_fsdp(value, d, 0)


def over_y(value, d):
    return over_seq(value, 0, d, 0)


def gather_quarters(own):
    from_low, from_high, from_far = (over_y(own, d) for d in (1, -1, 2))
    return [own, from_high, from_far, from_low]


def shards(
    inputs,
    first_gain,
    joint_weight,
    merge_weight,
    second_gain,
    expand_weight,
    shrink_weight,
    cotangent,
):
    x, zh, core, seq = place()
    fsdp = lax.axis_index("fsdp")
    source, upstream = inputs[0], cotangent[0]

    gains = jnp.pad(jnp.stack([first_gain, second_gain]), ((0, 6), (0, D - ROWS)))
    joint_own = joint_part(gains.astype(F32), joint_weight)
    packed_own, low_own, high_own, dy_mine, dy_give = other_parts(
        merge_weight, expand_weight, shrink_weight, source, upstream
    )
    joint_first = gather_first(joint_own)
    joint_mine = gather_second(joint_own, *joint_first)
    low_own, high_own, _ = lax.optimization_barrier((low_own, high_own, joint_first[3]))
    packed_own, _, _ = lax.optimization_barrier((packed_own, joint_mine[3], joint_mine[7]))
    low_halo = passed_along(low_own, 1)
    high_halo = passed_along(high_own, -1)
    packed_first = gather_first(packed_own)
    soon = [joint_mine[i] for i in (0, 1, 2, 4, 6)]
    *swapped, last = lax.optimization_barrier((*[core_swap(p) for p in soon], joint_mine[5]))
    joint_mine[5] = last

    frequencies = jnp.exp(
        jnp.arange(HEAD_DIM // 2, dtype=F32) * (-2.0 * math.log(10000.0) / HEAD_DIM)
    )
    positions = (seq * TOKENS - RIM + lax.iota(jnp.int32, WIDE)).astype(F32)
    angles = positions[:, None] * frequencies[None, :]
    cosine, sine = jnp.cos(angles), jnp.sin(angles)
    cosine = jnp.concatenate([cosine] * 4, 1)
    sine = jnp.concatenate([-sine, sine] * 2, 1)
    extended = jnp.concatenate([low_halo, source, high_halo], 0).astype(F32)
    normed, inverse = normalize(extended)

    *joint_mine, normed, cosine, sine = lax.optimization_barrier((*joint_mine, normed, cosine, sine))
    joint_swapped = [core_swap(joint_mine[i]) for i in (3, 5, 7)]
    joint_other = [swapped[0], swapped[1], swapped[2], joint_swapped[0], swapped[3]]
    joint_other += [joint_swapped[1], swapped[4], joint_swapped[2]]
    joint_pieces = joint_mine + joint_other
    q, k, v, h_first, attended, probs, gains, joint_w = joint_forward(
        normed, cosine, sine, joint_pieces
    )
    *packed_first, attended = lax.optimization_barrier((*packed_first, attended))
    packed_mine = gather_second(packed_own, *packed_first)
    packed_pieces = packed_mine + [core_swap(p) for p in packed_mine]
    dy_give, attended = lax.optimization_barrier((dy_give, attended))
    result, hidden, h_second, dx, datt, dz_mine, dz_give, dob_mine, dob_give = middle(
        gains, source, attended, upstream, packed_pieces
    )
    dj_mine, dj_give = attention_back(cosine, sine, q, k, v, datt, probs)
    swaps = [hidden, h_second, dz_give, attended, dob_give, h_first, dy_give]
    swaps = [core_swap(part) for part in swaps]
    *swaps, dj_mine, dj_give = lax.optimization_barrier((*swaps, dj_mine, dj_give))
    early = early_grads(
        h_second, swaps[1], dz_mine, swaps[2], hidden, swaps[0], dy_mine, swaps[6]
    )
    early_came = [over_y_pair(early[1], 1), over_y_pair(early[3], 3)]
    dj_got, dj_mine, _ = lax.optimization_barrier((core_swap(dj_give), dj_mine, early[0]))
    late = late_grads(
        h_first, swaps[5], dj_mine, dj_got, attended, swaps[3], dob_mine, swaps[4]
    )
    late_own, dj_mine = lax.optimization_barrier((late[0], dj_mine))
    late_came = [over_x_pair(late[1], 1), over_x_pair(late[3], 3)]
    base, low_back, high_back = input_back(inverse, gains, normed, dx, joint_w, dj_mine, dj_give)
    *came, base = lax.optimization_barrier((*early_came, *late_came, base))
    from_high, from_low = passed_along(low_back, -1), passed_along(high_back, 1)
    *came, base, from_high, from_low = lax.optimization_barrier(
        (*early_came, *late_came, base, from_high, from_low)
    )
    input_grad = (
        base
        + jnp.pad(from_high.astype(F32), ((TOKENS - RIM, 0), (0, 0)))
        + jnp.pad(from_low.astype(F32), ((0, TOKENS - RIM), (0, 0)))
    ).astype(BF16)
    early_a, early_a_give, early_b, early_b_give, late_a, late_a_give, late_b, late_b_give = pair_sum(
        [early[0], came[0], early[2], came[1], late_own, came[2], late[2], came[3]]
    )
    early_parts = [early_a, over_y_pair(early_a_give, 3), early_b, over_y_pair(early_b_give, 1)]
    late_parts = [late_a, over_x_pair(late_a_give, 3), late_b, over_x_pair(late_b_give, 1)]
    *late_parts, input_grad = lax.optimization_barrier((*late_parts, input_grad))
    late_quarters = around(late_sum(late_parts), over_y)
    keep, give = both_sum(around(early_sum(early_parts), over_x) + late_quarters)
    keeps = keep.astype(F32) + over_seq(keep, 1, 0, 0).astype(F32)
    gives = over_fsdp(give, 0, 1).astype(F32) + over_both_z(give).astype(F32)
    own = gather_quarters((keeps + gives).astype(BF16))
    joint_grad, merge_grad, expand_grad, shrink_grad, first_grad, second_grad = results(
        first_gain.astype(F32)[None],
        second_gain.astype(F32)[None],
        *own,
        *[core_swap(part) for part in own],
        joint_weight,
        expand_weight,
    )
    return (
        result[None],
        input_grad[None],
        first_grad[0],
        joint_grad,
        merge_grad,
        second_grad[0],
        expand_grad,
        shrink_grad,
    )


def solution(mesh):
    placed = (
        P("fsdp", "seq", None),
        P("fsdp"),
        P("fsdp", None),
        P("fsdp", None),
        P("fsdp"),
        P("fsdp", None),
        P("fsdp", None),
        P("fsdp", "seq", None),
    )
    return jax.shard_map(
        shards,
        mesh=mesh,
        in_specs=placed,
        out_specs=(
            P("fsdp", "seq", None),
            P("fsdp", "seq", None),
            P("fsdp"),
            P("fsdp", None),
            P("fsdp", None),
            P("fsdp"),
            P("fsdp", None),
            P("fsdp", None),
        ),
        check_vma=False,
    )
```
